32 devices in a mesh: groups: 2 (over y), dp: 8 (over z, x), width: 2 (over core).
Axes of the slice: x: 2, y: 2, z: 4, core: 2. Of those that a mesh axis runs over, the one named last changes fastest.
Arguments:
- decoder: bfloat16 [8192, 4096], P(('groups', 'dp'), 'width'), parts along dimension 0, may hold values from -0.09375 to 0.09375
- grad_out: bfloat16 [2048, 4096], P(('groups', 'dp'), 'width'), parts along dimension 0, may hold values from -6 to 6
- active_blocks: int32 [2048, 8], P(('groups', 'dp')), parts along dimension 0, may hold values from 0 to 31, as said below
- feature_idx: int32 [2048, 32], P(('groups', 'dp')), parts along dimension 0, may hold values from 0 to 127, as said below
- acts: bfloat16 [2048, 32], P(('groups', 'dp')), parts along dimension 0, may hold values from 0.19921875 to 5
- block_slot: int32 [64], P('groups'), parts along dimension 0, may hold values from 0 to 31, as said below
Outputs:
- decoder_grad: bfloat16 [8192, 4096], P(('groups', 'dp'), 'width'), parts along dimension 0
- act_grad: float32 [2048, 32], P(('groups', 'dp')), parts along dimension 0
The draws below stay inside these ranges and needn't reach their ends.
There are 2 independent parts, one for each index of `groups`. The reference program is written for one: setup_inputs(seed, part) draws one part's arguments, and reference() takes and returns one part's arrays. A program takes and returns all parts, laid end to end along the dimension named above; each array names one. Nothing has to cross between parts.
Inputs may be any that keep to these rules, and one draw needn't show every extreme that they name: `active_blocks`: the owner of block b is block_slot[b] // 4; each row names 8 blocks of 8 different owners; within the rows of one index of dp (aligned blocks of 128 rows) the blocks of one owner are named at most 128 times in all and one block by at most 43 rows, and both bounds are reached in every aligned block. `feature_idx`: the 4 entries of one active block of a row (columns a * 4 to a * 4 + 3) are distinct. A permutation; block b's weights are decoder rows block_slot[b] * 128 to block_slot[b] * 128 + 127.
All inputs are finite; a program needn't handle non-finite values.
Results may differ from the reference program's by a relative error of at most 0.001.
Values may be sent and summed in bfloat16 or wider, within the bound.
No kernel may reach another device: no remote copies, remote signals or barrier semaphores. Data moves between devices by JAX's collectives and lax.ppermute only.
A program may use at most 64 MiB of HBM per device.

```python
import math
import jax
import jax.numpy as jnp
from jax import lax

D = 4096
BW = 128
BLK_DEV = 4
ACT = 8
KPB = 4
TOK_DEV = 128
NBLOCKS = 32
TOKENS = 1024
N_DP = 8


def shared_order(key):
    return jax.random.permutation(key, NBLOCKS).astype(jnp.int32)


def draw_block_slot(key, part):
    stored = shared_order(key)
    return stored


def route_device(key):
    owner_count = TOKENS // TOK_DEV
    mean_load = TOK_DEV * ACT // owner_count
    spare = min(mean_load // 2, TOK_DEV - mean_load)
    subkeys = jax.random.split(key, 5)
    owner_order = jax.random.permutation(subkeys[0], owner_count).astype(jnp.int32)
    shifts = jax.random.randint(subkeys[1], (owner_count // 2,), 0, spare + 1).astype(jnp.int32)
    shifts = shifts.at[0].set(spare)
    counts = jnp.stack([mean_load + shifts, mean_load - shifts], axis=1).reshape(-1).astype(jnp.int32)
    finish = jnp.cumsum(counts).astype(jnp.int32)
    token_pos = jnp.arange(TOK_DEV * ACT, dtype=jnp.int32)
    position = jnp.sum((token_pos[:, None] >= finish[None, :]).astype(jnp.int32), axis=1)
    within = token_pos - finish[position] + counts[position]
    spread = jax.random.randint(subkeys[2], (owner_count,), 3, BLK_DEV + 1).astype(jnp.int32)
    spread = spread.at[0].set(3)
    offset = jax.random.randint(subkeys[3], (owner_count,), 0, BLK_DEV).astype(jnp.int32)
    block_here = (offset[position] + within % spread[position]) % BLK_DEV
    stored = owner_order[position] * BLK_DEV + block_here
    table = stored.reshape(ACT, TOK_DEV).T
    shuffle = jax.random.permutation(subkeys[4], TOK_DEV)
    return table[shuffle].astype(jnp.int32)


def draw_active_blocks(key, part):
    stored = shared_order(key)
    key = jax.random.fold_in(key, 11)
    inverse = jnp.zeros((NBLOCKS,), jnp.int32).at[stored].set(jnp.arange(NBLOCKS, dtype=jnp.int32))
    device_count = TOKENS // TOK_DEV
    tables = jax.vmap(lambda index: route_device(jax.random.fold_in(key, index)))(jnp.arange(device_count, dtype=jnp.int32))
    return inverse[tables.reshape(TOKENS, ACT)].astype(jnp.int32)


def draw_feature_idx(key, part):
    key = jax.random.fold_in(key, 7)
    subkeys = jax.random.split(key, TOKENS * ACT)
    chosen = jax.vmap(lambda subkey: jax.random.permutation(subkey, BW)[:KPB])(subkeys)
    return chosen.reshape(TOKENS, ACT * KPB).astype(jnp.int32)


def steps_of(stream_key, dims, pieces, smallest, largest):
    def one(axis_at, blocks):
        heights = jax.random.uniform(jax.random.fold_in(jax.random.fold_in(stream_key, 6), axis_at), (blocks,), jnp.float32, smallest / len(pieces), largest / len(pieces))
        return jnp.repeat(jnp.exp(heights), dims[axis_at] // blocks).reshape((-1,) + (1,) * (len(dims) - axis_at - 1))

    factor_of = one(*pieces[0])
    for cut in pieces[1:]:
        factor_of = factor_of * one(*cut)
    return factor_of


def centred(key, shape, scale, bound, shards=(), held_as=jnp.bfloat16):
    factor_of = steps_of(key, shape, shards, -0.22, 0.18) if shards else 1.0
    values = jax.random.normal(key, shape, jnp.float32) * scale * factor_of
    return jnp.minimum(jnp.maximum(values, -bound), bound).astype(held_as)


def setup_inputs(seed: int = 0, part: int = 0) -> dict:
    key_of = jax.random.split(jax.random.key(seed), 7)
    part_keys = jax.random.split(jax.random.fold_in(key_of[6], part), 7)
    decoder = centred(part_keys[0], (NBLOCKS * BW, D), D ** -0.5, 0.09375, ((0, 8), (1, 2)))
    grad_out = centred(part_keys[1], (TOKENS, D), 1.0, 6.0, ((0, 8), (1, 2)))
    active_blocks = draw_active_blocks(jax.random.fold_in(jax.random.fold_in(key_of[6], part), 71), part)
    feature_idx = draw_feature_idx(jax.random.fold_in(jax.random.fold_in(key_of[6], part), 71), part)
    acts = jnp.clip(jnp.exp(math.log(5.0) - 3.2227897 * jax.random.uniform(part_keys[4], (TOKENS, ACT * KPB), jnp.float32) ** steps_of(part_keys[4], (TOKENS, ACT * KPB), ((0, 8),), -0.2, 0.2)), 0.19921875, 5.0).astype(jnp.bfloat16)
    block_slot = draw_block_slot(jax.random.fold_in(jax.random.fold_in(key_of[6], part), 71), part)
    return dict(decoder=decoder, grad_out=grad_out, active_blocks=active_blocks, feature_idx=feature_idx, acts=acts, block_slot=block_slot)


def reference(decoder, grad_out, active_blocks, feature_idx, acts, block_slot):
    feature_row = (jnp.repeat(block_slot[active_blocks], KPB, axis=1) * BW + feature_idx).astype(jnp.int32)

    def add_block(step_idx, totals):
        grad_acc, act_acc = totals
        start = (step_idx * TOK_DEV).astype(jnp.int32)
        cotangent = lax.dynamic_slice_in_dim(grad_out, start, TOK_DEV, 0).astype(jnp.float32)
        rows_here = lax.dynamic_slice_in_dim(feature_row, start, TOK_DEV, 0)
        coeffs = lax.dynamic_slice_in_dim(acts, start, TOK_DEV, 0).astype(jnp.float32)
        weights = decoder[rows_here].astype(jnp.float32)
        act_part = jnp.einsum("rd,rkd->rk", cotangent, weights, precision=lax.Precision.HIGHEST)
        act_acc = lax.dynamic_update_slice_in_dim(act_acc, act_part, start, 0)
        terms = (coeffs[:, :, None] * cotangent[:, None, :]).reshape(-1, D)
        grad_acc = grad_acc.at[rows_here.reshape(-1)].add(terms)
        return grad_acc, act_acc

    initial = (jnp.zeros((NBLOCKS * BW, D), jnp.float32), jnp.zeros((TOKENS, ACT * KPB), jnp.float32))
    grad_acc, act_acc = lax.fori_loop(0, N_DP, add_block, initial)
    return grad_acc.astype(jnp.bfloat16), act_acc
```

```python
import jax
import jax.numpy as jnp
from jax import lax
from jax.sharding import PartitionSpec as P

BW = 128
BLK_DEV = 4
ACT = 8
KPB = 4


def slots_of(active_blocks, block_slot):
    table_pos = jnp.arange(block_slot.shape[0], dtype=jnp.int32)
    return jnp.sum(
        jnp.where(active_blocks[..., None] == table_pos, block_slot, 0), axis=-1
    )


def every_owner(decoder, grad_out, active_blocks, feature_idx, acts, block_slot):
    tok_rows, half_width = grad_out.shape
    owners = lax.axis_size("dp")
    slot_of = slots_of(active_blocks, block_slot)
    facts = jnp.concatenate(
        [
            slot_of.astype(jnp.float32),
            feature_idx.astype(jnp.float32),
            acts.astype(jnp.float32),
        ],
        axis=1,
    )
    facts = lax.all_gather(facts, "dp", axis=0, tiled=True)
    rows = lax.all_gather(grad_out, "dp", axis=0, tiled=True)
    tokens = rows.shape[0]
    me = lax.axis_index("dp")
    slots = facts[:, :ACT].astype(jnp.int32)
    mine = slots // BLK_DEV == me
    local = jnp.sum(jnp.where(mine, slots % BLK_DEV, 0), axis=1)
    feats = jnp.sum(
        jnp.where(mine[:, :, None], facts[:, ACT : ACT + ACT * KPB].reshape(tokens, ACT, KPB), 0),
        axis=1,
    ).astype(jnp.int32)
    coeffs = jnp.sum(
        jnp.where(mine[:, :, None], facts[:, ACT + ACT * KPB :].reshape(tokens, ACT, KPB), 0),
        axis=1,
    )
    at_row = local[:, None] * BW + feats
    row_axis = jnp.arange(BLK_DEV * BW, dtype=jnp.int32)
    scores = lax.dot_general(
        rows, decoder, (((1,), (1,)), ((), ())), preferred_element_type=jnp.float32
    )
    picked = jnp.stack(
        [
            jnp.sum(jnp.where(at_row[:, k : k + 1] == row_axis, scores, 0.0), axis=1)
            for k in range(KPB)
        ]
    )
    dense = jnp.zeros((tokens, BLK_DEV * BW), jnp.float32)
    for k in range(KPB):
        dense = jnp.where(at_row[:, k : k + 1] == row_axis, coeffs[:, k : k + 1], dense)
    dense = dense.astype(jnp.bfloat16)
    grads = lax.dot_general(
        dense, rows, (((0,), (0,)), ((), ())), preferred_element_type=jnp.float32
    )
    decoder_grad = grads.astype(jnp.bfloat16)
    returned = lax.all_to_all(
        picked.reshape(KPB, owners, tok_rows), "dp", split_axis=1, concat_axis=1, tiled=True
    )
    returned = lax.psum(returned, "width")
    act_grad = jnp.zeros((tok_rows, ACT, KPB), jnp.float32)
    for owner in range(owners):
        act_grad = jnp.where(
            (slot_of // BLK_DEV == owner)[:, :, None], returned[:, owner].T[:, None, :], act_grad
        )
    return (decoder_grad, act_grad.reshape(tok_rows, ACT * KPB))


def send_back(picked):
    return lax.all_to_all(picked, "dp", split_axis=1, concat_axis=1, tiled=True)


def pack_slots(grad_out, target, slots_all, pair_coeffs, pair_columns, source_row):
    slot_row = jnp.zeros((slots_all,), jnp.int32).at[target].set(source_row)
    used = jnp.zeros((slots_all,), jnp.bool_).at[target].set(True)
    send_rows = jnp.where(used[:, None], grad_out[slot_row], jnp.zeros((), grad_out.dtype))
    send_acts = jnp.zeros((slots_all, KPB), pair_coeffs.dtype).at[target].set(pair_coeffs)
    send_cols = jnp.zeros((slots_all, KPB), jnp.int32).at[target].set(pair_columns)
    return (send_rows, send_acts, send_cols)


def some_owners(decoder, grad_out, active_blocks, feature_idx, acts, block_slot):
    tok_rows, half_width = grad_out.shape
    owners = lax.axis_size("dp")
    mean_load = tok_rows * ACT // owners
    owner_cap = mean_load + min(mean_load // 2, tok_rows - mean_load)
    block_cap = (owner_cap + 2) // 3
    block_ids = active_blocks.reshape(-1)
    pair_count = block_ids.shape[0]
    table_pos = jnp.arange(block_slot.shape[0], dtype=jnp.int32)
    slot_of = jnp.sum(
        jnp.where(block_ids[:, None] == table_pos[None, :], block_slot[None, :], 0), axis=1
    )
    pair_pos = jnp.arange(pair_count, dtype=jnp.int32)
    source_row = pair_pos // ACT
    pair_coeffs = acts.reshape(pair_count, KPB)
    pair_feats = feature_idx.reshape(pair_count, KPB)
    earlier = (block_ids[:, None] == block_ids[None, :]) & (pair_pos[None, :] < pair_pos[:, None])
    position = jnp.sum(earlier.astype(jnp.int32), axis=1)
    slot_cols = owners * block_cap
    target = slot_of % BLK_DEV * slot_cols + slot_of // BLK_DEV * block_cap + position
    slots_all = BLK_DEV * slot_cols
    send_rows, send_acts, send_cols = pack_slots(
        grad_out, target, slots_all, pair_coeffs, pair_feats, source_row
    )
    rows, coeffs, feature_pos = (
        lax.all_to_all(
            send_rows.reshape(BLK_DEV, slot_cols, half_width),
            "dp",
            split_axis=1,
            concat_axis=1,
            tiled=True,
        ),
        lax.all_to_all(
            send_acts.reshape(BLK_DEV, slot_cols, KPB),
            "dp",
            split_axis=1,
            concat_axis=1,
            tiled=True,
        ),
        lax.all_to_all(
            send_cols.reshape(BLK_DEV, slot_cols, KPB),
            "dp",
            split_axis=1,
            concat_axis=1,
            tiled=True,
        ),
    )
    weights = decoder.reshape(BLK_DEV, BW, half_width)
    scores = jnp.einsum("bnd,bfd->bnf", rows, weights, preferred_element_type=jnp.float32)
    picked = jnp.take_along_axis(scores, feature_pos, axis=2)
    returned = send_back(picked)
    feature_axis = jnp.arange(BW, dtype=jnp.int32)
    matches = feature_pos[..., None] == feature_axis
    dense = jnp.sum(jnp.where(matches, coeffs[..., None].astype(jnp.float32), 0.0), axis=2).astype(
        jnp.bfloat16
    )
    grads = jnp.einsum("bnf,bnd->bfd", dense, rows, preferred_element_type=jnp.float32)
    decoder_grad = grads.astype(jnp.bfloat16).reshape(BLK_DEV * BW, half_width)
    pair_vals = returned.reshape(slots_all, KPB)[target]
    act_grad = pair_vals.reshape(tok_rows, ACT * KPB)
    act_grad = lax.psum(act_grad, "width")
    return (decoder_grad, act_grad)


def per_device(*args):
    if lax.axis_size("dp") == ACT:
        return every_owner(*args)
    return some_owners(*args)


def solution(mesh):
    in_specs = (
        P(("groups", "dp"), "width"),
        P(("groups", "dp"), "width"),
        P(("groups", "dp"), None),
        P(("groups", "dp"), None),
        P(("groups", "dp"), None),
        P("groups"),
    )
    out_specs = (P(("groups", "dp"), "width"), P(("groups", "dp"), None))
    return jax.shard_map(
        per_device, mesh=mesh, in_specs=in_specs, out_specs=out_specs, check_vma=False
    )
```

```python
import functools

import jax
import jax.numpy as jnp
from jax import lax
from jax.experimental import pallas as pl
from jax.experimental.pallas import tpu as pltpu
from jax.sharding import PartitionSpec as P

BW = 128
BLK_DEV = 4
ACT = 8
KPB = 4
SMEM = pl.BlockSpec(memory_space=pltpu.SMEM)
VMEM = pl.BlockSpec(memory_space=pltpu.VMEM)


def table_kernel(block_slot, active, feats, acts, table, slots, wide_acts):
    named = active[...]
    slot = jnp.zeros_like(named)
    for block in range(block_slot.shape[0]):
        slot = jnp.where(named == block, block_slot[block], slot)
    slots[...] = slot
    wide_acts[...] = acts[...].astype(jnp.float32)
    owner = slot // BLK_DEV
    first_row = slot % BLK_DEV * BW
    for k in range(KPB):
        at_row = (first_row + feats[pl.ds(k, ACT, stride=KPB), :]).astype(jnp.float32)
        coeff = wide_acts[pl.ds(k, ACT, stride=KPB), :]
        for o in range(table.shape[0]):
            mine = owner == o
            table[o, k, :] = jnp.sum(jnp.where(mine, at_row, 0.0), axis=0)
            table[o, KPB + k, :] = jnp.sum(jnp.where(mine, coeff, 0.0), axis=0)


def make_table(block_slot, active_blocks, feature_idx, acts, owners):
    tok_rows = active_blocks.shape[0]
    return pl.pallas_call(
        table_kernel,
        out_shape=(
            jax.ShapeDtypeStruct((owners, 2 * KPB, tok_rows), jnp.float32),
            jax.ShapeDtypeStruct((ACT, tok_rows), jnp.int32),
        ),
        in_specs=[SMEM, VMEM, VMEM, VMEM],
        out_specs=(VMEM, VMEM),
        scratch_shapes=[pltpu.VMEM((ACT * KPB, tok_rows), jnp.float32)],
        name="make_table",
    )(block_slot, active_blocks.T, feature_idx.T, acts.T)


def row_axis_of(rows, tok_rows):
    return lax.broadcasted_iota(jnp.int32, (rows, tok_rows), 0)


def dense_kernel(order, table, dense):
    rows, tokens = dense.shape
    tok_rows = tokens // table.shape[0]
    row_axis = row_axis_of(rows, tok_rows)
    for c in range(table.shape[0]):
        here = table[order[c]]
        at_row = here[:KPB].astype(jnp.int32)
        block = jnp.zeros((rows, tok_rows), jnp.float32)
        for k in range(KPB):
            block = jnp.where(
                row_axis == at_row[k : k + 1], here[KPB + k : KPB + k + 1], block
            )
        dense[:, c * tok_rows : (c + 1) * tok_rows] = block.astype(jnp.bfloat16)


def make_dense(order, table, rows):
    owners, _, tok_rows = table.shape
    return pl.pallas_call(
        dense_kernel,
        out_shape=jax.ShapeDtypeStruct((rows, owners * tok_rows), jnp.bfloat16),
        in_specs=[SMEM, VMEM],
        out_specs=VMEM,
        name="make_dense",
    )(order, table)


def score_kernel(first, count, has_before, order, table, decoder, *refs):
    chunks, refs = refs[: 2 * count], refs[2 * count :]
    if has_before:
        before, picked = refs
        picked[...] = before[...]
    else:
        (picked,) = refs
        picked[...] = jnp.zeros_like(picked)
    rows, half_width = decoder.shape
    tok_rows = table.shape[2]
    row_axis = row_axis_of(rows, tok_rows)
    cut = half_width // 2
    for c in range(count):
        scores = jnp.zeros((rows, tok_rows), jnp.float32)
        for side in range(2):
            scores += lax.dot_general(
                decoder[:, side * cut : (side + 1) * cut],
                chunks[2 * c + side][...],
                (((1,), (1,)), ((), ())),
                preferred_element_type=jnp.float32,
            )
        peer = order[first + c]
        at_row = table[peer, :KPB].astype(jnp.int32)
        for k in range(KPB):
            value = jnp.sum(
                jnp.where(row_axis == at_row[k : k + 1], scores, 0.0), axis=0
            )
            for side in range(2):
                picked[peer, side, k, :] = value


def score(first, chunks, order, table, decoder, before=None):
    owners, _, tok_rows = table.shape
    count = len(chunks)
    operands = [order, table, decoder] + [half for pair in chunks for half in pair]
    if before is not None:
        operands.append(before)
    return pl.pallas_call(
        functools.partial(score_kernel, first, count, before is not None),
        out_shape=jax.ShapeDtypeStruct((owners, 2, 2 * KPB, tok_rows), jnp.float32),
        in_specs=[SMEM] + [VMEM] * (len(operands) - 1),
        out_specs=VMEM,
        compiler_params=pltpu.CompilerParams(vmem_limit_bytes=40 * 2**20),
        name="score",
    )(*operands)


def grads_kernel(steps, dense, *refs):
    chunks, out = refs[:-1], refs[-1]

    def write(halves):
        rows = jnp.concatenate([half[...] for half in halves], axis=0)
        out[...] = jnp.dot(
            dense[...], rows, preferred_element_type=jnp.float32
        ).astype(out.dtype)

    @pl.when(pl.program_id(0) < steps)
    def _():
        write(chunks[0::2])

    @pl.when(pl.program_id(0) >= steps)
    def _():
        write(chunks[1::2])


def grads_of(dense, chunks, steps):
    rows = dense.shape[0]
    tok_rows, cut = chunks[0][0].shape
    block = cut // steps
    left = pl.BlockSpec((tok_rows, block), lambda i: (0, jnp.minimum(i, steps - 1)))
    right = pl.BlockSpec((tok_rows, block), lambda i: (0, jnp.maximum(i - steps, 0)))
    return pl.pallas_call(
        functools.partial(grads_kernel, steps),
        grid=(2 * steps,),
        out_shape=jax.ShapeDtypeStruct((rows, 2 * cut), jnp.bfloat16),
        in_specs=[pl.BlockSpec(dense.shape, lambda i: (0, 0))] + [left, right] * len(chunks),
        out_specs=pl.BlockSpec((rows, block), lambda i: (0, i)),
        compiler_params=pltpu.CompilerParams(vmem_limit_bytes=40 * 2**20),
        name="grads",
    )(dense, *[half for pair in chunks for half in pair])


def unpack_kernel(returned, slots, out):
    owner = slots[...] // BLK_DEV
    for k in range(KPB):
        total = jnp.zeros(owner.shape, jnp.float32)
        for o in range(returned.shape[0]):
            value = returned[o, 0, k : k + 1, :] + returned[o, 1, k : k + 1, :]
            total = jnp.where(owner == o, value, total)
        out[pl.ds(k, ACT, stride=KPB), :] = total


def unpack(returned, slots):
    tok_rows = slots.shape[1]
    return pl.pallas_call(
        unpack_kernel,
        out_shape=jax.ShapeDtypeStruct((ACT * KPB, tok_rows), jnp.float32),
        in_specs=[VMEM, VMEM],
        out_specs=VMEM,
        name="unpack",
    )(returned, slots).T


def every_owner(decoder, grad_out, active_blocks, feature_idx, acts, block_slot):
    tok_rows, half_width = grad_out.shape
    owners = lax.axis_size("dp")
    half_ring = owners // 2
    ring = list(range(0, owners, 2)) + list(range(owners - 1, 0, -2))
    onward = [(ring[i], ring[(i + 1) % owners]) for i in range(owners)]
    back = [(there, here) for here, there in onward]

    me = lax.axis_index("dp")
    place = jnp.where(me % 2 == 0, me // 2, owners - 1 - me // 2)
    offsets = [0]
    for d in range(1, half_ring):
        offsets += [-d, d]
    offsets.append(half_ring)
    at = (place + jnp.array(offsets, jnp.int32)) % owners
    order = jnp.where(at < half_ring, 2 * at, 2 * (owners - 1 - at) + 1)

    cut = half_width // 2
    own = (grad_out[:, :cut], grad_out[:, cut:])
    chunks = [own]
    ahead, behind = own, own
    for d in range(1, half_ring):
        ahead = tuple(lax.ppermute(half, "dp", onward) for half in ahead)
        behind = tuple(lax.ppermute(half, "dp", back) for half in behind)
        chunks += [ahead, behind]
    chunks.append((lax.ppermute(ahead[0], "dp", onward), lax.ppermute(behind[1], "dp", back)))

    table, slots = make_table(block_slot, active_blocks, feature_idx, acts, owners)
    table = lax.all_to_all(table, "dp", 0, 0, tiled=True)
    dense = make_dense(order, table, decoder.shape[0])
    early = 2 * half_ring - 3
    picked = score(0, chunks[:early], order, table, decoder)
    picked = score(early, chunks[early:], order, table, decoder, picked)
    sent = picked.reshape((2 * owners,) + picked.shape[2:])
    returned = lax.all_to_all(sent, ("dp", "width"), 0, 0, tiled=True)
    decoder_grad = grads_of(dense, chunks, 4)
    act_grad = unpack(returned.reshape(picked.shape), slots)
    return (decoder_grad, act_grad)


def send_back(picked):
    return lax.all_to_all(picked, "dp", split_axis=1, concat_axis=1, tiled=True)


def pack_slots(grad_out, target, slots_all, pair_coeffs, pair_columns, source_row):
    slot_row = jnp.zeros((slots_all,), jnp.int32).at[target].set(source_row)
    used = jnp.zeros((slots_all,), jnp.bool_).at[target].set(True)
    send_rows = jnp.where(used[:, None], grad_out[slot_row], jnp.zeros((), grad_out.dtype))
    send_acts = jnp.zeros((slots_all, KPB), pair_coeffs.dtype).at[target].set(pair_coeffs)
    send_cols = jnp.zeros((slots_all, KPB), jnp.int32).at[target].set(pair_columns)
    return (send_rows, send_acts, send_cols)


def some_owners(decoder, grad_out, active_blocks, feature_idx, acts, block_slot):
    tok_rows, half_width = grad_out.shape
    owners = lax.axis_size("dp")
    mean_load = tok_rows * ACT // owners
    owner_cap = mean_load + min(mean_load // 2, tok_rows - mean_load)
    block_cap = (owner_cap + 2) // 3
    block_ids = active_blocks.reshape(-1)
    pair_count = block_ids.shape[0]
    table_pos = jnp.arange(block_slot.shape[0], dtype=jnp.int32)
    slot_of = jnp.sum(
        jnp.where(block_ids[:, None] == table_pos[None, :], block_slot[None, :], 0), axis=1
    )
    pair_pos = jnp.arange(pair_count, dtype=jnp.int32)
    source_row = pair_pos // ACT
    pair_coeffs = acts.reshape(pair_count, KPB)
    pair_feats = feature_idx.reshape(pair_count, KPB)
    earlier = (block_ids[:, None] == block_ids[None, :]) & (pair_pos[None, :] < pair_pos[:, None])
    position = jnp.sum(earlier.astype(jnp.int32), axis=1)
    slot_cols = owners * block_cap
    target = slot_of % BLK_DEV * slot_cols + slot_of // BLK_DEV * block_cap + position
    slots_all = BLK_DEV * slot_cols
    send_rows, send_acts, send_cols = pack_slots(
        grad_out, target, slots_all, pair_coeffs, pair_feats, source_row
    )
    rows, coeffs, feature_pos = (
        lax.all_to_all(
            send_rows.reshape(BLK_DEV, slot_cols, half_width),
            "dp",
            split_axis=1,
            concat_axis=1,
            tiled=True,
        ),
        lax.all_to_all(
            send_acts.reshape(BLK_DEV, slot_cols, KPB),
            "dp",
            split_axis=1,
            concat_axis=1,
            tiled=True,
        ),
        lax.all_to_all(
            send_cols.reshape(BLK_DEV, slot_cols, KPB),
            "dp",
            split_axis=1,
            concat_axis=1,
            tiled=True,
        ),
    )
    weights = decoder.reshape(BLK_DEV, BW, half_width)
    scores = jnp.einsum("bnd,bfd->bnf", rows, weights, preferred_element_type=jnp.float32)
    picked = jnp.take_along_axis(scores, feature_pos, axis=2)
    returned = send_back(picked)
    feature_axis = jnp.arange(BW, dtype=jnp.int32)
    matches = feature_pos[..., None] == feature_axis
    dense = jnp.sum(jnp.where(matches, coeffs[..., None].astype(jnp.float32), 0.0), axis=2).astype(
        jnp.bfloat16
    )
    grads = jnp.einsum("bnf,bnd->bfd", dense, rows, preferred_element_type=jnp.float32)
    decoder_grad = grads.astype(jnp.bfloat16).reshape(BLK_DEV * BW, half_width)
    pair_vals = returned.reshape(slots_all, KPB)[target]
    act_grad = pair_vals.reshape(tok_rows, ACT * KPB)
    act_grad = lax.psum(act_grad, "width")
    return (decoder_grad, act_grad)


def per_device(*args):
    if lax.axis_size("dp") == ACT:
        return every_owner(*args)
    return some_owners(*args)


def solution(mesh):
    in_specs = (
        P(("groups", "dp"), "width"),
        P(("groups", "dp"), "width"),
        P(("groups", "dp"), None),
        P(("groups", "dp"), None),
        P(("groups", "dp"), None),
        P("groups"),
    )
    out_specs = (P(("groups", "dp"), "width"), P(("groups", "dp"), None))
    return jax.shard_map(
        per_device, mesh=mesh, in_specs=in_specs, out_specs=out_specs, check_vma=False
    )
```

```python
import functools

import jax
import jax.numpy as jnp
from jax import lax
from jax.experimental import pallas as pl
from jax.experimental.pallas import tpu as pltpu
from jax.sharding import PartitionSpec as P

BW = 128
BLK_DEV = 4
ACT = 8
KPB = 4
SMEM = pl.BlockSpec(memory_space=pltpu.SMEM)
VMEM = pl.BlockSpec(memory_space=pltpu.VMEM)
ANY = pl.BlockSpec(memory_space=pl.ANY)
LIMIT = pltpu.CompilerParams(vmem_limit_bytes=40 * 2**20)


def kept(x):
    return pltpu.with_memory_space_constraint(x, pltpu.VMEM)


def prepare_kernel(
    block_slot, active, feats, acts, decoder, table, slots, decoder_here, wide_acts, sem
):
    load = pltpu.make_async_copy(decoder, decoder_here, sem)
    load.start()
    named = active[...]
    slot = jnp.zeros_like(named)
    for block in range(block_slot.shape[0]):
        slot = jnp.where(named == block, block_slot[block], slot)
    slots[...] = slot
    wide_acts[...] = acts[...].astype(jnp.float32)
    owner = slot // BLK_DEV
    first_row = slot % BLK_DEV * BW
    for k in range(KPB):
        at_row = (first_row + feats[pl.ds(k, ACT, stride=KPB), :]).astype(jnp.float32)
        coeff = wide_acts[pl.ds(k, ACT, stride=KPB), :]
        for o in range(table.shape[0]):
            mine = owner == o
            table[o, k, :] = jnp.sum(jnp.where(mine, at_row, 0.0), axis=0)
            table[o, KPB + k, :] = jnp.sum(jnp.where(mine, coeff, 0.0), axis=0)
    load.wait()


def prepare(block_slot, active_blocks, feature_idx, acts, decoder, owners):
    tok_rows = active_blocks.shape[0]
    return pl.pallas_call(
        prepare_kernel,
        out_shape=(
            pltpu.VMEM((owners, 2 * KPB, tok_rows), jnp.float32),
            pltpu.VMEM((ACT, tok_rows), jnp.int32),
            pltpu.VMEM(decoder.shape, decoder.dtype),
        ),
        in_specs=[SMEM, VMEM, VMEM, VMEM, ANY],
        out_specs=(VMEM, VMEM, VMEM),
        scratch_shapes=[
            pltpu.VMEM((ACT * KPB, tok_rows), jnp.float32),
            pltpu.SemaphoreType.DMA,
        ],
        name="prepare",
    )(block_slot, active_blocks.T, feature_idx.T, acts.T, decoder)


def ring_of(owners):
    return list(range(0, owners, 2)) + list(range(owners - 1, 0, -2))


def peer_at(distance, owners):
    me = lax.axis_index("dp")
    half_ring = owners // 2
    place = jnp.where(lax.rem(me, 2) == 0, lax.div(me, 2), owners - 1 - lax.div(me, 2))
    at = lax.rem(place + owners + distance, owners)
    return jnp.where(at < half_ring, 2 * at, 2 * (owners - 1 - at) + 1)


def block_and_rows(here):
    at_row = here[:KPB].astype(jnp.int32)
    return at_row[:1] // BW, at_row % BW


def row_axis_of(tok_rows):
    return lax.broadcasted_iota(jnp.int32, (BW, tok_rows), 0)


def coefficients(here):
    block, feats = block_and_rows(here)
    row_axis = row_axis_of(here.shape[1])
    dense = jnp.zeros(row_axis.shape, jnp.float32)
    for k in range(KPB):
        dense = jnp.where(row_axis == feats[k : k + 1], here[KPB + k : KPB + k + 1], dense)
    parts = [jnp.where(block == b, dense, 0.0) for b in range(BLK_DEV)]
    return jnp.concatenate(parts, axis=0).astype(jnp.bfloat16)


def pick(scores, here):
    block, feats = block_and_rows(here)
    row_axis = row_axis_of(here.shape[1])
    mine = scores[:BW]
    for b in range(1, BLK_DEV):
        mine = jnp.where(block == b, scores[b * BW : (b + 1) * BW], mine)
    return [
        jnp.sum(jnp.where(row_axis == feats[k : k + 1], mine, 0.0), axis=0)
        for k in range(KPB)
    ]


def add_picks(peers, table, decoder, chunks, picked):
    tok_rows, cut = chunks[0].shape
    for first in range(0, len(peers), 2):
        some = peers[first : first + 2]
        scores = None
        for side in range(2):
            halves = [chunks[2 * (first + i) + side][...] for i in range(len(some))]
            rows = jnp.concatenate(halves, axis=0) if len(halves) > 1 else halves[0]
            part = lax.dot_general(
                decoder[:, side * cut : (side + 1) * cut],
                rows,
                (((1,), (1,)), ((), ())),
                preferred_element_type=jnp.float32,
            )
            scores = part if scores is None else scores + part
        for i, peer in enumerate(some):
            values = pick(scores[:, i * tok_rows : (i + 1) * tok_rows], table[peer])
            for k in range(KPB):
                for width in range(2):
                    picked[peer, width, k, :] = values[k]


def gradient_blocks(peers, table, chunks, block):
    cut = chunks[0].shape[1]
    dense = jnp.concatenate([coefficients(table[peer]) for peer in peers], axis=1)
    for side in range(2):
        for start in range(0, cut, block):
            rows = jnp.concatenate(
                [half[:, start : start + block] for half in chunks[side::2]], axis=0
            )
            part = jnp.dot(dense, rows, preferred_element_type=jnp.float32)
            yield slice(side * cut + start, side * cut + start + block), part


def absorb_kernel(distances, later, table, decoder, *refs):
    count = len(distances)
    chunks, refs = refs[: 2 * count], refs[2 * count :]
    picked, total = refs[-2:]
    peers = [peer_at(d, table.shape[0]) for d in distances]
    picked[...] = refs[0][...] if later else jnp.zeros_like(picked)
    add_picks(peers, table, decoder, chunks, picked)
    for columns, part in gradient_blocks(peers, table, chunks, 256):
        total[:, columns] = refs[1][:, columns] + part if later else part


def absorb(distances, chunks, table, decoder, state=()):
    owners, _, tok_rows = table.shape
    operands = [kept(table), decoder]
    operands += [kept(half) for pair in chunks for half in pair]
    operands += state
    return pl.pallas_call(
        functools.partial(absorb_kernel, distances, bool(state)),
        out_shape=(
            pltpu.VMEM((owners, 2, 2 * KPB, tok_rows), jnp.float32),
            pltpu.VMEM(decoder.shape, jnp.float32),
        ),
        in_specs=[VMEM] * len(operands),
        out_specs=(VMEM, VMEM),
        input_output_aliases={len(operands) - 2: 0, len(operands) - 1: 1} if state else {},
        compiler_params=LIMIT,
        name="absorb",
    )(*operands)


def last_scores_kernel(distance, table, decoder, left, right, before, picked):
    picked[...] = before[...]
    add_picks([peer_at(distance, table.shape[0])], table, decoder, (left, right), picked)


def last_scores(distance, chunk, table, decoder, picked):
    return pl.pallas_call(
        functools.partial(last_scores_kernel, distance),
        out_shape=pltpu.VMEM(picked.shape, picked.dtype),
        in_specs=[VMEM] * 5,
        out_specs=VMEM,
        input_output_aliases={4: 0},
        compiler_params=LIMIT,
        name="last_scores",
    )(kept(table), decoder, kept(chunk[0]), kept(chunk[1]), picked)


def last_gradients_kernel(distance, table, left, right, total, out, rounded, sems):
    peer = peer_at(distance, table.shape[0])
    copies = []
    for columns, part in gradient_blocks([peer], table, (left, right), 256):
        rounded[:, columns] = (total[:, columns] + part).astype(out.dtype)
        copies.append(
            pltpu.make_async_copy(
                rounded.at[:, columns], out.at[:, columns], sems.at[len(copies)]
            )
        )
        copies[-1].start()
    for copy in copies:
        copy.wait()


def last_gradients(distance, chunk, table, total):
    return pl.pallas_call(
        functools.partial(last_gradients_kernel, distance),
        out_shape=jax.ShapeDtypeStruct(total.shape, jnp.bfloat16),
        in_specs=[VMEM] * 4,
        out_specs=ANY,
        scratch_shapes=[
            pltpu.VMEM(total.shape, jnp.bfloat16),
            pltpu.SemaphoreType.DMA((total.shape[1] // 256,)),
        ],
        compiler_params=LIMIT,
        name="last_gradients",
    )(kept(table), kept(chunk[0]), kept(chunk[1]), total)


def unpack_kernel(returned, slots, out):
    owner = slots[...] // BLK_DEV
    for k in range(KPB):
        total = jnp.zeros(owner.shape, jnp.float32)
        for o in range(returned.shape[0]):
            value = returned[o, 0, k : k + 1, :] + returned[o, 1, k : k + 1, :]
            total = jnp.where(owner == o, value, total)
        out[pl.ds(k, ACT, stride=KPB), :] = total


def unpack(returned, slots):
    tok_rows = slots.shape[1]
    return pl.pallas_call(
        unpack_kernel,
        out_shape=jax.ShapeDtypeStruct((ACT * KPB, tok_rows), jnp.float32),
        in_specs=[VMEM, VMEM],
        out_specs=VMEM,
        name="unpack",
    )(kept(returned), slots).T


def every_owner(decoder, grad_out, active_blocks, feature_idx, acts, block_slot):
    half_width = grad_out.shape[1]
    owners = lax.axis_size("dp")
    ring = ring_of(owners)
    onward = [(ring[i], ring[(i + 1) % owners]) for i in range(owners)]
    back = [(there, here) for here, there in onward]

    def hop(pieces):
        left, right = pieces
        return lax.ppermute(left, "dp", onward), lax.ppermute(right, "dp", back)

    cut = half_width // 2
    own = (grad_out[:, :cut], grad_out[:, cut:])
    first_1 = hop(own)
    second_1 = hop(own[::-1])
    table, slots, decoder = prepare(
        block_slot, active_blocks, feature_idx, acts, decoder, owners
    )
    first_1, table, slots, decoder = lax.optimization_barrier((first_1, table, slots, decoder))
    first_2 = hop(first_1)
    table = lax.all_to_all(table, "dp", 0, 0, tiled=True)
    second_2 = hop(second_1)
    first_3 = hop(first_2)
    near = [own, (first_1[0], second_1[0]), (second_1[1], first_1[1])]
    state = absorb((0, -1, 1), near, table, decoder)
    state, second_2 = lax.optimization_barrier((state, second_2))
    second_3 = hop(second_2)
    state = absorb(
        (-2, 2),
        [(first_2[0], second_2[0]), (second_2[1], first_2[1])],
        table,
        decoder,
        state,
    )
    state, first_3 = lax.optimization_barrier((state, first_3))
    first_4 = hop(first_3)
    state = absorb(
        (-3, 3),
        [(first_3[0], second_3[0]), (second_3[1], first_3[1])],
        table,
        decoder,
        state,
    )
    state, first_4 = lax.optimization_barrier((state, first_4))
    picked, total = state
    picked = last_scores(4, first_4, table, decoder, picked)
    sent = picked.reshape((2 * owners,) + picked.shape[2:])
    returned = lax.all_to_all(sent, ("dp", "width"), 0, 0, tiled=True)
    decoder_grad = last_gradients(4, first_4, table, total)
    act_grad = unpack(returned.reshape(picked.shape), slots)
    return (decoder_grad, act_grad)


def send_back(picked):
    return lax.all_to_all(picked, "dp", split_axis=1, concat_axis=1, tiled=True)


def pack_slots(grad_out, target, slots_all, pair_coeffs, pair_columns, source_row):
    slot_row = jnp.zeros((slots_all,), jnp.int32).at[target].set(source_row)
    used = jnp.zeros((slots_all,), jnp.bool_).at[target].set(True)
    send_rows = jnp.where(used[:, None], grad_out[slot_row], jnp.zeros((), grad_out.dtype))
    send_acts = jnp.zeros((slots_all, KPB), pair_coeffs.dtype).at[target].set(pair_coeffs)
    send_cols = jnp.zeros((slots_all, KPB), jnp.int32).at[target].set(pair_columns)
    return (send_rows, send_acts, send_cols)


def some_owners(decoder, grad_out, active_blocks, feature_idx, acts, block_slot):
    tok_rows, half_width = grad_out.shape
    owners = lax.axis_size("dp")
    mean_load = tok_rows * ACT // owners
    owner_cap = mean_load + min(mean_load // 2, tok_rows - mean_load)
    block_cap = (owner_cap + 2) // 3
    block_ids = active_blocks.reshape(-1)
    pair_count = block_ids.shape[0]
    table_pos = jnp.arange(block_slot.shape[0], dtype=jnp.int32)
    slot_of = jnp.sum(
        jnp.where(block_ids[:, None] == table_pos[None, :], block_slot[None, :], 0), axis=1
    )
    pair_pos = jnp.arange(pair_count, dtype=jnp.int32)
    source_row = pair_pos // ACT
    pair_coeffs = acts.reshape(pair_count, KPB)
    pair_feats = feature_idx.reshape(pair_count, KPB)
    earlier = (block_ids[:, None] == block_ids[None, :]) & (pair_pos[None, :] < pair_pos[:, None])
    position = jnp.sum(earlier.astype(jnp.int32), axis=1)
    slot_cols = owners * block_cap
    target = slot_of % BLK_DEV * slot_cols + slot_of // BLK_DEV * block_cap + position
    slots_all = BLK_DEV * slot_cols
    send_rows, send_acts, send_cols = pack_slots(
        grad_out, target, slots_all, pair_coeffs, pair_feats, source_row
    )
    rows, coeffs, feature_pos = (
        lax.all_to_all(
            send_rows.reshape(BLK_DEV, slot_cols, half_width),
            "dp",
            split_axis=1,
            concat_axis=1,
            tiled=True,
        ),
        lax.all_to_all(
            send_acts.reshape(BLK_DEV, slot_cols, KPB),
            "dp",
            split_axis=1,
            concat_axis=1,
            tiled=True,
        ),
        lax.all_to_all(
            send_cols.reshape(BLK_DEV, slot_cols, KPB),
            "dp",
            split_axis=1,
            concat_axis=1,
            tiled=True,
        ),
    )
    weights = decoder.reshape(BLK_DEV, BW, half_width)
    scores = jnp.einsum("bnd,bfd->bnf", rows, weights, preferred_element_type=jnp.float32)
    picked = jnp.take_along_axis(scores, feature_pos, axis=2)
    returned = send_back(picked)
    feature_axis = jnp.arange(BW, dtype=jnp.int32)
    matches = feature_pos[..., None] == feature_axis
    dense = jnp.sum(jnp.where(matches, coeffs[..., None].astype(jnp.float32), 0.0), axis=2).astype(
        jnp.bfloat16
    )
    grads = jnp.einsum("bnf,bnd->bfd", dense, rows, preferred_element_type=jnp.float32)
    decoder_grad = grads.astype(jnp.bfloat16).reshape(BLK_DEV * BW, half_width)
    pair_vals = returned.reshape(slots_all, KPB)[target]
    act_grad = pair_vals.reshape(tok_rows, ACT * KPB)
    act_grad = lax.psum(act_grad, "width")
    return (decoder_grad, act_grad)


def per_device(*args):
    if lax.axis_size("dp") == ACT:
        return every_owner(*args)
    return some_owners(*args)


def solution(mesh):
    in_specs = (
        P(("groups", "dp"), "width"),
        P(("groups", "dp"), "width"),
        P(("groups", "dp"), None),
        P(("groups", "dp"), None),
        P(("groups", "dp"), None),
        P("groups"),
    )
    out_specs = (P(("groups", "dp"), "width"), P(("groups", "dp"), None))
    return jax.shard_map(
        per_device, mesh=mesh, in_specs=in_specs, out_specs=out_specs, check_vma=False
    )
```

```python
import functools

import jax
import jax.numpy as jnp
from jax import lax
from jax.experimental import pallas as pl
from jax.experimental.pallas import tpu as pltpu
from jax.sharding import PartitionSpec as P

BW = 128
BLK_DEV = 4
ACT = 8
KPB = 4
SMEM = pl.BlockSpec(memory_space=pltpu.SMEM)
VMEM = pl.BlockSpec(memory_space=pltpu.VMEM)
ANY = pl.BlockSpec(memory_space=pl.ANY)


def limit(mebibytes):
    return pltpu.CompilerParams(vmem_limit_bytes=mebibytes * 2**20)


def kept(x):
    return pltpu.with_memory_space_constraint(x, pltpu.VMEM)


def ring_of(owners):
    return list(range(0, owners, 2)) + list(range(owners - 1, 0, -2))


def peer_at(distance, owners):
    me = lax.axis_index("dp")
    half_ring = owners // 2
    place = jnp.where(lax.rem(me, 2) == 0, lax.div(me, 2), owners - 1 - lax.div(me, 2))
    at = lax.rem(place + owners + distance, owners)
    return jnp.where(at < half_ring, 2 * at, 2 * (owners - 1 - at) + 1)


ROW_SHIFT = BLK_DEV * BW // 2


def facts_for(owner_id, owner, first_row, feats, acts):
    mine = owner == owner_id
    rows = [
        jnp.sum(jnp.where(mine, first_row + feats[k], 0.0), axis=0, keepdims=True) - ROW_SHIFT
        for k in range(KPB)
    ]
    values = [
        jnp.sum(jnp.where(mine, acts[k], 0.0), axis=0, keepdims=True) for k in range(KPB)
    ]
    return jnp.concatenate(rows + values, axis=0)


def prepare_kernel(
    owners, block_slot, active, feats, acts, grad_out,
    left, right, own_facts, slots, wide_feats, wide_acts, sems,
):
    tok_rows, width = grad_out.shape
    parts = width // 256
    copies = []
    for j in range(parts):
        for target, side in ((left, 0), (right, 1)):
            column = (side * parts + j) * 128
            copies.append(
                pltpu.make_async_copy(
                    grad_out.at[:, column : column + 128],
                    target.at[j * tok_rows : (j + 1) * tok_rows, :],
                    sems.at[len(copies)],
                )
            )
            copies[-1].start()
    named = active[...]
    slot = jnp.zeros_like(named)
    for block in range(block_slot.shape[0]):
        slot = jnp.where(named == block, block_slot[block], slot)
    slots[...] = slot
    wide_feats[...] = feats[...].astype(jnp.float32)
    wide_acts[...] = acts[...].astype(jnp.float32)
    features = [wide_feats[pl.ds(k, ACT, stride=KPB), :] for k in range(KPB)]
    values = [wide_acts[pl.ds(k, ACT, stride=KPB), :] for k in range(KPB)]
    first_row = (slot % BLK_DEV * BW).astype(jnp.float32)

    def facts(distance):
        return facts_for(
            peer_at(distance, owners), slot // BLK_DEV, first_row, features, values
        )

    reach = owners // 2
    own_facts[...] = facts(0)
    start = parts * tok_rows
    for target, sign in ((left, 1), (right, -1)):
        ahead = [facts(sign * d) for d in range(1, reach + 1)]
        target[start:, :] = jnp.concatenate(ahead, axis=0).astype(jnp.bfloat16)
    for copy in copies:
        copy.wait()


def prepare(block_slot, active_blocks, feature_idx, acts, grad_out, owners):
    tok_rows, half_width = grad_out.shape
    plain = half_width // 256 * tok_rows
    extra = owners // 2 * 2 * KPB
    return pl.pallas_call(
        functools.partial(prepare_kernel, owners),
        out_shape=(
            pltpu.VMEM((plain + extra, 128), grad_out.dtype),
            pltpu.VMEM((plain + extra, 128), grad_out.dtype),
            pltpu.VMEM((2 * KPB, tok_rows), jnp.float32),
            pltpu.VMEM((ACT, tok_rows), jnp.int32),
        ),
        in_specs=[SMEM, VMEM, VMEM, VMEM, ANY],
        out_specs=(VMEM,) * 4,
        scratch_shapes=[
            pltpu.VMEM((ACT * KPB, tok_rows), jnp.float32),
            pltpu.VMEM((ACT * KPB, tok_rows), jnp.float32),
            pltpu.SemaphoreType.DMA((half_width // 128,)),
        ],
        compiler_params=limit(8),
        name="prepare",
    )(block_slot, active_blocks.T, feature_idx.T, acts.T, grad_out)


def fetch_kernel(source, target, sem):
    copy = pltpu.make_async_copy(source, target, sem)
    copy.start()
    copy.wait()


def fetch(x):
    return pl.pallas_call(
        fetch_kernel,
        out_shape=pltpu.VMEM(x.shape, x.dtype),
        in_specs=[ANY],
        out_specs=VMEM,
        scratch_shapes=[pltpu.SemaphoreType.DMA],
        compiler_params=limit(8),
        name="fetch",
    )(x)


def block_and_rows(here):
    at_row = here[:KPB].astype(jnp.int32) + ROW_SHIFT
    return at_row[:1] // BW, at_row % BW


def row_axis_of(tok_rows):
    return lax.broadcasted_iota(jnp.int32, (BW, tok_rows), 0)


def coefficients(here):
    block, feats = block_and_rows(here)
    row_axis = row_axis_of(here.shape[1])
    dense = jnp.zeros(row_axis.shape, jnp.float32)
    for k in range(KPB):
        dense = jnp.where(row_axis == feats[k : k + 1], here[KPB + k : KPB + k + 1], dense)
    parts = [jnp.where(block == b, dense, 0.0) for b in range(BLK_DEV)]
    return jnp.concatenate(parts, axis=0).astype(jnp.bfloat16)


def pick(scores, here):
    block, feats = block_and_rows(here)
    row_axis = row_axis_of(here.shape[1])
    mine = scores[:BW]
    for b in range(1, BLK_DEV):
        mine = jnp.where(block == b, scores[b * BW : (b + 1) * BW], mine)
    return [
        jnp.sum(jnp.where(row_axis == feats[k : k + 1], mine, 0.0), axis=0)
        for k in range(KPB)
    ]


def facts_in(piece, distance, tok_rows):
    extra = 2 * KPB * (lax.axis_size("dp") // 2)
    facts = piece[piece.shape[0] - extra :, :].astype(jnp.float32)
    return facts[(abs(distance) - 1) * 2 * KPB : abs(distance) * 2 * KPB]


def columns_of(pieces, tok_rows, parts):
    rows = [
        jnp.concatenate([piece[j * tok_rows : (j + 1) * tok_rows, :] for j in parts], axis=1)
        for piece in pieces
    ]
    return jnp.concatenate(rows, axis=0) if len(rows) > 1 else rows[0]


def add_picks(peers, facts, decoder, pieces, picked):
    tok_rows = facts[0].shape[1]
    cut = decoder.shape[1] // 2
    for first in range(0, len(peers), 2):
        some = peers[first : first + 2]
        scores = None
        for side in range(2):
            part = lax.dot_general(
                decoder[:, side * cut : (side + 1) * cut],
                columns_of(
                    pieces[2 * first + side : 2 * (first + len(some)) : 2],
                    tok_rows,
                    range(cut // 128),
                ),
                (((1,), (1,)), ((), ())),
                preferred_element_type=jnp.float32,
            )
            scores = part if scores is None else scores + part
        for i, peer in enumerate(some):
            values = pick(scores[:, i * tok_rows : (i + 1) * tok_rows], facts[first + i])
            for k in range(KPB):
                for width in range(2):
                    picked[peer, width, k, :] = values[k]


def gradient_blocks(facts, pieces, width):
    tok_rows = facts[0].shape[1]
    cut = width // 2
    dense = jnp.concatenate([coefficients(here) for here in facts], axis=1)
    for side in range(2):
        for j in range(0, cut // 128, 2):
            rows = columns_of(pieces[side::2], tok_rows, (j, j + 1))
            part = jnp.dot(dense, rows, preferred_element_type=jnp.float32)
            yield slice(side * cut + j * 128, side * cut + (j + 2) * 128), part


def absorb_kernel(distances, later, decoder, own_facts, *refs):
    count = len(distances)
    pieces, refs = refs[: 2 * count], refs[2 * count :]
    picked, total = refs[-2:]
    owners, _, _, tok_rows = picked.shape
    peers = [peer_at(d, owners) for d in distances]
    facts = [
        own_facts[...] if d == 0 else facts_in(pieces[2 * i + (d > 0)], d, tok_rows)
        for i, d in enumerate(distances)
    ]
    picked[...] = refs[0][...] if later else jnp.zeros_like(picked)
    add_picks(peers, facts, decoder, pieces, picked)
    for columns, part in gradient_blocks(facts, pieces, decoder.shape[1]):
        total[:, columns] = refs[1][:, columns] + part if later else part


def absorb(distances, pairs, decoder, own_facts, state=()):
    tok_rows = own_facts.shape[1]
    owners = lax.axis_size("dp")
    operands = [kept(decoder), kept(own_facts)]
    operands += [kept(piece) for pair in pairs for piece in pair]
    operands += [kept(x) for x in state]
    return pl.pallas_call(
        functools.partial(absorb_kernel, distances, bool(state)),
        out_shape=(
            pltpu.VMEM((owners, 2, 2 * KPB, tok_rows), jnp.float32),
            pltpu.VMEM(decoder.shape, jnp.float32),
        ),
        in_specs=[VMEM] * len(operands),
        out_specs=(VMEM, VMEM),
        input_output_aliases={len(operands) - 2: 0, len(operands) - 1: 1} if state else {},
        compiler_params=limit(16),
        name="absorb",
    )(*operands)


def last_scores_kernel(distance, decoder, left, right, before, picked):
    picked[...] = before[...]
    owners, _, _, tok_rows = picked.shape
    facts = [facts_in(left, distance, tok_rows)]
    add_picks([peer_at(distance, owners)], facts, decoder, (left, right), picked)


def last_scores(distance, pair, decoder, picked):
    return pl.pallas_call(
        functools.partial(last_scores_kernel, distance),
        out_shape=pltpu.VMEM(picked.shape, picked.dtype),
        in_specs=[VMEM] * 4,
        out_specs=VMEM,
        input_output_aliases={3: 0},
        compiler_params=limit(12),
        name="last_scores",
    )(kept(decoder), kept(pair[0]), kept(pair[1]), kept(picked))


def last_gradients_kernel(distance, tok_rows, left, right, total, out, rounded, sems):
    facts = [facts_in(left, distance, tok_rows)]
    copies = []
    for columns, part in gradient_blocks(facts, (left, right), out.shape[1]):
        rounded[:, columns] = (total[:, columns] + part).astype(out.dtype)
        copies.append(
            pltpu.make_async_copy(
                rounded.at[:, columns], out.at[:, columns], sems.at[len(copies)]
            )
        )
        copies[-1].start()
    for copy in copies:
        copy.wait()


def last_gradients(distance, pair, total, tok_rows):
    return pl.pallas_call(
        functools.partial(last_gradients_kernel, distance, tok_rows),
        out_shape=jax.ShapeDtypeStruct(total.shape, jnp.bfloat16),
        in_specs=[VMEM] * 3,
        out_specs=ANY,
        scratch_shapes=[
            pltpu.VMEM(total.shape, jnp.bfloat16),
            pltpu.SemaphoreType.DMA((total.shape[1] // 256,)),
        ],
        compiler_params=limit(16),
        name="last_gradients",
    )(kept(pair[0]), kept(pair[1]), kept(total))


def unpack_kernel(returned, slots, out):
    owner = slots[...] // BLK_DEV
    for k in range(KPB):
        total = jnp.zeros(owner.shape, jnp.float32)
        for o in range(returned.shape[0]):
            value = returned[o, 0, k : k + 1, :] + returned[o, 1, k : k + 1, :]
            total = jnp.where(owner == o, value, total)
        out[pl.ds(k, ACT, stride=KPB), :] = total


def unpack(returned, slots):
    tok_rows = slots.shape[1]
    return pl.pallas_call(
        unpack_kernel,
        out_shape=jax.ShapeDtypeStruct((ACT * KPB, tok_rows), jnp.float32),
        in_specs=[VMEM, VMEM],
        out_specs=VMEM,
        compiler_params=limit(4),
        name="unpack",
    )(kept(returned), kept(slots)).T


def every_owner(decoder, grad_out, active_blocks, feature_idx, acts, block_slot):
    owners = lax.axis_size("dp")
    ring = ring_of(owners)
    onward = [(ring[i], ring[(i + 1) % owners]) for i in range(owners)]
    back = [(there, here) for here, there in onward]

    def hop(pieces):
        left, right = pieces
        return lax.ppermute(left, "dp", onward), lax.ppermute(right, "dp", back)

    def crossed(pieces):
        right, left = pieces
        right, left = lax.ppermute(right, "dp", onward), lax.ppermute(left, "dp", back)
        return right, left

    left, right, own_facts, slots = prepare(
        block_slot, active_blocks, feature_idx, acts, grad_out, owners
    )
    first_1 = hop((left, right))
    second_1 = crossed((right, left))
    decoder = fetch(decoder)
    first_1, decoder = lax.optimization_barrier((first_1, decoder))
    first_2 = hop(first_1)
    second_2 = crossed(second_1)
    near = [(left, right), (first_1[0], second_1[0]), (second_1[1], first_1[1])]
    state = absorb((0, -1, 1), near, decoder, own_facts)
    first_3 = hop(first_2)
    state, second_2 = lax.optimization_barrier((state, second_2))
    second_3 = crossed(second_2)
    far = [(first_2[0], second_2[0]), (second_2[1], first_2[1])]
    state = absorb((-2, 2), far, decoder, own_facts, state)
    state, first_3 = lax.optimization_barrier((state, first_3))
    first_4 = hop(first_3)
    farther = [(first_3[0], second_3[0]), (second_3[1], first_3[1])]
    state = absorb((-3, 3), farther, decoder, own_facts, state)
    (picked, total), first_4 = lax.optimization_barrier((state, first_4))
    picked = last_scores(4, first_4, decoder, picked)
    sent = picked.reshape((2 * owners,) + picked.shape[2:])
    returned = lax.all_to_all(sent, ("dp", "width"), 0, 0, tiled=True)
    decoder_grad = last_gradients(4, first_4, total, grad_out.shape[0])
    act_grad = unpack(returned.reshape(picked.shape), slots)
    return (decoder_grad, act_grad)


def send_back(picked):
    return lax.all_to_all(picked, "dp", split_axis=1, concat_axis=1, tiled=True)


def pack_slots(grad_out, target, slots_all, pair_coeffs, pair_columns, source_row):
    slot_row = jnp.zeros((slots_all,), jnp.int32).at[target].set(source_row)
    used = jnp.zeros((slots_all,), jnp.bool_).at[target].set(True)
    send_rows = jnp.where(used[:, None], grad_out[slot_row], jnp.zeros((), grad_out.dtype))
    send_acts = jnp.zeros((slots_all, KPB), pair_coeffs.dtype).at[target].set(pair_coeffs)
    send_cols = jnp.zeros((slots_all, KPB), jnp.int32).at[target].set(pair_columns)
    return (send_rows, send_acts, send_cols)


def some_owners(decoder, grad_out, active_blocks, feature_idx, acts, block_slot):
    tok_rows, half_width = grad_out.shape
    owners = lax.axis_size("dp")
    mean_load = tok_rows * ACT // owners
    owner_cap = mean_load + min(mean_load // 2, tok_rows - mean_load)
    block_cap = (owner_cap + 2) // 3
    block_ids = active_blocks.reshape(-1)
    pair_count = block_ids.shape[0]
    table_pos = jnp.arange(block_slot.shape[0], dtype=jnp.int32)
    slot_of = jnp.sum(
        jnp.where(block_ids[:, None] == table_pos[None, :], block_slot[None, :], 0), axis=1
    )
    pair_pos = jnp.arange(pair_count, dtype=jnp.int32)
    source_row = pair_pos // ACT
    pair_coeffs = acts.reshape(pair_count, KPB)
    pair_feats = feature_idx.reshape(pair_count, KPB)
    earlier = (block_ids[:, None] == block_ids[None, :]) & (pair_pos[None, :] < pair_pos[:, None])
    position = jnp.sum(earlier.astype(jnp.int32), axis=1)
    slot_cols = owners * block_cap
    target = slot_of % BLK_DEV * slot_cols + slot_of // BLK_DEV * block_cap + position
    slots_all = BLK_DEV * slot_cols
    send_rows, send_acts, send_cols = pack_slots(
        grad_out, target, slots_all, pair_coeffs, pair_feats, source_row
    )
    rows, coeffs, feature_pos = (
        lax.all_to_all(
            send_rows.reshape(BLK_DEV, slot_cols, half_width),
            "dp",
            split_axis=1,
            concat_axis=1,
            tiled=True,
        ),
        lax.all_to_all(
            send_acts.reshape(BLK_DEV, slot_cols, KPB),
            "dp",
            split_axis=1,
            concat_axis=1,
            tiled=True,
        ),
        lax.all_to_all(
            send_cols.reshape(BLK_DEV, slot_cols, KPB),
            "dp",
            split_axis=1,
            concat_axis=1,
            tiled=True,
        ),
    )
    weights = decoder.reshape(BLK_DEV, BW, half_width)
    scores = jnp.einsum("bnd,bfd->bnf", rows, weights, preferred_element_type=jnp.float32)
    picked = jnp.take_along_axis(scores, feature_pos, axis=2)
    returned = send_back(picked)
    feature_axis = jnp.arange(BW, dtype=jnp.int32)
    matches = feature_pos[..., None] == feature_axis
    dense = jnp.sum(jnp.where(matches, coeffs[..., None].astype(jnp.float32), 0.0), axis=2).astype(
        jnp.bfloat16
    )
    grads = jnp.einsum("bnf,bnd->bfd", dense, rows, preferred_element_type=jnp.float32)
    decoder_grad = grads.astype(jnp.bfloat16).reshape(BLK_DEV * BW, half_width)
    pair_vals = returned.reshape(slots_all, KPB)[target]
    act_grad = pair_vals.reshape(tok_rows, ACT * KPB)
    act_grad = lax.psum(act_grad, "width")
    return (decoder_grad, act_grad)


def per_device(*args):
    if lax.axis_size("dp") == ACT:
        return every_owner(*args)
    return some_owners(*args)


def solution(mesh):
    in_specs = (
        P(("groups", "dp"), "width"),
        P(("groups", "dp"), "width"),
        P(("groups", "dp"), None),
        P(("groups", "dp"), None),
        P(("groups", "dp"), None),
        P("groups"),
    )
    out_specs = (P(("groups", "dp"), "width"), P(("groups", "dp"), None))
    return jax.shard_map(
        per_device, mesh=mesh, in_specs=in_specs, out_specs=out_specs, check_vma=False
    )
```

```python
import functools

import jax
import jax.numpy as jnp
from jax import lax
from jax.experimental import pallas as pl
from jax.experimental.pallas import tpu as pltpu
from jax.sharding import PartitionSpec as P

BW = 128
BLK_DEV = 4
ACT = 8
KPB = 4
SMEM = pl.BlockSpec(memory_space=pltpu.SMEM)
VMEM = pl.BlockSpec(memory_space=pltpu.VMEM)
ANY = pl.BlockSpec(memory_space=pl.ANY)
HBM = pl.BlockSpec(memory_space=pltpu.HBM)


def limit(mebibytes):
    return pltpu.CompilerParams(vmem_limit_bytes=mebibytes * 2**20)


def kept(x):
    return pltpu.with_memory_space_constraint(x, pltpu.VMEM)


def far(x):
    return pltpu.with_memory_space_constraint(x, pltpu.HBM)


def ring_of(owners):
    return list(range(0, owners, 2)) + list(range(owners - 1, 0, -2))


def peer_at(distance, owners):
    me = lax.axis_index("dp")
    half_ring = owners // 2
    place = jnp.where(lax.rem(me, 2) == 0, lax.div(me, 2), owners - 1 - lax.div(me, 2))
    at = lax.rem(place + owners + distance, owners)
    return jnp.where(at < half_ring, 2 * at, 2 * (owners - 1 - at) + 1)


ROW_SHIFT = BLK_DEV * BW // 2


def facts_for(owner_id, owner, first_row, feats, acts):
    mine = owner == owner_id
    rows = [
        jnp.sum(jnp.where(mine, first_row + feats[k], 0.0), axis=0, keepdims=True) - ROW_SHIFT
        for k in range(KPB)
    ]
    values = [
        jnp.sum(jnp.where(mine, acts[k], 0.0), axis=0, keepdims=True) for k in range(KPB)
    ]
    return jnp.concatenate(rows + values, axis=0)


def prepare_kernel(
    owners, *refs
):
    sources, refs = refs[:5], refs[5:]
    left, right, own_facts, slots = refs[:4]
    block_slot, active, feats, acts, wide_feats, wide_acts, sems = refs[4:]
    grad_out = sources[-1]
    tok_rows, width = grad_out.shape
    parts = width // 256
    small = []
    for source, target in zip(sources[:4], (block_slot, active, feats, acts)):
        small.append(pltpu.make_async_copy(source, target, sems.at[len(small)]))
        small[-1].start()
    copies = []
    for j in range(parts):
        for target, side in ((left, 0), (right, 1)):
            column = (side * parts + j) * 128
            copies.append(
                pltpu.make_async_copy(
                    grad_out.at[:, column : column + 128],
                    target.at[j * tok_rows : (j + 1) * tok_rows, :],
                    sems.at[len(small) + len(copies)],
                )
            )
            copies[-1].start()
    for copy in small:
        copy.wait()
    named = active[...]
    slot = jnp.zeros_like(named)
    for block in range(block_slot.shape[0]):
        slot = jnp.where(named == block, block_slot[block], slot)
    slots[...] = slot
    wide_feats[...] = feats[...].astype(jnp.float32)
    wide_acts[...] = acts[...].astype(jnp.float32)
    features = [wide_feats[pl.ds(k, ACT, stride=KPB), :] for k in range(KPB)]
    values = [wide_acts[pl.ds(k, ACT, stride=KPB), :] for k in range(KPB)]
    first_row = (slot % BLK_DEV * BW).astype(jnp.float32)

    def facts(distance):
        return facts_for(
            peer_at(distance, owners), slot // BLK_DEV, first_row, features, values
        )

    reach = owners // 2
    own_facts[...] = facts(0)
    start = parts * tok_rows
    for target, sign in ((left, 1), (right, -1)):
        ahead = [facts(sign * d) for d in range(1, reach + 1)]
        target[start:, :] = jnp.concatenate(ahead, axis=0).astype(jnp.bfloat16)
    for copy in copies:
        copy.wait()


def prepare(block_slot, active_blocks, feature_idx, acts, grad_out, owners):
    tok_rows, half_width = grad_out.shape
    plain = half_width // 256 * tok_rows
    extra = owners // 2 * 2 * KPB
    return pl.pallas_call(
        functools.partial(prepare_kernel, owners),
        out_shape=(
            pltpu.VMEM((plain + extra, 128), grad_out.dtype),
            pltpu.VMEM((plain + extra, 128), grad_out.dtype),
            pltpu.VMEM((2 * KPB, tok_rows), jnp.float32),
            pltpu.VMEM((ACT, tok_rows), jnp.int32),
        ),
        in_specs=[HBM] * 5,
        out_specs=(VMEM,) * 4,
        scratch_shapes=[
            pltpu.SMEM(block_slot.shape, jnp.int32),
            pltpu.VMEM((ACT, tok_rows), jnp.int32),
            pltpu.VMEM((ACT * KPB, tok_rows), jnp.int32),
            pltpu.VMEM((ACT * KPB, tok_rows), acts.dtype),
            pltpu.VMEM((ACT * KPB, tok_rows), jnp.float32),
            pltpu.VMEM((ACT * KPB, tok_rows), jnp.float32),
            pltpu.SemaphoreType.DMA((4 + half_width // 128,)),
        ],
        compiler_params=limit(8),
        name="prepare",
    )(far(block_slot), far(active_blocks.T), far(feature_idx.T), far(acts.T), far(grad_out))


def fetch_kernel(source, target, sem):
    copy = pltpu.make_async_copy(source, target, sem)
    copy.start()
    copy.wait()


def fetch(x):
    return pl.pallas_call(
        fetch_kernel,
        out_shape=pltpu.VMEM(x.shape, x.dtype),
        in_specs=[HBM],
        out_specs=VMEM,
        scratch_shapes=[pltpu.SemaphoreType.DMA],
        compiler_params=limit(8),
        name="fetch",
    )(far(x))


def block_and_rows(here):
    at_row = here[:KPB].astype(jnp.int32) + ROW_SHIFT
    return at_row[:1] // BW, at_row % BW


def row_axis_of(tok_rows):
    return lax.broadcasted_iota(jnp.int32, (BW, tok_rows), 0)


def coefficients(here):
    block, feats = block_and_rows(here)
    row_axis = row_axis_of(here.shape[1])
    dense = jnp.zeros(row_axis.shape, jnp.float32)
    for k in range(KPB):
        dense = jnp.where(row_axis == feats[k : k + 1], here[KPB + k : KPB + k + 1], dense)
    parts = [jnp.where(block == b, dense, 0.0) for b in range(BLK_DEV)]
    return jnp.concatenate(parts, axis=0).astype(jnp.bfloat16)


def pick(scores, here):
    block, feats = block_and_rows(here)
    row_axis = row_axis_of(here.shape[1])
    mine = scores[:BW]
    for b in range(1, BLK_DEV):
        mine = jnp.where(block == b, scores[b * BW : (b + 1) * BW], mine)
    return [
        jnp.sum(jnp.where(row_axis == feats[k : k + 1], mine, 0.0), axis=0, keepdims=True)
        for k in range(KPB)
    ]


def facts_in(piece, distance, tok_rows):
    extra = 2 * KPB * (lax.axis_size("dp") // 2)
    facts = piece[piece.shape[0] - extra :, :].astype(jnp.float32)
    return facts[(abs(distance) - 1) * 2 * KPB : abs(distance) * 2 * KPB]


def columns_of(pieces, tok_rows, parts):
    rows = [
        jnp.concatenate([piece[j * tok_rows : (j + 1) * tok_rows, :] for j in parts], axis=1)
        for piece in pieces
    ]
    return jnp.concatenate(rows, axis=0) if len(rows) > 1 else rows[0]


def add_picks(facts, decoder, pieces, picked):
    tok_rows = facts[0].shape[1]
    cut = decoder.shape[1] // 2
    for first in range(0, len(facts), 2):
        count = min(2, len(facts) - first)
        scores = None
        for side in range(2):
            part = lax.dot_general(
                decoder[:, side * cut : (side + 1) * cut],
                columns_of(
                    pieces[2 * first + side : 2 * (first + count) : 2],
                    tok_rows,
                    range(cut // 128),
                ),
                (((1,), (1,)), ((), ())),
                preferred_element_type=jnp.float32,
            )
            scores = part if scores is None else scores + part
        for i in range(first, first + count):
            here = scores[:, (i - first) * tok_rows : (i - first + 1) * tok_rows]
            picked[i][...] = jnp.concatenate(pick(here, facts[i]) * 2, axis=0)


def gradient_blocks(facts, pieces, width):
    tok_rows = facts[0].shape[1]
    cut = width // 2
    dense = jnp.concatenate([coefficients(here) for here in facts], axis=1)
    for side in range(2):
        for j in range(0, cut // 128, 2):
            rows = columns_of(pieces[side::2], tok_rows, (j, j + 1))
            part = jnp.dot(dense, rows, preferred_element_type=jnp.float32)
            yield slice(side * cut + j * 128, side * cut + (j + 2) * 128), part


def absorb_kernel(distances, later, decoder, own_facts, *refs):
    count = len(distances)
    pieces, refs = refs[: 2 * count], refs[2 * count :]
    picked, total = refs[-1 - count : -1], refs[-1]
    tok_rows = own_facts.shape[1]
    facts = [
        own_facts[...] if d == 0 else facts_in(pieces[2 * i + (d > 0)], d, tok_rows)
        for i, d in enumerate(distances)
    ]
    add_picks(facts, decoder, pieces, picked)
    for columns, part in gradient_blocks(facts, pieces, decoder.shape[1]):
        total[:, columns] = refs[0][:, columns] + part if later else part


def absorb(distances, pairs, decoder, own_facts, total=None):
    tok_rows = own_facts.shape[1]
    operands = [kept(decoder), kept(own_facts)]
    operands += [kept(piece) for pair in pairs for piece in pair]
    operands += [] if total is None else [kept(total)]
    count = len(distances)
    *picked, total = pl.pallas_call(
        functools.partial(absorb_kernel, distances, total is not None),
        out_shape=(
            *[pltpu.VMEM((2 * KPB, tok_rows), jnp.float32)] * count,
            pltpu.VMEM(decoder.shape, jnp.float32),
        ),
        in_specs=[VMEM] * len(operands),
        out_specs=(VMEM,) * (count + 1),
        input_output_aliases={} if total is None else {len(operands) - 1: count},
        compiler_params=limit(16),
        name="absorb",
    )(*operands)
    return picked, total


def last_scores_kernel(distance, decoder, left, right, picked):
    facts = [facts_in(left, distance, picked.shape[1])]
    add_picks(facts, decoder, (left, right), [picked])


def last_scores(distance, pair, decoder, tok_rows):
    return pl.pallas_call(
        functools.partial(last_scores_kernel, distance),
        out_shape=pltpu.VMEM((2 * KPB, tok_rows), jnp.float32),
        in_specs=[VMEM] * 3,
        out_specs=VMEM,
        compiler_params=limit(12),
        name="last_scores",
    )(kept(decoder), kept(pair[0]), kept(pair[1]))


def last_gradients_kernel(distance, tok_rows, left, right, total, out, rounded, sems):
    facts = [facts_in(left, distance, tok_rows)]
    copies = []
    for columns, part in gradient_blocks(facts, (left, right), out.shape[1]):
        rounded[:, columns] = (total[:, columns] + part).astype(out.dtype)
        copies.append(
            pltpu.make_async_copy(
                rounded.at[:, columns], out.at[:, columns], sems.at[len(copies)]
            )
        )
        copies[-1].start()
    for copy in copies:
        copy.wait()


def last_gradients(distance, pair, total, tok_rows):
    return pl.pallas_call(
        functools.partial(last_gradients_kernel, distance, tok_rows),
        out_shape=jax.ShapeDtypeStruct(total.shape, jnp.bfloat16),
        in_specs=[VMEM] * 3,
        out_specs=ANY,
        scratch_shapes=[
            pltpu.VMEM(total.shape, jnp.bfloat16),
            pltpu.SemaphoreType.DMA((total.shape[1] // 256,)),
        ],
        compiler_params=limit(16),
        name="last_gradients",
    )(kept(pair[0]), kept(pair[1]), kept(total))


def unpack_kernel(distances, owners, slots, *refs):
    returned, out = refs[:-1], refs[-1]
    owner = slots[...] // BLK_DEV
    mine = [owner == peer_at(d, owners) for d in distances]
    for k in range(KPB):
        total = jnp.zeros(owner.shape, jnp.float32)
        for here, values in zip(mine, returned):
            total = jnp.where(here, values[k : k + 1, :], total)
        out[pl.ds(k, ACT, stride=KPB), :] = total


def unpack(distances, returned, slots):
    tok_rows = slots.shape[1]
    return pl.pallas_call(
        functools.partial(unpack_kernel, distances, lax.axis_size("dp")),
        out_shape=pltpu.VMEM((ACT * KPB, tok_rows), jnp.float32),
        in_specs=[VMEM] * (1 + len(returned)),
        out_specs=VMEM,
        compiler_params=limit(4),
        name="unpack",
    )(kept(slots), *[kept(x) for x in returned])


def every_owner(decoder, grad_out, active_blocks, feature_idx, acts, block_slot):
    tok_rows = grad_out.shape[0]
    owners = lax.axis_size("dp")
    ring = ring_of(owners)

    def shift(x, by):
        pairs = [(ring[i], ring[(i + by) % owners]) for i in range(owners)]
        return lax.ppermute(x, "dp", pairs)

    def hop(pieces):
        left, right = pieces
        return shift(left, 1), shift(right, -1)

    def crossed(pieces):
        right, left = pieces
        return shift(right, 1), shift(left, -1)

    left, right, own_facts, slots = prepare(
        block_slot, active_blocks, feature_idx, acts, grad_out, owners
    )
    first_1 = hop((left, right))
    second_1 = crossed((right, left))
    decoder = fetch(decoder)
    first_1, decoder = lax.optimization_barrier((first_1, decoder))
    first_2 = hop(first_1)
    second_2 = crossed(second_1)
    first_3 = hop(first_2)
    pairs = [(left, right), (first_1[0], second_1[0]), (second_1[1], first_1[1])]
    (own, onward, back), total = absorb((0, -1, 1), pairs, decoder, own_facts)
    returned = [own, shift(onward, -1), shift(back, 1)]
    total, second_2, returned = lax.optimization_barrier((total, second_2, returned))
    second_3 = crossed(second_2)
    pairs = [(first_2[0], second_2[0]), (second_2[1], first_2[1])]
    (onward, back), total = absorb((-2, 2), pairs, decoder, own_facts, total)
    total, first_3 = lax.optimization_barrier((total, first_3))
    returned += [shift(onward, -2), shift(back, 2)]
    first_4 = hop(first_3)
    pairs = [(first_3[0], second_3[0]), (second_3[1], first_3[1])]
    (onward, back), total = absorb((-3, 3), pairs, decoder, own_facts, total)
    returned += [shift(onward, -3), shift(back, 3)]
    total, first_4, returned[3:5] = lax.optimization_barrier((total, first_4, returned[3:5]))
    onward = last_scores(4, first_4, decoder, tok_rows)
    returned.append(shift(onward, -4))
    decoder_grad = last_gradients(4, first_4, total, tok_rows)
    act_grad = unpack((0, 1, -1, 2, -2, 3, -3, 4), returned, slots)
    act_grad = act_grad + lax.ppermute(act_grad, "width", ((0, 1), (1, 0)))
    return (decoder_grad, act_grad.T)


def send_back(picked):
    return lax.all_to_all(picked, "dp", split_axis=1, concat_axis=1, tiled=True)


def pack_slots(grad_out, target, slots_all, pair_coeffs, pair_columns, source_row):
    slot_row = jnp.zeros((slots_all,), jnp.int32).at[target].set(source_row)
    used = jnp.zeros((slots_all,), jnp.bool_).at[target].set(True)
    send_rows = jnp.where(used[:, None], grad_out[slot_row], jnp.zeros((), grad_out.dtype))
    send_acts = jnp.zeros((slots_all, KPB), pair_coeffs.dtype).at[target].set(pair_coeffs)
    send_cols = jnp.zeros((slots_all, KPB), jnp.int32).at[target].set(pair_columns)
    return (send_rows, send_acts, send_cols)


def some_owners(decoder, grad_out, active_blocks, feature_idx, acts, block_slot):
    tok_rows, half_width = grad_out.shape
    owners = lax.axis_size("dp")
    mean_load = tok_rows * ACT // owners
    owner_cap = mean_load + min(mean_load // 2, tok_rows - mean_load)
    block_cap = (owner_cap + 2) // 3
    block_ids = active_blocks.reshape(-1)
    pair_count = block_ids.shape[0]
    table_pos = jnp.arange(block_slot.shape[0], dtype=jnp.int32)
    slot_of = jnp.sum(
        jnp.where(block_ids[:, None] == table_pos[None, :], block_slot[None, :], 0), axis=1
    )
    pair_pos = jnp.arange(pair_count, dtype=jnp.int32)
    source_row = pair_pos // ACT
    pair_coeffs = acts.reshape(pair_count, KPB)
    pair_feats = feature_idx.reshape(pair_count, KPB)
    earlier = (block_ids[:, None] == block_ids[None, :]) & (pair_pos[None, :] < pair_pos[:, None])
    position = jnp.sum(earlier.astype(jnp.int32), axis=1)
    slot_cols = owners * block_cap
    target = slot_of % BLK_DEV * slot_cols + slot_of // BLK_DEV * block_cap + position
    slots_all = BLK_DEV * slot_cols
    send_rows, send_acts, send_cols = pack_slots(
        grad_out, target, slots_all, pair_coeffs, pair_feats, source_row
    )
    rows, coeffs, feature_pos = (
        lax.all_to_all(
            send_rows.reshape(BLK_DEV, slot_cols, half_width),
            "dp",
            split_axis=1,
            concat_axis=1,
            tiled=True,
        ),
        lax.all_to_all(
            send_acts.reshape(BLK_DEV, slot_cols, KPB),
            "dp",
            split_axis=1,
            concat_axis=1,
            tiled=True,
        ),
        lax.all_to_all(
            send_cols.reshape(BLK_DEV, slot_cols, KPB),
            "dp",
            split_axis=1,
            concat_axis=1,
            tiled=True,
        ),
    )
    weights = decoder.reshape(BLK_DEV, BW, half_width)
    scores = jnp.einsum("bnd,bfd->bnf", rows, weights, preferred_element_type=jnp.float32)
    picked = jnp.take_along_axis(scores, feature_pos, axis=2)
    returned = send_back(picked)
    feature_axis = jnp.arange(BW, dtype=jnp.int32)
    matches = feature_pos[..., None] == feature_axis
    dense = jnp.sum(jnp.where(matches, coeffs[..., None].astype(jnp.float32), 0.0), axis=2).astype(
        jnp.bfloat16
    )
    grads = jnp.einsum("bnf,bnd->bfd", dense, rows, preferred_element_type=jnp.float32)
    decoder_grad = grads.astype(jnp.bfloat16).reshape(BLK_DEV * BW, half_width)
    pair_vals = returned.reshape(slots_all, KPB)[target]
    act_grad = pair_vals.reshape(tok_rows, ACT * KPB)
    act_grad = lax.psum(act_grad, "width")
    return (decoder_grad, act_grad)


def per_device(*args):
    if lax.axis_size("dp") == ACT:
        return every_owner(*args)
    return some_owners(*args)


def solution(mesh):
    in_specs = (
        P(("groups", "dp"), "width"),
        P(("groups", "dp"), "width"),
        P(("groups", "dp"), None),
        P(("groups", "dp"), None),
        P(("groups", "dp"), None),
        P("groups"),
    )
    out_specs = (P(("groups", "dp"), "width"), P(("groups", "dp"), None))
    return jax.shard_map(
        per_device, mesh=mesh, in_specs=in_specs, out_specs=out_specs, check_vma=False
    )
```

```python
import functools

import jax
import jax.numpy as jnp
from jax import lax
from jax.experimental import pallas as pl
from jax.experimental.pallas import tpu as pltpu
from jax.sharding import PartitionSpec as P

BW = 128
BLK_DEV = 4
ACT = 8
KPB = 4
SMEM = pl.BlockSpec(memory_space=pltpu.SMEM)
VMEM = pl.BlockSpec(memory_space=pltpu.VMEM)
ANY = pl.BlockSpec(memory_space=pl.ANY)
HBM = pl.BlockSpec(memory_space=pltpu.HBM)


def limit(mebibytes):
    return pltpu.CompilerParams(vmem_limit_bytes=mebibytes * 2**20)


def kept(x):
    return pltpu.with_memory_space_constraint(x, pltpu.VMEM)


def far(x):
    return pltpu.with_memory_space_constraint(x, pltpu.HBM)


def ring_of(owners):
    return list(range(0, owners, 2)) + list(range(owners - 1, 0, -2))


def peer_at(distance, owners):
    me = lax.axis_index("dp")
    half_ring = owners // 2
    place = jnp.where(lax.rem(me, 2) == 0, lax.div(me, 2), owners - 1 - lax.div(me, 2))
    at = lax.rem(place + owners + distance, owners)
    return jnp.where(at < half_ring, 2 * at, 2 * (owners - 1 - at) + 1)


ROW_SHIFT = BLK_DEV * BW // 2
FACTS = ACT // 2 * 2 * KPB


def facts_for(owner_id, owner, first_row, feats, acts):
    mine = owner == owner_id
    rows = [
        jnp.sum(jnp.where(mine, first_row + feats[k], 0.0), axis=0, keepdims=True) - ROW_SHIFT
        for k in range(KPB)
    ]
    values = [
        jnp.sum(jnp.where(mine, acts[k], 0.0), axis=0, keepdims=True) for k in range(KPB)
    ]
    return jnp.concatenate(rows + values, axis=0)


def prepare_kernel(
    owners, *refs
):
    sources, refs = refs[:5], refs[5:]
    left, right, own_facts, slots = refs[:4]
    block_slot, active, feats, acts, wide_feats, wide_acts, sems = refs[4:]
    grad_out = sources[-1]
    tok_rows, width = grad_out.shape
    parts = width // 256
    small = []
    for source, target in zip(sources[:4], (block_slot, active, feats, acts)):
        small.append(pltpu.make_async_copy(source, target, sems.at[len(small)]))
        small[-1].start()
    copies = []
    for j in range(parts):
        for target, side in ((left, 0), (right, 1)):
            column = (side * parts + j) * 128
            copies.append(
                pltpu.make_async_copy(
                    grad_out.at[:, column : column + 128],
                    target.at[j * tok_rows : (j + 1) * tok_rows, :],
                    sems.at[len(small) + len(copies)],
                )
            )
            copies[-1].start()
    for copy in small:
        copy.wait()
    named = active[...]
    slot = jnp.zeros_like(named)
    for block in range(block_slot.shape[0]):
        slot = jnp.where(named == block, block_slot[block], slot)
    slots[...] = slot
    wide_feats[...] = feats[...].astype(jnp.float32)
    wide_acts[...] = acts[...].astype(jnp.float32)
    features = [wide_feats[pl.ds(k, ACT, stride=KPB), :] for k in range(KPB)]
    values = [wide_acts[pl.ds(k, ACT, stride=KPB), :] for k in range(KPB)]
    first_row = (slot % BLK_DEV * BW).astype(jnp.float32)

    def facts(distance):
        return facts_for(
            peer_at(distance, owners), slot // BLK_DEV, first_row, features, values
        )

    reach = owners // 2
    own_facts[...] = facts(0)
    start = parts * tok_rows
    for target, sign in ((left, 1), (right, -1)):
        ahead = [facts(sign * d) for d in range(1, reach + 1)]
        target[start:, :] = jnp.concatenate(ahead, axis=0).astype(jnp.bfloat16)
    for copy in copies:
        copy.wait()


def prepare(block_slot, active_blocks, feature_idx, acts, grad_out, owners):
    tok_rows, half_width = grad_out.shape
    plain = half_width // 256 * tok_rows
    return pl.pallas_call(
        functools.partial(prepare_kernel, owners),
        out_shape=(
            pltpu.VMEM((plain + FACTS, 128), grad_out.dtype),
            pltpu.VMEM((plain + FACTS, 128), grad_out.dtype),
            pltpu.VMEM((2 * KPB, tok_rows), jnp.float32),
            pltpu.VMEM((ACT, tok_rows), jnp.int32),
        ),
        in_specs=[HBM] * 5,
        out_specs=(VMEM,) * 4,
        scratch_shapes=[
            pltpu.SMEM(block_slot.shape, jnp.int32),
            pltpu.VMEM((ACT, tok_rows), jnp.int32),
            pltpu.VMEM((ACT * KPB, tok_rows), jnp.int32),
            pltpu.VMEM((ACT * KPB, tok_rows), acts.dtype),
            pltpu.VMEM((ACT * KPB, tok_rows), jnp.float32),
            pltpu.VMEM((ACT * KPB, tok_rows), jnp.float32),
            pltpu.SemaphoreType.DMA((4 + half_width // 128,)),
        ],
        compiler_params=limit(8),
        name="prepare",
    )(far(block_slot), far(active_blocks.T), far(feature_idx.T), far(acts.T), far(grad_out))


def fetch_kernel(source, target, sem):
    copy = pltpu.make_async_copy(source, target, sem)
    copy.start()
    copy.wait()


def fetch(x):
    return pl.pallas_call(
        fetch_kernel,
        out_shape=pltpu.VMEM(x.shape, x.dtype),
        in_specs=[HBM],
        out_specs=VMEM,
        scratch_shapes=[pltpu.SemaphoreType.DMA],
        compiler_params=limit(8),
        name="fetch",
    )(far(x))


def block_and_rows(here):
    at_row = here[:KPB].astype(jnp.int32) + ROW_SHIFT
    return at_row[:1] // BW, at_row % BW


def row_axis_of(tok_rows):
    return lax.broadcasted_iota(jnp.int32, (BW, tok_rows), 0)


def coefficients(here):
    block, feats = block_and_rows(here)
    row_axis = row_axis_of(here.shape[1])
    dense = jnp.zeros(row_axis.shape, jnp.float32)
    for k in range(KPB):
        dense = jnp.where(row_axis == feats[k : k + 1], here[KPB + k : KPB + k + 1], dense)
    parts = [jnp.where(block == b, dense, 0.0) for b in range(BLK_DEV)]
    return jnp.concatenate(parts, axis=0).astype(jnp.bfloat16)


def pick(scores, here):
    block, feats = block_and_rows(here)
    row_axis = row_axis_of(here.shape[1])
    mine = scores[:BW]
    for b in range(1, BLK_DEV):
        mine = jnp.where(block == b, scores[b * BW : (b + 1) * BW], mine)
    return [
        jnp.sum(jnp.where(row_axis == feats[k : k + 1], mine, 0.0), axis=0, keepdims=True)
        for k in range(KPB)
    ]


def facts_in(piece, distance, tok_rows):
    facts = piece[piece.shape[0] - FACTS :, :].astype(jnp.float32)
    return facts[(abs(distance) - 1) * 2 * KPB : abs(distance) * 2 * KPB]


def columns_of(pieces, tok_rows, parts):
    rows = [
        jnp.concatenate([piece[j * tok_rows : (j + 1) * tok_rows, :] for j in parts], axis=1)
        for piece in pieces
    ]
    return jnp.concatenate(rows, axis=0) if len(rows) > 1 else rows[0]


def picks_of(facts, decoder, pieces):
    picks = []
    tok_rows = facts[0].shape[1]
    cut = decoder.shape[1] // 2
    for first in range(0, len(facts), 2):
        count = min(2, len(facts) - first)
        scores = None
        for side in range(2):
            part = lax.dot_general(
                decoder[:, side * cut : (side + 1) * cut],
                columns_of(
                    pieces[2 * first + side : 2 * (first + count) : 2],
                    tok_rows,
                    range(cut // 128),
                ),
                (((1,), (1,)), ((), ())),
                preferred_element_type=jnp.float32,
            )
            scores = part if scores is None else scores + part
        for i in range(first, first + count):
            here = scores[:, (i - first) * tok_rows : (i - first + 1) * tok_rows]
            picks.append(jnp.concatenate(pick(here, facts[i]) * 2, axis=0))
    return picks


def gradient_blocks(facts, pieces, width):
    tok_rows = facts[0].shape[1]
    cut = width // 2
    dense = jnp.concatenate([coefficients(here) for here in facts], axis=1)
    for side in range(2):
        for j in range(0, cut // 128, 2):
            rows = columns_of(pieces[side::2], tok_rows, (j, j + 1))
            part = jnp.dot(dense, rows, preferred_element_type=jnp.float32)
            yield slice(side * cut + j * 128, side * cut + (j + 2) * 128), part


def absorb_kernel(distances, later, split, decoder, own_facts, *refs):
    count = len(distances)
    pieces, refs = refs[: 2 * count], refs[2 * count :]
    picked, total = refs[-1 - count : -1], refs[-1]
    tok_rows = own_facts.shape[1]
    facts = [
        own_facts[...] if d == 0 else facts_in(pieces[2 * i + (d > 0)], d, tok_rows)
        for i, d in enumerate(distances)
    ]
    picks = picks_of(facts, decoder, pieces)
    if split:
        first = lax.axis_index("width") == 0
        picks = jnp.where(first, *picks), jnp.where(first, *picks[::-1])
    for target, values in zip(picked, picks):
        target[...] = values
    for columns, part in gradient_blocks(facts, pieces, decoder.shape[1]):
        total[:, columns] = refs[0][:, columns] + part if later else part


def absorb(distances, pairs, decoder, own_facts, total=None):
    later = total is not None
    tok_rows = own_facts.shape[1]
    operands = [kept(decoder), kept(own_facts)]
    operands += [kept(piece) for pair in pairs for piece in pair]
    operands += [] if total is None else [kept(total)]
    count = len(distances)
    *picked, total = pl.pallas_call(
        functools.partial(absorb_kernel, distances, later, later),
        out_shape=(
            *[pltpu.VMEM((2 * KPB, tok_rows), jnp.float32)] * count,
            pltpu.VMEM(decoder.shape, jnp.float32),
        ),
        in_specs=[VMEM] * len(operands),
        out_specs=(VMEM,) * (count + 1),
        input_output_aliases={} if total is None else {len(operands) - 1: count},
        compiler_params=limit(16),
        name="absorb",
    )(*operands)
    return picked, total


def last_scores_kernel(distance, decoder, left, right, picked):
    facts = [facts_in(left, distance, picked.shape[1])]
    picked[...] = picks_of(facts, decoder, (left, right))[0]


def last_scores(distance, pair, decoder, tok_rows):
    return pl.pallas_call(
        functools.partial(last_scores_kernel, distance),
        out_shape=pltpu.VMEM((2 * KPB, tok_rows), jnp.float32),
        in_specs=[VMEM] * 3,
        out_specs=VMEM,
        compiler_params=limit(12),
        name="last_scores",
    )(kept(decoder), kept(pair[0]), kept(pair[1]))


def last_gradients_kernel(distance, tok_rows, left, right, total, out, rounded, sems):
    facts = [facts_in(left, distance, tok_rows)]
    copies = []
    for columns, part in gradient_blocks(facts, (left, right), out.shape[1]):
        rounded[:, columns] = (total[:, columns] + part).astype(out.dtype)
        copies.append(
            pltpu.make_async_copy(
                rounded.at[:, columns], out.at[:, columns], sems.at[len(copies)]
            )
        )
        copies[-1].start()
    for copy in copies:
        copy.wait()


def last_gradients(distance, pair, total, tok_rows):
    return pl.pallas_call(
        functools.partial(last_gradients_kernel, distance, tok_rows),
        out_shape=jax.ShapeDtypeStruct(total.shape, jnp.bfloat16),
        in_specs=[VMEM] * 3,
        out_specs=ANY,
        scratch_shapes=[
            pltpu.VMEM(total.shape, jnp.bfloat16),
            pltpu.SemaphoreType.DMA((total.shape[1] // 256,)),
        ],
        compiler_params=limit(16),
        name="last_gradients",
    )(kept(pair[0]), kept(pair[1]), kept(total))


def stamp_kernel(left, right, for_left, for_right, left_out, right_out, rows, sems):
    start = left.shape[0] - FACTS
    targets = (left_out, right_out)
    for i, piece in enumerate((left, right)):
        pltpu.make_async_copy(
            piece.at[start : start + 16, :], rows.at[i], sems.at[i]
        ).start()
    for i, values in enumerate((for_left, for_right)):
        pltpu.make_async_copy(
            left.at[start : start + 16, :], rows.at[i], sems.at[i]
        ).wait()
        value = values[:KPB]
        high = value.astype(jnp.bfloat16).astype(jnp.float32)
        low = value - high
        facts = rows[i].astype(jnp.float32)[2 * KPB :]
        rows[i] = jnp.concatenate([high, low, facts], axis=0).astype(jnp.bfloat16)
        pltpu.make_async_copy(
            rows.at[i], targets[i].at[start : start + 16, :], sems.at[2 + i]
        ).start()
    for i in range(2):
        pltpu.make_async_copy(
            rows.at[i], targets[i].at[start : start + 16, :], sems.at[2 + i]
        ).wait()


def stamp(pieces, values):
    return pl.pallas_call(
        stamp_kernel,
        out_shape=tuple(pltpu.VMEM(piece.shape, piece.dtype) for piece in pieces),
        in_specs=[ANY, ANY, VMEM, VMEM],
        out_specs=(ANY, ANY),
        scratch_shapes=[
            pltpu.VMEM((2, 16, 128), jnp.bfloat16),
            pltpu.SemaphoreType.DMA((4,)),
        ],
        input_output_aliases={0: 0, 1: 1},
        compiler_params=limit(4),
        name="stamp",
    )(*[kept(piece) for piece in pieces], *[kept(value) for value in values])


def unpack_kernel(owners, slots, own, left, right, second, third, opposite, out):
    owner = slots[...] // BLK_DEV
    start = left.shape[0] - FACTS
    way = 1 - 2 * lax.axis_index("width")
    returned = [(0, own[...])]
    for distance, piece in ((-1, left), (1, right)):
        rows = piece[start : start + 16, :].astype(jnp.float32)
        returned.append((distance, rows[:KPB] + rows[KPB : 2 * KPB]))
    returned += [(2 * way, second[...]), (3 * way, third[...]), (4, opposite[...])]
    mine = [owner == peer_at(distance, owners) for distance, _ in returned]
    for k in range(KPB):
        total = jnp.zeros(owner.shape, jnp.float32)
        for here, (_, values) in zip(mine, returned):
            total = jnp.where(here, values[k : k + 1, :], total)
        out[pl.ds(k, ACT, stride=KPB), :] = total


def unpack(slots, *returned):
    tok_rows = slots.shape[1]
    return pl.pallas_call(
        functools.partial(unpack_kernel, lax.axis_size("dp")),
        out_shape=pltpu.VMEM((ACT * KPB, tok_rows), jnp.float32),
        in_specs=[VMEM] * (1 + len(returned)),
        out_specs=VMEM,
        compiler_params=limit(4),
        name="unpack",
    )(kept(slots), *[kept(x) for x in returned])


def every_owner(decoder, grad_out, active_blocks, feature_idx, acts, block_slot):
    tok_rows = grad_out.shape[0]
    owners = lax.axis_size("dp")
    ring = ring_of(owners)

    def shift(x, by):
        pairs = [(ring[i], ring[(i + by) % owners]) for i in range(owners)]
        return lax.ppermute(x, "dp", pairs)

    def hop(pieces):
        left, right = pieces
        return shift(left, 1), shift(right, -1)

    def crossed(pieces):
        right, left = pieces
        return shift(right, 1), shift(left, -1)

    def other_core(x):
        return lax.ppermute(x, "width", ((0, 1), (1, 0)))

    def return_by(distance, mine, others):
        pairs = []
        for i in range(owners):
            pairs.append((2 * ring[i], 2 * ring[(i - distance) % owners]))
            pairs.append((2 * ring[i] + 1, 2 * ring[(i + distance) % owners] + 1))
        return lax.ppermute(mine + other_core(others), ("dp", "width"), pairs)

    left, right, own_facts, slots = prepare(
        block_slot, active_blocks, feature_idx, acts, grad_out, owners
    )
    first_1 = hop((left, right))
    second_1 = crossed((right, left))
    decoder = fetch(decoder)
    first_1, decoder = lax.optimization_barrier((first_1, decoder))
    first_2 = hop(first_1)
    second_2 = crossed(second_1)
    pairs = [(left, right), (first_1[0], second_1[0]), (second_1[1], first_1[1])]
    (own, onward, back), total = absorb((0, -1, 1), pairs, decoder, own_facts)
    first_2 = stamp(first_2, (back, onward))
    first_3 = hop(first_2)
    second_3 = crossed(second_2)
    pairs = [(first_2[0], second_2[0]), (second_2[1], first_2[1])]
    (mine, others), total = absorb((-2, 2), pairs, decoder, own_facts, total)
    total, first_3 = lax.optimization_barrier((total, first_3))
    second = return_by(2, mine, others)
    first_4 = hop(first_3)
    pairs = [(first_3[0], second_3[0]), (second_3[1], first_3[1])]
    (mine, others), total = absorb((-3, 3), pairs, decoder, own_facts, total)
    third = return_by(3, mine, others)
    total, first_4, second = lax.optimization_barrier((total, first_4, second))
    opposite = shift(last_scores(4, first_4, decoder, tok_rows), -4)
    decoder_grad = last_gradients(4, first_4, total, tok_rows)
    act_grad = unpack(slots, own, *first_3, second, third, opposite)
    act_grad = act_grad + other_core(act_grad)
    return (decoder_grad, act_grad.T)


def send_back(picked):
    return lax.all_to_all(picked, "dp", split_axis=1, concat_axis=1, tiled=True)


def pack_slots(grad_out, target, slots_all, pair_coeffs, pair_columns, source_row):
    slot_row = jnp.zeros((slots_all,), jnp.int32).at[target].set(source_row)
    used = jnp.zeros((slots_all,), jnp.bool_).at[target].set(True)
    send_rows = jnp.where(used[:, None], grad_out[slot_row], jnp.zeros((), grad_out.dtype))
    send_acts = jnp.zeros((slots_all, KPB), pair_coeffs.dtype).at[target].set(pair_coeffs)
    send_cols = jnp.zeros((slots_all, KPB), jnp.int32).at[target].set(pair_columns)
    return (send_rows, send_acts, send_cols)


def some_owners(decoder, grad_out, active_blocks, feature_idx, acts, block_slot):
    tok_rows, half_width = grad_out.shape
    owners = lax.axis_size("dp")
    mean_load = tok_rows * ACT // owners
    owner_cap = mean_load + min(mean_load // 2, tok_rows - mean_load)
    block_cap = (owner_cap + 2) // 3
    block_ids = active_blocks.reshape(-1)
    pair_count = block_ids.shape[0]
    table_pos = jnp.arange(block_slot.shape[0], dtype=jnp.int32)
    slot_of = jnp.sum(
        jnp.where(block_ids[:, None] == table_pos[None, :], block_slot[None, :], 0), axis=1
    )
    pair_pos = jnp.arange(pair_count, dtype=jnp.int32)
    source_row = pair_pos // ACT
    pair_coeffs = acts.reshape(pair_count, KPB)
    pair_feats = feature_idx.reshape(pair_count, KPB)
    earlier = (block_ids[:, None] == block_ids[None, :]) & (pair_pos[None, :] < pair_pos[:, None])
    position = jnp.sum(earlier.astype(jnp.int32), axis=1)
    slot_cols = owners * block_cap
    target = slot_of % BLK_DEV * slot_cols + slot_of // BLK_DEV * block_cap + position
    slots_all = BLK_DEV * slot_cols
    send_rows, send_acts, send_cols = pack_slots(
        grad_out, target, slots_all, pair_coeffs, pair_feats, source_row
    )
    rows, coeffs, feature_pos = (
        lax.all_to_all(
            send_rows.reshape(BLK_DEV, slot_cols, half_width),
            "dp",
            split_axis=1,
            concat_axis=1,
            tiled=True,
        ),
        lax.all_to_all(
            send_acts.reshape(BLK_DEV, slot_cols, KPB),
            "dp",
            split_axis=1,
            concat_axis=1,
            tiled=True,
        ),
        lax.all_to_all(
            send_cols.reshape(BLK_DEV, slot_cols, KPB),
            "dp",
            split_axis=1,
            concat_axis=1,
            tiled=True,
        ),
    )
    weights = decoder.reshape(BLK_DEV, BW, half_width)
    scores = jnp.einsum("bnd,bfd->bnf", rows, weights, preferred_element_type=jnp.float32)
    picked = jnp.take_along_axis(scores, feature_pos, axis=2)
    returned = send_back(picked)
    feature_axis = jnp.arange(BW, dtype=jnp.int32)
    matches = feature_pos[..., None] == feature_axis
    dense = jnp.sum(jnp.where(matches, coeffs[..., None].astype(jnp.float32), 0.0), axis=2).astype(
        jnp.bfloat16
    )
    grads = jnp.einsum("bnf,bnd->bfd", dense, rows, preferred_element_type=jnp.float32)
    decoder_grad = grads.astype(jnp.bfloat16).reshape(BLK_DEV * BW, half_width)
    pair_vals = returned.reshape(slots_all, KPB)[target]
    act_grad = pair_vals.reshape(tok_rows, ACT * KPB)
    act_grad = lax.psum(act_grad, "width")
    return (decoder_grad, act_grad)


def per_device(*args):
    if lax.axis_size("dp") == ACT:
        return every_owner(*args)
    return some_owners(*args)


def solution(mesh):
    in_specs = (
        P(("groups", "dp"), "width"),
        P(("groups", "dp"), "width"),
        P(("groups", "dp"), None),
        P(("groups", "dp"), None),
        P(("groups", "dp"), None),
        P("groups"),
    )
    out_specs = (P(("groups", "dp"), "width"), P(("groups", "dp"), None))
    return jax.shard_map(
        per_device, mesh=mesh, in_specs=in_specs, out_specs=out_specs, check_vma=False
    )
```

```python
import functools

import jax
import jax.numpy as jnp
from jax import lax
from jax.experimental import pallas as pl
from jax.experimental.pallas import tpu as pltpu
from jax.sharding import PartitionSpec as P

BW = 128
BLK_DEV = 4
ACT = 8
KPB = 4
SMEM = pl.BlockSpec(memory_space=pltpu.SMEM)
VMEM = pl.BlockSpec(memory_space=pltpu.VMEM)
ANY = pl.BlockSpec(memory_space=pl.ANY)
HBM = pl.BlockSpec(memory_space=pltpu.HBM)


def limit(mebibytes):
    return pltpu.CompilerParams(vmem_limit_bytes=mebibytes * 2**20)


def kept(x):
    return pltpu.with_memory_space_constraint(x, pltpu.VMEM)


def far(x):
    return pltpu.with_memory_space_constraint(x, pltpu.HBM)


def ring_of(owners):
    return list(range(0, owners, 2)) + list(range(owners - 1, 0, -2))


def peer_at(distance, owners):
    me = lax.axis_index("dp")
    half_ring = owners // 2
    place = jnp.where(lax.rem(me, 2) == 0, lax.div(me, 2), owners - 1 - lax.div(me, 2))
    at = lax.rem(place + owners + distance, owners)
    return jnp.where(at < half_ring, 2 * at, 2 * (owners - 1 - at) + 1)


ROW_SHIFT = BLK_DEV * BW // 2
FACTS = ACT // 2 * 2 * KPB


def facts_for(owner_id, owner, first_row, feats, acts):
    mine = owner == owner_id
    rows = [
        jnp.sum(jnp.where(mine, first_row + feats[k], 0.0), axis=0, keepdims=True) - ROW_SHIFT
        for k in range(KPB)
    ]
    values = [
        jnp.sum(jnp.where(mine, acts[k], 0.0), axis=0, keepdims=True) for k in range(KPB)
    ]
    return jnp.concatenate(rows + values, axis=0)


def prepare_kernel(
    owners, *refs
):
    sources, refs = refs[:5], refs[5:]
    left, right, own_facts, slots = refs[:4]
    block_slot, active, feats, acts, wide_feats, wide_acts, sems = refs[4:]
    grad_out = sources[-1]
    tok_rows, width = grad_out.shape
    parts = width // 256
    small = []
    for source, target in zip(sources[:4], (block_slot, active, feats, acts)):
        small.append(pltpu.make_async_copy(source, target, sems.at[len(small)]))
        small[-1].start()
    copies = []
    for j in range(parts):
        for target, side in ((left, 0), (right, 1)):
            column = (side * parts + j) * 128
            copies.append(
                pltpu.make_async_copy(
                    grad_out.at[:, column : column + 128],
                    target.at[j * tok_rows : (j + 1) * tok_rows, :],
                    sems.at[len(small) + len(copies)],
                )
            )
            copies[-1].start()
    for copy in small:
        copy.wait()
    named = active[...]
    slot = jnp.zeros_like(named)
    for block in range(block_slot.shape[0]):
        slot = jnp.where(named == block, block_slot[block], slot)
    slots[...] = slot
    wide_feats[...] = feats[...].astype(jnp.float32)
    wide_acts[...] = acts[...].astype(jnp.float32)
    features = [wide_feats[pl.ds(k, ACT, stride=KPB), :] for k in range(KPB)]
    values = [wide_acts[pl.ds(k, ACT, stride=KPB), :] for k in range(KPB)]
    first_row = (slot % BLK_DEV * BW).astype(jnp.float32)

    def facts(distance):
        return facts_for(
            peer_at(distance, owners), slot // BLK_DEV, first_row, features, values
        )

    reach = owners // 2
    own_facts[...] = facts(0)
    start = parts * tok_rows
    for target, sign in ((left, 1), (right, -1)):
        ahead = [facts(sign * d) for d in range(1, reach + 1)]
        target[start:, :] = jnp.concatenate(ahead, axis=0).astype(jnp.bfloat16)
    for copy in copies:
        copy.wait()


def prepare(block_slot, active_blocks, feature_idx, acts, grad_out, owners):
    tok_rows, half_width = grad_out.shape
    plain = half_width // 256 * tok_rows
    return pl.pallas_call(
        functools.partial(prepare_kernel, owners),
        out_shape=(
            pltpu.VMEM((plain + FACTS, 128), grad_out.dtype),
            pltpu.VMEM((plain + FACTS, 128), grad_out.dtype),
            pltpu.VMEM((2 * KPB, tok_rows), jnp.float32),
            pltpu.VMEM((ACT, tok_rows), jnp.int32),
        ),
        in_specs=[HBM] * 5,
        out_specs=(VMEM,) * 4,
        scratch_shapes=[
            pltpu.SMEM(block_slot.shape, jnp.int32),
            pltpu.VMEM((ACT, tok_rows), jnp.int32),
            pltpu.VMEM((ACT * KPB, tok_rows), jnp.int32),
            pltpu.VMEM((ACT * KPB, tok_rows), acts.dtype),
            pltpu.VMEM((ACT * KPB, tok_rows), jnp.float32),
            pltpu.VMEM((ACT * KPB, tok_rows), jnp.float32),
            pltpu.SemaphoreType.DMA((4 + half_width // 128,)),
        ],
        compiler_params=limit(8),
        name="prepare",
    )(far(block_slot), far(active_blocks.T), far(feature_idx.T), far(acts.T), far(grad_out))


def fetch_kernel(source, target, sem):
    copy = pltpu.make_async_copy(source, target, sem)
    copy.start()
    copy.wait()


def fetch(x):
    return pl.pallas_call(
        fetch_kernel,
        out_shape=pltpu.VMEM(x.shape, x.dtype),
        in_specs=[HBM],
        out_specs=VMEM,
        scratch_shapes=[pltpu.SemaphoreType.DMA],
        compiler_params=limit(8),
        name="fetch",
    )(far(x))


def block_and_rows(here):
    at_row = here[:KPB].astype(jnp.int32) + ROW_SHIFT
    return at_row[:1] // BW, at_row % BW


def row_axis_of(tok_rows):
    return lax.broadcasted_iota(jnp.int32, (BW, tok_rows), 0)


def coefficients(here):
    block, feats = block_and_rows(here)
    row_axis = row_axis_of(here.shape[1])
    dense = jnp.zeros(row_axis.shape, jnp.float32)
    for k in range(KPB):
        dense = jnp.where(row_axis == feats[k : k + 1], here[KPB + k : KPB + k + 1], dense)
    parts = [jnp.where(block == b, dense, 0.0) for b in range(BLK_DEV)]
    return jnp.concatenate(parts, axis=0).astype(jnp.bfloat16)


def pick(scores, here):
    block, feats = block_and_rows(here)
    row_axis = row_axis_of(here.shape[1])
    mine = scores[:BW]
    for b in range(1, BLK_DEV):
        mine = jnp.where(block == b, scores[b * BW : (b + 1) * BW], mine)
    return [
        jnp.sum(jnp.where(row_axis == feats[k : k + 1], mine, 0.0), axis=0, keepdims=True)
        for k in range(KPB)
    ]


def facts_in(piece, distance, tok_rows):
    facts = piece[piece.shape[0] - FACTS :, :].astype(jnp.float32)
    return facts[(abs(distance) - 1) * 2 * KPB : abs(distance) * 2 * KPB]


def columns_of(pieces, tok_rows, parts):
    rows = [
        jnp.concatenate([piece[j * tok_rows : (j + 1) * tok_rows, :] for j in parts], axis=1)
        for piece in pieces
    ]
    return jnp.concatenate(rows, axis=0) if len(rows) > 1 else rows[0]


def picks_of(facts, decoder, pieces):
    picks = []
    tok_rows = facts[0].shape[1]
    cut = decoder.shape[1] // 2
    for first in range(0, len(facts), 2):
        count = min(2, len(facts) - first)
        scores = None
        for side in range(2):
            part = lax.dot_general(
                decoder[:, side * cut : (side + 1) * cut],
                columns_of(
                    pieces[2 * first + side : 2 * (first + count) : 2],
                    tok_rows,
                    range(cut // 128),
                ),
                (((1,), (1,)), ((), ())),
                preferred_element_type=jnp.float32,
            )
            scores = part if scores is None else scores + part
        for i in range(first, first + count):
            here = scores[:, (i - first) * tok_rows : (i - first + 1) * tok_rows]
            picks.append(jnp.concatenate(pick(here, facts[i]) * 2, axis=0))
    return picks


def gradient_blocks(facts, pieces, width):
    tok_rows = facts[0].shape[1]
    cut = width // 2
    dense = jnp.concatenate([coefficients(here) for here in facts], axis=1)
    for side in range(2):
        for j in range(0, cut // 128, 2):
            rows = columns_of(pieces[side::2], tok_rows, (j, j + 1))
            part = jnp.dot(dense, rows, preferred_element_type=jnp.float32)
            yield slice(side * cut + j * 128, side * cut + (j + 2) * 128), part


def absorb_kernel(distances, later, split, decoder, own_facts, *refs):
    count = len(distances)
    pieces, refs = refs[: 2 * count], refs[2 * count :]
    picked, total = refs[-1 - count : -1], refs[-1]
    tok_rows = own_facts.shape[1]
    facts = [
        own_facts[...] if d == 0 else facts_in(pieces[2 * i + (d > 0)], d, tok_rows)
        for i, d in enumerate(distances)
    ]
    picks = picks_of(facts, decoder, pieces)
    if split:
        first = lax.axis_index("width") == 0
        picks = jnp.where(first, *picks), jnp.where(first, *picks[::-1])
    for target, values in zip(picked, picks):
        target[...] = values
    for columns, part in gradient_blocks(facts, pieces, decoder.shape[1]):
        total[:, columns] = refs[0][:, columns] + part if later else part


def absorb(distances, pairs, decoder, own_facts, total=None):
    later = total is not None
    tok_rows = own_facts.shape[1]
    operands = [kept(decoder), kept(own_facts)]
    operands += [kept(piece) for pair in pairs for piece in pair]
    operands += [] if total is None else [kept(total)]
    count = len(distances)
    *picked, total = pl.pallas_call(
        functools.partial(absorb_kernel, distances, later, later),
        out_shape=(
            *[pltpu.VMEM((2 * KPB, tok_rows), jnp.float32)] * count,
            pltpu.VMEM(decoder.shape, jnp.float32),
        ),
        in_specs=[VMEM] * len(operands),
        out_specs=(VMEM,) * (count + 1),
        input_output_aliases={} if total is None else {len(operands) - 1: count},
        compiler_params=limit(16),
        name="absorb",
    )(*operands)
    return picked, total


def last_scores_kernel(distance, decoder, left, right, picked):
    facts = [facts_in(left, distance, picked.shape[1])]
    picked[...] = picks_of(facts, decoder, (left, right))[0]


def last_scores(distance, pair, decoder, tok_rows):
    return pl.pallas_call(
        functools.partial(last_scores_kernel, distance),
        out_shape=pltpu.VMEM((2 * KPB, tok_rows), jnp.float32),
        in_specs=[VMEM] * 3,
        out_specs=VMEM,
        compiler_params=limit(12),
        name="last_scores",
    )(kept(decoder), kept(pair[0]), kept(pair[1]))


def last_gradients_kernel(distance, tok_rows, left, right, total, out, rounded, sems):
    facts = [facts_in(left, distance, tok_rows)]
    copies = []
    for columns, part in gradient_blocks(facts, (left, right), out.shape[1]):
        rounded[:, columns] = (total[:, columns] + part).astype(out.dtype)
        copies.append(
            pltpu.make_async_copy(
                rounded.at[:, columns], out.at[:, columns], sems.at[len(copies)]
            )
        )
        copies[-1].start()
    for copy in copies:
        copy.wait()


def last_gradients(distance, pair, total, tok_rows):
    return pl.pallas_call(
        functools.partial(last_gradients_kernel, distance, tok_rows),
        out_shape=jax.ShapeDtypeStruct(total.shape, jnp.bfloat16),
        in_specs=[VMEM] * 3,
        out_specs=ANY,
        scratch_shapes=[
            pltpu.VMEM(total.shape, jnp.bfloat16),
            pltpu.SemaphoreType.DMA((total.shape[1] // 256,)),
        ],
        compiler_params=limit(16),
        name="last_gradients",
    )(kept(pair[0]), kept(pair[1]), kept(total))


def stamp_kernel(left, right, for_left, for_right, left_out, right_out, rows, sems):
    start = left.shape[0] - FACTS
    targets = (left_out, right_out)
    for i, piece in enumerate((left, right)):
        pltpu.make_async_copy(
            piece.at[start : start + 16, :], rows.at[i], sems.at[i]
        ).start()
    for i, values in enumerate((for_left, for_right)):
        pltpu.make_async_copy(
            left.at[start : start + 16, :], rows.at[i], sems.at[i]
        ).wait()
        value = values[:KPB]
        high = value.astype(jnp.bfloat16).astype(jnp.float32)
        low = value - high
        facts = rows[i].astype(jnp.float32)[2 * KPB :]
        rows[i] = jnp.concatenate([high, low, facts], axis=0).astype(jnp.bfloat16)
        pltpu.make_async_copy(
            rows.at[i], targets[i].at[start : start + 16, :], sems.at[2 + i]
        ).start()
    for i in range(2):
        pltpu.make_async_copy(
            rows.at[i], targets[i].at[start : start + 16, :], sems.at[2 + i]
        ).wait()


def stamp(pieces, values):
    return pl.pallas_call(
        stamp_kernel,
        out_shape=tuple(pltpu.VMEM(piece.shape, piece.dtype) for piece in pieces),
        in_specs=[ANY, ANY, VMEM, VMEM],
        out_specs=(ANY, ANY),
        scratch_shapes=[
            pltpu.VMEM((2, 16, 128), jnp.bfloat16),
            pltpu.SemaphoreType.DMA((4,)),
        ],
        input_output_aliases={0: 0, 1: 1},
        compiler_params=limit(4),
        name="stamp",
    )(*[kept(piece) for piece in pieces], *[kept(value) for value in values])


def unpack_kernel(owners, slots, own, left, right, second, third, opposite, out):
    owner = slots[...] // BLK_DEV
    start = left.shape[0] - FACTS
    way = 1 - 2 * lax.axis_index("width")
    returned = [(0, own[...])]
    for distance, piece in ((-1, left), (1, right)):
        rows = piece[start : start + 16, :].astype(jnp.float32)
        returned.append((distance, rows[:KPB] + rows[KPB : 2 * KPB]))
    returned += [(2 * way, second[...]), (3 * way, third[...]), (4, opposite[...])]
    mine = [owner == peer_at(distance, owners) for distance, _ in returned]
    for k in range(KPB):
        total = jnp.zeros(owner.shape, jnp.float32)
        for here, (_, values) in zip(mine, returned):
            total = jnp.where(here, values[k : k + 1, :], total)
        out[pl.ds(k, ACT, stride=KPB), :] = total


def unpack(slots, *returned):
    tok_rows = slots.shape[1]
    return pl.pallas_call(
        functools.partial(unpack_kernel, lax.axis_size("dp")),
        out_shape=pltpu.VMEM((ACT * KPB, tok_rows), jnp.float32),
        in_specs=[VMEM] * (1 + len(returned)),
        out_specs=VMEM,
        compiler_params=limit(4),
        name="unpack",
    )(kept(slots), *[kept(x) for x in returned])


def every_owner(decoder, grad_out, active_blocks, feature_idx, acts, block_slot):
    tok_rows = grad_out.shape[0]
    owners = lax.axis_size("dp")
    ring = ring_of(owners)

    def shift(x, by):
        pairs = [(ring[i], ring[(i + by) % owners]) for i in range(owners)]
        return lax.ppermute(x, "dp", pairs)

    def hop(pieces):
        left, right = pieces
        return shift(left, 1), shift(right, -1)

    def crossed(pieces):
        right, left = pieces
        return shift(right, 1), shift(left, -1)

    def other_core(x):
        return lax.ppermute(x, "width", ((0, 1), (1, 0)))

    def return_by(distance, mine, others):
        pairs = []
        for i in range(owners):
            pairs.append((2 * ring[i], 2 * ring[(i - distance) % owners]))
            pairs.append((2 * ring[i] + 1, 2 * ring[(i + distance) % owners] + 1))
        return lax.ppermute(mine + other_core(others), ("dp", "width"), pairs)

    left, right, own_facts, slots = prepare(
        block_slot, active_blocks, feature_idx, acts, grad_out, owners
    )
    first_1 = hop((left, right))
    second_1 = crossed((right, left))
    decoder = fetch(decoder)
    first_1, decoder = lax.optimization_barrier((first_1, decoder))
    first_2 = hop(first_1)
    second_2 = crossed(second_1)
    pairs = [(left, right), (first_1[0], second_1[0]), (second_1[1], first_1[1])]
    (own, onward, back), total = absorb((0, -1, 1), pairs, decoder, own_facts)
    first_2 = stamp(first_2, (back, onward))
    first_3 = hop(first_2)
    second_3 = crossed(second_2)
    pairs = [(first_2[0], second_2[0]), (second_2[1], first_2[1])]
    (mine, others), total = absorb((-2, 2), pairs, decoder, own_facts, total)
    total, first_3 = lax.optimization_barrier((total, first_3))
    second = return_by(2, mine, others)
    first_4 = hop(first_3)
    pairs = [(first_3[0], second_3[0]), (second_3[1], first_3[1])]
    (mine, others), total = absorb((-3, 3), pairs, decoder, own_facts, total)
    third = return_by(3, mine, others)
    total, first_4, second = lax.optimization_barrier((total, first_4, second))
    opposite = shift(last_scores(4, first_4, decoder, tok_rows), -4)
    decoder_grad = last_gradients(4, first_4, total, tok_rows)
    decoder_grad, opposite = lax.optimization_barrier((decoder_grad, opposite))
    act_grad = unpack(slots, own, *first_3, second, third, opposite)
    act_grad = act_grad + other_core(act_grad)
    return (decoder_grad, act_grad.T)


def send_back(picked):
    return lax.all_to_all(picked, "dp", split_axis=1, concat_axis=1, tiled=True)


def pack_slots(grad_out, target, slots_all, pair_coeffs, pair_columns, source_row):
    slot_row = jnp.zeros((slots_all,), jnp.int32).at[target].set(source_row)
    used = jnp.zeros((slots_all,), jnp.bool_).at[target].set(True)
    send_rows = jnp.where(used[:, None], grad_out[slot_row], jnp.zeros((), grad_out.dtype))
    send_acts = jnp.zeros((slots_all, KPB), pair_coeffs.dtype).at[target].set(pair_coeffs)
    send_cols = jnp.zeros((slots_all, KPB), jnp.int32).at[target].set(pair_columns)
    return (send_rows, send_acts, send_cols)


def some_owners(decoder, grad_out, active_blocks, feature_idx, acts, block_slot):
    tok_rows, half_width = grad_out.shape
    owners = lax.axis_size("dp")
    mean_load = tok_rows * ACT // owners
    owner_cap = mean_load + min(mean_load // 2, tok_rows - mean_load)
    block_cap = (owner_cap + 2) // 3
    block_ids = active_blocks.reshape(-1)
    pair_count = block_ids.shape[0]
    table_pos = jnp.arange(block_slot.shape[0], dtype=jnp.int32)
    slot_of = jnp.sum(
        jnp.where(block_ids[:, None] == table_pos[None, :], block_slot[None, :], 0), axis=1
    )
    pair_pos = jnp.arange(pair_count, dtype=jnp.int32)
    source_row = pair_pos // ACT
    pair_coeffs = acts.reshape(pair_count, KPB)
    pair_feats = feature_idx.reshape(pair_count, KPB)
    earlier = (block_ids[:, None] == block_ids[None, :]) & (pair_pos[None, :] < pair_pos[:, None])
    position = jnp.sum(earlier.astype(jnp.int32), axis=1)
    slot_cols = owners * block_cap
    target = slot_of % BLK_DEV * slot_cols + slot_of // BLK_DEV * block_cap + position
    slots_all = BLK_DEV * slot_cols
    send_rows, send_acts, send_cols = pack_slots(
        grad_out, target, slots_all, pair_coeffs, pair_feats, source_row
    )
    rows, coeffs, feature_pos = (
        lax.all_to_all(
            send_rows.reshape(BLK_DEV, slot_cols, half_width),
            "dp",
            split_axis=1,
            concat_axis=1,
            tiled=True,
        ),
        lax.all_to_all(
            send_acts.reshape(BLK_DEV, slot_cols, KPB),
            "dp",
            split_axis=1,
            concat_axis=1,
            tiled=True,
        ),
        lax.all_to_all(
            send_cols.reshape(BLK_DEV, slot_cols, KPB),
            "dp",
            split_axis=1,
            concat_axis=1,
            tiled=True,
        ),
    )
    weights = decoder.reshape(BLK_DEV, BW, half_width)
    scores = jnp.einsum("bnd,bfd->bnf", rows, weights, preferred_element_type=jnp.float32)
    picked = jnp.take_along_axis(scores, feature_pos, axis=2)
    returned = send_back(picked)
    feature_axis = jnp.arange(BW, dtype=jnp.int32)
    matches = feature_pos[..., None] == feature_axis
    dense = jnp.sum(jnp.where(matches, coeffs[..., None].astype(jnp.float32), 0.0), axis=2).astype(
        jnp.bfloat16
    )
    grads = jnp.einsum("bnf,bnd->bfd", dense, rows, preferred_element_type=jnp.float32)
    decoder_grad = grads.astype(jnp.bfloat16).reshape(BLK_DEV * BW, half_width)
    pair_vals = returned.reshape(slots_all, KPB)[target]
    act_grad = pair_vals.reshape(tok_rows, ACT * KPB)
    act_grad = lax.psum(act_grad, "width")
    return (decoder_grad, act_grad)


def per_device(*args):
    if lax.axis_size("dp") == ACT:
        return every_owner(*args)
    return some_owners(*args)


def solution(mesh):
    in_specs = (
        P(("groups", "dp"), "width"),
        P(("groups", "dp"), "width"),
        P(("groups", "dp"), None),
        P(("groups", "dp"), None),
        P(("groups", "dp"), None),
        P("groups"),
    )
    out_specs = (P(("groups", "dp"), "width"), P(("groups", "dp"), None))
    return jax.shard_map(
        per_device, mesh=mesh, in_specs=in_specs, out_specs=out_specs, check_vma=False
    )
```

```python
import functools

import jax
import jax.numpy as jnp
from jax import lax
from jax.experimental import pallas as pl
from jax.experimental.pallas import tpu as pltpu
from jax.sharding import PartitionSpec as P

BW = 128
BLK_DEV = 4
ACT = 8
KPB = 4
SMEM = pl.BlockSpec(memory_space=pltpu.SMEM)
VMEM = pl.BlockSpec(memory_space=pltpu.VMEM)
ANY = pl.BlockSpec(memory_space=pl.ANY)
HBM = pl.BlockSpec(memory_space=pltpu.HBM)


def limit(mebibytes):
    return pltpu.CompilerParams(vmem_limit_bytes=mebibytes * 2**20)


def kept(x):
    return pltpu.with_memory_space_constraint(x, pltpu.VMEM)


def far(x):
    return pltpu.with_memory_space_constraint(x, pltpu.HBM)


def ring_of(owners):
    return list(range(0, owners, 2)) + list(range(owners - 1, 0, -2))


def peer_at(distance, owners):
    me = lax.axis_index("dp")
    half_ring = owners // 2
    place = jnp.where(lax.rem(me, 2) == 0, lax.div(me, 2), owners - 1 - lax.div(me, 2))
    at = lax.rem(place + owners + distance, owners)
    return jnp.where(at < half_ring, 2 * at, 2 * (owners - 1 - at) + 1)


ROW_SHIFT = BLK_DEV * BW // 2
FACTS = ACT // 2 * 2 * KPB


def facts_for(owner_id, owner, first_row, feats, acts):
    mine = owner == owner_id
    rows = [
        jnp.sum(jnp.where(mine, first_row + feats[k], 0.0), axis=0, keepdims=True) - ROW_SHIFT
        for k in range(KPB)
    ]
    values = [
        jnp.sum(jnp.where(mine, acts[k], 0.0), axis=0, keepdims=True) for k in range(KPB)
    ]
    return jnp.concatenate(rows + values, axis=0)


def prepare_kernel(
    owners, *refs
):
    sources, refs = refs[:5], refs[5:]
    left, right, own_facts, slots = refs[:4]
    block_slot, active, feats, acts, wide_feats, wide_acts, sems = refs[4:]
    grad_out = sources[-1]
    tok_rows, width = grad_out.shape
    parts = width // 256
    small = []
    for source, target in zip(sources[:4], (block_slot, active, feats, acts)):
        small.append(pltpu.make_async_copy(source, target, sems.at[len(small)]))
        small[-1].start()
    copies = []
    for j in range(parts):
        for target, side in ((left, 0), (right, 1)):
            column = (side * parts + j) * 128
            copies.append(
                pltpu.make_async_copy(
                    grad_out.at[:, column : column + 128],
                    target.at[j * tok_rows : (j + 1) * tok_rows, :],
                    sems.at[len(small) + len(copies)],
                )
            )
            copies[-1].start()
    for copy in small:
        copy.wait()
    named = active[...]
    slot = jnp.zeros_like(named)
    for block in range(block_slot.shape[0]):
        slot = jnp.where(named == block, block_slot[block], slot)
    slots[...] = slot
    wide_feats[...] = feats[...].astype(jnp.float32)
    wide_acts[...] = acts[...].astype(jnp.float32)
    features = [wide_feats[pl.ds(k, ACT, stride=KPB), :] for k in range(KPB)]
    values = [wide_acts[pl.ds(k, ACT, stride=KPB), :] for k in range(KPB)]
    first_row = (slot % BLK_DEV * BW).astype(jnp.float32)

    def facts(distance):
        return facts_for(
            peer_at(distance, owners), slot // BLK_DEV, first_row, features, values
        )

    reach = owners // 2
    own_facts[...] = facts(0)
    start = parts * tok_rows
    for target, sign in ((left, 1), (right, -1)):
        ahead = [facts(sign * d) for d in range(1, reach + 1)]
        target[start:, :] = jnp.concatenate(ahead, axis=0).astype(jnp.bfloat16)
    for copy in copies:
        copy.wait()


def prepare(block_slot, active_blocks, feature_idx, acts, grad_out, owners):
    tok_rows, half_width = grad_out.shape
    plain = half_width // 256 * tok_rows
    return pl.pallas_call(
        functools.partial(prepare_kernel, owners),
        out_shape=(
            pltpu.VMEM((plain + FACTS, 128), grad_out.dtype),
            pltpu.VMEM((plain + FACTS, 128), grad_out.dtype),
            pltpu.VMEM((2 * KPB, tok_rows), jnp.float32),
            pltpu.VMEM((ACT, tok_rows), jnp.int32),
        ),
        in_specs=[HBM] * 5,
        out_specs=(VMEM,) * 4,
        scratch_shapes=[
            pltpu.SMEM(block_slot.shape, jnp.int32),
            pltpu.VMEM((ACT, tok_rows), jnp.int32),
            pltpu.VMEM((ACT * KPB, tok_rows), jnp.int32),
            pltpu.VMEM((ACT * KPB, tok_rows), acts.dtype),
            pltpu.VMEM((ACT * KPB, tok_rows), jnp.float32),
            pltpu.VMEM((ACT * KPB, tok_rows), jnp.float32),
            pltpu.SemaphoreType.DMA((4 + half_width // 128,)),
        ],
        compiler_params=limit(8),
        name="prepare",
    )(far(block_slot), far(active_blocks.T), far(feature_idx.T), far(acts.T), far(grad_out))


def fetch_kernel(source, target, sem):
    copy = pltpu.make_async_copy(source, target, sem)
    copy.start()
    copy.wait()


def fetch(x):
    return pl.pallas_call(
        fetch_kernel,
        out_shape=pltpu.VMEM(x.shape, x.dtype),
        in_specs=[HBM],
        out_specs=VMEM,
        scratch_shapes=[pltpu.SemaphoreType.DMA],
        compiler_params=limit(8),
        name="fetch",
    )(far(x))


def block_and_rows(here):
    at_row = here[:KPB].astype(jnp.int32) + ROW_SHIFT
    return at_row[:1] // BW, at_row % BW


def row_axis_of(tok_rows):
    return lax.broadcasted_iota(jnp.int32, (BW, tok_rows), 0)


def coefficients(here):
    block, feats = block_and_rows(here)
    row_axis = row_axis_of(here.shape[1])
    dense = jnp.zeros(row_axis.shape, jnp.float32)
    for k in range(KPB):
        dense = jnp.where(row_axis == feats[k : k + 1], here[KPB + k : KPB + k + 1], dense)
    parts = [jnp.where(block == b, dense, 0.0) for b in range(BLK_DEV)]
    return jnp.concatenate(parts, axis=0).astype(jnp.bfloat16)


def pick(scores, here):
    block, feats = block_and_rows(here)
    row_axis = row_axis_of(here.shape[1])
    mine = scores[:BW]
    for b in range(1, BLK_DEV):
        mine = jnp.where(block == b, scores[b * BW : (b + 1) * BW], mine)
    return [
        jnp.sum(jnp.where(row_axis == feats[k : k + 1], mine, 0.0), axis=0, keepdims=True)
        for k in range(KPB)
    ]


def facts_in(piece, distance, tok_rows):
    facts = piece[piece.shape[0] - FACTS :, :].astype(jnp.float32)
    return facts[(abs(distance) - 1) * 2 * KPB : abs(distance) * 2 * KPB]


def columns_of(pieces, tok_rows, parts):
    rows = [
        jnp.concatenate([piece[j * tok_rows : (j + 1) * tok_rows, :] for j in parts], axis=1)
        for piece in pieces
    ]
    return jnp.concatenate(rows, axis=0) if len(rows) > 1 else rows[0]


def picks_of(facts, decoder, pieces):
    picks = []
    tok_rows = facts[0].shape[1]
    cut = decoder.shape[1] // 2
    for first in range(0, len(facts), 2):
        count = min(2, len(facts) - first)
        scores = None
        for side in range(2):
            part = lax.dot_general(
                decoder[:, side * cut : (side + 1) * cut],
                columns_of(
                    pieces[2 * first + side : 2 * (first + count) : 2],
                    tok_rows,
                    range(cut // 128),
                ),
                (((1,), (1,)), ((), ())),
                preferred_element_type=jnp.float32,
            )
            scores = part if scores is None else scores + part
        for i in range(first, first + count):
            here = scores[:, (i - first) * tok_rows : (i - first + 1) * tok_rows]
            picks.append(jnp.concatenate(pick(here, facts[i]) * 2, axis=0))
    return picks


def gradient_blocks(facts, pieces, width):
    tok_rows = facts[0].shape[1]
    cut = width // 2
    dense = jnp.concatenate([coefficients(here) for here in facts], axis=1)
    for side in range(2):
        for j in range(0, cut // 128, 2):
            rows = columns_of(pieces[side::2], tok_rows, (j, j + 1))
            part = jnp.dot(dense, rows, preferred_element_type=jnp.float32)
            yield slice(side * cut + j * 128, side * cut + (j + 2) * 128), part


def facts_of(distances, own_facts, pieces):
    tok_rows = own_facts.shape[1]
    return [
        own_facts[...] if d == 0 else facts_in(pieces[2 * i + (d > 0)], d, tok_rows)
        for i, d in enumerate(distances)
    ]


def scores_kernel(distances, split, decoder, own_facts, *refs):
    pieces, picked = refs[: 2 * len(distances)], refs[2 * len(distances) :]
    picks = picks_of(facts_of(distances, own_facts, pieces), decoder, pieces)
    if split:
        first = lax.axis_index("width") == 0
        picks = jnp.where(first, *picks), jnp.where(first, *picks[::-1])
    for target, values in zip(picked, picks):
        target[...] = values


def scores_of(distances, pairs, decoder, own_facts, split=False):
    pieces = [kept(piece) for pair in pairs for piece in pair]
    shape = pltpu.VMEM(own_facts.shape, jnp.float32)
    return pl.pallas_call(
        functools.partial(scores_kernel, distances, split),
        out_shape=(shape,) * len(distances),
        in_specs=[VMEM] * (2 + len(pieces)),
        out_specs=(VMEM,) * len(distances),
        compiler_params=limit(12),
        name="scores",
    )(kept(decoder), kept(own_facts), *pieces)


def gradients_kernel(distances, own_facts, *refs):
    pieces, refs = refs[: 2 * len(distances)], refs[2 * len(distances) :]
    total = refs[-1]
    facts = facts_of(distances, own_facts, pieces)
    for columns, part in gradient_blocks(facts, pieces, total.shape[1]):
        total[:, columns] = part if len(refs) == 1 else refs[0][:, columns] + part


def gradients_of(distances, pairs, own_facts, shape, total=None):
    operands = [kept(own_facts)] + [kept(piece) for pair in pairs for piece in pair]
    operands += [] if total is None else [kept(total)]
    return pl.pallas_call(
        functools.partial(gradients_kernel, distances),
        out_shape=pltpu.VMEM(shape, jnp.float32),
        in_specs=[VMEM] * len(operands),
        out_specs=VMEM,
        input_output_aliases={} if total is None else {len(operands) - 1: 0},
        compiler_params=limit(16),
        name="gradients",
    )(*operands)


def last_gradients_kernel(distance, tok_rows, left, right, total, out, rounded, sems):
    facts = [facts_in(left, distance, tok_rows)]
    copies = []
    for columns, part in gradient_blocks(facts, (left, right), out.shape[1]):
        rounded[:, columns] = (total[:, columns] + part).astype(out.dtype)
        copies.append(
            pltpu.make_async_copy(
                rounded.at[:, columns], out.at[:, columns], sems.at[len(copies)]
            )
        )
        copies[-1].start()
    for copy in copies:
        copy.wait()


def last_gradients(distance, pair, total, tok_rows):
    return pl.pallas_call(
        functools.partial(last_gradients_kernel, distance, tok_rows),
        out_shape=jax.ShapeDtypeStruct(total.shape, jnp.bfloat16),
        in_specs=[VMEM] * 3,
        out_specs=ANY,
        scratch_shapes=[
            pltpu.VMEM(total.shape, jnp.bfloat16),
            pltpu.SemaphoreType.DMA((total.shape[1] // 256,)),
        ],
        compiler_params=limit(16),
        name="last_gradients",
    )(kept(pair[0]), kept(pair[1]), kept(total))


def stamp_kernel(left, right, for_left, for_right, left_out, right_out, rows, sems):
    start = left.shape[0] - FACTS
    targets = (left_out, right_out)
    for i, piece in enumerate((left, right)):
        pltpu.make_async_copy(
            piece.at[start : start + 16, :], rows.at[i], sems.at[i]
        ).start()
    for i, values in enumerate((for_left, for_right)):
        pltpu.make_async_copy(
            left.at[start : start + 16, :], rows.at[i], sems.at[i]
        ).wait()
        value = values[:KPB]
        high = value.astype(jnp.bfloat16).astype(jnp.float32)
        low = value - high
        facts = rows[i].astype(jnp.float32)[2 * KPB :]
        rows[i] = jnp.concatenate([high, low, facts], axis=0).astype(jnp.bfloat16)
        pltpu.make_async_copy(
            rows.at[i], targets[i].at[start : start + 16, :], sems.at[2 + i]
        ).start()
    for i in range(2):
        pltpu.make_async_copy(
            rows.at[i], targets[i].at[start : start + 16, :], sems.at[2 + i]
        ).wait()


def stamp(pieces, values):
    return pl.pallas_call(
        stamp_kernel,
        out_shape=tuple(pltpu.VMEM(piece.shape, piece.dtype) for piece in pieces),
        in_specs=[ANY, ANY, VMEM, VMEM],
        out_specs=(ANY, ANY),
        scratch_shapes=[
            pltpu.VMEM((2, 16, 128), jnp.bfloat16),
            pltpu.SemaphoreType.DMA((4,)),
        ],
        input_output_aliases={0: 0, 1: 1},
        compiler_params=limit(4),
        name="stamp",
    )(*[kept(piece) for piece in pieces], *[kept(value) for value in values])


def unpack_kernel(owners, slots, own, left, right, second, third, opposite, out):
    owner = slots[...] // BLK_DEV
    start = left.shape[0] - FACTS
    way = 1 - 2 * lax.axis_index("width")
    returned = [(0, own[...])]
    for distance, piece in ((-1, left), (1, right)):
        rows = piece[start : start + 16, :].astype(jnp.float32)
        returned.append((distance, rows[:KPB] + rows[KPB : 2 * KPB]))
    returned += [(2 * way, second[...]), (3 * way, third[...]), (4, opposite[...])]
    mine = [owner == peer_at(distance, owners) for distance, _ in returned]
    for k in range(KPB):
        total = jnp.zeros(owner.shape, jnp.float32)
        for here, (_, values) in zip(mine, returned):
            total = jnp.where(here, values[k : k + 1, :], total)
        out[pl.ds(k, ACT, stride=KPB), :] = total


def unpack(slots, *returned):
    tok_rows = slots.shape[1]
    return pl.pallas_call(
        functools.partial(unpack_kernel, lax.axis_size("dp")),
        out_shape=pltpu.VMEM((ACT * KPB, tok_rows), jnp.float32),
        in_specs=[VMEM] * (1 + len(returned)),
        out_specs=VMEM,
        compiler_params=limit(4),
        name="unpack",
    )(kept(slots), *[kept(x) for x in returned])


def every_owner(decoder, grad_out, active_blocks, feature_idx, acts, block_slot):
    tok_rows = grad_out.shape[0]
    owners = lax.axis_size("dp")
    ring = ring_of(owners)

    def shift(x, by):
        pairs = [(ring[i], ring[(i + by) % owners]) for i in range(owners)]
        return lax.ppermute(x, "dp", pairs)

    def hop(pieces):
        left, right = pieces
        return shift(left, 1), shift(right, -1)

    def crossed(pieces):
        right, left = pieces
        return shift(right, 1), shift(left, -1)

    def other_core(x):
        return lax.ppermute(x, "width", ((0, 1), (1, 0)))

    def return_by(distance, x):
        pairs = []
        for i in range(owners):
            pairs.append((2 * ring[i], 2 * ring[(i - distance) % owners]))
            pairs.append((2 * ring[i] + 1, 2 * ring[(i + distance) % owners] + 1))
        return lax.ppermute(x, ("dp", "width"), pairs)

    left, right, own_facts, slots = prepare(
        block_slot, active_blocks, feature_idx, acts, grad_out, owners
    )
    first_1 = hop((left, right))
    second_1 = crossed((right, left))
    decoder = fetch(decoder)
    first_1, decoder = lax.optimization_barrier((first_1, decoder))
    first_2 = hop(first_1)
    second_2 = crossed(second_1)
    pairs = [(left, right), (first_1[0], second_1[0]), (second_1[1], first_1[1])]
    distances = (0, -1, 1)
    own, onward, back = scores_of(distances, pairs, decoder, own_facts)
    total = gradients_of(distances, pairs, own_facts, decoder.shape)
    first_2 = stamp(first_2, (back, onward))
    first_3 = hop(first_2)
    second_3 = crossed(second_2)
    pairs = [(first_2[0], second_2[0]), (second_2[1], first_2[1])]
    mine, others = scores_of((-2, 2), pairs, decoder, own_facts, True)
    total = gradients_of((-2, 2), pairs, own_facts, decoder.shape, total)
    second = mine + other_core(others)
    total, first_3, second = lax.optimization_barrier((total, first_3, second))
    second = return_by(2, jnp.concatenate([second, jnp.zeros((24, 128), jnp.float32)]))[:8]
    first_4 = hop(first_3)
    pairs = [(first_3[0], second_3[0]), (second_3[1], first_3[1])]
    mine, others = scores_of((-3, 3), pairs, decoder, own_facts, True)
    total = gradients_of((-3, 3), pairs, own_facts, decoder.shape, total)
    third = mine + other_core(others)
    total, third = lax.optimization_barrier((total, third))
    third = return_by(3, third)
    total, first_4 = lax.optimization_barrier((total, first_4))
    (opposite,) = scores_of((4,), [first_4], decoder, own_facts)
    opposite = shift(opposite, -4)
    total, third = lax.optimization_barrier((total, third))
    decoder_grad = last_gradients(4, first_4, total, tok_rows)
    decoder_grad, opposite = lax.optimization_barrier((decoder_grad, opposite))
    act_grad = unpack(slots, own, *first_3, second, third, opposite)
    act_grad = act_grad + other_core(act_grad)
    return (decoder_grad, act_grad.T)


def send_back(picked):
    return lax.all_to_all(picked, "dp", split_axis=1, concat_axis=1, tiled=True)


def pack_slots(grad_out, target, slots_all, pair_coeffs, pair_columns, source_row):
    slot_row = jnp.zeros((slots_all,), jnp.int32).at[target].set(source_row)
    used = jnp.zeros((slots_all,), jnp.bool_).at[target].set(True)
    send_rows = jnp.where(used[:, None], grad_out[slot_row], jnp.zeros((), grad_out.dtype))
    send_acts = jnp.zeros((slots_all, KPB), pair_coeffs.dtype).at[target].set(pair_coeffs)
    send_cols = jnp.zeros((slots_all, KPB), jnp.int32).at[target].set(pair_columns)
    return (send_rows, send_acts, send_cols)


def some_owners(decoder, grad_out, active_blocks, feature_idx, acts, block_slot):
    tok_rows, half_width = grad_out.shape
    owners = lax.axis_size("dp")
    mean_load = tok_rows * ACT // owners
    owner_cap = mean_load + min(mean_load // 2, tok_rows - mean_load)
    block_cap = (owner_cap + 2) // 3
    block_ids = active_blocks.reshape(-1)
    pair_count = block_ids.shape[0]
    table_pos = jnp.arange(block_slot.shape[0], dtype=jnp.int32)
    slot_of = jnp.sum(
        jnp.where(block_ids[:, None] == table_pos[None, :], block_slot[None, :], 0), axis=1
    )
    pair_pos = jnp.arange(pair_count, dtype=jnp.int32)
    source_row = pair_pos // ACT
    pair_coeffs = acts.reshape(pair_count, KPB)
    pair_feats = feature_idx.reshape(pair_count, KPB)
    earlier = (block_ids[:, None] == block_ids[None, :]) & (pair_pos[None, :] < pair_pos[:, None])
    position = jnp.sum(earlier.astype(jnp.int32), axis=1)
    slot_cols = owners * block_cap
    target = slot_of % BLK_DEV * slot_cols + slot_of // BLK_DEV * block_cap + position
    slots_all = BLK_DEV * slot_cols
    send_rows, send_acts, send_cols = pack_slots(
        grad_out, target, slots_all, pair_coeffs, pair_feats, source_row
    )
    rows, coeffs, feature_pos = (
        lax.all_to_all(
            send_rows.reshape(BLK_DEV, slot_cols, half_width),
            "dp",
            split_axis=1,
            concat_axis=1,
            tiled=True,
        ),
        lax.all_to_all(
            send_acts.reshape(BLK_DEV, slot_cols, KPB),
            "dp",
            split_axis=1,
            concat_axis=1,
            tiled=True,
        ),
        lax.all_to_all(
            send_cols.reshape(BLK_DEV, slot_cols, KPB),
            "dp",
            split_axis=1,
            concat_axis=1,
            tiled=True,
        ),
    )
    weights = decoder.reshape(BLK_DEV, BW, half_width)
    scores = jnp.einsum("bnd,bfd->bnf", rows, weights, preferred_element_type=jnp.float32)
    picked = jnp.take_along_axis(scores, feature_pos, axis=2)
    returned = send_back(picked)
    feature_axis = jnp.arange(BW, dtype=jnp.int32)
    matches = feature_pos[..., None] == feature_axis
    dense = jnp.sum(jnp.where(matches, coeffs[..., None].astype(jnp.float32), 0.0), axis=2).astype(
        jnp.bfloat16
    )
    grads = jnp.einsum("bnf,bnd->bfd", dense, rows, preferred_element_type=jnp.float32)
    decoder_grad = grads.astype(jnp.bfloat16).reshape(BLK_DEV * BW, half_width)
    pair_vals = returned.reshape(slots_all, KPB)[target]
    act_grad = pair_vals.reshape(tok_rows, ACT * KPB)
    act_grad = lax.psum(act_grad, "width")
    return (decoder_grad, act_grad)


def per_device(*args):
    if lax.axis_size("dp") == ACT:
        return every_owner(*args)
    return some_owners(*args)


def solution(mesh):
    in_specs = (
        P(("groups", "dp"), "width"),
        P(("groups", "dp"), "width"),
        P(("groups", "dp"), None),
        P(("groups", "dp"), None),
        P(("groups", "dp"), None),
        P("groups"),
    )
    out_specs = (P(("groups", "dp"), "width"), P(("groups", "dp"), None))
    return jax.shard_map(
        per_device, mesh=mesh, in_specs=in_specs, out_specs=out_specs, check_vma=False
    )
```

```python
import functools

import jax
import jax.numpy as jnp
from jax import lax
from jax.experimental import pallas as pl
from jax.experimental.pallas import tpu as pltpu
from jax.sharding import PartitionSpec as P

BW = 128
BLK_DEV = 4
ACT = 8
KPB = 4
SMEM = pl.BlockSpec(memory_space=pltpu.SMEM)
VMEM = pl.BlockSpec(memory_space=pltpu.VMEM)
ANY = pl.BlockSpec(memory_space=pl.ANY)
HBM = pl.BlockSpec(memory_space=pltpu.HBM)


def limit(mebibytes):
    return pltpu.CompilerParams(vmem_limit_bytes=mebibytes * 2**20)


def kept(x):
    return pltpu.with_memory_space_constraint(x, pltpu.VMEM)


def far(x):
    return pltpu.with_memory_space_constraint(x, pltpu.HBM)


def ring_of(owners):
    return list(range(0, owners, 2)) + list(range(owners - 1, 0, -2))


def peer_at(distance, owners):
    me = lax.axis_index("dp")
    half_ring = owners // 2
    place = jnp.where(lax.rem(me, 2) == 0, lax.div(me, 2), owners - 1 - lax.div(me, 2))
    at = lax.rem(place + owners + distance, owners)
    return jnp.where(at < half_ring, 2 * at, 2 * (owners - 1 - at) + 1)


ROW_SHIFT = BLK_DEV * BW // 2
FACTS = ACT // 2 * 2 * KPB


def facts_for(owner_id, owner, first_row, feats, acts):
    mine = owner == owner_id
    rows = [
        jnp.sum(jnp.where(mine, first_row + feats[k], 0.0), axis=0, keepdims=True) - ROW_SHIFT
        for k in range(KPB)
    ]
    values = [
        jnp.sum(jnp.where(mine, acts[k], 0.0), axis=0, keepdims=True) for k in range(KPB)
    ]
    return jnp.concatenate(rows + values, axis=0)


def prepare_kernel(
    owners, *refs
):
    sources, refs = refs[:5], refs[5:]
    left, right, own_facts, slots = refs[:4]
    block_slot, active, feats, acts, wide_feats, wide_acts, sems = refs[4:]
    grad_out = sources[-1]
    tok_rows, width = grad_out.shape
    parts = width // 256
    small = []
    for source, target in zip(sources[:4], (block_slot, active, feats, acts)):
        small.append(pltpu.make_async_copy(source, target, sems.at[len(small)]))
        small[-1].start()
    copies = []
    for j in range(parts):
        for target, side in ((left, 0), (right, 1)):
            column = (side * parts + j) * 128
            copies.append(
                pltpu.make_async_copy(
                    grad_out.at[:, column : column + 128],
                    target.at[j * tok_rows : (j + 1) * tok_rows, :],
                    sems.at[len(small) + len(copies)],
                )
            )
            copies[-1].start()
    for copy in small:
        copy.wait()
    named = active[...]
    slot = jnp.zeros_like(named)
    for block in range(block_slot.shape[0]):
        slot = jnp.where(named == block, block_slot[block], slot)
    slots[...] = slot
    wide_feats[...] = feats[...].astype(jnp.float32)
    wide_acts[...] = acts[...].astype(jnp.float32)
    features = [wide_feats[pl.ds(k, ACT, stride=KPB), :] for k in range(KPB)]
    values = [wide_acts[pl.ds(k, ACT, stride=KPB), :] for k in range(KPB)]
    first_row = (slot % BLK_DEV * BW).astype(jnp.float32)

    def facts(distance):
        return facts_for(
            peer_at(distance, owners), slot // BLK_DEV, first_row, features, values
        )

    reach = owners // 2
    own_facts[...] = facts(0)
    start = parts * tok_rows
    for target, sign in ((left, 1), (right, -1)):
        ahead = [facts(sign * d) for d in range(1, reach + 1)]
        target[start:, :] = jnp.concatenate(ahead, axis=0).astype(jnp.bfloat16)
    for copy in copies:
        copy.wait()


def prepare(block_slot, active_blocks, feature_idx, acts, grad_out, owners):
    tok_rows, half_width = grad_out.shape
    plain = half_width // 256 * tok_rows
    return pl.pallas_call(
        functools.partial(prepare_kernel, owners),
        out_shape=(
            pltpu.VMEM((plain + FACTS, 128), grad_out.dtype),
            pltpu.VMEM((plain + FACTS, 128), grad_out.dtype),
            pltpu.VMEM((2 * KPB, tok_rows), jnp.float32),
            pltpu.VMEM((ACT, tok_rows), jnp.int32),
        ),
        in_specs=[HBM] * 5,
        out_specs=(VMEM,) * 4,
        scratch_shapes=[
            pltpu.SMEM(block_slot.shape, jnp.int32),
            pltpu.VMEM((ACT, tok_rows), jnp.int32),
            pltpu.VMEM((ACT * KPB, tok_rows), jnp.int32),
            pltpu.VMEM((ACT * KPB, tok_rows), acts.dtype),
            pltpu.VMEM((ACT * KPB, tok_rows), jnp.float32),
            pltpu.VMEM((ACT * KPB, tok_rows), jnp.float32),
            pltpu.SemaphoreType.DMA((4 + half_width // 128,)),
        ],
        compiler_params=limit(8),
        name="prepare",
    )(far(block_slot), far(active_blocks.T), far(feature_idx.T), far(acts.T), far(grad_out))


def fetch_kernel(source, target, sem):
    copy = pltpu.make_async_copy(source, target, sem)
    copy.start()
    copy.wait()


def fetch(x):
    return pl.pallas_call(
        fetch_kernel,
        out_shape=pltpu.VMEM(x.shape, x.dtype),
        in_specs=[HBM],
        out_specs=VMEM,
        scratch_shapes=[pltpu.SemaphoreType.DMA],
        compiler_params=limit(8),
        name="fetch",
    )(far(x))


def block_and_rows(here):
    at_row = here[:KPB].astype(jnp.int32) + ROW_SHIFT
    return at_row[:1] // BW, at_row % BW


def row_axis_of(tok_rows):
    return lax.broadcasted_iota(jnp.int32, (BW, tok_rows), 0)


def coefficients(here):
    block, feats = block_and_rows(here)
    row_axis = row_axis_of(here.shape[1])
    dense = jnp.zeros(row_axis.shape, jnp.float32)
    for k in range(KPB):
        dense = jnp.where(row_axis == feats[k : k + 1], here[KPB + k : KPB + k + 1], dense)
    parts = [jnp.where(block == b, dense, 0.0) for b in range(BLK_DEV)]
    return jnp.concatenate(parts, axis=0).astype(jnp.bfloat16)


def pick(scores, here):
    block, feats = block_and_rows(here)
    row_axis = row_axis_of(here.shape[1])
    mine = scores[:BW]
    for b in range(1, BLK_DEV):
        mine = jnp.where(block == b, scores[b * BW : (b + 1) * BW], mine)
    return [
        jnp.sum(jnp.where(row_axis == feats[k : k + 1], mine, 0.0), axis=0, keepdims=True)
        for k in range(KPB)
    ]


def facts_in(piece, distance, tok_rows):
    facts = piece[piece.shape[0] - FACTS :, :].astype(jnp.float32)
    return facts[(abs(distance) - 1) * 2 * KPB : abs(distance) * 2 * KPB]


def columns_of(pieces, tok_rows, parts):
    rows = [
        jnp.concatenate([piece[j * tok_rows : (j + 1) * tok_rows, :] for j in parts], axis=1)
        for piece in pieces
    ]
    return jnp.concatenate(rows, axis=0) if len(rows) > 1 else rows[0]


def picks_of(facts, decoder, pieces):
    picks = []
    tok_rows = facts[0].shape[1]
    cut = decoder.shape[1] // 2
    for first in range(0, len(facts), 2):
        count = min(2, len(facts) - first)
        scores = None
        for side in range(2):
            part = lax.dot_general(
                decoder[:, side * cut : (side + 1) * cut],
                columns_of(
                    pieces[2 * first + side : 2 * (first + count) : 2],
                    tok_rows,
                    range(cut // 128),
                ),
                (((1,), (1,)), ((), ())),
                preferred_element_type=jnp.float32,
            )
            scores = part if scores is None else scores + part
        for i in range(first, first + count):
            here = scores[:, (i - first) * tok_rows : (i - first + 1) * tok_rows]
            picks.append(jnp.concatenate(pick(here, facts[i]) * 2, axis=0))
    return picks


def gradient_blocks(facts, pieces, width):
    tok_rows = facts[0].shape[1]
    cut = width // 2
    dense = jnp.concatenate([coefficients(here) for here in facts], axis=1)
    for side in range(2):
        for j in range(0, cut // 128, 2):
            rows = columns_of(pieces[side::2], tok_rows, (j, j + 1))
            part = jnp.dot(dense, rows, preferred_element_type=jnp.float32)
            yield slice(side * cut + j * 128, side * cut + (j + 2) * 128), part


def facts_of(distances, own_facts, pieces):
    tok_rows = own_facts.shape[1]
    return [
        own_facts[...] if d == 0 else facts_in(pieces[2 * i + (d > 0)], d, tok_rows)
        for i, d in enumerate(distances)
    ]


def scores_kernel(distances, split, decoder, own_facts, *refs):
    pieces, picked = refs[: 2 * len(distances)], refs[2 * len(distances) :]
    picks = picks_of(facts_of(distances, own_facts, pieces), decoder, pieces)
    if split:
        first = lax.axis_index("width") == 0
        picks = jnp.where(first, *picks), jnp.where(first, *picks[::-1])
    for target, values in zip(picked, picks):
        target[...] = values


def scores_of(distances, pairs, decoder, own_facts, split=False):
    pieces = [kept(piece) for pair in pairs for piece in pair]
    shape = pltpu.VMEM(own_facts.shape, jnp.float32)
    return pl.pallas_call(
        functools.partial(scores_kernel, distances, split),
        out_shape=(shape,) * len(distances),
        in_specs=[VMEM] * (2 + len(pieces)),
        out_specs=(VMEM,) * len(distances),
        compiler_params=limit(12),
        name="scores",
    )(kept(decoder), kept(own_facts), *pieces)


def gradients_kernel(distances, own_facts, *refs):
    pieces, refs = refs[: 2 * len(distances)], refs[2 * len(distances) :]
    total = refs[-1]
    facts = facts_of(distances, own_facts, pieces)
    for columns, part in gradient_blocks(facts, pieces, total.shape[1]):
        total[:, columns] = part if len(refs) == 1 else refs[0][:, columns] + part


def gradients_of(distances, pairs, own_facts, shape, total=None):
    operands = [kept(own_facts)] + [kept(piece) for pair in pairs for piece in pair]
    operands += [] if total is None else [kept(total)]
    return pl.pallas_call(
        functools.partial(gradients_kernel, distances),
        out_shape=pltpu.VMEM(shape, jnp.float32),
        in_specs=[VMEM] * len(operands),
        out_specs=VMEM,
        input_output_aliases={} if total is None else {len(operands) - 1: 0},
        compiler_params=limit(16),
        name="gradients",
    )(*operands)


def last_gradients_kernel(distance, tok_rows, left, right, total, out, rounded, sems):
    facts = [facts_in(left, distance, tok_rows)]
    copies = []
    for columns, part in gradient_blocks(facts, (left, right), out.shape[1]):
        rounded[:, columns] = (total[:, columns] + part).astype(out.dtype)
        copies.append(
            pltpu.make_async_copy(
                rounded.at[:, columns], out.at[:, columns], sems.at[len(copies)]
            )
        )
        copies[-1].start()
    for copy in copies:
        copy.wait()


def last_gradients(distance, pair, total, tok_rows):
    return pl.pallas_call(
        functools.partial(last_gradients_kernel, distance, tok_rows),
        out_shape=jax.ShapeDtypeStruct(total.shape, jnp.bfloat16),
        in_specs=[VMEM] * 3,
        out_specs=ANY,
        scratch_shapes=[
            pltpu.VMEM(total.shape, jnp.bfloat16),
            pltpu.SemaphoreType.DMA((total.shape[1] // 256,)),
        ],
        compiler_params=limit(16),
        name="last_gradients",
    )(kept(pair[0]), kept(pair[1]), kept(total))


def stamp_kernel(left, right, for_left, for_right, left_out, right_out, rows, sems):
    start = left.shape[0] - FACTS
    targets = (left_out, right_out)
    for i, piece in enumerate((left, right)):
        pltpu.make_async_copy(
            piece.at[start : start + 16, :], rows.at[i], sems.at[i]
        ).start()
    for i, values in enumerate((for_left, for_right)):
        pltpu.make_async_copy(
            left.at[start : start + 16, :], rows.at[i], sems.at[i]
        ).wait()
        value = values[:KPB]
        high = value.astype(jnp.bfloat16).astype(jnp.float32)
        low = value - high
        facts = rows[i].astype(jnp.float32)[2 * KPB :]
        rows[i] = jnp.concatenate([high, low, facts], axis=0).astype(jnp.bfloat16)
        pltpu.make_async_copy(
            rows.at[i], targets[i].at[start : start + 16, :], sems.at[2 + i]
        ).start()
    for i in range(2):
        pltpu.make_async_copy(
            rows.at[i], targets[i].at[start : start + 16, :], sems.at[2 + i]
        ).wait()


def stamp(pieces, values):
    return pl.pallas_call(
        stamp_kernel,
        out_shape=tuple(pltpu.VMEM(piece.shape, piece.dtype) for piece in pieces),
        in_specs=[ANY, ANY, VMEM, VMEM],
        out_specs=(ANY, ANY),
        scratch_shapes=[
            pltpu.VMEM((2, 16, 128), jnp.bfloat16),
            pltpu.SemaphoreType.DMA((4,)),
        ],
        input_output_aliases={0: 0, 1: 1},
        compiler_params=limit(4),
        name="stamp",
    )(*[kept(piece) for piece in pieces], *[kept(value) for value in values])


def place(owner, owners, returned, out):
    mine = [owner == peer_at(distance, owners) for distance, _ in returned]
    for k in range(KPB):
        total = jnp.zeros(owner.shape, jnp.float32)
        for here, (_, values) in zip(mine, returned):
            total = jnp.where(here, values[k : k + 1, :], total)
        out[pl.ds(k, ACT, stride=KPB), :] = total


def unpack_kernel(owners, slots, own, left, right, second, third, opposite, out):
    start = left.shape[0] - FACTS
    way = 1 - 2 * lax.axis_index("width")
    returned = [(0, own[...])]
    for distance, piece in ((-1, left), (1, right)):
        rows = piece[start : start + 16, :].astype(jnp.float32)
        returned.append((distance, rows[:KPB] + rows[KPB : 2 * KPB]))
    returned += [(2 * way, second[...]), (3 * way, third[...]), (4, opposite[...])]
    place(slots[...] // BLK_DEV, owners, returned, out)


def unpack(slots, *returned):
    tok_rows = slots.shape[1]
    return pl.pallas_call(
        functools.partial(unpack_kernel, lax.axis_size("dp")),
        out_shape=pltpu.VMEM((ACT * KPB, tok_rows), jnp.float32),
        in_specs=[VMEM] * (1 + len(returned)),
        out_specs=VMEM,
        compiler_params=limit(4),
        name="unpack",
    )(kept(slots), *[kept(x) for x in returned])


def finish_kernel(owners, slots, here, there, to_first, to_second, out, rest):
    opposite = to_first[...] + to_second[...]
    place(slots[...] // BLK_DEV, owners, [(4, opposite)], rest)
    out[...] = here[...] + there[...] + rest[...]


def finish(slots, *parts):
    shape = parts[0].shape
    return pl.pallas_call(
        functools.partial(finish_kernel, lax.axis_size("dp")),
        out_shape=jax.ShapeDtypeStruct(shape, jnp.float32),
        in_specs=[VMEM] * (1 + len(parts)),
        out_specs=VMEM,
        scratch_shapes=[pltpu.VMEM(shape, jnp.float32)],
        compiler_params=limit(4),
        name="finish",
    )(kept(slots), *[kept(x) for x in parts])


def every_owner(decoder, grad_out, active_blocks, feature_idx, acts, block_slot):
    tok_rows = grad_out.shape[0]
    owners = lax.axis_size("dp")
    ring = ring_of(owners)

    def shift(x, by):
        pairs = [(ring[i], ring[(i + by) % owners]) for i in range(owners)]
        return lax.ppermute(x, "dp", pairs)

    def hop(pieces):
        left, right = pieces
        return shift(left, 1), shift(right, -1)

    def crossed(pieces):
        right, left = pieces
        return shift(right, 1), shift(left, -1)

    def other_core(x):
        return lax.ppermute(x, "width", ((0, 1), (1, 0)))

    def return_by(distance, x):
        pairs = []
        for i in range(owners):
            pairs.append((2 * ring[i], 2 * ring[(i - distance) % owners]))
            pairs.append((2 * ring[i] + 1, 2 * ring[(i + distance) % owners] + 1))
        return lax.ppermute(x, ("dp", "width"), pairs)

    def to_opposite(x, core, core_there):
        pairs = []
        for i in range(owners):
            there = ring[(i + owners // 2) % owners]
            pairs.append((2 * ring[i] + core, 2 * there + core_there))
        return lax.ppermute(x, ("dp", "width"), pairs)

    left, right, own_facts, slots = prepare(
        block_slot, active_blocks, feature_idx, acts, grad_out, owners
    )
    first_1 = hop((left, right))
    second_1 = crossed((right, left))
    decoder = fetch(decoder)
    first_1, decoder = lax.optimization_barrier((first_1, decoder))
    first_2 = hop(first_1)
    second_2 = crossed(second_1)
    pairs = [(left, right), (first_1[0], second_1[0]), (second_1[1], first_1[1])]
    distances = (0, -1, 1)
    own, onward, back = scores_of(distances, pairs, decoder, own_facts)
    total = gradients_of(distances, pairs, own_facts, decoder.shape)
    first_2 = stamp(first_2, (back, onward))
    first_3 = hop(first_2)
    second_3 = crossed(second_2)
    pairs = [(first_2[0], second_2[0]), (second_2[1], first_2[1])]
    mine, others = scores_of((-2, 2), pairs, decoder, own_facts, True)
    total = gradients_of((-2, 2), pairs, own_facts, decoder.shape, total)
    second = mine + other_core(others)
    total, first_3, second = lax.optimization_barrier((total, first_3, second))
    second = return_by(2, jnp.concatenate([second, jnp.zeros((24, 128), jnp.float32)]))[:8]
    first_4 = hop(first_3)
    pairs = [(first_3[0], second_3[0]), (second_3[1], first_3[1])]
    mine, others = scores_of((-3, 3), pairs, decoder, own_facts, True)
    total = gradients_of((-3, 3), pairs, own_facts, decoder.shape, total)
    third = mine + other_core(others)
    total, third = lax.optimization_barrier((total, third))
    third = return_by(3, third)
    total, first_4 = lax.optimization_barrier((total, first_4))
    (opposite,) = scores_of((4,), [first_4], decoder, own_facts)
    from_second = to_opposite(opposite, 1, 1)
    padded = jnp.concatenate([opposite, jnp.zeros((24, 128), jnp.float32)])
    to_first, to_second = to_opposite(padded, 0, 0)[:8], to_opposite(padded, 0, 1)[:8]
    total, third = lax.optimization_barrier((total, third))
    decoder_grad = last_gradients(4, first_4, total, tok_rows)
    decoder_grad, from_second = lax.optimization_barrier((decoder_grad, from_second))
    most = unpack(slots, own, *first_3, second, third, from_second)
    act_grad = finish(slots, most, other_core(most), to_first, to_second)
    return (decoder_grad, act_grad.T)


def send_back(picked):
    return lax.all_to_all(picked, "dp", split_axis=1, concat_axis=1, tiled=True)


def pack_slots(grad_out, target, slots_all, pair_coeffs, pair_columns, source_row):
    slot_row = jnp.zeros((slots_all,), jnp.int32).at[target].set(source_row)
    used = jnp.zeros((slots_all,), jnp.bool_).at[target].set(True)
    send_rows = jnp.where(used[:, None], grad_out[slot_row], jnp.zeros((), grad_out.dtype))
    send_acts = jnp.zeros((slots_all, KPB), pair_coeffs.dtype).at[target].set(pair_coeffs)
    send_cols = jnp.zeros((slots_all, KPB), jnp.int32).at[target].set(pair_columns)
    return (send_rows, send_acts, send_cols)


def some_owners(decoder, grad_out, active_blocks, feature_idx, acts, block_slot):
    tok_rows, half_width = grad_out.shape
    owners = lax.axis_size("dp")
    mean_load = tok_rows * ACT // owners
    owner_cap = mean_load + min(mean_load // 2, tok_rows - mean_load)
    block_cap = (owner_cap + 2) // 3
    block_ids = active_blocks.reshape(-1)
    pair_count = block_ids.shape[0]
    table_pos = jnp.arange(block_slot.shape[0], dtype=jnp.int32)
    slot_of = jnp.sum(
        jnp.where(block_ids[:, None] == table_pos[None, :], block_slot[None, :], 0), axis=1
    )
    pair_pos = jnp.arange(pair_count, dtype=jnp.int32)
    source_row = pair_pos // ACT
    pair_coeffs = acts.reshape(pair_count, KPB)
    pair_feats = feature_idx.reshape(pair_count, KPB)
    earlier = (block_ids[:, None] == block_ids[None, :]) & (pair_pos[None, :] < pair_pos[:, None])
    position = jnp.sum(earlier.astype(jnp.int32), axis=1)
    slot_cols = owners * block_cap
    target = slot_of % BLK_DEV * slot_cols + slot_of // BLK_DEV * block_cap + position
    slots_all = BLK_DEV * slot_cols
    send_rows, send_acts, send_cols = pack_slots(
        grad_out, target, slots_all, pair_coeffs, pair_feats, source_row
    )
    rows, coeffs, feature_pos = (
        lax.all_to_all(
            send_rows.reshape(BLK_DEV, slot_cols, half_width),
            "dp",
            split_axis=1,
            concat_axis=1,
            tiled=True,
        ),
        lax.all_to_all(
            send_acts.reshape(BLK_DEV, slot_cols, KPB),
            "dp",
            split_axis=1,
            concat_axis=1,
            tiled=True,
        ),
        lax.all_to_all(
            send_cols.reshape(BLK_DEV, slot_cols, KPB),
            "dp",
            split_axis=1,
            concat_axis=1,
            tiled=True,
        ),
    )
    weights = decoder.reshape(BLK_DEV, BW, half_width)
    scores = jnp.einsum("bnd,bfd->bnf", rows, weights, preferred_element_type=jnp.float32)
    picked = jnp.take_along_axis(scores, feature_pos, axis=2)
    returned = send_back(picked)
    feature_axis = jnp.arange(BW, dtype=jnp.int32)
    matches = feature_pos[..., None] == feature_axis
    dense = jnp.sum(jnp.where(matches, coeffs[..., None].astype(jnp.float32), 0.0), axis=2).astype(
        jnp.bfloat16
    )
    grads = jnp.einsum("bnf,bnd->bfd", dense, rows, preferred_element_type=jnp.float32)
    decoder_grad = grads.astype(jnp.bfloat16).reshape(BLK_DEV * BW, half_width)
    pair_vals = returned.reshape(slots_all, KPB)[target]
    act_grad = pair_vals.reshape(tok_rows, ACT * KPB)
    act_grad = lax.psum(act_grad, "width")
    return (decoder_grad, act_grad)


def per_device(*args):
    if lax.axis_size("dp") == ACT:
        return every_owner(*args)
    return some_owners(*args)


def solution(mesh):
    in_specs = (
        P(("groups", "dp"), "width"),
        P(("groups", "dp"), "width"),
        P(("groups", "dp"), None),
        P(("groups", "dp"), None),
        P(("groups", "dp"), None),
        P("groups"),
    )
    out_specs = (P(("groups", "dp"), "width"), P(("groups", "dp"), None))
    return jax.shard_map(
        per_device, mesh=mesh, in_specs=in_specs, out_specs=out_specs, check_vma=False
    )
```

```python
import functools

import jax
import jax.numpy as jnp
from jax import lax
from jax.experimental import pallas as pl
from jax.experimental.pallas import tpu as pltpu
from jax.sharding import PartitionSpec as P

BW = 128
BLK_DEV = 4
ACT = 8
KPB = 4
SMEM = pl.BlockSpec(memory_space=pltpu.SMEM)
VMEM = pl.BlockSpec(memory_space=pltpu.VMEM)
ANY = pl.BlockSpec(memory_space=pl.ANY)
HBM = pl.BlockSpec(memory_space=pltpu.HBM)


def limit(mebibytes):
    return pltpu.CompilerParams(vmem_limit_bytes=mebibytes * 2**20)


def kept(x):
    return pltpu.with_memory_space_constraint(x, pltpu.VMEM)


def far(x):
    return pltpu.with_memory_space_constraint(x, pltpu.HBM)


def ring_of(owners):
    return list(range(0, owners, 2)) + list(range(owners - 1, 0, -2))


def peer_at(distance, owners):
    me = lax.axis_index("dp")
    half_ring = owners // 2
    place = jnp.where(lax.rem(me, 2) == 0, lax.div(me, 2), owners - 1 - lax.div(me, 2))
    at = lax.rem(place + owners + distance, owners)
    return jnp.where(at < half_ring, 2 * at, 2 * (owners - 1 - at) + 1)


def copies_to_pieces(grad_out, left, right, sems):
    tok_rows, width = grad_out.shape
    parts = width // 256
    copies = []
    for j in range(parts):
        for target, side in ((left, 0), (right, 1)):
            column = (side * parts + j) * 128
            copies.append(
                pltpu.make_async_copy(
                    grad_out.at[:, column : column + 128],
                    target.at[j * tok_rows : (j + 1) * tok_rows, :],
                    sems.at[len(copies)],
                )
            )
    return copies


def pieces_kernel(grad_out, left, right, sems):
    copies = copies_to_pieces(grad_out, left, right, sems)
    for copy in copies:
        copy.start()
    for copy in copies:
        copy.wait()


def pieces_of(grad_out):
    tok_rows, width = grad_out.shape
    shape = pltpu.VMEM((width // 256 * tok_rows, 128), grad_out.dtype)
    return pl.pallas_call(
        pieces_kernel,
        out_shape=(shape, shape),
        in_specs=[HBM],
        out_specs=(VMEM, VMEM),
        scratch_shapes=[pltpu.SemaphoreType.DMA((width // 128,))],
        compiler_params=limit(8),
        name="pieces",
    )(far(grad_out))


ROW_SHIFT = BLK_DEV * BW // 2
FACTS = ACT // 2 * 2 * KPB


def facts_for(owner_id, owner, first_row, feats, acts):
    mine = owner == owner_id
    rows = [
        jnp.sum(jnp.where(mine, first_row + feats[k], 0.0), axis=0, keepdims=True) - ROW_SHIFT
        for k in range(KPB)
    ]
    values = [
        jnp.sum(jnp.where(mine, acts[k], 0.0), axis=0, keepdims=True) for k in range(KPB)
    ]
    return jnp.concatenate(rows + values, axis=0)


def prepare_kernel(owners, *refs):
    sources, refs = refs[:5], refs[5:]
    left, right, own_facts, slots = refs[:4]
    block_slot, active, feats, acts, wide_feats, wide_acts, sems = refs[4:]
    small = []
    for source, target in zip(sources[:4], (block_slot, active, feats, acts)):
        small.append(pltpu.make_async_copy(source, target, sems.at[len(small)]))
        small[-1].start()
    copies = copies_to_pieces(sources[-1], left, right, sems.at[4:])
    for copy in copies:
        copy.start()
    for copy in small:
        copy.wait()
    named = active[...]
    slot = jnp.zeros_like(named)
    for block in range(block_slot.shape[0]):
        slot = jnp.where(named == block, block_slot[block], slot)
    slots[...] = slot
    wide_feats[...] = feats[...].astype(jnp.float32)
    wide_acts[...] = acts[...].astype(jnp.float32)
    features = [wide_feats[pl.ds(k, ACT, stride=KPB), :] for k in range(KPB)]
    values = [wide_acts[pl.ds(k, ACT, stride=KPB), :] for k in range(KPB)]
    first_row = (slot % BLK_DEV * BW).astype(jnp.float32)

    def facts(distance):
        return facts_for(
            peer_at(distance, owners), slot // BLK_DEV, first_row, features, values
        )

    own_facts[...] = facts(0)
    for target, sign in ((left, -1), (right, 1)):
        ahead = [facts(sign * d) for d in range(1, owners // 2 + 1)]
        target[target.shape[0] - FACTS :, :] = jnp.concatenate(ahead, axis=0).astype(
            jnp.bfloat16
        )
    for copy in copies:
        copy.wait()


def prepare(block_slot, active_blocks, feature_idx, acts, grad_out, owners):
    tok_rows, width = grad_out.shape
    piece = pltpu.VMEM((width // 256 * tok_rows + FACTS, 128), grad_out.dtype)
    facts = pltpu.VMEM((2 * KPB, tok_rows), jnp.float32)
    return pl.pallas_call(
        functools.partial(prepare_kernel, owners),
        out_shape=(piece, piece, facts, pltpu.VMEM((ACT, tok_rows), jnp.int32)),
        in_specs=[HBM] * 5,
        out_specs=(VMEM,) * 4,
        scratch_shapes=[
            pltpu.SMEM(block_slot.shape, jnp.int32),
            pltpu.VMEM((ACT, tok_rows), jnp.int32),
            pltpu.VMEM((ACT * KPB, tok_rows), jnp.int32),
            pltpu.VMEM((ACT * KPB, tok_rows), acts.dtype),
            pltpu.VMEM((ACT * KPB, tok_rows), jnp.float32),
            pltpu.VMEM((ACT * KPB, tok_rows), jnp.float32),
            pltpu.SemaphoreType.DMA((4 + width // 128,)),
        ],
        compiler_params=limit(8),
        name="prepare",
    )(far(block_slot), far(active_blocks.T), far(feature_idx.T), far(acts.T), far(grad_out))


def fetch_kernel(source, target, sem):
    copy = pltpu.make_async_copy(source, target, sem)
    copy.start()
    copy.wait()


def fetch(x):
    return pl.pallas_call(
        fetch_kernel,
        out_shape=pltpu.VMEM(x.shape, x.dtype),
        in_specs=[HBM],
        out_specs=VMEM,
        scratch_shapes=[pltpu.SemaphoreType.DMA],
        compiler_params=limit(8),
        name="fetch",
    )(far(x))


def block_and_rows(here):
    at_row = here[:KPB].astype(jnp.int32) + ROW_SHIFT
    return at_row[:1] // BW, at_row % BW


def row_axis_of(tok_rows):
    return lax.broadcasted_iota(jnp.int32, (BW, tok_rows), 0)


def coefficients(here):
    block, feats = block_and_rows(here)
    row_axis = row_axis_of(here.shape[1])
    dense = jnp.zeros(row_axis.shape, jnp.float32)
    for k in range(KPB):
        dense = jnp.where(row_axis == feats[k : k + 1], here[KPB + k : KPB + k + 1], dense)
    parts = [jnp.where(block == b, dense, 0.0) for b in range(BLK_DEV)]
    return jnp.concatenate(parts, axis=0).astype(jnp.bfloat16)


def pick(scores, here):
    block, feats = block_and_rows(here)
    row_axis = row_axis_of(here.shape[1])
    mine = scores[:BW]
    for b in range(1, BLK_DEV):
        mine = jnp.where(block == b, scores[b * BW : (b + 1) * BW], mine)
    return [
        jnp.sum(jnp.where(row_axis == feats[k : k + 1], mine, 0.0), axis=0, keepdims=True)
        for k in range(KPB)
    ]


def facts_in(piece, distance, tok_rows):
    facts = piece[piece.shape[0] - FACTS :, :].astype(jnp.float32)
    return facts[(abs(distance) - 1) * 2 * KPB : abs(distance) * 2 * KPB]


def columns_of(pieces, tok_rows, parts):
    rows = [
        jnp.concatenate([piece[j * tok_rows : (j + 1) * tok_rows, :] for j in parts], axis=1)
        for piece in pieces
    ]
    return jnp.concatenate(rows, axis=0) if len(rows) > 1 else rows[0]


def picks_of(facts, decoder, pieces):
    picks = []
    tok_rows = facts[0].shape[1]
    cut = decoder.shape[1] // 2
    for first in range(0, len(facts), 2):
        count = min(2, len(facts) - first)
        scores = None
        for side in range(2):
            part = lax.dot_general(
                decoder[:, side * cut : (side + 1) * cut],
                columns_of(
                    pieces[2 * first + side : 2 * (first + count) : 2],
                    tok_rows,
                    range(cut // 128),
                ),
                (((1,), (1,)), ((), ())),
                preferred_element_type=jnp.float32,
            )
            scores = part if scores is None else scores + part
        for i in range(first, first + count):
            here = scores[:, (i - first) * tok_rows : (i - first + 1) * tok_rows]
            picks.append(jnp.concatenate(pick(here, facts[i]) * 2, axis=0))
    return picks


def gradient_blocks(facts, pieces, width):
    tok_rows = facts[0].shape[1]
    cut = width // 2
    dense = jnp.concatenate([coefficients(here) for here in facts], axis=1)
    for side in range(2):
        for j in range(0, cut // 128, 2):
            rows = columns_of(pieces[side::2], tok_rows, (j, j + 1))
            part = jnp.dot(dense, rows, preferred_element_type=jnp.float32)
            yield slice(side * cut + j * 128, side * cut + (j + 2) * 128), part


def facts_of(distances, given, pieces):
    tok_rows = given.shape[1]
    return [
        given[...] if d in (0, 4) else facts_in(pieces[2 * i + (d < 0)], d, tok_rows)
        for i, d in enumerate(distances)
    ]


def scores_kernel(distances, split, decoder, given, *refs):
    pieces, picked = refs[: 2 * len(distances)], refs[2 * len(distances) :]
    picks = picks_of(facts_of(distances, given, pieces), decoder, pieces)
    if split:
        first = lax.axis_index("width") == 0
        picks = jnp.where(first, *picks), jnp.where(first, *picks[::-1])
    for target, values in zip(picked, picks):
        target[...] = values


def scores_of(distances, pairs, decoder, given, split=False):
    pieces = [kept(piece) for pair in pairs for piece in pair]
    shape = pltpu.VMEM(given.shape, jnp.float32)
    return pl.pallas_call(
        functools.partial(scores_kernel, distances, split),
        out_shape=(shape,) * len(distances),
        in_specs=[VMEM] * (2 + len(pieces)),
        out_specs=(VMEM,) * len(distances),
        compiler_params=limit(12),
        name="scores",
    )(kept(decoder), kept(given), *pieces)


def gradients_kernel(distances, given, *refs):
    pieces, refs = refs[: 2 * len(distances)], refs[2 * len(distances) :]
    total = refs[-1]
    facts = facts_of(distances, given, pieces)
    for columns, part in gradient_blocks(facts, pieces, total.shape[1]):
        total[:, columns] = part if len(refs) == 1 else refs[0][:, columns] + part


def gradients_of(distances, pairs, given, shape, total=None):
    operands = [kept(given)] + [kept(piece) for pair in pairs for piece in pair]
    operands += [] if total is None else [kept(total)]
    return pl.pallas_call(
        functools.partial(gradients_kernel, distances),
        out_shape=pltpu.VMEM(shape, jnp.float32),
        in_specs=[VMEM] * len(operands),
        out_specs=VMEM,
        input_output_aliases={} if total is None else {len(operands) - 1: 0},
        compiler_params=limit(16),
        name="gradients",
    )(*operands)


def last_gradients_kernel(given, left, right, total, out, rounded, sems):
    copies = []
    for columns, part in gradient_blocks([given[...]], (left, right), out.shape[1]):
        rounded[:, columns] = (total[:, columns] + part).astype(out.dtype)
        copies.append(
            pltpu.make_async_copy(
                rounded.at[:, columns], out.at[:, columns], sems.at[len(copies)]
            )
        )
        copies[-1].start()
    for copy in copies:
        copy.wait()


def last_gradients(given, pair, total):
    return pl.pallas_call(
        last_gradients_kernel,
        out_shape=jax.ShapeDtypeStruct(total.shape, jnp.bfloat16),
        in_specs=[VMEM] * 4,
        out_specs=ANY,
        scratch_shapes=[
            pltpu.VMEM(total.shape, jnp.bfloat16),
            pltpu.SemaphoreType.DMA((total.shape[1] // 256,)),
        ],
        compiler_params=limit(16),
        name="last_gradients",
    )(kept(given), kept(pair[0]), kept(pair[1]), kept(total))


def stamp_kernel(onward, back, for_onward, for_back, onward_out, back_out, rows, sems):
    start = onward.shape[0] - FACTS
    targets = (onward_out, back_out)
    for i, piece in enumerate((onward, back)):
        pltpu.make_async_copy(
            piece.at[start : start + 16, :], rows.at[i], sems.at[i]
        ).start()
    for i, values in enumerate((for_onward, for_back)):
        pltpu.make_async_copy(
            onward.at[start : start + 16, :], rows.at[i], sems.at[i]
        ).wait()
        value = values[:KPB]
        high = value.astype(jnp.bfloat16).astype(jnp.float32)
        low = value - high
        facts = rows[i].astype(jnp.float32)[2 * KPB :]
        rows[i] = jnp.concatenate([high, low, facts], axis=0).astype(jnp.bfloat16)
        pltpu.make_async_copy(
            rows.at[i], targets[i].at[start : start + 16, :], sems.at[2 + i]
        ).start()
    for i in range(2):
        pltpu.make_async_copy(
            rows.at[i], targets[i].at[start : start + 16, :], sems.at[2 + i]
        ).wait()


def stamp(pieces, values):
    return pl.pallas_call(
        stamp_kernel,
        out_shape=tuple(pltpu.VMEM(piece.shape, piece.dtype) for piece in pieces),
        in_specs=[ANY, ANY, VMEM, VMEM],
        out_specs=(ANY, ANY),
        scratch_shapes=[
            pltpu.VMEM((2, 16, 128), jnp.bfloat16),
            pltpu.SemaphoreType.DMA((4,)),
        ],
        input_output_aliases={0: 0, 1: 1},
        compiler_params=limit(4),
        name="stamp",
    )(*[kept(piece) for piece in pieces], *[kept(value) for value in values])


def unpack_kernel(owners, slots, own, onward, back, second, third, opposite, out):
    owner = slots[...] // BLK_DEV
    start = onward.shape[0] - FACTS
    way = 1 - 2 * lax.axis_index("width")
    returned = [(0, own[...])]
    for distance, piece in ((-1, onward), (1, back)):
        rows = piece[start : start + 16, :].astype(jnp.float32)
        returned.append((distance, rows[:KPB] + rows[KPB : 2 * KPB]))
    returned += [(2 * way, second[...]), (3 * way, third[...]), (4, opposite[...])]
    mine = [owner == peer_at(distance, owners) for distance, _ in returned]
    for k in range(KPB):
        total = jnp.zeros(owner.shape, jnp.float32)
        for here, (_, values) in zip(mine, returned):
            total = jnp.where(here, values[k : k + 1, :], total)
        out[pl.ds(k, ACT, stride=KPB), :] = total


def unpack(slots, *returned):
    tok_rows = slots.shape[1]
    return pl.pallas_call(
        functools.partial(unpack_kernel, lax.axis_size("dp")),
        out_shape=pltpu.VMEM((ACT * KPB, tok_rows), jnp.float32),
        in_specs=[VMEM] * (1 + len(returned)),
        out_specs=VMEM,
        compiler_params=limit(4),
        name="unpack",
    )(kept(slots), *[kept(x) for x in returned])


def every_owner(decoder, grad_out, active_blocks, feature_idx, acts, block_slot):
    tok_rows = grad_out.shape[0]
    owners = lax.axis_size("dp")
    ring = ring_of(owners)

    def shift(x, by):
        pairs = [(ring[i], ring[(i + by) % owners]) for i in range(owners)]
        return lax.ppermute(x, "dp", pairs)

    def hop(pieces):
        left, right = pieces
        return shift(left, 1), shift(right, -1)

    def crossed(pieces):
        right, left = pieces
        return shift(right, 1), shift(left, -1)

    def other_core(x):
        return lax.ppermute(x, "width", ((0, 1), (1, 0)))

    def return_by(distance, x):
        pairs = []
        for i in range(owners):
            pairs.append((2 * ring[i], 2 * ring[(i - distance) % owners]))
            pairs.append((2 * ring[i] + 1, 2 * ring[(i + distance) % owners] + 1))
        return lax.ppermute(x, ("dp", "width"), pairs)

    left, right = pieces_of(grad_out)
    first_1 = hop((left, right))
    known_left, known_right, own_facts, slots = prepare(
        block_slot, active_blocks, feature_idx, acts, grad_out, owners
    )
    second_1 = crossed((known_right, known_left))
    decoder = fetch(decoder)
    first_1, decoder = lax.optimization_barrier((first_1, decoder))
    first_2 = hop(first_1)
    second_2 = crossed(second_1)
    pairs = [(left, right), (first_1[0], second_1[0]), (second_1[1], first_1[1])]
    distances = (0, -1, 1)
    own, onward, back = scores_of(distances, pairs, decoder, own_facts)
    total = gradients_of(distances, pairs, own_facts, decoder.shape)
    first_3 = hop(first_2)
    second_2 = stamp(second_2, (back, onward))
    second_3 = crossed(second_2)
    pairs = [(first_2[0], second_2[0]), (second_2[1], first_2[1])]
    mine, others = scores_of((-2, 2), pairs, decoder, own_facts, True)
    total = gradients_of((-2, 2), pairs, own_facts, decoder.shape, total)
    second = mine + other_core(others)
    relayed = [piece[-2 * KPB :].astype(jnp.float32) for piece in second_2]
    relayed = jnp.where(lax.axis_index("width") == 0, relayed[1], relayed[0])
    total, first_3, second = lax.optimization_barrier((total, first_3, second))
    returned = return_by(2, jnp.concatenate([second, relayed, jnp.zeros((48, 128), jnp.float32)]))
    second, opposite_facts = returned[: 2 * KPB], returned[2 * KPB : 4 * KPB]
    first_4 = hop(first_3)
    total, second, opposite_facts = lax.optimization_barrier((total, second, opposite_facts))
    second_3, total = lax.optimization_barrier((second_3, total))
    pairs = [(first_3[0], second_3[0]), (second_3[1], first_3[1])]
    mine, others = scores_of((-3, 3), pairs, decoder, own_facts, True)
    total = gradients_of((-3, 3), pairs, own_facts, decoder.shape, total)
    third = mine + other_core(others)
    total, third = lax.optimization_barrier((total, third))
    third = return_by(3, third)
    total, first_4 = lax.optimization_barrier((total, first_4))
    (opposite,) = scores_of((4,), [first_4], decoder, opposite_facts)
    opposite = shift(opposite, -owners // 2)
    total, third = lax.optimization_barrier((total, third))
    decoder_grad = last_gradients(opposite_facts, first_4, total)
    decoder_grad, opposite = lax.optimization_barrier((decoder_grad, opposite))
    act_grad = unpack(slots, own, *second_3, second, third, opposite)
    act_grad = act_grad + other_core(act_grad)
    return (decoder_grad, act_grad.T)


def send_back(picked):
    return lax.all_to_all(picked, "dp", split_axis=1, concat_axis=1, tiled=True)


def pack_slots(grad_out, target, slots_all, pair_coeffs, pair_columns, source_row):
    slot_row = jnp.zeros((slots_all,), jnp.int32).at[target].set(source_row)
    used = jnp.zeros((slots_all,), jnp.bool_).at[target].set(True)
    send_rows = jnp.where(used[:, None], grad_out[slot_row], jnp.zeros((), grad_out.dtype))
    send_acts = jnp.zeros((slots_all, KPB), pair_coeffs.dtype).at[target].set(pair_coeffs)
    send_cols = jnp.zeros((slots_all, KPB), jnp.int32).at[target].set(pair_columns)
    return (send_rows, send_acts, send_cols)


def some_owners(decoder, grad_out, active_blocks, feature_idx, acts, block_slot):
    tok_rows, half_width = grad_out.shape
    owners = lax.axis_size("dp")
    mean_load = tok_rows * ACT // owners
    owner_cap = mean_load + min(mean_load // 2, tok_rows - mean_load)
    block_cap = (owner_cap + 2) // 3
    block_ids = active_blocks.reshape(-1)
    pair_count = block_ids.shape[0]
    table_pos = jnp.arange(block_slot.shape[0], dtype=jnp.int32)
    slot_of = jnp.sum(
        jnp.where(block_ids[:, None] == table_pos[None, :], block_slot[None, :], 0), axis=1
    )
    pair_pos = jnp.arange(pair_count, dtype=jnp.int32)
    source_row = pair_pos // ACT
    pair_coeffs = acts.reshape(pair_count, KPB)
    pair_feats = feature_idx.reshape(pair_count, KPB)
    earlier = (block_ids[:, None] == block_ids[None, :]) & (pair_pos[None, :] < pair_pos[:, None])
    position = jnp.sum(earlier.astype(jnp.int32), axis=1)
    slot_cols = owners * block_cap
    target = slot_of % BLK_DEV * slot_cols + slot_of // BLK_DEV * block_cap + position
    slots_all = BLK_DEV * slot_cols
    send_rows, send_acts, send_cols = pack_slots(
        grad_out, target, slots_all, pair_coeffs, pair_feats, source_row
    )
    rows, coeffs, feature_pos = (
        lax.all_to_all(
            send_rows.reshape(BLK_DEV, slot_cols, half_width),
            "dp",
            split_axis=1,
            concat_axis=1,
            tiled=True,
        ),
        lax.all_to_all(
            send_acts.reshape(BLK_DEV, slot_cols, KPB),
            "dp",
            split_axis=1,
            concat_axis=1,
            tiled=True,
        ),
        lax.all_to_all(
            send_cols.reshape(BLK_DEV, slot_cols, KPB),
            "dp",
            split_axis=1,
            concat_axis=1,
            tiled=True,
        ),
    )
    weights = decoder.reshape(BLK_DEV, BW, half_width)
    scores = jnp.einsum("bnd,bfd->bnf", rows, weights, preferred_element_type=jnp.float32)
    picked = jnp.take_along_axis(scores, feature_pos, axis=2)
    returned = send_back(picked)
    feature_axis = jnp.arange(BW, dtype=jnp.int32)
    matches = feature_pos[..., None] == feature_axis
    dense = jnp.sum(jnp.where(matches, coeffs[..., None].astype(jnp.float32), 0.0), axis=2).astype(
        jnp.bfloat16
    )
    grads = jnp.einsum("bnf,bnd->bfd", dense, rows, preferred_element_type=jnp.float32)
    decoder_grad = grads.astype(jnp.bfloat16).reshape(BLK_DEV * BW, half_width)
    pair_vals = returned.reshape(slots_all, KPB)[target]
    act_grad = pair_vals.reshape(tok_rows, ACT * KPB)
    act_grad = lax.psum(act_grad, "width")
    return (decoder_grad, act_grad)


def per_device(*args):
    if lax.axis_size("dp") == ACT:
        return every_owner(*args)
    return some_owners(*args)


def solution(mesh):
    in_specs = (
        P(("groups", "dp"), "width"),
        P(("groups", "dp"), "width"),
        P(("groups", "dp"), None),
        P(("groups", "dp"), None),
        P(("groups", "dp"), None),
        P("groups"),
    )
    out_specs = (P(("groups", "dp"), "width"), P(("groups", "dp"), None))
    return jax.shard_map(
        per_device, mesh=mesh, in_specs=in_specs, out_specs=out_specs, check_vma=False
    )
```

```python
import functools

import jax
import jax.numpy as jnp
from jax import lax
from jax.experimental import pallas as pl
from jax.experimental.pallas import tpu as pltpu
from jax.sharding import PartitionSpec as P

BW = 128
BLK_DEV = 4
ACT = 8
KPB = 4
SMEM = pl.BlockSpec(memory_space=pltpu.SMEM)
VMEM = pl.BlockSpec(memory_space=pltpu.VMEM)
ANY = pl.BlockSpec(memory_space=pl.ANY)
HBM = pl.BlockSpec(memory_space=pltpu.HBM)


def limit(mebibytes):
    return pltpu.CompilerParams(vmem_limit_bytes=mebibytes * 2**20)


def kept(x):
    return pltpu.with_memory_space_constraint(x, pltpu.VMEM)


def far(x):
    return pltpu.with_memory_space_constraint(x, pltpu.HBM)


def ring_of(owners):
    return list(range(0, owners, 2)) + list(range(owners - 1, 0, -2))


def peer_at(distance, owners):
    me = lax.axis_index("dp")
    half_ring = owners // 2
    place = jnp.where(lax.rem(me, 2) == 0, lax.div(me, 2), owners - 1 - lax.div(me, 2))
    at = lax.rem(place + owners + distance, owners)
    return jnp.where(at < half_ring, 2 * at, 2 * (owners - 1 - at) + 1)


def copies_to_pieces(grad_out, left, right, sems):
    tok_rows, width = grad_out.shape
    parts = width // 256
    copies = []
    for j in range(parts):
        for target, side in ((left, 0), (right, 1)):
            column = (side * parts + j) * 128
            copies.append(
                pltpu.make_async_copy(
                    grad_out.at[:, column : column + 128],
                    target.at[j * tok_rows : (j + 1) * tok_rows, :],
                    sems.at[len(copies)],
                )
            )
    return copies


def pieces_kernel(grad_out, left, right, sems):
    copies = copies_to_pieces(grad_out, left, right, sems)
    for copy in copies:
        copy.start()
    for copy in copies:
        copy.wait()


def pieces_of(grad_out):
    tok_rows, width = grad_out.shape
    shape = pltpu.VMEM((width // 256 * tok_rows, 128), grad_out.dtype)
    return pl.pallas_call(
        pieces_kernel,
        out_shape=(shape, shape),
        in_specs=[HBM],
        out_specs=(VMEM, VMEM),
        scratch_shapes=[pltpu.SemaphoreType.DMA((width // 128,))],
        compiler_params=limit(8),
        name="pieces",
    )(far(grad_out))


ROW_SHIFT = BLK_DEV * BW // 2
FACTS = ACT // 2 * 2 * KPB


def facts_for(owner_id, owner, first_row, feats, acts):
    mine = owner == owner_id
    rows = [
        jnp.sum(jnp.where(mine, first_row + feats[k], 0.0), axis=0, keepdims=True) - ROW_SHIFT
        for k in range(KPB)
    ]
    values = [
        jnp.sum(jnp.where(mine, acts[k], 0.0), axis=0, keepdims=True) for k in range(KPB)
    ]
    return jnp.concatenate(rows + values, axis=0)


def prepare_kernel(owners, *refs):
    sources, refs = refs[:5], refs[5:]
    left, right, own_facts, slots = refs[:4]
    block_slot, active, feats, acts, wide_feats, wide_acts, sems = refs[4:]
    small = []
    for source, target in zip(sources[:4], (block_slot, active, feats, acts)):
        small.append(pltpu.make_async_copy(source, target, sems.at[len(small)]))
        small[-1].start()
    copies = copies_to_pieces(sources[-1], left, right, sems.at[4:])
    for copy in copies:
        copy.start()
    for copy in small:
        copy.wait()
    named = active[...]
    slot = jnp.zeros_like(named)
    for block in range(block_slot.shape[0]):
        slot = jnp.where(named == block, block_slot[block], slot)
    slots[...] = slot
    wide_feats[...] = feats[...].astype(jnp.float32)
    wide_acts[...] = acts[...].astype(jnp.float32)
    features = [wide_feats[pl.ds(k, ACT, stride=KPB), :] for k in range(KPB)]
    values = [wide_acts[pl.ds(k, ACT, stride=KPB), :] for k in range(KPB)]
    first_row = (slot % BLK_DEV * BW).astype(jnp.float32)

    def facts(distance):
        return facts_for(
            peer_at(distance, owners), slot // BLK_DEV, first_row, features, values
        )

    own_facts[...] = facts(0)
    for target, sign in ((left, -1), (right, 1)):
        ahead = [facts(sign * d) for d in range(1, owners // 2 + 1)]
        target[target.shape[0] - FACTS :, :] = jnp.concatenate(ahead, axis=0).astype(
            jnp.bfloat16
        )
    for copy in copies:
        copy.wait()


def prepare(block_slot, active_blocks, feature_idx, acts, grad_out, owners):
    tok_rows, width = grad_out.shape
    piece = pltpu.VMEM((width // 256 * tok_rows + FACTS, 128), grad_out.dtype)
    facts = pltpu.VMEM((2 * KPB, tok_rows), jnp.float32)
    return pl.pallas_call(
        functools.partial(prepare_kernel, owners),
        out_shape=(piece, piece, facts, pltpu.VMEM((ACT, tok_rows), jnp.int32)),
        in_specs=[HBM] * 5,
        out_specs=(VMEM,) * 4,
        scratch_shapes=[
            pltpu.SMEM(block_slot.shape, jnp.int32),
            pltpu.VMEM((ACT, tok_rows), jnp.int32),
            pltpu.VMEM((ACT * KPB, tok_rows), jnp.int32),
            pltpu.VMEM((ACT * KPB, tok_rows), acts.dtype),
            pltpu.VMEM((ACT * KPB, tok_rows), jnp.float32),
            pltpu.VMEM((ACT * KPB, tok_rows), jnp.float32),
            pltpu.SemaphoreType.DMA((4 + width // 128,)),
        ],
        compiler_params=limit(8),
        name="prepare",
    )(far(block_slot), far(active_blocks.T), far(feature_idx.T), far(acts.T), far(grad_out))


def fetch_kernel(source, target, sem):
    copy = pltpu.make_async_copy(source, target, sem)
    copy.start()
    copy.wait()


def fetch(x):
    return pl.pallas_call(
        fetch_kernel,
        out_shape=pltpu.VMEM(x.shape, x.dtype),
        in_specs=[HBM],
        out_specs=VMEM,
        scratch_shapes=[pltpu.SemaphoreType.DMA],
        compiler_params=limit(8),
        name="fetch",
    )(far(x))


def block_and_rows(here):
    at_row = here[:KPB].astype(jnp.int32) + ROW_SHIFT
    return at_row[:1] // BW, at_row % BW


def row_axis_of(tok_rows):
    return lax.broadcasted_iota(jnp.int32, (BW, tok_rows), 0)


def coefficients(here):
    block, feats = block_and_rows(here)
    row_axis = row_axis_of(here.shape[1])
    dense = jnp.zeros(row_axis.shape, jnp.float32)
    for k in range(KPB):
        dense = jnp.where(row_axis == feats[k : k + 1], here[KPB + k : KPB + k + 1], dense)
    parts = [jnp.where(block == b, dense, 0.0) for b in range(BLK_DEV)]
    return jnp.concatenate(parts, axis=0).astype(jnp.bfloat16)


def pick(scores, here):
    block, feats = block_and_rows(here)
    row_axis = row_axis_of(here.shape[1])
    mine = scores[:BW]
    for b in range(1, BLK_DEV):
        mine = jnp.where(block == b, scores[b * BW : (b + 1) * BW], mine)
    return [
        jnp.sum(jnp.where(row_axis == feats[k : k + 1], mine, 0.0), axis=0, keepdims=True)
        for k in range(KPB)
    ]


def facts_in(piece, distance, tok_rows):
    facts = piece[piece.shape[0] - FACTS :, :].astype(jnp.float32)
    return facts[(abs(distance) - 1) * 2 * KPB : abs(distance) * 2 * KPB]


def columns_of(pieces, tok_rows, parts):
    rows = [
        jnp.concatenate([piece[j * tok_rows : (j + 1) * tok_rows, :] for j in parts], axis=1)
        for piece in pieces
    ]
    return jnp.concatenate(rows, axis=0) if len(rows) > 1 else rows[0]


def picks_of(facts, decoder, pieces):
    picks = []
    tok_rows = facts[0].shape[1]
    cut = decoder.shape[1] // 2
    for first in range(0, len(facts), 2):
        count = min(2, len(facts) - first)
        scores = None
        for side in range(2):
            part = lax.dot_general(
                decoder[:, side * cut : (side + 1) * cut],
                columns_of(
                    pieces[2 * first + side : 2 * (first + count) : 2],
                    tok_rows,
                    range(cut // 128),
                ),
                (((1,), (1,)), ((), ())),
                preferred_element_type=jnp.float32,
            )
            scores = part if scores is None else scores + part
        for i in range(first, first + count):
            here = scores[:, (i - first) * tok_rows : (i - first + 1) * tok_rows]
            picks.append(jnp.concatenate(pick(here, facts[i]) * 2, axis=0))
    return picks


def gradient_blocks(facts, pieces, width):
    tok_rows = facts[0].shape[1]
    cut = width // 2
    dense = jnp.concatenate([coefficients(here) for here in facts], axis=1)
    for side in range(2):
        for j in range(0, cut // 128, 2):
            rows = columns_of(pieces[side::2], tok_rows, (j, j + 1))
            part = jnp.dot(dense, rows, preferred_element_type=jnp.float32)
            yield slice(side * cut + j * 128, side * cut + (j + 2) * 128), part


def facts_of(distances, given, pieces):
    tok_rows = given.shape[1]
    return [
        given[...] if d in (0, 4) else facts_in(pieces[2 * i + (d < 0)], d, tok_rows)
        for i, d in enumerate(distances)
    ]


def scores_kernel(distances, split, relay, decoder, given, *refs):
    pieces, picked = refs[: 2 * len(distances)], refs[2 * len(distances) :]
    picks = picks_of(facts_of(distances, given, pieces), decoder, pieces)
    if split:
        first = lax.axis_index("width") == 0
        picks = [jnp.where(first, *picks), jnp.where(first, *picks[::-1])]
    if relay:
        onward, back = (facts_in(piece, 4, given.shape[1]) for piece in pieces[1:3])
        picks.append(jnp.where(first, back, onward))
    for target, values in zip(picked, picks):
        target[...] = values


def scores_of(distances, pairs, decoder, given, split=False, relay=False):
    pieces = [kept(piece) for pair in pairs for piece in pair]
    shape = pltpu.VMEM(given.shape, jnp.float32)
    return pl.pallas_call(
        functools.partial(scores_kernel, distances, split, relay),
        out_shape=(shape,) * (len(distances) + relay),
        in_specs=[VMEM] * (2 + len(pieces)),
        out_specs=(VMEM,) * (len(distances) + relay),
        compiler_params=limit(12),
        name="scores",
    )(kept(decoder), kept(given), *pieces)


def gradients_kernel(distances, given, *refs):
    pieces, refs = refs[: 2 * len(distances)], refs[2 * len(distances) :]
    total = refs[-1]
    facts = facts_of(distances, given, pieces)
    for columns, part in gradient_blocks(facts, pieces, total.shape[1]):
        total[:, columns] = part if len(refs) == 1 else refs[0][:, columns] + part


def gradients_of(distances, pairs, given, shape, total=None):
    operands = [kept(given)] + [kept(piece) for pair in pairs for piece in pair]
    operands += [] if total is None else [kept(total)]
    return pl.pallas_call(
        functools.partial(gradients_kernel, distances),
        out_shape=pltpu.VMEM(shape, jnp.float32),
        in_specs=[VMEM] * len(operands),
        out_specs=VMEM,
        input_output_aliases={} if total is None else {len(operands) - 1: 0},
        compiler_params=limit(16),
        name="gradients",
    )(*operands)


def last_gradients_kernel(given, left, right, total, out, rounded, sems):
    copies = []
    for columns, part in gradient_blocks([given[...]], (left, right), out.shape[1]):
        rounded[:, columns] = (total[:, columns] + part).astype(out.dtype)
        copies.append(
            pltpu.make_async_copy(
                rounded.at[:, columns], out.at[:, columns], sems.at[len(copies)]
            )
        )
        copies[-1].start()
    for copy in copies:
        copy.wait()


def last_gradients(given, pair, total):
    return pl.pallas_call(
        last_gradients_kernel,
        out_shape=jax.ShapeDtypeStruct(total.shape, jnp.bfloat16),
        in_specs=[VMEM] * 4,
        out_specs=ANY,
        scratch_shapes=[
            pltpu.VMEM(total.shape, jnp.bfloat16),
            pltpu.SemaphoreType.DMA((total.shape[1] // 256,)),
        ],
        compiler_params=limit(16),
        name="last_gradients",
    )(kept(given), kept(pair[0]), kept(pair[1]), kept(total))


def stamp_kernel(onward, back, for_onward, for_back, onward_out, back_out, rows, sems):
    start = onward.shape[0] - FACTS
    targets = (onward_out, back_out)
    for i, piece in enumerate((onward, back)):
        pltpu.make_async_copy(
            piece.at[start : start + 16, :], rows.at[i], sems.at[i]
        ).start()
    for i, values in enumerate((for_onward, for_back)):
        pltpu.make_async_copy(
            onward.at[start : start + 16, :], rows.at[i], sems.at[i]
        ).wait()
        value = values[:KPB]
        high = value.astype(jnp.bfloat16).astype(jnp.float32)
        low = value - high
        facts = rows[i].astype(jnp.float32)[2 * KPB :]
        rows[i] = jnp.concatenate([high, low, facts], axis=0).astype(jnp.bfloat16)
        pltpu.make_async_copy(
            rows.at[i], targets[i].at[start : start + 16, :], sems.at[2 + i]
        ).start()
    for i in range(2):
        pltpu.make_async_copy(
            rows.at[i], targets[i].at[start : start + 16, :], sems.at[2 + i]
        ).wait()


def stamp(pieces, values):
    return pl.pallas_call(
        stamp_kernel,
        out_shape=tuple(pltpu.VMEM(piece.shape, piece.dtype) for piece in pieces),
        in_specs=[ANY, ANY, VMEM, VMEM],
        out_specs=(ANY, ANY),
        scratch_shapes=[
            pltpu.VMEM((2, 16, 128), jnp.bfloat16),
            pltpu.SemaphoreType.DMA((4,)),
        ],
        input_output_aliases={0: 0, 1: 1},
        compiler_params=limit(4),
        name="stamp",
    )(*[kept(piece) for piece in pieces], *[kept(value) for value in values])


def unpack_kernel(owners, slots, own, onward, back, second, third, opposite, out):
    owner = slots[...] // BLK_DEV
    start = onward.shape[0] - FACTS
    way = 1 - 2 * lax.axis_index("width")
    returned = [(0, own[...])]
    for distance, piece in ((-1, onward), (1, back)):
        rows = piece[start : start + 16, :].astype(jnp.float32)
        returned.append((distance, rows[:KPB] + rows[KPB : 2 * KPB]))
    returned += [(2 * way, second[...]), (3 * way, third[...]), (4, opposite[...])]
    mine = [owner == peer_at(distance, owners) for distance, _ in returned]
    for k in range(KPB):
        total = jnp.zeros(owner.shape, jnp.float32)
        for here, (_, values) in zip(mine, returned):
            total = jnp.where(here, values[k : k + 1, :], total)
        out[pl.ds(k, ACT, stride=KPB), :] = total


def unpack(slots, *returned):
    tok_rows = slots.shape[1]
    return pl.pallas_call(
        functools.partial(unpack_kernel, lax.axis_size("dp")),
        out_shape=pltpu.VMEM((ACT * KPB, tok_rows), jnp.float32),
        in_specs=[VMEM] * (1 + len(returned)),
        out_specs=VMEM,
        compiler_params=limit(4),
        name="unpack",
    )(kept(slots), *[kept(x) for x in returned])


def every_owner(decoder, grad_out, active_blocks, feature_idx, acts, block_slot):
    tok_rows = grad_out.shape[0]
    owners = lax.axis_size("dp")
    ring = ring_of(owners)

    def shift(x, by):
        pairs = [(ring[i], ring[(i + by) % owners]) for i in range(owners)]
        return lax.ppermute(x, "dp", pairs)

    def hop(pieces):
        left, right = pieces
        return shift(left, 1), shift(right, -1)

    def crossed(pieces):
        right, left = pieces
        return shift(right, 1), shift(left, -1)

    def other_core(x):
        return lax.ppermute(x, "width", ((0, 1), (1, 0)))

    def return_by(distance, x):
        pairs = []
        for i in range(owners):
            pairs.append((2 * ring[i], 2 * ring[(i - distance) % owners]))
            pairs.append((2 * ring[i] + 1, 2 * ring[(i + distance) % owners] + 1))
        return lax.ppermute(x, ("dp", "width"), pairs)

    left, right = pieces_of(grad_out)
    first_1 = hop((left, right))
    known_left, known_right, own_facts, slots = prepare(
        block_slot, active_blocks, feature_idx, acts, grad_out, owners
    )
    second_1 = crossed((known_right, known_left))
    decoder = fetch(decoder)
    first_1, decoder = lax.optimization_barrier((first_1, decoder))
    first_2 = hop(first_1)
    second_2 = crossed(second_1)
    pairs = [(left, right), (first_1[0], second_1[0]), (second_1[1], first_1[1])]
    distances = (0, -1, 1)
    own, onward, back = scores_of(distances, pairs, decoder, own_facts)
    total = gradients_of(distances, pairs, own_facts, decoder.shape)
    first_3 = hop(first_2)
    second_2 = stamp(second_2, (back, onward))
    second_3 = crossed(second_2)
    pairs = [(first_2[0], second_2[0]), (second_2[1], first_2[1])]
    mine, others, relayed = scores_of((-2, 2), pairs, decoder, own_facts, True, True)
    total = gradients_of((-2, 2), pairs, own_facts, decoder.shape, total)
    second = mine + other_core(others)
    total, first_3, second = lax.optimization_barrier((total, first_3, second))
    returned = return_by(2, jnp.concatenate([second, relayed, jnp.zeros((48, 128), jnp.float32)]))
    second, opposite_facts = returned[: 2 * KPB], returned[2 * KPB : 4 * KPB]
    first_4 = hop(first_3)
    total, second, opposite_facts = lax.optimization_barrier((total, second, opposite_facts))
    second_3, total = lax.optimization_barrier((second_3, total))
    pairs = [(first_3[0], second_3[0]), (second_3[1], first_3[1])]
    mine, others = scores_of((-3, 3), pairs, decoder, own_facts, True)
    total = gradients_of((-3, 3), pairs, own_facts, decoder.shape, total)
    third = mine + other_core(others)
    total, third = lax.optimization_barrier((total, third))
    third = return_by(3, third)
    total, first_4 = lax.optimization_barrier((total, first_4))
    (opposite,) = scores_of((4,), [first_4], decoder, opposite_facts)
    opposite = shift(opposite, -owners // 2)
    total, third = lax.optimization_barrier((total, third))
    decoder_grad = last_gradients(opposite_facts, first_4, total)
    decoder_grad, opposite = lax.optimization_barrier((decoder_grad, opposite))
    act_grad = unpack(slots, own, *second_3, second, third, opposite)
    act_grad = act_grad + other_core(act_grad)
    return (decoder_grad, act_grad.T)


def send_back(picked):
    return lax.all_to_all(picked, "dp", split_axis=1, concat_axis=1, tiled=True)


def pack_slots(grad_out, target, slots_all, pair_coeffs, pair_columns, source_row):
    slot_row = jnp.zeros((slots_all,), jnp.int32).at[target].set(source_row)
    used = jnp.zeros((slots_all,), jnp.bool_).at[target].set(True)
    send_rows = jnp.where(used[:, None], grad_out[slot_row], jnp.zeros((), grad_out.dtype))
    send_acts = jnp.zeros((slots_all, KPB), pair_coeffs.dtype).at[target].set(pair_coeffs)
    send_cols = jnp.zeros((slots_all, KPB), jnp.int32).at[target].set(pair_columns)
    return (send_rows, send_acts, send_cols)


def some_owners(decoder, grad_out, active_blocks, feature_idx, acts, block_slot):
    tok_rows, half_width = grad_out.shape
    owners = lax.axis_size("dp")
    mean_load = tok_rows * ACT // owners
    owner_cap = mean_load + min(mean_load // 2, tok_rows - mean_load)
    block_cap = (owner_cap + 2) // 3
    block_ids = active_blocks.reshape(-1)
    pair_count = block_ids.shape[0]
    table_pos = jnp.arange(block_slot.shape[0], dtype=jnp.int32)
    slot_of = jnp.sum(
        jnp.where(block_ids[:, None] == table_pos[None, :], block_slot[None, :], 0), axis=1
    )
    pair_pos = jnp.arange(pair_count, dtype=jnp.int32)
    source_row = pair_pos // ACT
    pair_coeffs = acts.reshape(pair_count, KPB)
    pair_feats = feature_idx.reshape(pair_count, KPB)
    earlier = (block_ids[:, None] == block_ids[None, :]) & (pair_pos[None, :] < pair_pos[:, None])
    position = jnp.sum(earlier.astype(jnp.int32), axis=1)
    slot_cols = owners * block_cap
    target = slot_of % BLK_DEV * slot_cols + slot_of // BLK_DEV * block_cap + position
    slots_all = BLK_DEV * slot_cols
    send_rows, send_acts, send_cols = pack_slots(
        grad_out, target, slots_all, pair_coeffs, pair_feats, source_row
    )
    rows, coeffs, feature_pos = (
        lax.all_to_all(
            send_rows.reshape(BLK_DEV, slot_cols, half_width),
            "dp",
            split_axis=1,
            concat_axis=1,
            tiled=True,
        ),
        lax.all_to_all(
            send_acts.reshape(BLK_DEV, slot_cols, KPB),
            "dp",
            split_axis=1,
            concat_axis=1,
            tiled=True,
        ),
        lax.all_to_all(
            send_cols.reshape(BLK_DEV, slot_cols, KPB),
            "dp",
            split_axis=1,
            concat_axis=1,
            tiled=True,
        ),
    )
    weights = decoder.reshape(BLK_DEV, BW, half_width)
    scores = jnp.einsum("bnd,bfd->bnf", rows, weights, preferred_element_type=jnp.float32)
    picked = jnp.take_along_axis(scores, feature_pos, axis=2)
    returned = send_back(picked)
    feature_axis = jnp.arange(BW, dtype=jnp.int32)
    matches = feature_pos[..., None] == feature_axis
    dense = jnp.sum(jnp.where(matches, coeffs[..., None].astype(jnp.float32), 0.0), axis=2).astype(
        jnp.bfloat16
    )
    grads = jnp.einsum("bnf,bnd->bfd", dense, rows, preferred_element_type=jnp.float32)
    decoder_grad = grads.astype(jnp.bfloat16).reshape(BLK_DEV * BW, half_width)
    pair_vals = returned.reshape(slots_all, KPB)[target]
    act_grad = pair_vals.reshape(tok_rows, ACT * KPB)
    act_grad = lax.psum(act_grad, "width")
    return (decoder_grad, act_grad)


def per_device(*args):
    if lax.axis_size("dp") == ACT:
        return every_owner(*args)
    return some_owners(*args)


def solution(mesh):
    in_specs = (
        P(("groups", "dp"), "width"),
        P(("groups", "dp"), "width"),
        P(("groups", "dp"), None),
        P(("groups", "dp"), None),
        P(("groups", "dp"), None),
        P("groups"),
    )
    out_specs = (P(("groups", "dp"), "width"), P(("groups", "dp"), None))
    return jax.shard_map(
        per_device, mesh=mesh, in_specs=in_specs, out_specs=out_specs, check_vma=False
    )
```

```python
import functools

import jax
import jax.numpy as jnp
from jax import lax
from jax.experimental import pallas as pl
from jax.experimental.pallas import tpu as pltpu
from jax.sharding import PartitionSpec as P

BW = 128
BLK_DEV = 4
ACT = 8
KPB = 4
SMEM = pl.BlockSpec(memory_space=pltpu.SMEM)
VMEM = pl.BlockSpec(memory_space=pltpu.VMEM)
ANY = pl.BlockSpec(memory_space=pl.ANY)
HBM = pl.BlockSpec(memory_space=pltpu.HBM)


def limit(mebibytes):
    return pltpu.CompilerParams(vmem_limit_bytes=mebibytes * 2**20)


def kept(x):
    return pltpu.with_memory_space_constraint(x, pltpu.VMEM)


def far(x):
    return pltpu.with_memory_space_constraint(x, pltpu.HBM)


def ring_of(owners):
    return list(range(0, owners, 2)) + list(range(owners - 1, 0, -2))


def peer_at(distance, owners):
    me = lax.axis_index("dp")
    half_ring = owners // 2
    place = jnp.where(lax.rem(me, 2) == 0, lax.div(me, 2), owners - 1 - lax.div(me, 2))
    at = lax.rem(place + owners + distance, owners)
    return jnp.where(at < half_ring, 2 * at, 2 * (owners - 1 - at) + 1)


ROW_SHIFT = BLK_DEV * BW // 2
FACTS = ACT // 2 * 2 * KPB
LAST_FACTS = 16


def facts_for(owner_id, owner, first_row, feats, acts):
    mine = owner == owner_id
    rows = [
        jnp.sum(jnp.where(mine, first_row + feats[k], 0.0), axis=0, keepdims=True) - ROW_SHIFT
        for k in range(KPB)
    ]
    values = [
        jnp.sum(jnp.where(mine, acts[k], 0.0), axis=0, keepdims=True) for k in range(KPB)
    ]
    return jnp.concatenate(rows + values, axis=0)


def prepare_kernel(owners, *refs):
    sources, refs = refs[:5], refs[5:]
    outs, refs = refs[:6], refs[6:]
    first_left, first_right, left, right, own_facts, slots = outs
    block_slot, active, feats, acts, halves, wide_feats, wide_acts, sems = refs
    cut = halves.shape[2]
    copies = []
    for source, target in zip(sources[:4], (block_slot, active, feats, acts)):
        copies.append(pltpu.make_async_copy(source, target, sems.at[len(copies)]))
    for side in range(2):
        copies.append(
            pltpu.make_async_copy(
                sources[4].at[:, side * cut : (side + 1) * cut],
                halves.at[side],
                sems.at[len(copies)],
            )
        )
    for copy in copies:
        copy.start()
    for copy in copies[:4]:
        copy.wait()
    named = active[...]
    slot = jnp.zeros_like(named)
    for block in range(block_slot.shape[0]):
        slot = jnp.where(named == block, block_slot[block], slot)
    slots[...] = slot
    wide_feats[...] = feats[...].astype(jnp.float32)
    wide_acts[...] = acts[...].astype(jnp.float32)
    features = [wide_feats[pl.ds(k, ACT, stride=KPB), :] for k in range(KPB)]
    values = [wide_acts[pl.ds(k, ACT, stride=KPB), :] for k in range(KPB)]
    first_row = (slot % BLK_DEV * BW).astype(jnp.float32)

    def facts(distance):
        return facts_for(
            peer_at(distance, owners), slot // BLK_DEV, first_row, features, values
        )

    def store_facts(target, blocks):
        rows = jnp.concatenate(blocks, axis=0)
        target[target.shape[0] - rows.shape[0] :, :] = rows.astype(jnp.bfloat16)

    own_facts[...] = facts(0)
    opposite = facts(owners // 2)
    none = jnp.zeros_like(opposite)
    store_facts(first_left, [opposite, none])
    for target, sign in ((left, -1), (right, 1)):
        store_facts(target, [facts(sign * d) for d in range(1, owners // 2)] + [none])
    tok_rows = halves.shape[1]
    for side, targets in ((0, (first_left, left)), (1, (first_right, right))):
        copies[4 + side].wait()
        for j in range(cut // 128):
            part = halves[side, :, j * 128 : (j + 1) * 128]
            for target in targets:
                target[j * tok_rows : (j + 1) * tok_rows, :] = part


def prepare(block_slot, active_blocks, feature_idx, acts, grad_out, owners):
    tok_rows, width = grad_out.shape
    plain = width // 256 * tok_rows

    def piece(extra):
        return pltpu.VMEM((plain + extra, 128), grad_out.dtype)

    return pl.pallas_call(
        functools.partial(prepare_kernel, owners),
        out_shape=(
            piece(LAST_FACTS),
            piece(0),
            piece(FACTS),
            piece(FACTS),
            pltpu.VMEM((2 * KPB, tok_rows), jnp.float32),
            pltpu.VMEM((ACT, tok_rows), jnp.int32),
        ),
        in_specs=[HBM] * 5,
        out_specs=(VMEM,) * 6,
        scratch_shapes=[
            pltpu.SMEM(block_slot.shape, jnp.int32),
            pltpu.VMEM((ACT, tok_rows), jnp.int32),
            pltpu.VMEM((ACT * KPB, tok_rows), jnp.int32),
            pltpu.VMEM((ACT * KPB, tok_rows), acts.dtype),
            pltpu.VMEM((2, tok_rows, width // 2), grad_out.dtype),
            pltpu.VMEM((ACT * KPB, tok_rows), jnp.float32),
            pltpu.VMEM((ACT * KPB, tok_rows), jnp.float32),
            pltpu.SemaphoreType.DMA((6,)),
        ],
        compiler_params=limit(8),
        name="prepare",
    )(far(block_slot), far(active_blocks.T), far(feature_idx.T), far(acts.T), far(grad_out))


def fetch_kernel(source, target, sem):
    copy = pltpu.make_async_copy(source, target, sem)
    copy.start()
    copy.wait()


def fetch(x):
    return pl.pallas_call(
        fetch_kernel,
        out_shape=pltpu.VMEM(x.shape, x.dtype),
        in_specs=[HBM],
        out_specs=VMEM,
        scratch_shapes=[pltpu.SemaphoreType.DMA],
        compiler_params=limit(8),
        name="fetch",
    )(far(x))


def block_and_rows(here):
    at_row = here[:KPB].astype(jnp.int32) + ROW_SHIFT
    return at_row[:1] // BW, at_row % BW


def row_axis_of(tok_rows):
    return lax.broadcasted_iota(jnp.int32, (BW, tok_rows), 0)


def coefficients(here):
    block, feats = block_and_rows(here)
    row_axis = row_axis_of(here.shape[1])
    dense = jnp.zeros(row_axis.shape, jnp.float32)
    for k in range(KPB):
        dense = jnp.where(row_axis == feats[k : k + 1], here[KPB + k : KPB + k + 1], dense)
    parts = [jnp.where(block == b, dense, 0.0) for b in range(BLK_DEV)]
    return jnp.concatenate(parts, axis=0).astype(jnp.bfloat16)


def pick(scores, here):
    block, feats = block_and_rows(here)
    row_axis = row_axis_of(here.shape[1])
    mine = scores[:BW]
    for b in range(1, BLK_DEV):
        mine = jnp.where(block == b, scores[b * BW : (b + 1) * BW], mine)
    return [
        jnp.sum(jnp.where(row_axis == feats[k : k + 1], mine, 0.0), axis=0, keepdims=True)
        for k in range(KPB)
    ]


def facts_in(piece, distance, tok_rows):
    facts = piece[piece.shape[0] - FACTS :, :].astype(jnp.float32)
    return facts[(abs(distance) - 1) * 2 * KPB : abs(distance) * 2 * KPB]


def columns_of(pieces, tok_rows, parts):
    rows = [
        jnp.concatenate([piece[j * tok_rows : (j + 1) * tok_rows, :] for j in parts], axis=1)
        for piece in pieces
    ]
    return jnp.concatenate(rows, axis=0) if len(rows) > 1 else rows[0]


def picks_of(facts, decoder, pieces):
    picks = []
    tok_rows = facts[0].shape[1]
    cut = decoder.shape[1] // 2
    for first in range(0, len(facts), 2):
        count = min(2, len(facts) - first)
        scores = None
        for side in range(2):
            part = lax.dot_general(
                decoder[:, side * cut : (side + 1) * cut],
                columns_of(
                    pieces[2 * first + side : 2 * (first + count) : 2],
                    tok_rows,
                    range(cut // 128),
                ),
                (((1,), (1,)), ((), ())),
                preferred_element_type=jnp.float32,
            )
            scores = part if scores is None else scores + part
        for i in range(first, first + count):
            here = scores[:, (i - first) * tok_rows : (i - first + 1) * tok_rows]
            picks.append(jnp.concatenate(pick(here, facts[i]) * 2, axis=0))
    return picks


def gradient_blocks(facts, pieces, width):
    tok_rows = facts[0].shape[1]
    cut = width // 2
    dense = jnp.concatenate([coefficients(here) for here in facts], axis=1)
    for side in range(2):
        for j in range(0, cut // 128, 2):
            rows = columns_of(pieces[side::2], tok_rows, (j, j + 1))
            part = jnp.dot(dense, rows, preferred_element_type=jnp.float32)
            yield slice(side * cut + j * 128, side * cut + (j + 2) * 128), part


def last_facts_in(piece):
    return piece[piece.shape[0] - LAST_FACTS :, :].astype(jnp.float32)[: 2 * KPB]


def facts_of(distances, own_facts, pieces):
    facts = []
    for i, d in enumerate(distances):
        if d == 0:
            facts.append(own_facts[...])
        elif d == 4:
            facts.append(last_facts_in(pieces[2 * i]))
        else:
            facts.append(facts_in(pieces[2 * i + (d < 0)], d, own_facts.shape[1]))
    return facts


def scores_kernel(distances, split, decoder, own_facts, *refs):
    pieces, picked = refs[: 2 * len(distances)], refs[2 * len(distances) :]
    picks = picks_of(facts_of(distances, own_facts, pieces), decoder, pieces)
    if split:
        first = lax.axis_index("width") == 0
        picks = [jnp.where(first, *picks), jnp.where(first, *picks[::-1])]
    for target, values in zip(picked, picks):
        target[...] = values


def scores_of(distances, pairs, decoder, own_facts, split=False):
    pieces = [kept(piece) for pair in pairs for piece in pair]
    shape = pltpu.VMEM(own_facts.shape, jnp.float32)
    return pl.pallas_call(
        functools.partial(scores_kernel, distances, split),
        out_shape=(shape,) * len(distances),
        in_specs=[VMEM] * (2 + len(pieces)),
        out_specs=(VMEM,) * len(distances),
        compiler_params=limit(12),
        name="scores",
    )(kept(decoder), kept(own_facts), *pieces)


def gradients_kernel(distances, own_facts, *refs):
    pieces, refs = refs[: 2 * len(distances)], refs[2 * len(distances) :]
    total = refs[-1]
    facts = facts_of(distances, own_facts, pieces)
    for columns, part in gradient_blocks(facts, pieces, total.shape[1]):
        total[:, columns] = part if len(refs) == 1 else refs[0][:, columns] + part


def gradients_of(distances, pairs, own_facts, shape, total=None):
    operands = [kept(own_facts)] + [kept(piece) for pair in pairs for piece in pair]
    operands += [] if total is None else [kept(total)]
    return pl.pallas_call(
        functools.partial(gradients_kernel, distances),
        out_shape=pltpu.VMEM(shape, jnp.float32),
        in_specs=[VMEM] * len(operands),
        out_specs=VMEM,
        input_output_aliases={} if total is None else {len(operands) - 1: 0},
        compiler_params=limit(16),
        name="gradients",
    )(*operands)


def last_gradients_kernel(left, right, total, out, rounded, sems):
    copies = []
    facts = [last_facts_in(left)]
    for columns, part in gradient_blocks(facts, (left, right), out.shape[1]):
        rounded[:, columns] = (total[:, columns] + part).astype(out.dtype)
        copies.append(
            pltpu.make_async_copy(
                rounded.at[:, columns], out.at[:, columns], sems.at[len(copies)]
            )
        )
        copies[-1].start()
    for copy in copies:
        copy.wait()


def last_gradients(pair, total):
    return pl.pallas_call(
        last_gradients_kernel,
        out_shape=jax.ShapeDtypeStruct(total.shape, jnp.bfloat16),
        in_specs=[VMEM] * 3,
        out_specs=ANY,
        scratch_shapes=[
            pltpu.VMEM(total.shape, jnp.bfloat16),
            pltpu.SemaphoreType.DMA((total.shape[1] // 256,)),
        ],
        compiler_params=limit(16),
        name="last_gradients",
    )(kept(pair[0]), kept(pair[1]), kept(total))


def stamp_kernel(onward, back, for_onward, for_back, onward_out, back_out, rows, sems):
    start = onward.shape[0] - FACTS
    targets = (onward_out, back_out)
    for i, piece in enumerate((onward, back)):
        pltpu.make_async_copy(
            piece.at[start : start + 16, :], rows.at[i], sems.at[i]
        ).start()
    for i, values in enumerate((for_onward, for_back)):
        pltpu.make_async_copy(
            onward.at[start : start + 16, :], rows.at[i], sems.at[i]
        ).wait()
        value = values[:KPB]
        high = value.astype(jnp.bfloat16).astype(jnp.float32)
        low = value - high
        facts = rows[i].astype(jnp.float32)[2 * KPB :]
        rows[i] = jnp.concatenate([high, low, facts], axis=0).astype(jnp.bfloat16)
        pltpu.make_async_copy(
            rows.at[i], targets[i].at[start : start + 16, :], sems.at[2 + i]
        ).start()
    for i in range(2):
        pltpu.make_async_copy(
            rows.at[i], targets[i].at[start : start + 16, :], sems.at[2 + i]
        ).wait()


def stamp(pieces, values):
    return pl.pallas_call(
        stamp_kernel,
        out_shape=tuple(pltpu.VMEM(piece.shape, piece.dtype) for piece in pieces),
        in_specs=[ANY, ANY, VMEM, VMEM],
        out_specs=(ANY, ANY),
        scratch_shapes=[
            pltpu.VMEM((2, 16, 128), jnp.bfloat16),
            pltpu.SemaphoreType.DMA((4,)),
        ],
        input_output_aliases={0: 0, 1: 1},
        compiler_params=limit(4),
        name="stamp",
    )(*[kept(piece) for piece in pieces], *[kept(value) for value in values])


def unpack_kernel(owners, slots, own, onward, back, second, third, opposite, out):
    owner = slots[...] // BLK_DEV
    start = onward.shape[0] - FACTS
    way = 1 - 2 * lax.axis_index("width")
    returned = [(0, own[...])]
    for distance, piece in ((-1, onward), (1, back)):
        rows = piece[start : start + 16, :].astype(jnp.float32)
        returned.append((distance, rows[:KPB] + rows[KPB : 2 * KPB]))
    returned += [(2 * way, second[...]), (3 * way, third[...]), (4, opposite[...])]
    mine = [owner == peer_at(distance, owners) for distance, _ in returned]
    for k in range(KPB):
        total = jnp.zeros(owner.shape, jnp.float32)
        for here, (_, values) in zip(mine, returned):
            total = jnp.where(here, values[k : k + 1, :], total)
        out[pl.ds(k, ACT, stride=KPB), :] = total


def unpack(slots, *returned):
    tok_rows = slots.shape[1]
    return pl.pallas_call(
        functools.partial(unpack_kernel, lax.axis_size("dp")),
        out_shape=pltpu.VMEM((ACT * KPB, tok_rows), jnp.float32),
        in_specs=[VMEM] * (1 + len(returned)),
        out_specs=VMEM,
        compiler_params=limit(4),
        name="unpack",
    )(kept(slots), *[kept(x) for x in returned])


def every_owner(decoder, grad_out, active_blocks, feature_idx, acts, block_slot):
    tok_rows = grad_out.shape[0]
    owners = lax.axis_size("dp")
    ring = ring_of(owners)

    def shift(x, by):
        pairs = [(ring[i], ring[(i + by) % owners]) for i in range(owners)]
        return lax.ppermute(x, "dp", pairs)

    def hop(pieces):
        left, right = pieces
        return shift(left, 1), shift(right, -1)

    def crossed(pieces):
        right, left = pieces
        return shift(right, 1), shift(left, -1)

    def other_core(x):
        return lax.ppermute(x, "width", ((0, 1), (1, 0)))

    def return_by(distance, x):
        pairs = []
        for i in range(owners):
            pairs.append((2 * ring[i], 2 * ring[(i - distance) % owners]))
            pairs.append((2 * ring[i] + 1, 2 * ring[(i + distance) % owners] + 1))
        return lax.ppermute(x, ("dp", "width"), pairs)

    first_left, first_right, left, right, own_facts, slots = prepare(
        block_slot, active_blocks, feature_idx, acts, grad_out, owners
    )
    first_1 = hop((first_left, first_right))
    second_1 = crossed((right, left))
    decoder = fetch(decoder)
    first_1, decoder = lax.optimization_barrier((first_1, decoder))
    first_2 = hop(first_1)
    second_2 = crossed(second_1)
    pairs = [(first_left, first_right), (first_1[0], second_1[0]), (second_1[1], first_1[1])]
    distances = (0, -1, 1)
    own, onward, back = scores_of(distances, pairs, decoder, own_facts)
    total = gradients_of(distances, pairs, own_facts, decoder.shape)
    first_3 = hop(first_2)
    second_2 = stamp(second_2, (back, onward))
    second_3 = crossed(second_2)
    pairs = [(first_2[0], second_2[0]), (second_2[1], first_2[1])]
    mine, others = scores_of((-2, 2), pairs, decoder, own_facts, True)
    total = gradients_of((-2, 2), pairs, own_facts, decoder.shape, total)
    second = mine + other_core(others)
    total, first_3, second = lax.optimization_barrier((total, first_3, second))
    second = return_by(2, jnp.concatenate([second, jnp.zeros((24, 128), jnp.float32)]))[:8]
    first_4 = hop(first_3)
    pairs = [(first_3[0], second_3[0]), (second_3[1], first_3[1])]
    mine, others = scores_of((-3, 3), pairs, decoder, own_facts, True)
    total = gradients_of((-3, 3), pairs, own_facts, decoder.shape, total)
    third = mine + other_core(others)
    total, third = lax.optimization_barrier((total, third))
    third = return_by(3, third)
    total, first_4 = lax.optimization_barrier((total, first_4))
    (opposite,) = scores_of((4,), [first_4], decoder, own_facts)
    opposite = shift(opposite, -owners // 2)
    total, third = lax.optimization_barrier((total, third))
    decoder_grad = last_gradients(first_4, total)
    decoder_grad, opposite = lax.optimization_barrier((decoder_grad, opposite))
    act_grad = unpack(slots, own, *second_3, second, third, opposite)
    act_grad = act_grad + other_core(act_grad)
    return (decoder_grad, act_grad.T)


def send_back(picked):
    return lax.all_to_all(picked, "dp", split_axis=1, concat_axis=1, tiled=True)


def pack_slots(grad_out, target, slots_all, pair_coeffs, pair_columns, source_row):
    slot_row = jnp.zeros((slots_all,), jnp.int32).at[target].set(source_row)
    used = jnp.zeros((slots_all,), jnp.bool_).at[target].set(True)
    send_rows = jnp.where(used[:, None], grad_out[slot_row], jnp.zeros((), grad_out.dtype))
    send_acts = jnp.zeros((slots_all, KPB), pair_coeffs.dtype).at[target].set(pair_coeffs)
    send_cols = jnp.zeros((slots_all, KPB), jnp.int32).at[target].set(pair_columns)
    return (send_rows, send_acts, send_cols)


def some_owners(decoder, grad_out, active_blocks, feature_idx, acts, block_slot):
    tok_rows, half_width = grad_out.shape
    owners = lax.axis_size("dp")
    mean_load = tok_rows * ACT // owners
    owner_cap = mean_load + min(mean_load // 2, tok_rows - mean_load)
    block_cap = (owner_cap + 2) // 3
    block_ids = active_blocks.reshape(-1)
    pair_count = block_ids.shape[0]
    table_pos = jnp.arange(block_slot.shape[0], dtype=jnp.int32)
    slot_of = jnp.sum(
        jnp.where(block_ids[:, None] == table_pos[None, :], block_slot[None, :], 0), axis=1
    )
    pair_pos = jnp.arange(pair_count, dtype=jnp.int32)
    source_row = pair_pos // ACT
    pair_coeffs = acts.reshape(pair_count, KPB)
    pair_feats = feature_idx.reshape(pair_count, KPB)
    earlier = (block_ids[:, None] == block_ids[None, :]) & (pair_pos[None, :] < pair_pos[:, None])
    position = jnp.sum(earlier.astype(jnp.int32), axis=1)
    slot_cols = owners * block_cap
    target = slot_of % BLK_DEV * slot_cols + slot_of // BLK_DEV * block_cap + position
    slots_all = BLK_DEV * slot_cols
    send_rows, send_acts, send_cols = pack_slots(
        grad_out, target, slots_all, pair_coeffs, pair_feats, source_row
    )
    rows, coeffs, feature_pos = (
        lax.all_to_all(
            send_rows.reshape(BLK_DEV, slot_cols, half_width),
            "dp",
            split_axis=1,
            concat_axis=1,
            tiled=True,
        ),
        lax.all_to_all(
            send_acts.reshape(BLK_DEV, slot_cols, KPB),
            "dp",
            split_axis=1,
            concat_axis=1,
            tiled=True,
        ),
        lax.all_to_all(
            send_cols.reshape(BLK_DEV, slot_cols, KPB),
            "dp",
            split_axis=1,
            concat_axis=1,
            tiled=True,
        ),
    )
    weights = decoder.reshape(BLK_DEV, BW, half_width)
    scores = jnp.einsum("bnd,bfd->bnf", rows, weights, preferred_element_type=jnp.float32)
    picked = jnp.take_along_axis(scores, feature_pos, axis=2)
    returned = send_back(picked)
    feature_axis = jnp.arange(BW, dtype=jnp.int32)
    matches = feature_pos[..., None] == feature_axis
    dense = jnp.sum(jnp.where(matches, coeffs[..., None].astype(jnp.float32), 0.0), axis=2).astype(
        jnp.bfloat16
    )
    grads = jnp.einsum("bnf,bnd->bfd", dense, rows, preferred_element_type=jnp.float32)
    decoder_grad = grads.astype(jnp.bfloat16).reshape(BLK_DEV * BW, half_width)
    pair_vals = returned.reshape(slots_all, KPB)[target]
    act_grad = pair_vals.reshape(tok_rows, ACT * KPB)
    act_grad = lax.psum(act_grad, "width")
    return (decoder_grad, act_grad)


def per_device(*args):
    if lax.axis_size("dp") == ACT:
        return every_owner(*args)
    return some_owners(*args)


def solution(mesh):
    in_specs = (
        P(("groups", "dp"), "width"),
        P(("groups", "dp"), "width"),
        P(("groups", "dp"), None),
        P(("groups", "dp"), None),
        P(("groups", "dp"), None),
        P("groups"),
    )
    out_specs = (P(("groups", "dp"), "width"), P(("groups", "dp"), None))
    return jax.shard_map(
        per_device, mesh=mesh, in_specs=in_specs, out_specs=out_specs, check_vma=False
    )
```

```python
import functools

import jax
import jax.numpy as jnp
from jax import lax
from jax.experimental import pallas as pl
from jax.experimental.pallas import tpu as pltpu
from jax.sharding import PartitionSpec as P

BW = 128
BLK_DEV = 4
ACT = 8
KPB = 4
SMEM = pl.BlockSpec(memory_space=pltpu.SMEM)
VMEM = pl.BlockSpec(memory_space=pltpu.VMEM)
ANY = pl.BlockSpec(memory_space=pl.ANY)
HBM = pl.BlockSpec(memory_space=pltpu.HBM)


def limit(mebibytes):
    return pltpu.CompilerParams(vmem_limit_bytes=mebibytes * 2**20)


def kept(x):
    return pltpu.with_memory_space_constraint(x, pltpu.VMEM)


def far(x):
    return pltpu.with_memory_space_constraint(x, pltpu.HBM)


def ring_of(owners):
    return list(range(0, owners, 2)) + list(range(owners - 1, 0, -2))


def peer_at(distance, owners):
    me = lax.axis_index("dp")
    half_ring = owners // 2
    place = jnp.where(lax.rem(me, 2) == 0, lax.div(me, 2), owners - 1 - lax.div(me, 2))
    at = lax.rem(place + owners + distance, owners)
    return jnp.where(at < half_ring, 2 * at, 2 * (owners - 1 - at) + 1)


ROW_SHIFT = BLK_DEV * BW // 2
FACTS = 2 * 2 * KPB


def facts_for(owner_id, owner, first_row, feats, acts):
    mine = owner == owner_id
    rows = [
        jnp.sum(jnp.where(mine, first_row + feats[k], 0.0), axis=0, keepdims=True) - ROW_SHIFT
        for k in range(KPB)
    ]
    values = [
        jnp.sum(jnp.where(mine, acts[k], 0.0), axis=0, keepdims=True) for k in range(KPB)
    ]
    return jnp.concatenate(rows + values, axis=0)


def prepare_kernel(owners, first, *refs):
    sources, refs = refs[:5], refs[5:]
    outs, refs = refs[: 2 if first else 4], refs[2 if first else 4 :]
    block_slot, active, feats, acts, halves, wide_feats, wide_acts, sems = refs
    cut = halves.shape[2]
    copies = []
    for source, target in zip(sources[:4], (block_slot, active, feats, acts)):
        copies.append(pltpu.make_async_copy(source, target, sems.at[len(copies)]))
    for side in range(2):
        copies.append(
            pltpu.make_async_copy(
                sources[4].at[:, side * cut : (side + 1) * cut],
                halves.at[side],
                sems.at[len(copies)],
            )
        )
    for copy in copies:
        copy.start()
    for copy in copies[:4]:
        copy.wait()
    named = active[...]
    slot = jnp.zeros_like(named)
    for block in range(block_slot.shape[0]):
        slot = jnp.where(named == block, block_slot[block], slot)
    wide_feats[...] = feats[...].astype(jnp.float32)
    wide_acts[...] = acts[...].astype(jnp.float32)
    features = [wide_feats[pl.ds(k, ACT, stride=KPB), :] for k in range(KPB)]
    values = [wide_acts[pl.ds(k, ACT, stride=KPB), :] for k in range(KPB)]
    first_row = (slot % BLK_DEV * BW).astype(jnp.float32)

    def facts(distance):
        return facts_for(
            peer_at(distance, owners), slot // BLK_DEV, first_row, features, values
        )

    if not first:
        outs[2][...] = facts(0)
        outs[3][...] = slot
    tok_rows = halves.shape[1]
    for side, sign in ((0, 1), (1, -1)):
        ahead = [facts(sign * d) for d in (3, 4)] if first else [facts(-sign * d) for d in (1, 2)]
        rows = jnp.concatenate(ahead, axis=0).astype(jnp.bfloat16)
        outs[side][outs[side].shape[0] - FACTS :, :] = rows
    for side in range(2):
        copies[4 + side].wait()
        for j in range(cut // 128):
            part = halves[side, :, j * 128 : (j + 1) * 128]
            outs[side][j * tok_rows : (j + 1) * tok_rows, :] = part


def prepare(first, block_slot, active_blocks, feature_idx, acts, grad_out, owners):
    tok_rows, width = grad_out.shape
    piece = pltpu.VMEM((width // 256 * tok_rows + FACTS, 128), grad_out.dtype)
    facts = pltpu.VMEM((2 * KPB, tok_rows), jnp.float32)
    slots = pltpu.VMEM((ACT, tok_rows), jnp.int32)
    out_shape = (piece, piece) if first else (piece, piece, facts, slots)
    return pl.pallas_call(
        functools.partial(prepare_kernel, owners, first),
        out_shape=out_shape,
        in_specs=[HBM] * 5,
        out_specs=(VMEM,) * len(out_shape),
        scratch_shapes=[
            pltpu.SMEM(block_slot.shape, jnp.int32),
            pltpu.VMEM((ACT, tok_rows), jnp.int32),
            pltpu.VMEM((ACT * KPB, tok_rows), jnp.int32),
            pltpu.VMEM((ACT * KPB, tok_rows), acts.dtype),
            pltpu.VMEM((2, tok_rows, width // 2), grad_out.dtype),
            pltpu.VMEM((ACT * KPB, tok_rows), jnp.float32),
            pltpu.VMEM((ACT * KPB, tok_rows), jnp.float32),
            pltpu.SemaphoreType.DMA((6,)),
        ],
        compiler_params=limit(8),
        name="prepare",
    )(far(block_slot), far(active_blocks.T), far(feature_idx.T), far(acts.T), far(grad_out))


def fetch_kernel(source, target, sem):
    copy = pltpu.make_async_copy(source, target, sem)
    copy.start()
    copy.wait()


def fetch(x):
    return pl.pallas_call(
        fetch_kernel,
        out_shape=pltpu.VMEM(x.shape, x.dtype),
        in_specs=[HBM],
        out_specs=VMEM,
        scratch_shapes=[pltpu.SemaphoreType.DMA],
        compiler_params=limit(8),
        name="fetch",
    )(far(x))


def block_and_rows(here):
    at_row = here[:KPB].astype(jnp.int32) + ROW_SHIFT
    return at_row[:1] // BW, at_row % BW


def row_axis_of(tok_rows):
    return lax.broadcasted_iota(jnp.int32, (BW, tok_rows), 0)


def coefficients(here):
    block, feats = block_and_rows(here)
    row_axis = row_axis_of(here.shape[1])
    dense = jnp.zeros(row_axis.shape, jnp.float32)
    for k in range(KPB):
        dense = jnp.where(row_axis == feats[k : k + 1], here[KPB + k : KPB + k + 1], dense)
    parts = [jnp.where(block == b, dense, 0.0) for b in range(BLK_DEV)]
    return jnp.concatenate(parts, axis=0).astype(jnp.bfloat16)


def pick(scores, here):
    block, feats = block_and_rows(here)
    row_axis = row_axis_of(here.shape[1])
    mine = scores[:BW]
    for b in range(1, BLK_DEV):
        mine = jnp.where(block == b, scores[b * BW : (b + 1) * BW], mine)
    return [
        jnp.sum(jnp.where(row_axis == feats[k : k + 1], mine, 0.0), axis=0, keepdims=True)
        for k in range(KPB)
    ]


def facts_in(left, right, distance):
    near = abs(distance) <= 2
    piece = (right if near else left) if distance in (-1, -2, -3, 4) else (left if near else right)
    facts = piece[piece.shape[0] - FACTS :, :].astype(jnp.float32)
    slot = (abs(distance) - 1) % 2
    return facts[slot * 2 * KPB : (slot + 1) * 2 * KPB]


def columns_of(pieces, tok_rows, parts):
    rows = [
        jnp.concatenate([piece[j * tok_rows : (j + 1) * tok_rows, :] for j in parts], axis=1)
        for piece in pieces
    ]
    return jnp.concatenate(rows, axis=0) if len(rows) > 1 else rows[0]


def picks_of(facts, decoder, pieces):
    picks = []
    tok_rows = facts[0].shape[1]
    cut = decoder.shape[1] // 2
    for first in range(0, len(facts), 2):
        count = min(2, len(facts) - first)
        scores = None
        for side in range(2):
            part = lax.dot_general(
                decoder[:, side * cut : (side + 1) * cut],
                columns_of(
                    pieces[2 * first + side : 2 * (first + count) : 2],
                    tok_rows,
                    range(cut // 128),
                ),
                (((1,), (1,)), ((), ())),
                preferred_element_type=jnp.float32,
            )
            scores = part if scores is None else scores + part
        for i in range(first, first + count):
            here = scores[:, (i - first) * tok_rows : (i - first + 1) * tok_rows]
            picks.append(jnp.concatenate(pick(here, facts[i]) * 2, axis=0))
    return picks


def gradient_blocks(facts, pieces, width):
    tok_rows = facts[0].shape[1]
    cut = width // 2
    dense = jnp.concatenate([coefficients(here) for here in facts], axis=1)
    for side in range(2):
        for j in range(0, cut // 128, 2):
            rows = columns_of(pieces[side::2], tok_rows, (j, j + 1))
            part = jnp.dot(dense, rows, preferred_element_type=jnp.float32)
            yield slice(side * cut + j * 128, side * cut + (j + 2) * 128), part


def facts_of(distances, own_facts, pieces):
    return [
        own_facts[...] if d == 0 else facts_in(pieces[2 * i], pieces[2 * i + 1], d)
        for i, d in enumerate(distances)
    ]


def scores_kernel(distances, split, decoder, own_facts, *refs):
    pieces, picked = refs[: 2 * len(distances)], refs[2 * len(distances) :]
    picks = picks_of(facts_of(distances, own_facts, pieces), decoder, pieces)
    if split:
        first = lax.axis_index("width") == 0
        picks = [jnp.where(first, *picks), jnp.where(first, *picks[::-1])]
    for target, values in zip(picked, picks):
        target[...] = values


def scores_of(distances, pairs, decoder, own_facts, split=False):
    pieces = [kept(piece) for pair in pairs for piece in pair]
    shape = pltpu.VMEM(own_facts.shape, jnp.float32)
    return pl.pallas_call(
        functools.partial(scores_kernel, distances, split),
        out_shape=(shape,) * len(distances),
        in_specs=[VMEM] * (2 + len(pieces)),
        out_specs=(VMEM,) * len(distances),
        compiler_params=limit(12),
        name="scores",
    )(kept(decoder), kept(own_facts), *pieces)


def gradients_kernel(distances, own_facts, *refs):
    pieces, refs = refs[: 2 * len(distances)], refs[2 * len(distances) :]
    total = refs[-1]
    facts = facts_of(distances, own_facts, pieces)
    for columns, part in gradient_blocks(facts, pieces, total.shape[1]):
        total[:, columns] = part if len(refs) == 1 else refs[0][:, columns] + part


def gradients_of(distances, pairs, own_facts, shape, total=None):
    operands = [kept(own_facts)] + [kept(piece) for pair in pairs for piece in pair]
    operands += [] if total is None else [kept(total)]
    return pl.pallas_call(
        functools.partial(gradients_kernel, distances),
        out_shape=pltpu.VMEM(shape, jnp.float32),
        in_specs=[VMEM] * len(operands),
        out_specs=VMEM,
        input_output_aliases={} if total is None else {len(operands) - 1: 0},
        compiler_params=limit(16),
        name="gradients",
    )(*operands)


def last_gradients_kernel(left, right, total, out, rounded, sems):
    copies = []
    facts = [facts_in(left, right, 4)]
    for columns, part in gradient_blocks(facts, (left, right), out.shape[1]):
        rounded[:, columns] = (total[:, columns] + part).astype(out.dtype)
        copies.append(
            pltpu.make_async_copy(
                rounded.at[:, columns], out.at[:, columns], sems.at[len(copies)]
            )
        )
        copies[-1].start()
    for copy in copies:
        copy.wait()


def last_gradients(pair, total):
    return pl.pallas_call(
        last_gradients_kernel,
        out_shape=jax.ShapeDtypeStruct(total.shape, jnp.bfloat16),
        in_specs=[VMEM] * 3,
        out_specs=ANY,
        scratch_shapes=[
            pltpu.VMEM(total.shape, jnp.bfloat16),
            pltpu.SemaphoreType.DMA((total.shape[1] // 256,)),
        ],
        compiler_params=limit(16),
        name="last_gradients",
    )(kept(pair[0]), kept(pair[1]), kept(total))


def stamp_kernel(onward, back, for_onward, for_back, onward_out, back_out, rows, sems):
    start = onward.shape[0] - FACTS
    targets = (onward_out, back_out)
    for i, piece in enumerate((onward, back)):
        pltpu.make_async_copy(
            piece.at[start : start + 16, :], rows.at[i], sems.at[i]
        ).start()
    for i, values in enumerate((for_onward, for_back)):
        pltpu.make_async_copy(
            onward.at[start : start + 16, :], rows.at[i], sems.at[i]
        ).wait()
        value = values[:KPB]
        high = value.astype(jnp.bfloat16).astype(jnp.float32)
        low = value - high
        facts = rows[i].astype(jnp.float32)[2 * KPB :]
        rows[i] = jnp.concatenate([high, low, facts], axis=0).astype(jnp.bfloat16)
        pltpu.make_async_copy(
            rows.at[i], targets[i].at[start : start + 16, :], sems.at[2 + i]
        ).start()
    for i in range(2):
        pltpu.make_async_copy(
            rows.at[i], targets[i].at[start : start + 16, :], sems.at[2 + i]
        ).wait()


def stamp(pieces, values):
    return pl.pallas_call(
        stamp_kernel,
        out_shape=tuple(pltpu.VMEM(piece.shape, piece.dtype) for piece in pieces),
        in_specs=[ANY, ANY, VMEM, VMEM],
        out_specs=(ANY, ANY),
        scratch_shapes=[
            pltpu.VMEM((2, 16, 128), jnp.bfloat16),
            pltpu.SemaphoreType.DMA((4,)),
        ],
        input_output_aliases={0: 0, 1: 1},
        compiler_params=limit(4),
        name="stamp",
    )(*[kept(piece) for piece in pieces], *[kept(value) for value in values])


def unpack_kernel(owners, slots, own, onward, back, second, third, opposite, out):
    owner = slots[...] // BLK_DEV
    start = onward.shape[0] - FACTS
    way = 1 - 2 * lax.axis_index("width")
    returned = [(0, own[...])]
    for distance, piece in ((-1, onward), (1, back)):
        rows = piece[start : start + 16, :].astype(jnp.float32)
        returned.append((distance, rows[:KPB] + rows[KPB : 2 * KPB]))
    returned += [(2 * way, second[...]), (3 * way, third[...]), (4, opposite[...])]
    mine = [owner == peer_at(distance, owners) for distance, _ in returned]
    for k in range(KPB):
        total = jnp.zeros(owner.shape, jnp.float32)
        for here, (_, values) in zip(mine, returned):
            total = jnp.where(here, values[k : k + 1, :], total)
        out[pl.ds(k, ACT, stride=KPB), :] = total


def unpack(slots, *returned):
    tok_rows = slots.shape[1]
    return pl.pallas_call(
        functools.partial(unpack_kernel, lax.axis_size("dp")),
        out_shape=pltpu.VMEM((ACT * KPB, tok_rows), jnp.float32),
        in_specs=[VMEM] * (1 + len(returned)),
        out_specs=VMEM,
        compiler_params=limit(4),
        name="unpack",
    )(kept(slots), *[kept(x) for x in returned])


def every_owner(decoder, grad_out, active_blocks, feature_idx, acts, block_slot):
    tok_rows = grad_out.shape[0]
    owners = lax.axis_size("dp")
    ring = ring_of(owners)

    def shift(x, by):
        pairs = [(ring[i], ring[(i + by) % owners]) for i in range(owners)]
        return lax.ppermute(x, "dp", pairs)

    def hop(pieces):
        left, right = pieces
        return shift(left, 1), shift(right, -1)

    def crossed(pieces):
        right, left = pieces
        return shift(right, 1), shift(left, -1)

    def other_core(x):
        return lax.ppermute(x, "width", ((0, 1), (1, 0)))

    def return_by(distance, x):
        pairs = []
        for i in range(owners):
            pairs.append((2 * ring[i], 2 * ring[(i - distance) % owners]))
            pairs.append((2 * ring[i] + 1, 2 * ring[(i + distance) % owners] + 1))
        return lax.ppermute(x, ("dp", "width"), pairs)

    tokens = (block_slot, active_blocks, feature_idx, acts, grad_out, owners)
    first_left, first_right = prepare(True, *tokens)
    first_1 = hop((first_left, first_right))
    left, right, own_facts, slots = prepare(False, *tokens)
    second_1 = crossed((right, left))
    decoder = fetch(decoder)
    first_1, decoder = lax.optimization_barrier((first_1, decoder))
    first_2 = hop(first_1)
    second_2 = crossed(second_1)
    pairs = [(first_left, first_right), (first_1[0], second_1[0]), (second_1[1], first_1[1])]
    distances = (0, -1, 1)
    own, onward, back = scores_of(distances, pairs, decoder, own_facts)
    total = gradients_of(distances, pairs, own_facts, decoder.shape)
    first_3 = hop(first_2)
    second_2 = stamp(second_2, (back, onward))
    second_3 = crossed(second_2)
    pairs = [(first_2[0], second_2[0]), (second_2[1], first_2[1])]
    mine, others = scores_of((-2, 2), pairs, decoder, own_facts, True)
    total = gradients_of((-2, 2), pairs, own_facts, decoder.shape, total)
    second = mine + other_core(others)
    total, first_3, second = lax.optimization_barrier((total, first_3, second))
    second = return_by(2, jnp.concatenate([second, jnp.zeros((24, 128), jnp.float32)]))[:8]
    first_4 = hop(first_3)
    pairs = [(first_3[0], second_3[0]), (second_3[1], first_3[1])]
    mine, others = scores_of((-3, 3), pairs, decoder, own_facts, True)
    total = gradients_of((-3, 3), pairs, own_facts, decoder.shape, total)
    third = mine + other_core(others)
    total, third = lax.optimization_barrier((total, third))
    third = return_by(3, third)
    total, first_4 = lax.optimization_barrier((total, first_4))
    (opposite,) = scores_of((4,), [first_4], decoder, own_facts)
    opposite = shift(opposite, -owners // 2)
    total, third = lax.optimization_barrier((total, third))
    decoder_grad = last_gradients(first_4, total)
    decoder_grad, opposite = lax.optimization_barrier((decoder_grad, opposite))
    act_grad = unpack(slots, own, *second_3, second, third, opposite)
    act_grad = act_grad + other_core(act_grad)
    return (decoder_grad, act_grad.T)


def send_back(picked):
    return lax.all_to_all(picked, "dp", split_axis=1, concat_axis=1, tiled=True)


def pack_slots(grad_out, target, slots_all, pair_coeffs, pair_columns, source_row):
    slot_row = jnp.zeros((slots_all,), jnp.int32).at[target].set(source_row)
    used = jnp.zeros((slots_all,), jnp.bool_).at[target].set(True)
    send_rows = jnp.where(used[:, None], grad_out[slot_row], jnp.zeros((), grad_out.dtype))
    send_acts = jnp.zeros((slots_all, KPB), pair_coeffs.dtype).at[target].set(pair_coeffs)
    send_cols = jnp.zeros((slots_all, KPB), jnp.int32).at[target].set(pair_columns)
    return (send_rows, send_acts, send_cols)


def some_owners(decoder, grad_out, active_blocks, feature_idx, acts, block_slot):
    tok_rows, half_width = grad_out.shape
    owners = lax.axis_size("dp")
    mean_load = tok_rows * ACT // owners
    owner_cap = mean_load + min(mean_load // 2, tok_rows - mean_load)
    block_cap = (owner_cap + 2) // 3
    block_ids = active_blocks.reshape(-1)
    pair_count = block_ids.shape[0]
    table_pos = jnp.arange(block_slot.shape[0], dtype=jnp.int32)
    slot_of = jnp.sum(
        jnp.where(block_ids[:, None] == table_pos[None, :], block_slot[None, :], 0), axis=1
    )
    pair_pos = jnp.arange(pair_count, dtype=jnp.int32)
    source_row = pair_pos // ACT
    pair_coeffs = acts.reshape(pair_count, KPB)
    pair_feats = feature_idx.reshape(pair_count, KPB)
    earlier = (block_ids[:, None] == block_ids[None, :]) & (pair_pos[None, :] < pair_pos[:, None])
    position = jnp.sum(earlier.astype(jnp.int32), axis=1)
    slot_cols = owners * block_cap
    target = slot_of % BLK_DEV * slot_cols + slot_of // BLK_DEV * block_cap + position
    slots_all = BLK_DEV * slot_cols
    send_rows, send_acts, send_cols = pack_slots(
        grad_out, target, slots_all, pair_coeffs, pair_feats, source_row
    )
    rows, coeffs, feature_pos = (
        lax.all_to_all(
            send_rows.reshape(BLK_DEV, slot_cols, half_width),
            "dp",
            split_axis=1,
            concat_axis=1,
            tiled=True,
        ),
        lax.all_to_all(
            send_acts.reshape(BLK_DEV, slot_cols, KPB),
            "dp",
            split_axis=1,
            concat_axis=1,
            tiled=True,
        ),
        lax.all_to_all(
            send_cols.reshape(BLK_DEV, slot_cols, KPB),
            "dp",
            split_axis=1,
            concat_axis=1,
            tiled=True,
        ),
    )
    weights = decoder.reshape(BLK_DEV, BW, half_width)
    scores = jnp.einsum("bnd,bfd->bnf", rows, weights, preferred_element_type=jnp.float32)
    picked = jnp.take_along_axis(scores, feature_pos, axis=2)
    returned = send_back(picked)
    feature_axis = jnp.arange(BW, dtype=jnp.int32)
    matches = feature_pos[..., None] == feature_axis
    dense = jnp.sum(jnp.where(matches, coeffs[..., None].astype(jnp.float32), 0.0), axis=2).astype(
        jnp.bfloat16
    )
    grads = jnp.einsum("bnf,bnd->bfd", dense, rows, preferred_element_type=jnp.float32)
    decoder_grad = grads.astype(jnp.bfloat16).reshape(BLK_DEV * BW, half_width)
    pair_vals = returned.reshape(slots_all, KPB)[target]
    act_grad = pair_vals.reshape(tok_rows, ACT * KPB)
    act_grad = lax.psum(act_grad, "width")
    return (decoder_grad, act_grad)


def per_device(*args):
    if lax.axis_size("dp") == ACT:
        return every_owner(*args)
    return some_owners(*args)


def solution(mesh):
    in_specs = (
        P(("groups", "dp"), "width"),
        P(("groups", "dp"), "width"),
        P(("groups", "dp"), None),
        P(("groups", "dp"), None),
        P(("groups", "dp"), None),
        P("groups"),
    )
    out_specs = (P(("groups", "dp"), "width"), P(("groups", "dp"), None))
    return jax.shard_map(
        per_device, mesh=mesh, in_specs=in_specs, out_specs=out_specs, check_vma=False
    )
```

```python
import functools

import jax
import jax.numpy as jnp
from jax import lax
from jax.experimental import pallas as pl
from jax.experimental.pallas import tpu as pltpu
from jax.sharding import PartitionSpec as P

BW = 128
BLK_DEV = 4
ACT = 8
KPB = 4
SMEM = pl.BlockSpec(memory_space=pltpu.SMEM)
VMEM = pl.BlockSpec(memory_space=pltpu.VMEM)
ANY = pl.BlockSpec(memory_space=pl.ANY)
HBM = pl.BlockSpec(memory_space=pltpu.HBM)


def limit(mebibytes):
    return pltpu.CompilerParams(vmem_limit_bytes=mebibytes * 2**20)


def kept(x):
    return pltpu.with_memory_space_constraint(x, pltpu.VMEM)


def far(x):
    return pltpu.with_memory_space_constraint(x, pltpu.HBM)


def ring_of(owners):
    return list(range(0, owners, 2)) + list(range(owners - 1, 0, -2))


def peer_at(distance, owners):
    me = lax.axis_index("dp")
    half_ring = owners // 2
    place = jnp.where(lax.rem(me, 2) == 0, lax.div(me, 2), owners - 1 - lax.div(me, 2))
    at = lax.rem(place + owners + distance, owners)
    return jnp.where(at < half_ring, 2 * at, 2 * (owners - 1 - at) + 1)


ROW_SHIFT = BLK_DEV * BW // 2
FACTS = 2 * 2 * KPB


def facts_for(owner_id, owner, first_row, feats, acts):
    mine = owner == owner_id
    rows = [
        jnp.sum(jnp.where(mine, first_row + feats[k], 0.0), axis=0, keepdims=True) - ROW_SHIFT
        for k in range(KPB)
    ]
    values = [
        jnp.sum(jnp.where(mine, acts[k], 0.0), axis=0, keepdims=True) for k in range(KPB)
    ]
    return jnp.concatenate(rows + values, axis=0)


def prepare_kernel(owners, *refs):
    sources, refs = refs[:5], refs[5:]
    outs, refs = refs[:6], refs[6:]
    block_slot, active, feats, acts, halves, wide_feats, wide_acts, sems = refs
    cut = halves.shape[2]
    copies = []
    for source, target in zip(sources[:4], (block_slot, active, feats, acts)):
        copies.append(pltpu.make_async_copy(source, target, sems.at[len(copies)]))
    for side in range(2):
        copies.append(
            pltpu.make_async_copy(
                sources[4].at[:, side * cut : (side + 1) * cut],
                halves.at[side],
                sems.at[len(copies)],
            )
        )
    for copy in copies:
        copy.start()
    for copy in copies[:4]:
        copy.wait()
    named = active[...]
    slot = jnp.zeros_like(named)
    for block in range(block_slot.shape[0]):
        slot = jnp.where(named == block, block_slot[block], slot)
    wide_feats[...] = feats[...].astype(jnp.float32)
    wide_acts[...] = acts[...].astype(jnp.float32)
    features = [wide_feats[pl.ds(k, ACT, stride=KPB), :] for k in range(KPB)]
    values = [wide_acts[pl.ds(k, ACT, stride=KPB), :] for k in range(KPB)]
    first_row = (slot % BLK_DEV * BW).astype(jnp.float32)

    def facts(distance):
        return facts_for(
            peer_at(distance, owners), slot // BLK_DEV, first_row, features, values
        )

    outs[4][...] = facts(0)
    outs[5][...] = slot
    for piece, sign, distances in (
        (outs[0], 1, (3, 4)), (outs[1], -1, (3, 4)), (outs[2], -1, (1, 2)), (outs[3], 1, (1, 2))
    ):
        rows = jnp.concatenate([facts(sign * d) for d in distances], axis=0)
        piece[piece.shape[0] - FACTS :, :] = rows.astype(jnp.bfloat16)
    tok_rows = halves.shape[1]
    for side in range(2):
        copies[4 + side].wait()
        for j in range(cut // 128):
            part = halves[side, :, j * 128 : (j + 1) * 128]
            for piece in (outs[side], outs[2 + side]):
                piece[j * tok_rows : (j + 1) * tok_rows, :] = part


def prepare(block_slot, active_blocks, feature_idx, acts, grad_out, owners):
    tok_rows, width = grad_out.shape
    piece = pltpu.VMEM((width // 256 * tok_rows + FACTS, 128), grad_out.dtype)
    facts = pltpu.VMEM((2 * KPB, tok_rows), jnp.float32)
    slots = pltpu.VMEM((ACT, tok_rows), jnp.int32)
    out_shape = (piece,) * 4 + (facts, slots)
    return pl.pallas_call(
        functools.partial(prepare_kernel, owners),
        out_shape=out_shape,
        in_specs=[HBM] * 5,
        out_specs=(VMEM,) * len(out_shape),
        scratch_shapes=[
            pltpu.SMEM(block_slot.shape, jnp.int32),
            pltpu.VMEM((ACT, tok_rows), jnp.int32),
            pltpu.VMEM((ACT * KPB, tok_rows), jnp.int32),
            pltpu.VMEM((ACT * KPB, tok_rows), acts.dtype),
            pltpu.VMEM((2, tok_rows, width // 2), grad_out.dtype),
            pltpu.VMEM((ACT * KPB, tok_rows), jnp.float32),
            pltpu.VMEM((ACT * KPB, tok_rows), jnp.float32),
            pltpu.SemaphoreType.DMA((6,)),
        ],
        compiler_params=limit(8),
        name="prepare",
    )(far(block_slot), far(active_blocks.T), far(feature_idx.T), far(acts.T), far(grad_out))


def fetch_kernel(source, target, sem):
    copy = pltpu.make_async_copy(source, target, sem)
    copy.start()
    copy.wait()


def fetch(x):
    return pl.pallas_call(
        fetch_kernel,
        out_shape=pltpu.VMEM(x.shape, x.dtype),
        in_specs=[HBM],
        out_specs=VMEM,
        scratch_shapes=[pltpu.SemaphoreType.DMA],
        compiler_params=limit(8),
        name="fetch",
    )(far(x))


def block_and_rows(here):
    at_row = here[:KPB].astype(jnp.int32) + ROW_SHIFT
    return at_row[:1] // BW, at_row % BW


def row_axis_of(tok_rows):
    return lax.broadcasted_iota(jnp.int32, (BW, tok_rows), 0)


def coefficients(here):
    block, feats = block_and_rows(here)
    row_axis = row_axis_of(here.shape[1])
    dense = jnp.zeros(row_axis.shape, jnp.float32)
    for k in range(KPB):
        dense = jnp.where(row_axis == feats[k : k + 1], here[KPB + k : KPB + k + 1], dense)
    parts = [jnp.where(block == b, dense, 0.0) for b in range(BLK_DEV)]
    return jnp.concatenate(parts, axis=0).astype(jnp.bfloat16)


def pick(scores, here):
    block, feats = block_and_rows(here)
    row_axis = row_axis_of(here.shape[1])
    mine = scores[:BW]
    for b in range(1, BLK_DEV):
        mine = jnp.where(block == b, scores[b * BW : (b + 1) * BW], mine)
    return [
        jnp.sum(jnp.where(row_axis == feats[k : k + 1], mine, 0.0), axis=0, keepdims=True)
        for k in range(KPB)
    ]


def facts_in(left, right, distance):
    near = abs(distance) <= 2
    piece = (right if near else left) if distance in (-1, -2, -3, 4) else (left if near else right)
    facts = piece[piece.shape[0] - FACTS :, :].astype(jnp.float32)
    slot = (abs(distance) - 1) % 2
    return facts[slot * 2 * KPB : (slot + 1) * 2 * KPB]


def columns_of(pieces, tok_rows, parts):
    rows = [
        jnp.concatenate([piece[j * tok_rows : (j + 1) * tok_rows, :] for j in parts], axis=1)
        for piece in pieces
    ]
    return jnp.concatenate(rows, axis=0) if len(rows) > 1 else rows[0]


def picks_of(facts, decoder, pieces):
    picks = []
    tok_rows = facts[0].shape[1]
    cut = decoder.shape[1] // 2
    for first in range(0, len(facts), 2):
        count = min(2, len(facts) - first)
        scores = None
        for side in range(2):
            part = lax.dot_general(
                decoder[:, side * cut : (side + 1) * cut],
                columns_of(
                    pieces[2 * first + side : 2 * (first + count) : 2],
                    tok_rows,
                    range(cut // 128),
                ),
                (((1,), (1,)), ((), ())),
                preferred_element_type=jnp.float32,
            )
            scores = part if scores is None else scores + part
        for i in range(first, first + count):
            here = scores[:, (i - first) * tok_rows : (i - first + 1) * tok_rows]
            picks.append(jnp.concatenate(pick(here, facts[i]) * 2, axis=0))
    return picks


def gradient_blocks(facts, pieces, width):
    tok_rows = facts[0].shape[1]
    cut = width // 2
    dense = jnp.concatenate([coefficients(here) for here in facts], axis=1)
    for side in range(2):
        for j in range(0, cut // 128, 2):
            rows = columns_of(pieces[side::2], tok_rows, (j, j + 1))
            part = jnp.dot(dense, rows, preferred_element_type=jnp.float32)
            yield slice(side * cut + j * 128, side * cut + (j + 2) * 128), part


def facts_of(distances, own_facts, pieces):
    return [
        own_facts[...] if d == 0 else facts_in(pieces[2 * i], pieces[2 * i + 1], d)
        for i, d in enumerate(distances)
    ]


def scores_kernel(distances, split, decoder, own_facts, *refs):
    pieces, picked = refs[: 2 * len(distances)], refs[2 * len(distances) :]
    picks = picks_of(facts_of(distances, own_facts, pieces), decoder, pieces)
    if split:
        first = lax.axis_index("width") == 0
        picks = [jnp.where(first, *picks), jnp.where(first, *picks[::-1])]
    for target, values in zip(picked, picks):
        target[...] = values


def scores_of(distances, pairs, decoder, own_facts, split=False):
    pieces = [kept(piece) for pair in pairs for piece in pair]
    shape = pltpu.VMEM(own_facts.shape, jnp.float32)
    return pl.pallas_call(
        functools.partial(scores_kernel, distances, split),
        out_shape=(shape,) * len(distances),
        in_specs=[VMEM] * (2 + len(pieces)),
        out_specs=(VMEM,) * len(distances),
        compiler_params=limit(12),
        name="scores",
    )(kept(decoder), kept(own_facts), *pieces)


def gradients_kernel(distances, own_facts, *refs):
    pieces, refs = refs[: 2 * len(distances)], refs[2 * len(distances) :]
    total = refs[-1]
    facts = facts_of(distances, own_facts, pieces)
    for columns, part in gradient_blocks(facts, pieces, total.shape[1]):
        total[:, columns] = part if len(refs) == 1 else refs[0][:, columns] + part


def gradients_of(distances, pairs, own_facts, shape, total=None):
    operands = [kept(own_facts)] + [kept(piece) for pair in pairs for piece in pair]
    operands += [] if total is None else [kept(total)]
    return pl.pallas_call(
        functools.partial(gradients_kernel, distances),
        out_shape=pltpu.VMEM(shape, jnp.float32),
        in_specs=[VMEM] * len(operands),
        out_specs=VMEM,
        input_output_aliases={} if total is None else {len(operands) - 1: 0},
        compiler_params=limit(16),
        name="gradients",
    )(*operands)


def last_gradients_kernel(left, right, total, out, rounded, sems):
    copies = []
    facts = [facts_in(left, right, 4)]
    for columns, part in gradient_blocks(facts, (left, right), out.shape[1]):
        rounded[:, columns] = (total[:, columns] + part).astype(out.dtype)
        copies.append(
            pltpu.make_async_copy(
                rounded.at[:, columns], out.at[:, columns], sems.at[len(copies)]
            )
        )
        copies[-1].start()
    for copy in copies:
        copy.wait()


def last_gradients(pair, total):
    return pl.pallas_call(
        last_gradients_kernel,
        out_shape=jax.ShapeDtypeStruct(total.shape, jnp.bfloat16),
        in_specs=[VMEM] * 3,
        out_specs=ANY,
        scratch_shapes=[
            pltpu.VMEM(total.shape, jnp.bfloat16),
            pltpu.SemaphoreType.DMA((total.shape[1] // 256,)),
        ],
        compiler_params=limit(16),
        name="last_gradients",
    )(kept(pair[0]), kept(pair[1]), kept(total))


def stamp_kernel(onward, back, for_onward, for_back, onward_out, back_out, rows, sems):
    start = onward.shape[0] - FACTS
    targets = (onward_out, back_out)
    for i, piece in enumerate((onward, back)):
        pltpu.make_async_copy(
            piece.at[start : start + 16, :], rows.at[i], sems.at[i]
        ).start()
    for i, values in enumerate((for_onward, for_back)):
        pltpu.make_async_copy(
            onward.at[start : start + 16, :], rows.at[i], sems.at[i]
        ).wait()
        value = values[:KPB]
        high = value.astype(jnp.bfloat16).astype(jnp.float32)
        low = value - high
        facts = rows[i].astype(jnp.float32)[2 * KPB :]
        rows[i] = jnp.concatenate([high, low, facts], axis=0).astype(jnp.bfloat16)
        pltpu.make_async_copy(
            rows.at[i], targets[i].at[start : start + 16, :], sems.at[2 + i]
        ).start()
    for i in range(2):
        pltpu.make_async_copy(
            rows.at[i], targets[i].at[start : start + 16, :], sems.at[2 + i]
        ).wait()


def stamp(pieces, values):
    return pl.pallas_call(
        stamp_kernel,
        out_shape=tuple(pltpu.VMEM(piece.shape, piece.dtype) for piece in pieces),
        in_specs=[ANY, ANY, VMEM, VMEM],
        out_specs=(ANY, ANY),
        scratch_shapes=[
            pltpu.VMEM((2, 16, 128), jnp.bfloat16),
            pltpu.SemaphoreType.DMA((4,)),
        ],
        input_output_aliases={0: 0, 1: 1},
        compiler_params=limit(4),
        name="stamp",
    )(*[kept(piece) for piece in pieces], *[kept(value) for value in values])


def unpack_kernel(owners, slots, own, onward, back, second, third, opposite, out):
    owner = slots[...] // BLK_DEV
    start = onward.shape[0] - FACTS
    way = 1 - 2 * lax.axis_index("width")
    returned = [(0, own[...])]
    for distance, piece in ((-1, onward), (1, back)):
        rows = piece[start : start + 16, :].astype(jnp.float32)
        returned.append((distance, rows[:KPB] + rows[KPB : 2 * KPB]))
    returned += [(2 * way, second[...]), (3 * way, third[...]), (4, opposite[...])]
    mine = [owner == peer_at(distance, owners) for distance, _ in returned]
    for k in range(KPB):
        total = jnp.zeros(owner.shape, jnp.float32)
        for here, (_, values) in zip(mine, returned):
            total = jnp.where(here, values[k : k + 1, :], total)
        out[pl.ds(k, ACT, stride=KPB), :] = total


def unpack(slots, *returned):
    tok_rows = slots.shape[1]
    return pl.pallas_call(
        functools.partial(unpack_kernel, lax.axis_size("dp")),
        out_shape=pltpu.VMEM((ACT * KPB, tok_rows), jnp.float32),
        in_specs=[VMEM] * (1 + len(returned)),
        out_specs=VMEM,
        compiler_params=limit(4),
        name="unpack",
    )(kept(slots), *[kept(x) for x in returned])


def every_owner(decoder, grad_out, active_blocks, feature_idx, acts, block_slot):
    tok_rows = grad_out.shape[0]
    owners = lax.axis_size("dp")
    ring = ring_of(owners)

    def shift(x, by):
        pairs = [(ring[i], ring[(i + by) % owners]) for i in range(owners)]
        return lax.ppermute(x, "dp", pairs)

    def hop(pieces):
        left, right = pieces
        return shift(left, 1), shift(right, -1)

    def crossed(pieces):
        right, left = pieces
        return shift(right, 1), shift(left, -1)

    def other_core(x):
        return lax.ppermute(x, "width", ((0, 1), (1, 0)))

    def return_by(distance, x):
        pairs = []
        for i in range(owners):
            pairs.append((2 * ring[i], 2 * ring[(i - distance) % owners]))
            pairs.append((2 * ring[i] + 1, 2 * ring[(i + distance) % owners] + 1))
        return lax.ppermute(x, ("dp", "width"), pairs)

    first_left, first_right, left, right, own_facts, slots = prepare(
        block_slot, active_blocks, feature_idx, acts, grad_out, owners
    )
    first_1 = hop((first_left, first_right))
    second_1 = crossed((right, left))
    decoder = fetch(decoder)
    first_1, decoder = lax.optimization_barrier((first_1, decoder))
    first_2 = hop(first_1)
    second_2 = crossed(second_1)
    pairs = [(first_left, first_right), (first_1[0], second_1[0]), (second_1[1], first_1[1])]
    distances = (0, -1, 1)
    own, onward, back = scores_of(distances, pairs, decoder, own_facts)
    total = gradients_of(distances, pairs, own_facts, decoder.shape)
    first_3 = hop(first_2)
    second_2 = stamp(second_2, (back, onward))
    second_3 = crossed(second_2)
    pairs = [(first_2[0], second_2[0]), (second_2[1], first_2[1])]
    mine, others = scores_of((-2, 2), pairs, decoder, own_facts, True)
    total = gradients_of((-2, 2), pairs, own_facts, decoder.shape, total)
    second = mine + other_core(others)
    total, first_3, second = lax.optimization_barrier((total, first_3, second))
    second = return_by(2, jnp.concatenate([second, jnp.zeros((16, 128), jnp.float32)]))[:8]
    first_4 = hop(first_3)
    pairs = [(first_3[0], second_3[0]), (second_3[1], first_3[1])]
    mine, others = scores_of((-3, 3), pairs, decoder, own_facts, True)
    total = gradients_of((-3, 3), pairs, own_facts, decoder.shape, total)
    third = mine + other_core(others)
    total, third = lax.optimization_barrier((total, third))
    third = return_by(3, third)
    total, first_4 = lax.optimization_barrier((total, first_4))
    (opposite,) = scores_of((4,), [first_4], decoder, own_facts)
    opposite = shift(opposite, -owners // 2)
    total, third = lax.optimization_barrier((total, third))
    decoder_grad = last_gradients(first_4, total)
    decoder_grad, opposite = lax.optimization_barrier((decoder_grad, opposite))
    act_grad = unpack(slots, own, *second_3, second, third, opposite)
    act_grad = act_grad + other_core(act_grad)
    return (decoder_grad, act_grad.T)


def send_back(picked):
    return lax.all_to_all(picked, "dp", split_axis=1, concat_axis=1, tiled=True)


def pack_slots(grad_out, target, slots_all, pair_coeffs, pair_columns, source_row):
    slot_row = jnp.zeros((slots_all,), jnp.int32).at[target].set(source_row)
    used = jnp.zeros((slots_all,), jnp.bool_).at[target].set(True)
    send_rows = jnp.where(used[:, None], grad_out[slot_row], jnp.zeros((), grad_out.dtype))
    send_acts = jnp.zeros((slots_all, KPB), pair_coeffs.dtype).at[target].set(pair_coeffs)
    send_cols = jnp.zeros((slots_all, KPB), jnp.int32).at[target].set(pair_columns)
    return (send_rows, send_acts, send_cols)


def some_owners(decoder, grad_out, active_blocks, feature_idx, acts, block_slot):
    tok_rows, half_width = grad_out.shape
    owners = lax.axis_size("dp")
    mean_load = tok_rows * ACT // owners
    owner_cap = mean_load + min(mean_load // 2, tok_rows - mean_load)
    block_cap = (owner_cap + 2) // 3
    block_ids = active_blocks.reshape(-1)
    pair_count = block_ids.shape[0]
    table_pos = jnp.arange(block_slot.shape[0], dtype=jnp.int32)
    slot_of = jnp.sum(
        jnp.where(block_ids[:, None] == table_pos[None, :], block_slot[None, :], 0), axis=1
    )
    pair_pos = jnp.arange(pair_count, dtype=jnp.int32)
    source_row = pair_pos // ACT
    pair_coeffs = acts.reshape(pair_count, KPB)
    pair_feats = feature_idx.reshape(pair_count, KPB)
    earlier = (block_ids[:, None] == block_ids[None, :]) & (pair_pos[None, :] < pair_pos[:, None])
    position = jnp.sum(earlier.astype(jnp.int32), axis=1)
    slot_cols = owners * block_cap
    target = slot_of % BLK_DEV * slot_cols + slot_of // BLK_DEV * block_cap + position
    slots_all = BLK_DEV * slot_cols
    send_rows, send_acts, send_cols = pack_slots(
        grad_out, target, slots_all, pair_coeffs, pair_feats, source_row
    )
    rows, coeffs, feature_pos = (
        lax.all_to_all(
            send_rows.reshape(BLK_DEV, slot_cols, half_width),
            "dp",
            split_axis=1,
            concat_axis=1,
            tiled=True,
        ),
        lax.all_to_all(
            send_acts.reshape(BLK_DEV, slot_cols, KPB),
            "dp",
            split_axis=1,
            concat_axis=1,
            tiled=True,
        ),
        lax.all_to_all(
            send_cols.reshape(BLK_DEV, slot_cols, KPB),
            "dp",
            split_axis=1,
            concat_axis=1,
            tiled=True,
        ),
    )
    weights = decoder.reshape(BLK_DEV, BW, half_width)
    scores = jnp.einsum("bnd,bfd->bnf", rows, weights, preferred_element_type=jnp.float32)
    picked = jnp.take_along_axis(scores, feature_pos, axis=2)
    returned = send_back(picked)
    feature_axis = jnp.arange(BW, dtype=jnp.int32)
    matches = feature_pos[..., None] == feature_axis
    dense = jnp.sum(jnp.where(matches, coeffs[..., None].astype(jnp.float32), 0.0), axis=2).astype(
        jnp.bfloat16
    )
    grads = jnp.einsum("bnf,bnd->bfd", dense, rows, preferred_element_type=jnp.float32)
    decoder_grad = grads.astype(jnp.bfloat16).reshape(BLK_DEV * BW, half_width)
    pair_vals = returned.reshape(slots_all, KPB)[target]
    act_grad = pair_vals.reshape(tok_rows, ACT * KPB)
    act_grad = lax.psum(act_grad, "width")
    return (decoder_grad, act_grad)


def per_device(*args):
    if lax.axis_size("dp") == ACT:
        return every_owner(*args)
    return some_owners(*args)


def solution(mesh):
    in_specs = (
        P(("groups", "dp"), "width"),
        P(("groups", "dp"), "width"),
        P(("groups", "dp"), None),
        P(("groups", "dp"), None),
        P(("groups", "dp"), None),
        P("groups"),
    )
    out_specs = (P(("groups", "dp"), "width"), P(("groups", "dp"), None))
    return jax.shard_map(
        per_device, mesh=mesh, in_specs=in_specs, out_specs=out_specs, check_vma=False
    )
```

```python
import functools

import jax
import jax.numpy as jnp
from jax import lax
from jax.experimental import pallas as pl
from jax.experimental.pallas import tpu as pltpu
from jax.sharding import PartitionSpec as P

BW = 128
BLK_DEV = 4
ACT = 8
KPB = 4
SMEM = pl.BlockSpec(memory_space=pltpu.SMEM)
VMEM = pl.BlockSpec(memory_space=pltpu.VMEM)
ANY = pl.BlockSpec(memory_space=pl.ANY)
HBM = pl.BlockSpec(memory_space=pltpu.HBM)


def limit(mebibytes):
    return pltpu.CompilerParams(vmem_limit_bytes=mebibytes * 2**20)


def kept(x):
    return pltpu.with_memory_space_constraint(x, pltpu.VMEM)


def far(x):
    return pltpu.with_memory_space_constraint(x, pltpu.HBM)


def ring_of(owners):
    return list(range(0, owners, 2)) + list(range(owners - 1, 0, -2))


def peer_at(distance, owners):
    me = lax.axis_index("dp")
    half_ring = owners // 2
    place = jnp.where(lax.rem(me, 2) == 0, lax.div(me, 2), owners - 1 - lax.div(me, 2))
    at = lax.rem(place + owners + distance, owners)
    return jnp.where(at < half_ring, 2 * at, 2 * (owners - 1 - at) + 1)


ROW_SHIFT = BLK_DEV * BW // 2
FACTS = 2 * 2 * KPB


def facts_for(owner_id, owner, first_row, feats, acts):
    mine = owner == owner_id
    rows = [
        jnp.sum(jnp.where(mine, first_row + feats[k], 0.0), axis=0, keepdims=True) - ROW_SHIFT
        for k in range(KPB)
    ]
    values = [
        jnp.sum(jnp.where(mine, acts[k], 0.0), axis=0, keepdims=True) for k in range(KPB)
    ]
    return jnp.concatenate(rows + values, axis=0)


def prepare_kernel(owners, *refs):
    sources, refs = refs[:5], refs[5:]
    outs, refs = refs[:6], refs[6:]
    block_slot, active, feats, acts, halves, wide_feats, wide_acts, sems = refs
    cut = halves.shape[2]
    copies = []
    for source, target in zip(sources[:4], (block_slot, active, feats, acts)):
        copies.append(pltpu.make_async_copy(source, target, sems.at[len(copies)]))
    for side in range(2):
        copies.append(
            pltpu.make_async_copy(
                sources[4].at[:, side * cut : (side + 1) * cut],
                halves.at[side],
                sems.at[len(copies)],
            )
        )
    for copy in copies:
        copy.start()
    for copy in copies[:4]:
        copy.wait()
    named = active[...]
    slot = jnp.zeros_like(named)
    for block in range(block_slot.shape[0]):
        slot = jnp.where(named == block, block_slot[block], slot)
    wide_feats[...] = feats[...].astype(jnp.float32)
    wide_acts[...] = acts[...].astype(jnp.float32)
    features = [wide_feats[pl.ds(k, ACT, stride=KPB), :] for k in range(KPB)]
    values = [wide_acts[pl.ds(k, ACT, stride=KPB), :] for k in range(KPB)]
    first_row = (slot % BLK_DEV * BW).astype(jnp.float32)

    def facts(distance):
        return facts_for(
            peer_at(distance, owners), slot // BLK_DEV, first_row, features, values
        )

    outs[4][...] = facts(0)
    outs[5][...] = slot
    for piece, sign, distances in (
        (outs[0], 1, (3, 4)), (outs[1], -1, (3, 4)), (outs[2], -1, (1, 2)), (outs[3], 1, (1, 2))
    ):
        rows = jnp.concatenate([facts(sign * d) for d in distances], axis=0)
        piece[piece.shape[0] - FACTS :, :] = rows.astype(jnp.bfloat16)
    tok_rows = halves.shape[1]
    for side in range(2):
        copies[4 + side].wait()
        for j in range(cut // 128):
            part = halves[side, :, j * 128 : (j + 1) * 128]
            for piece in (outs[side], outs[2 + side]):
                piece[j * tok_rows : (j + 1) * tok_rows, :] = part


def prepare(block_slot, active_blocks, feature_idx, acts, grad_out, owners):
    tok_rows, width = grad_out.shape
    piece = pltpu.VMEM((width // 256 * tok_rows + FACTS, 128), grad_out.dtype)
    facts = pltpu.VMEM((2 * KPB, tok_rows), jnp.float32)
    slots = pltpu.VMEM((ACT, tok_rows), jnp.int32)
    out_shape = (piece,) * 4 + (facts, slots)
    return pl.pallas_call(
        functools.partial(prepare_kernel, owners),
        out_shape=out_shape,
        in_specs=[HBM] * 5,
        out_specs=(VMEM,) * len(out_shape),
        scratch_shapes=[
            pltpu.SMEM(block_slot.shape, jnp.int32),
            pltpu.VMEM((ACT, tok_rows), jnp.int32),
            pltpu.VMEM((ACT * KPB, tok_rows), jnp.int32),
            pltpu.VMEM((ACT * KPB, tok_rows), acts.dtype),
            pltpu.VMEM((2, tok_rows, width // 2), grad_out.dtype),
            pltpu.VMEM((ACT * KPB, tok_rows), jnp.float32),
            pltpu.VMEM((ACT * KPB, tok_rows), jnp.float32),
            pltpu.SemaphoreType.DMA((6,)),
        ],
        compiler_params=limit(8),
        name="prepare",
    )(far(block_slot), far(active_blocks.T), far(feature_idx.T), far(acts.T), far(grad_out))


def fetch_kernel(source, target, sem):
    copy = pltpu.make_async_copy(source, target, sem)
    copy.start()
    copy.wait()


def fetch(x):
    return pl.pallas_call(
        fetch_kernel,
        out_shape=pltpu.VMEM(x.shape, x.dtype),
        in_specs=[HBM],
        out_specs=VMEM,
        scratch_shapes=[pltpu.SemaphoreType.DMA],
        compiler_params=limit(8),
        name="fetch",
    )(far(x))


def block_and_rows(here):
    at_row = here[:KPB].astype(jnp.int32) + ROW_SHIFT
    return at_row[:1] // BW, at_row % BW


def row_axis_of(tok_rows):
    return lax.broadcasted_iota(jnp.int32, (BW, tok_rows), 0)


def coefficients(here):
    block, feats = block_and_rows(here)
    row_axis = row_axis_of(here.shape[1])
    dense = jnp.zeros(row_axis.shape, jnp.float32)
    for k in range(KPB):
        dense = jnp.where(row_axis == feats[k : k + 1], here[KPB + k : KPB + k + 1], dense)
    parts = [jnp.where(block == b, dense, 0.0) for b in range(BLK_DEV)]
    return jnp.concatenate(parts, axis=0).astype(jnp.bfloat16)


def pick(scores, here):
    block, feats = block_and_rows(here)
    row_axis = row_axis_of(here.shape[1])
    mine = scores[:BW]
    for b in range(1, BLK_DEV):
        mine = jnp.where(block == b, scores[b * BW : (b + 1) * BW], mine)
    return [
        jnp.sum(jnp.where(row_axis == feats[k : k + 1], mine, 0.0), axis=0, keepdims=True)
        for k in range(KPB)
    ]


def facts_in(left, right, distance):
    near = abs(distance) <= 2
    piece = (right if near else left) if distance in (-1, -2, -3, 4) else (left if near else right)
    facts = piece[piece.shape[0] - FACTS :, :].astype(jnp.float32)
    slot = (abs(distance) - 1) % 2
    return facts[slot * 2 * KPB : (slot + 1) * 2 * KPB]


def columns_of(pieces, tok_rows, parts):
    rows = [
        jnp.concatenate([piece[j * tok_rows : (j + 1) * tok_rows, :] for j in parts], axis=1)
        for piece in pieces
    ]
    return jnp.concatenate(rows, axis=0) if len(rows) > 1 else rows[0]


def picks_of(facts, decoder, pieces):
    picks = []
    tok_rows = facts[0].shape[1]
    cut = decoder.shape[1] // 2
    for first in range(0, len(facts), 2):
        count = min(2, len(facts) - first)
        scores = None
        for side in range(2):
            part = lax.dot_general(
                decoder[:, side * cut : (side + 1) * cut],
                columns_of(
                    pieces[2 * first + side : 2 * (first + count) : 2],
                    tok_rows,
                    range(cut // 128),
                ),
                (((1,), (1,)), ((), ())),
                preferred_element_type=jnp.float32,
            )
            scores = part if scores is None else scores + part
        for i in range(first, first + count):
            here = scores[:, (i - first) * tok_rows : (i - first + 1) * tok_rows]
            picks.append(jnp.concatenate(pick(here, facts[i]) * 2, axis=0))
    return picks


def gradient_blocks(facts, pieces, width):
    tok_rows = facts[0].shape[1]
    cut = width // 2
    dense = jnp.concatenate([coefficients(here) for here in facts], axis=1)
    for side in range(2):
        for j in range(0, cut // 128, 2):
            rows = columns_of(pieces[side::2], tok_rows, (j, j + 1))
            part = jnp.dot(dense, rows, preferred_element_type=jnp.float32)
            yield slice(side * cut + j * 128, side * cut + (j + 2) * 128), part


def facts_of(distances, own_facts, pieces):
    return [
        own_facts[...] if d == 0 else facts_in(pieces[2 * i], pieces[2 * i + 1], d)
        for i, d in enumerate(distances)
    ]


def scores_kernel(distances, split, decoder, own_facts, *refs):
    pieces, picked = refs[: 2 * len(distances)], refs[2 * len(distances) :]
    picks = picks_of(facts_of(distances, own_facts, pieces), decoder, pieces)
    if split:
        first = lax.axis_index("width") == 0
        picks = [jnp.where(first, *picks), jnp.where(first, *picks[::-1])]
    for target, values in zip(picked, picks):
        target[...] = values


def scores_of(distances, pairs, decoder, own_facts, split=False):
    pieces = [kept(piece) for pair in pairs for piece in pair]
    shape = pltpu.VMEM(own_facts.shape, jnp.float32)
    return pl.pallas_call(
        functools.partial(scores_kernel, distances, split),
        out_shape=(shape,) * len(distances),
        in_specs=[VMEM] * (2 + len(pieces)),
        out_specs=(VMEM,) * len(distances),
        compiler_params=limit(12),
        name="scores",
    )(kept(decoder), kept(own_facts), *pieces)


def half_kernel(decoder, piece, partial):
    cut = decoder.shape[1] // 2
    rows = columns_of([piece], partial.shape[1], range(cut // 128))
    partial[...] = lax.dot_general(
        decoder[:, cut:], rows, (((1,), (1,)), ((), ())), preferred_element_type=jnp.float32
    )


def half_scores(decoder, piece, tok_rows):
    return pl.pallas_call(
        half_kernel,
        out_shape=pltpu.VMEM((decoder.shape[0], tok_rows), jnp.float32),
        in_specs=[VMEM] * 2,
        out_specs=VMEM,
        compiler_params=limit(8),
        name="half_scores",
    )(kept(decoder), kept(piece))


def rest_kernel(decoder, partial, piece, picked):
    cut = decoder.shape[1] // 2
    rows = columns_of([piece], partial.shape[1], range(cut // 128))
    scores = partial[...] + lax.dot_general(
        decoder[:, :cut], rows, (((1,), (1,)), ((), ())), preferred_element_type=jnp.float32
    )
    facts = facts_in(piece, None, 4)
    picked[...] = jnp.concatenate(pick(scores, facts) * 2, axis=0)


def rest_scores(decoder, partial, piece):
    return pl.pallas_call(
        rest_kernel,
        out_shape=pltpu.VMEM((2 * KPB, partial.shape[1]), jnp.float32),
        in_specs=[VMEM] * 3,
        out_specs=VMEM,
        compiler_params=limit(8),
        name="rest_scores",
    )(kept(decoder), kept(partial), kept(piece))


def gradients_kernel(distances, own_facts, *refs):
    pieces, refs = refs[: 2 * len(distances)], refs[2 * len(distances) :]
    total = refs[-1]
    facts = facts_of(distances, own_facts, pieces)
    for columns, part in gradient_blocks(facts, pieces, total.shape[1]):
        total[:, columns] = part if len(refs) == 1 else refs[0][:, columns] + part


def gradients_of(distances, pairs, own_facts, shape, total=None):
    operands = [kept(own_facts)] + [kept(piece) for pair in pairs for piece in pair]
    operands += [] if total is None else [kept(total)]
    return pl.pallas_call(
        functools.partial(gradients_kernel, distances),
        out_shape=pltpu.VMEM(shape, jnp.float32),
        in_specs=[VMEM] * len(operands),
        out_specs=VMEM,
        input_output_aliases={} if total is None else {len(operands) - 1: 0},
        compiler_params=limit(16),
        name="gradients",
    )(*operands)


def last_gradients_kernel(left, right, total, out, rounded, sems):
    copies = []
    facts = [facts_in(left, right, 4)]
    for columns, part in gradient_blocks(facts, (left, right), out.shape[1]):
        rounded[:, columns] = (total[:, columns] + part).astype(out.dtype)
        copies.append(
            pltpu.make_async_copy(
                rounded.at[:, columns], out.at[:, columns], sems.at[len(copies)]
            )
        )
        copies[-1].start()
    for copy in copies:
        copy.wait()


def last_gradients(pair, total):
    return pl.pallas_call(
        last_gradients_kernel,
        out_shape=jax.ShapeDtypeStruct(total.shape, jnp.bfloat16),
        in_specs=[VMEM] * 3,
        out_specs=ANY,
        scratch_shapes=[
            pltpu.VMEM(total.shape, jnp.bfloat16),
            pltpu.SemaphoreType.DMA((total.shape[1] // 256,)),
        ],
        compiler_params=limit(16),
        name="last_gradients",
    )(kept(pair[0]), kept(pair[1]), kept(total))


def stamp_kernel(onward, back, for_onward, for_back, onward_out, back_out, rows, sems):
    start = onward.shape[0] - FACTS
    targets = (onward_out, back_out)
    for i, piece in enumerate((onward, back)):
        pltpu.make_async_copy(
            piece.at[start : start + 16, :], rows.at[i], sems.at[i]
        ).start()
    for i, values in enumerate((for_onward, for_back)):
        pltpu.make_async_copy(
            onward.at[start : start + 16, :], rows.at[i], sems.at[i]
        ).wait()
        value = values[:KPB]
        high = value.astype(jnp.bfloat16).astype(jnp.float32)
        low = value - high
        facts = rows[i].astype(jnp.float32)[2 * KPB :]
        rows[i] = jnp.concatenate([high, low, facts], axis=0).astype(jnp.bfloat16)
        pltpu.make_async_copy(
            rows.at[i], targets[i].at[start : start + 16, :], sems.at[2 + i]
        ).start()
    for i in range(2):
        pltpu.make_async_copy(
            rows.at[i], targets[i].at[start : start + 16, :], sems.at[2 + i]
        ).wait()


def stamp(pieces, values):
    return pl.pallas_call(
        stamp_kernel,
        out_shape=tuple(pltpu.VMEM(piece.shape, piece.dtype) for piece in pieces),
        in_specs=[ANY, ANY, VMEM, VMEM],
        out_specs=(ANY, ANY),
        scratch_shapes=[
            pltpu.VMEM((2, 16, 128), jnp.bfloat16),
            pltpu.SemaphoreType.DMA((4,)),
        ],
        input_output_aliases={0: 0, 1: 1},
        compiler_params=limit(4),
        name="stamp",
    )(*[kept(piece) for piece in pieces], *[kept(value) for value in values])


def unpack_kernel(owners, slots, own, onward, back, second, third, opposite, out):
    owner = slots[...] // BLK_DEV
    start = onward.shape[0] - FACTS
    way = 1 - 2 * lax.axis_index("width")
    returned = [(0, own[...])]
    for distance, piece in ((-1, onward), (1, back)):
        rows = piece[start : start + 16, :].astype(jnp.float32)
        returned.append((distance, rows[:KPB] + rows[KPB : 2 * KPB]))
    returned += [(2 * way, second[...]), (3 * way, third[...]), (4, opposite[...])]
    mine = [owner == peer_at(distance, owners) for distance, _ in returned]
    for k in range(KPB):
        total = jnp.zeros(owner.shape, jnp.float32)
        for here, (_, values) in zip(mine, returned):
            total = jnp.where(here, values[k : k + 1, :], total)
        out[pl.ds(k, ACT, stride=KPB), :] = total


def unpack(slots, *returned):
    tok_rows = slots.shape[1]
    return pl.pallas_call(
        functools.partial(unpack_kernel, lax.axis_size("dp")),
        out_shape=pltpu.VMEM((ACT * KPB, tok_rows), jnp.float32),
        in_specs=[VMEM] * (1 + len(returned)),
        out_specs=VMEM,
        compiler_params=limit(4),
        name="unpack",
    )(kept(slots), *[kept(x) for x in returned])


def every_owner(decoder, grad_out, active_blocks, feature_idx, acts, block_slot):
    tok_rows = grad_out.shape[0]
    owners = lax.axis_size("dp")
    ring = ring_of(owners)

    def shift(x, by):
        pairs = [(ring[i], ring[(i + by) % owners]) for i in range(owners)]
        return lax.ppermute(x, "dp", pairs)

    def hop(pieces):
        left, right = pieces
        return shift(left, 1), shift(right, -1)

    def crossed(pieces):
        right, left = pieces
        return shift(right, 1), shift(left, -1)

    def other_core(x):
        return lax.ppermute(x, "width", ((0, 1), (1, 0)))

    def return_by(distance, x):
        pairs = []
        for i in range(owners):
            pairs.append((2 * ring[i], 2 * ring[(i - distance) % owners]))
            pairs.append((2 * ring[i] + 1, 2 * ring[(i + distance) % owners] + 1))
        return lax.ppermute(x, ("dp", "width"), pairs)

    first_left, first_right, left, right, own_facts, slots = prepare(
        block_slot, active_blocks, feature_idx, acts, grad_out, owners
    )
    first_1 = hop((first_left, first_right))
    second_1 = crossed((right, left))
    decoder = fetch(decoder)
    first_1, decoder = lax.optimization_barrier((first_1, decoder))
    first_2 = hop(first_1)
    second_2 = crossed(second_1)
    pairs = [(first_left, first_right), (first_1[0], second_1[0]), (second_1[1], first_1[1])]
    distances = (0, -1, 1)
    own, onward, back = scores_of(distances, pairs, decoder, own_facts)
    total = gradients_of(distances, pairs, own_facts, decoder.shape)
    first_3 = hop(first_2)
    second_2 = stamp(second_2, (back, onward))
    second_3 = crossed(second_2)
    pairs = [(first_2[0], second_2[0]), (second_2[1], first_2[1])]
    mine, others = scores_of((-2, 2), pairs, decoder, own_facts, True)
    total = gradients_of((-2, 2), pairs, own_facts, decoder.shape, total)
    second = mine + other_core(others)
    total, first_3, second = lax.optimization_barrier((total, first_3, second))
    second = return_by(2, jnp.concatenate([second, jnp.zeros((16, 128), jnp.float32)]))[:8]
    first_4 = hop(first_3)
    pairs = [(first_3[0], second_3[0]), (second_3[1], first_3[1])]
    mine, others = scores_of((-3, 3), pairs, decoder, own_facts, True)
    total = gradients_of((-3, 3), pairs, own_facts, decoder.shape, total)
    third = mine + other_core(others)
    total, third = lax.optimization_barrier((total, third))
    third = return_by(3, third)
    last_left, last_right = first_4
    total, last_right = lax.optimization_barrier((total, last_right))
    partial = half_scores(decoder, last_right, tok_rows)
    partial, last_left = lax.optimization_barrier((partial, last_left))
    opposite = rest_scores(decoder, partial, last_left)
    first_4 = last_left, last_right
    opposite = shift(opposite, -owners // 2)
    total, third = lax.optimization_barrier((total, third))
    decoder_grad = last_gradients(first_4, total)
    decoder_grad, opposite = lax.optimization_barrier((decoder_grad, opposite))
    act_grad = unpack(slots, own, *second_3, second, third, opposite)
    act_grad = act_grad + other_core(act_grad)
    return (decoder_grad, act_grad.T)


def send_back(picked):
    return lax.all_to_all(picked, "dp", split_axis=1, concat_axis=1, tiled=True)


def pack_slots(grad_out, target, slots_all, pair_coeffs, pair_columns, source_row):
    slot_row = jnp.zeros((slots_all,), jnp.int32).at[target].set(source_row)
    used = jnp.zeros((slots_all,), jnp.bool_).at[target].set(True)
    send_rows = jnp.where(used[:, None], grad_out[slot_row], jnp.zeros((), grad_out.dtype))
    send_acts = jnp.zeros((slots_all, KPB), pair_coeffs.dtype).at[target].set(pair_coeffs)
    send_cols = jnp.zeros((slots_all, KPB), jnp.int32).at[target].set(pair_columns)
    return (send_rows, send_acts, send_cols)


def some_owners(decoder, grad_out, active_blocks, feature_idx, acts, block_slot):
    tok_rows, half_width = grad_out.shape
    owners = lax.axis_size("dp")
    mean_load = tok_rows * ACT // owners
    owner_cap = mean_load + min(mean_load // 2, tok_rows - mean_load)
    block_cap = (owner_cap + 2) // 3
    block_ids = active_blocks.reshape(-1)
    pair_count = block_ids.shape[0]
    table_pos = jnp.arange(block_slot.shape[0], dtype=jnp.int32)
    slot_of = jnp.sum(
        jnp.where(block_ids[:, None] == table_pos[None, :], block_slot[None, :], 0), axis=1
    )
    pair_pos = jnp.arange(pair_count, dtype=jnp.int32)
    source_row = pair_pos // ACT
    pair_coeffs = acts.reshape(pair_count, KPB)
    pair_feats = feature_idx.reshape(pair_count, KPB)
    earlier = (block_ids[:, None] == block_ids[None, :]) & (pair_pos[None, :] < pair_pos[:, None])
    position = jnp.sum(earlier.astype(jnp.int32), axis=1)
    slot_cols = owners * block_cap
    target = slot_of % BLK_DEV * slot_cols + slot_of // BLK_DEV * block_cap + position
    slots_all = BLK_DEV * slot_cols
    send_rows, send_acts, send_cols = pack_slots(
        grad_out, target, slots_all, pair_coeffs, pair_feats, source_row
    )
    rows, coeffs, feature_pos = (
        lax.all_to_all(
            send_rows.reshape(BLK_DEV, slot_cols, half_width),
            "dp",
            split_axis=1,
            concat_axis=1,
            tiled=True,
        ),
        lax.all_to_all(
            send_acts.reshape(BLK_DEV, slot_cols, KPB),
            "dp",
            split_axis=1,
            concat_axis=1,
            tiled=True,
        ),
        lax.all_to_all(
            send_cols.reshape(BLK_DEV, slot_cols, KPB),
            "dp",
            split_axis=1,
            concat_axis=1,
            tiled=True,
        ),
    )
    weights = decoder.reshape(BLK_DEV, BW, half_width)
    scores = jnp.einsum("bnd,bfd->bnf", rows, weights, preferred_element_type=jnp.float32)
    picked = jnp.take_along_axis(scores, feature_pos, axis=2)
    returned = send_back(picked)
    feature_axis = jnp.arange(BW, dtype=jnp.int32)
    matches = feature_pos[..., None] == feature_axis
    dense = jnp.sum(jnp.where(matches, coeffs[..., None].astype(jnp.float32), 0.0), axis=2).astype(
        jnp.bfloat16
    )
    grads = jnp.einsum("bnf,bnd->bfd", dense, rows, preferred_element_type=jnp.float32)
    decoder_grad = grads.astype(jnp.bfloat16).reshape(BLK_DEV * BW, half_width)
    pair_vals = returned.reshape(slots_all, KPB)[target]
    act_grad = pair_vals.reshape(tok_rows, ACT * KPB)
    act_grad = lax.psum(act_grad, "width")
    return (decoder_grad, act_grad)


def per_device(*args):
    if lax.axis_size("dp") == ACT:
        return every_owner(*args)
    return some_owners(*args)


def solution(mesh):
    in_specs = (
        P(("groups", "dp"), "width"),
        P(("groups", "dp"), "width"),
        P(("groups", "dp"), None),
        P(("groups", "dp"), None),
        P(("groups", "dp"), None),
        P("groups"),
    )
    out_specs = (P(("groups", "dp"), "width"), P(("groups", "dp"), None))
    return jax.shard_map(
        per_device, mesh=mesh, in_specs=in_specs, out_specs=out_specs, check_vma=False
    )
```

```python
import functools

import jax
import jax.numpy as jnp
from jax import lax
from jax.experimental import pallas as pl
from jax.experimental.pallas import tpu as pltpu
from jax.sharding import PartitionSpec as P

BW = 128
BLK_DEV = 4
ACT = 8
KPB = 4
SMEM = pl.BlockSpec(memory_space=pltpu.SMEM)
VMEM = pl.BlockSpec(memory_space=pltpu.VMEM)
ANY = pl.BlockSpec(memory_space=pl.ANY)
HBM = pl.BlockSpec(memory_space=pltpu.HBM)


def limit(mebibytes):
    return pltpu.CompilerParams(vmem_limit_bytes=mebibytes * 2**20)


def kept(x):
    return pltpu.with_memory_space_constraint(x, pltpu.VMEM)


def far(x):
    return pltpu.with_memory_space_constraint(x, pltpu.HBM)


def ring_of(owners):
    return list(range(0, owners, 2)) + list(range(owners - 1, 0, -2))


def peer_at(distance, owners):
    me = lax.axis_index("dp")
    half_ring = owners // 2
    place = jnp.where(lax.rem(me, 2) == 0, lax.div(me, 2), owners - 1 - lax.div(me, 2))
    at = lax.rem(place + owners + distance, owners)
    return jnp.where(at < half_ring, 2 * at, 2 * (owners - 1 - at) + 1)


ROW_SHIFT = BLK_DEV * BW // 2
FACTS = ACT // 2 * 2 * KPB
LAST_FACTS = 16


def facts_for(owner_id, owner, first_row, feats, acts):
    mine = owner == owner_id
    rows = [
        jnp.sum(jnp.where(mine, first_row + feats[k], 0.0), axis=0, keepdims=True) - ROW_SHIFT
        for k in range(KPB)
    ]
    values = [
        jnp.sum(jnp.where(mine, acts[k], 0.0), axis=0, keepdims=True) for k in range(KPB)
    ]
    return jnp.concatenate(rows + values, axis=0)


def prepare_kernel(owners, *refs):
    sources, refs = refs[:5], refs[5:]
    outs, refs = refs[:6], refs[6:]
    first_left, first_right, left, right, own_facts, slots = outs
    block_slot, active, feats, acts, whole, wide_feats, wide_acts, sems = refs
    tok_rows, width = whole.shape
    cut = width // 2
    copies = []
    for source, target in zip(sources[:4], (block_slot, active, feats, acts)):
        copies.append(pltpu.make_async_copy(source, target, sems.at[len(copies)]))
    for start in range(0, tok_rows, 16):
        rows = pl.ds(start, 16)
        copies.append(
            pltpu.make_async_copy(sources[4].at[rows], whole.at[rows], sems.at[len(copies)])
        )
    for copy in copies:
        copy.start()
    for copy in copies[:4]:
        copy.wait()
    named = active[...]
    slot = jnp.zeros_like(named)
    for block in range(block_slot.shape[0]):
        slot = jnp.where(named == block, block_slot[block], slot)
    slots[...] = slot
    wide_feats[...] = feats[...].astype(jnp.float32)
    wide_acts[...] = acts[...].astype(jnp.float32)
    features = [wide_feats[pl.ds(k, ACT, stride=KPB), :] for k in range(KPB)]
    values = [wide_acts[pl.ds(k, ACT, stride=KPB), :] for k in range(KPB)]
    first_row = (slot % BLK_DEV * BW).astype(jnp.float32)

    def facts(distance):
        return facts_for(
            peer_at(distance, owners), slot // BLK_DEV, first_row, features, values
        )

    def store_facts(target, blocks):
        rows = jnp.concatenate(blocks, axis=0)
        target[target.shape[0] - rows.shape[0] :, :] = rows.astype(jnp.bfloat16)

    own_facts[...] = facts(0)
    opposite = facts(owners // 2)
    none = jnp.zeros_like(opposite)
    store_facts(first_left, [opposite, none])
    for target, sign in ((left, -1), (right, 1)):
        store_facts(target, [facts(sign * d) for d in range(1, owners // 2)] + [none])
    for copy in copies[4:]:
        copy.wait()
    for side, targets in ((0, (first_left, left)), (1, (first_right, right))):
        for j in range(cut // 128):
            column = side * cut + j * 128
            part = whole[:, column : column + 128]
            for target in targets:
                target[j * tok_rows : (j + 1) * tok_rows, :] = part


def prepare(block_slot, active_blocks, feature_idx, acts, grad_out, owners):
    tok_rows, width = grad_out.shape
    plain = width // 256 * tok_rows

    def piece(extra):
        return pltpu.VMEM((plain + extra, 128), grad_out.dtype)

    return pl.pallas_call(
        functools.partial(prepare_kernel, owners),
        out_shape=(
            piece(LAST_FACTS),
            piece(0),
            piece(FACTS),
            piece(FACTS),
            pltpu.VMEM((2 * KPB, tok_rows), jnp.float32),
            pltpu.VMEM((ACT, tok_rows), jnp.int32),
        ),
        in_specs=[HBM] * 5,
        out_specs=(VMEM,) * 6,
        scratch_shapes=[
            pltpu.SMEM(block_slot.shape, jnp.int32),
            pltpu.VMEM((ACT, tok_rows), jnp.int32),
            pltpu.VMEM((ACT * KPB, tok_rows), jnp.int32),
            pltpu.VMEM((ACT * KPB, tok_rows), acts.dtype),
            pltpu.VMEM((tok_rows, width), grad_out.dtype),
            pltpu.VMEM((ACT * KPB, tok_rows), jnp.float32),
            pltpu.VMEM((ACT * KPB, tok_rows), jnp.float32),
            pltpu.SemaphoreType.DMA((4 + tok_rows // 16,)),
        ],
        compiler_params=limit(8),
        name="prepare",
    )(far(block_slot), far(active_blocks.T), far(feature_idx.T), far(acts.T), far(grad_out))


def fetch_kernel(source, target, sem):
    copy = pltpu.make_async_copy(source, target, sem)
    copy.start()
    copy.wait()


def fetch(x):
    return pl.pallas_call(
        fetch_kernel,
        out_shape=pltpu.VMEM(x.shape, x.dtype),
        in_specs=[HBM],
        out_specs=VMEM,
        scratch_shapes=[pltpu.SemaphoreType.DMA],
        compiler_params=limit(8),
        name="fetch",
    )(far(x))


def block_and_rows(here):
    at_row = here[:KPB].astype(jnp.int32) + ROW_SHIFT
    return at_row[:1] // BW, at_row % BW


def row_axis_of(tok_rows):
    return lax.broadcasted_iota(jnp.int32, (BW, tok_rows), 0)


def coefficients(here):
    block, feats = block_and_rows(here)
    row_axis = row_axis_of(here.shape[1])
    dense = jnp.zeros(row_axis.shape, jnp.float32)
    for k in range(KPB):
        dense = jnp.where(row_axis == feats[k : k + 1], here[KPB + k : KPB + k + 1], dense)
    parts = [jnp.where(block == b, dense, 0.0) for b in range(BLK_DEV)]
    return jnp.concatenate(parts, axis=0).astype(jnp.bfloat16)


def pick(scores, here):
    block, feats = block_and_rows(here)
    row_axis = row_axis_of(here.shape[1])
    mine = scores[:BW]
    for b in range(1, BLK_DEV):
        mine = jnp.where(block == b, scores[b * BW : (b + 1) * BW], mine)
    return [
        jnp.sum(jnp.where(row_axis == feats[k : k + 1], mine, 0.0), axis=0, keepdims=True)
        for k in range(KPB)
    ]


def facts_in(piece, distance, tok_rows):
    facts = piece[piece.shape[0] - FACTS :, :].astype(jnp.float32)
    return facts[(abs(distance) - 1) * 2 * KPB : abs(distance) * 2 * KPB]


def columns_of(pieces, tok_rows, parts):
    rows = [
        jnp.concatenate([piece[j * tok_rows : (j + 1) * tok_rows, :] for j in parts], axis=1)
        for piece in pieces
    ]
    return jnp.concatenate(rows, axis=0) if len(rows) > 1 else rows[0]


def picks_of(facts, decoder, pieces):
    picks = []
    tok_rows = facts[0].shape[1]
    cut = decoder.shape[1] // 2
    for first in range(0, len(facts), 2):
        count = min(2, len(facts) - first)
        scores = None
        for side in range(2):
            part = lax.dot_general(
                decoder[:, side * cut : (side + 1) * cut],
                columns_of(
                    pieces[2 * first + side : 2 * (first + count) : 2],
                    tok_rows,
                    range(cut // 128),
                ),
                (((1,), (1,)), ((), ())),
                preferred_element_type=jnp.float32,
            )
            scores = part if scores is None else scores + part
        for i in range(first, first + count):
            here = scores[:, (i - first) * tok_rows : (i - first + 1) * tok_rows]
            picks.append(jnp.concatenate(pick(here, facts[i]) * 2, axis=0))
    return picks


def gradient_blocks(facts, pieces, width):
    tok_rows = facts[0].shape[1]
    cut = width // 2
    dense = jnp.concatenate([coefficients(here) for here in facts], axis=1)
    for side in range(2):
        for j in range(0, cut // 128, 2):
            rows = columns_of(pieces[side::2], tok_rows, (j, j + 1))
            part = jnp.dot(dense, rows, preferred_element_type=jnp.float32)
            yield slice(side * cut + j * 128, side * cut + (j + 2) * 128), part


def last_facts_in(piece):
    return piece[piece.shape[0] - LAST_FACTS :, :].astype(jnp.float32)[: 2 * KPB]


def facts_of(distances, own_facts, pieces):
    facts = []
    for i, d in enumerate(distances):
        if d == 0:
            facts.append(own_facts[...])
        elif d == 4:
            facts.append(last_facts_in(pieces[2 * i]))
        else:
            facts.append(facts_in(pieces[2 * i + (d < 0)], d, own_facts.shape[1]))
    return facts


def scores_kernel(distances, split, decoder, own_facts, *refs):
    pieces, picked = refs[: 2 * len(distances)], refs[2 * len(distances) :]
    picks = picks_of(facts_of(distances, own_facts, pieces), decoder, pieces)
    if split:
        first = lax.axis_index("width") == 0
        picks = [jnp.where(first, *picks), jnp.where(first, *picks[::-1])]
    for target, values in zip(picked, picks):
        target[...] = values


def scores_of(distances, pairs, decoder, own_facts, split=False):
    pieces = [kept(piece) for pair in pairs for piece in pair]
    shape = pltpu.VMEM(own_facts.shape, jnp.float32)
    return pl.pallas_call(
        functools.partial(scores_kernel, distances, split),
        out_shape=(shape,) * len(distances),
        in_specs=[VMEM] * (2 + len(pieces)),
        out_specs=(VMEM,) * len(distances),
        compiler_params=limit(12),
        name="scores",
    )(kept(decoder), kept(own_facts), *pieces)


def gradients_kernel(distances, own_facts, *refs):
    pieces, refs = refs[: 2 * len(distances)], refs[2 * len(distances) :]
    total = refs[-1]
    facts = facts_of(distances, own_facts, pieces)
    for columns, part in gradient_blocks(facts, pieces, total.shape[1]):
        total[:, columns] = part if len(refs) == 1 else refs[0][:, columns] + part


def gradients_of(distances, pairs, own_facts, shape, total=None):
    operands = [kept(own_facts)] + [kept(piece) for pair in pairs for piece in pair]
    operands += [] if total is None else [kept(total)]
    return pl.pallas_call(
        functools.partial(gradients_kernel, distances),
        out_shape=pltpu.VMEM(shape, jnp.float32),
        in_specs=[VMEM] * len(operands),
        out_specs=VMEM,
        input_output_aliases={} if total is None else {len(operands) - 1: 0},
        compiler_params=limit(16),
        name="gradients",
    )(*operands)


def last_gradients_kernel(left, right, total, out, rounded, sems):
    copies = []
    facts = [last_facts_in(left)]
    for columns, part in gradient_blocks(facts, (left, right), out.shape[1]):
        rounded[:, columns] = (total[:, columns] + part).astype(out.dtype)
        copies.append(
            pltpu.make_async_copy(
                rounded.at[:, columns], out.at[:, columns], sems.at[len(copies)]
            )
        )
        copies[-1].start()
    for copy in copies:
        copy.wait()


def last_gradients(pair, total):
    return pl.pallas_call(
        last_gradients_kernel,
        out_shape=jax.ShapeDtypeStruct(total.shape, jnp.bfloat16),
        in_specs=[VMEM] * 3,
        out_specs=ANY,
        scratch_shapes=[
            pltpu.VMEM(total.shape, jnp.bfloat16),
            pltpu.SemaphoreType.DMA((total.shape[1] // 256,)),
        ],
        compiler_params=limit(16),
        name="last_gradients",
    )(kept(pair[0]), kept(pair[1]), kept(total))


def stamp_kernel(onward, back, for_onward, for_back, onward_out, back_out, rows, sems):
    start = onward.shape[0] - FACTS
    targets = (onward_out, back_out)
    for i, piece in enumerate((onward, back)):
        pltpu.make_async_copy(
            piece.at[start : start + 16, :], rows.at[i], sems.at[i]
        ).start()
    for i, values in enumerate((for_onward, for_back)):
        pltpu.make_async_copy(
            onward.at[start : start + 16, :], rows.at[i], sems.at[i]
        ).wait()
        value = values[:KPB]
        high = value.astype(jnp.bfloat16).astype(jnp.float32)
        low = value - high
        facts = rows[i].astype(jnp.float32)[2 * KPB :]
        rows[i] = jnp.concatenate([high, low, facts], axis=0).astype(jnp.bfloat16)
        pltpu.make_async_copy(
            rows.at[i], targets[i].at[start : start + 16, :], sems.at[2 + i]
        ).start()
    for i in range(2):
        pltpu.make_async_copy(
            rows.at[i], targets[i].at[start : start + 16, :], sems.at[2 + i]
        ).wait()


def stamp(pieces, values):
    return pl.pallas_call(
        stamp_kernel,
        out_shape=tuple(pltpu.VMEM(piece.shape, piece.dtype) for piece in pieces),
        in_specs=[ANY, ANY, VMEM, VMEM],
        out_specs=(ANY, ANY),
        scratch_shapes=[
            pltpu.VMEM((2, 16, 128), jnp.bfloat16),
            pltpu.SemaphoreType.DMA((4,)),
        ],
        input_output_aliases={0: 0, 1: 1},
        compiler_params=limit(4),
        name="stamp",
    )(*[kept(piece) for piece in pieces], *[kept(value) for value in values])


def unpack_kernel(owners, slots, own, onward, back, second, third, opposite, out):
    owner = slots[...] // BLK_DEV
    start = onward.shape[0] - FACTS
    way = 1 - 2 * lax.axis_index("width")
    returned = [(0, own[...])]
    for distance, piece in ((-1, onward), (1, back)):
        rows = piece[start : start + 16, :].astype(jnp.float32)
        returned.append((distance, rows[:KPB] + rows[KPB : 2 * KPB]))
    returned += [(2 * way, second[...]), (3 * way, third[...]), (4, opposite[...])]
    mine = [owner == peer_at(distance, owners) for distance, _ in returned]
    for k in range(KPB):
        total = jnp.zeros(owner.shape, jnp.float32)
        for here, (_, values) in zip(mine, returned):
            total = jnp.where(here, values[k : k + 1, :], total)
        out[pl.ds(k, ACT, stride=KPB), :] = total


def unpack(slots, *returned):
    tok_rows = slots.shape[1]
    return pl.pallas_call(
        functools.partial(unpack_kernel, lax.axis_size("dp")),
        out_shape=pltpu.VMEM((ACT * KPB, tok_rows), jnp.float32),
        in_specs=[VMEM] * (1 + len(returned)),
        out_specs=VMEM,
        compiler_params=limit(4),
        name="unpack",
    )(kept(slots), *[kept(x) for x in returned])


def every_owner(decoder, grad_out, active_blocks, feature_idx, acts, block_slot):
    tok_rows = grad_out.shape[0]
    owners = lax.axis_size("dp")
    ring = ring_of(owners)

    def shift(x, by):
        pairs = [(ring[i], ring[(i + by) % owners]) for i in range(owners)]
        return lax.ppermute(x, "dp", pairs)

    def hop(pieces):
        left, right = pieces
        return shift(left, 1), shift(right, -1)

    def crossed(pieces):
        right, left = pieces
        return shift(right, 1), shift(left, -1)

    def other_core(x):
        return lax.ppermute(x, "width", ((0, 1), (1, 0)))

    def return_by(distance, x):
        pairs = []
        for i in range(owners):
            pairs.append((2 * ring[i], 2 * ring[(i - distance) % owners]))
            pairs.append((2 * ring[i] + 1, 2 * ring[(i + distance) % owners] + 1))
        return lax.ppermute(x, ("dp", "width"), pairs)

    first_left, first_right, left, right, own_facts, slots = prepare(
        block_slot, active_blocks, feature_idx, acts, grad_out, owners
    )
    first_1 = hop((first_left, first_right))
    second_1 = crossed((right, left))
    decoder = fetch(decoder)
    first_1, decoder = lax.optimization_barrier((first_1, decoder))
    first_2 = hop(first_1)
    second_2 = crossed(second_1)
    pairs = [(first_left, first_right), (first_1[0], second_1[0]), (second_1[1], first_1[1])]
    distances = (0, -1, 1)
    own, onward, back = scores_of(distances, pairs, decoder, own_facts)
    total = gradients_of(distances, pairs, own_facts, decoder.shape)
    first_3 = hop(first_2)
    second_2 = stamp(second_2, (back, onward))
    second_3 = crossed(second_2)
    pairs = [(first_2[0], second_2[0]), (second_2[1], first_2[1])]
    mine, others = scores_of((-2, 2), pairs, decoder, own_facts, True)
    total = gradients_of((-2, 2), pairs, own_facts, decoder.shape, total)
    second = mine + other_core(others)
    total, first_3, second = lax.optimization_barrier((total, first_3, second))
    second = return_by(2, jnp.concatenate([second, jnp.zeros((24, 128), jnp.float32)]))[:8]
    first_4 = hop(first_3)
    pairs = [(first_3[0], second_3[0]), (second_3[1], first_3[1])]
    mine, others = scores_of((-3, 3), pairs, decoder, own_facts, True)
    total = gradients_of((-3, 3), pairs, own_facts, decoder.shape, total)
    third = mine + other_core(others)
    total, third = lax.optimization_barrier((total, third))
    third = return_by(3, third)
    total, first_4 = lax.optimization_barrier((total, first_4))
    (opposite,) = scores_of((4,), [first_4], decoder, own_facts)
    opposite = shift(opposite, -owners // 2)
    total, third = lax.optimization_barrier((total, third))
    decoder_grad = last_gradients(first_4, total)
    decoder_grad, opposite = lax.optimization_barrier((decoder_grad, opposite))
    act_grad = unpack(slots, own, *second_3, second, third, opposite)
    act_grad = act_grad + other_core(act_grad)
    return (decoder_grad, act_grad.T)


def send_back(picked):
    return lax.all_to_all(picked, "dp", split_axis=1, concat_axis=1, tiled=True)


def pack_slots(grad_out, target, slots_all, pair_coeffs, pair_columns, source_row):
    slot_row = jnp.zeros((slots_all,), jnp.int32).at[target].set(source_row)
    used = jnp.zeros((slots_all,), jnp.bool_).at[target].set(True)
    send_rows = jnp.where(used[:, None], grad_out[slot_row], jnp.zeros((), grad_out.dtype))
    send_acts = jnp.zeros((slots_all, KPB), pair_coeffs.dtype).at[target].set(pair_coeffs)
    send_cols = jnp.zeros((slots_all, KPB), jnp.int32).at[target].set(pair_columns)
    return (send_rows, send_acts, send_cols)


def some_owners(decoder, grad_out, active_blocks, feature_idx, acts, block_slot):
    tok_rows, half_width = grad_out.shape
    owners = lax.axis_size("dp")
    mean_load = tok_rows * ACT // owners
    owner_cap = mean_load + min(mean_load // 2, tok_rows - mean_load)
    block_cap = (owner_cap + 2) // 3
    block_ids = active_blocks.reshape(-1)
    pair_count = block_ids.shape[0]
    table_pos = jnp.arange(block_slot.shape[0], dtype=jnp.int32)
    slot_of = jnp.sum(
        jnp.where(block_ids[:, None] == table_pos[None, :], block_slot[None, :], 0), axis=1
    )
    pair_pos = jnp.arange(pair_count, dtype=jnp.int32)
    source_row = pair_pos // ACT
    pair_coeffs = acts.reshape(pair_count, KPB)
    pair_feats = feature_idx.reshape(pair_count, KPB)
    earlier = (block_ids[:, None] == block_ids[None, :]) & (pair_pos[None, :] < pair_pos[:, None])
    position = jnp.sum(earlier.astype(jnp.int32), axis=1)
    slot_cols = owners * block_cap
    target = slot_of % BLK_DEV * slot_cols + slot_of // BLK_DEV * block_cap + position
    slots_all = BLK_DEV * slot_cols
    send_rows, send_acts, send_cols = pack_slots(
        grad_out, target, slots_all, pair_coeffs, pair_feats, source_row
    )
    rows, coeffs, feature_pos = (
        lax.all_to_all(
            send_rows.reshape(BLK_DEV, slot_cols, half_width),
            "dp",
            split_axis=1,
            concat_axis=1,
            tiled=True,
        ),
        lax.all_to_all(
            send_acts.reshape(BLK_DEV, slot_cols, KPB),
            "dp",
            split_axis=1,
            concat_axis=1,
            tiled=True,
        ),
        lax.all_to_all(
            send_cols.reshape(BLK_DEV, slot_cols, KPB),
            "dp",
            split_axis=1,
            concat_axis=1,
            tiled=True,
        ),
    )
    weights = decoder.reshape(BLK_DEV, BW, half_width)
    scores = jnp.einsum("bnd,bfd->bnf", rows, weights, preferred_element_type=jnp.float32)
    picked = jnp.take_along_axis(scores, feature_pos, axis=2)
    returned = send_back(picked)
    feature_axis = jnp.arange(BW, dtype=jnp.int32)
    matches = feature_pos[..., None] == feature_axis
    dense = jnp.sum(jnp.where(matches, coeffs[..., None].astype(jnp.float32), 0.0), axis=2).astype(
        jnp.bfloat16
    )
    grads = jnp.einsum("bnf,bnd->bfd", dense, rows, preferred_element_type=jnp.float32)
    decoder_grad = grads.astype(jnp.bfloat16).reshape(BLK_DEV * BW, half_width)
    pair_vals = returned.reshape(slots_all, KPB)[target]
    act_grad = pair_vals.reshape(tok_rows, ACT * KPB)
    act_grad = lax.psum(act_grad, "width")
    return (decoder_grad, act_grad)


def per_device(*args):
    if lax.axis_size("dp") == ACT:
        return every_owner(*args)
    return some_owners(*args)


def solution(mesh):
    in_specs = (
        P(("groups", "dp"), "width"),
        P(("groups", "dp"), "width"),
        P(("groups", "dp"), None),
        P(("groups", "dp"), None),
        P(("groups", "dp"), None),
        P("groups"),
    )
    out_specs = (P(("groups", "dp"), "width"), P(("groups", "dp"), None))
    return jax.shard_map(
        per_device, mesh=mesh, in_specs=in_specs, out_specs=out_specs, check_vma=False
    )
```

```python
import functools

import jax
import jax.numpy as jnp
from jax import lax
from jax.experimental import pallas as pl
from jax.experimental.pallas import tpu as pltpu
from jax.sharding import PartitionSpec as P

BW = 128
BLK_DEV = 4
ACT = 8
KPB = 4
SMEM = pl.BlockSpec(memory_space=pltpu.SMEM)
VMEM = pl.BlockSpec(memory_space=pltpu.VMEM)
ANY = pl.BlockSpec(memory_space=pl.ANY)
HBM = pl.BlockSpec(memory_space=pltpu.HBM)


def limit(mebibytes):
    return pltpu.CompilerParams(vmem_limit_bytes=mebibytes * 2**20)


def kept(x):
    return pltpu.with_memory_space_constraint(x, pltpu.VMEM)


def far(x):
    return pltpu.with_memory_space_constraint(x, pltpu.HBM)


def ring_of(owners):
    return list(range(0, owners, 2)) + list(range(owners - 1, 0, -2))


def peer_at(distance, owners):
    me = lax.axis_index("dp")
    half_ring = owners // 2
    place = jnp.where(lax.rem(me, 2) == 0, lax.div(me, 2), owners - 1 - lax.div(me, 2))
    at = lax.rem(place + owners + distance, owners)
    return jnp.where(at < half_ring, 2 * at, 2 * (owners - 1 - at) + 1)


ROW_SHIFT = BLK_DEV * BW // 2
FACTS = ACT // 2 * 2 * KPB
LAST_FACTS = 16


def facts_for(owner_id, owner, first_row, feats, acts):
    mine = owner == owner_id
    rows = [
        jnp.sum(jnp.where(mine, first_row + feats[k], 0.0), axis=0, keepdims=True) - ROW_SHIFT
        for k in range(KPB)
    ]
    values = [
        jnp.sum(jnp.where(mine, acts[k], 0.0), axis=0, keepdims=True) for k in range(KPB)
    ]
    return jnp.concatenate(rows + values, axis=0)


def prepare_kernel(owners, *refs):
    sources, refs = refs[:5], refs[5:]
    outs, refs = refs[:6], refs[6:]
    first_left, first_right, left, right, own_facts, slots = outs
    block_slot, active, feats, acts, halves, wide_feats, wide_acts, sems = refs
    cut = halves.shape[2]
    copies = []
    for source, target in zip(sources[:4], (block_slot, active, feats, acts)):
        copies.append(pltpu.make_async_copy(source, target, sems.at[len(copies)]))
    for side in range(2):
        copies.append(
            pltpu.make_async_copy(
                sources[4].at[:, side * cut : (side + 1) * cut],
                halves.at[side],
                sems.at[len(copies)],
            )
        )
    for copy in copies:
        copy.start()
    for copy in copies[:4]:
        copy.wait()
    named = active[...]
    slot = jnp.zeros_like(named)
    for block in range(block_slot.shape[0]):
        slot = jnp.where(named == block, block_slot[block], slot)
    slots[...] = slot
    wide_feats[...] = feats[...].astype(jnp.float32)
    wide_acts[...] = acts[...].astype(jnp.float32)
    features = [wide_feats[pl.ds(k, ACT, stride=KPB), :] for k in range(KPB)]
    values = [wide_acts[pl.ds(k, ACT, stride=KPB), :] for k in range(KPB)]
    first_row = (slot % BLK_DEV * BW).astype(jnp.float32)

    def facts(distance):
        return facts_for(
            peer_at(distance, owners), slot // BLK_DEV, first_row, features, values
        )

    def store_facts(target, blocks):
        rows = jnp.concatenate(blocks, axis=0)
        target[target.shape[0] - rows.shape[0] :, :] = rows.astype(jnp.bfloat16)

    own_facts[...] = facts(0)
    opposite = facts(owners // 2)
    none = jnp.zeros_like(opposite)
    store_facts(first_left, [opposite, none])
    for target, sign in ((left, -1), (right, 1)):
        store_facts(target, [facts(sign * d) for d in range(1, owners // 2)] + [none])
    tok_rows = halves.shape[1]
    for side, targets in ((0, (first_left, left)), (1, (first_right, right))):
        copies[4 + side].wait()
        for j in range(cut // 128):
            part = halves[side, :, j * 128 : (j + 1) * 128]
            for target in targets:
                target[j * tok_rows : (j + 1) * tok_rows, :] = part


def prepare(block_slot, active_blocks, feature_idx, acts, grad_out, owners):
    tok_rows, width = grad_out.shape
    plain = width // 256 * tok_rows

    def piece(extra):
        return pltpu.VMEM((plain + extra, 128), grad_out.dtype)

    return pl.pallas_call(
        functools.partial(prepare_kernel, owners),
        out_shape=(
            piece(LAST_FACTS),
            piece(0),
            piece(FACTS),
            piece(FACTS),
            pltpu.VMEM((2 * KPB, tok_rows), jnp.float32),
            pltpu.VMEM((ACT, tok_rows), jnp.int32),
        ),
        in_specs=[HBM] * 5,
        out_specs=(VMEM,) * 6,
        scratch_shapes=[
            pltpu.SMEM(block_slot.shape, jnp.int32),
            pltpu.VMEM((ACT, tok_rows), jnp.int32),
            pltpu.VMEM((ACT * KPB, tok_rows), jnp.int32),
            pltpu.VMEM((ACT * KPB, tok_rows), acts.dtype),
            pltpu.VMEM((2, tok_rows, width // 2), grad_out.dtype),
            pltpu.VMEM((ACT * KPB, tok_rows), jnp.float32),
            pltpu.VMEM((ACT * KPB, tok_rows), jnp.float32),
            pltpu.SemaphoreType.DMA((6,)),
        ],
        compiler_params=limit(8),
        name="prepare",
    )(far(block_slot), far(active_blocks.T), far(feature_idx.T), far(acts.T), far(grad_out))


def fetch_kernel(source, target, sem):
    copy = pltpu.make_async_copy(source, target, sem)
    copy.start()
    copy.wait()


def fetch(x):
    return pl.pallas_call(
        fetch_kernel,
        out_shape=pltpu.VMEM(x.shape, x.dtype),
        in_specs=[HBM],
        out_specs=VMEM,
        scratch_shapes=[pltpu.SemaphoreType.DMA],
        compiler_params=limit(8),
        name="fetch",
    )(far(x))


def block_and_rows(here):
    at_row = here[:KPB].astype(jnp.int32) + ROW_SHIFT
    return at_row[:1] // BW, at_row % BW


def row_axis_of(tok_rows):
    return lax.broadcasted_iota(jnp.int32, (BW, tok_rows), 0)


def coefficients(here):
    block, feats = block_and_rows(here)
    row_axis = row_axis_of(here.shape[1])
    dense = jnp.zeros(row_axis.shape, jnp.float32)
    for k in range(KPB):
        dense = jnp.where(row_axis == feats[k : k + 1], here[KPB + k : KPB + k + 1], dense)
    parts = [jnp.where(block == b, dense, 0.0) for b in range(BLK_DEV)]
    return jnp.concatenate(parts, axis=0).astype(jnp.bfloat16)


def pick(scores, here):
    block, feats = block_and_rows(here)
    row_axis = row_axis_of(here.shape[1])
    mine = scores[:BW]
    for b in range(1, BLK_DEV):
        mine = jnp.where(block == b, scores[b * BW : (b + 1) * BW], mine)
    return [
        jnp.sum(jnp.where(row_axis == feats[k : k + 1], mine, 0.0), axis=0, keepdims=True)
        for k in range(KPB)
    ]


def facts_in(piece, distance, tok_rows):
    facts = piece[piece.shape[0] - FACTS :, :].astype(jnp.float32)
    return facts[(abs(distance) - 1) * 2 * KPB : abs(distance) * 2 * KPB]


def columns_of(pieces, tok_rows, parts):
    rows = [
        jnp.concatenate([piece[j * tok_rows : (j + 1) * tok_rows, :] for j in parts], axis=1)
        for piece in pieces
    ]
    return jnp.concatenate(rows, axis=0) if len(rows) > 1 else rows[0]


def picks_of(facts, decoder, pieces):
    picks = []
    tok_rows = facts[0].shape[1]
    cut = decoder.shape[1] // 2
    for first in range(0, len(facts), 2):
        count = min(2, len(facts) - first)
        scores = None
        for side in range(2):
            part = lax.dot_general(
                decoder[:, side * cut : (side + 1) * cut],
                columns_of(
                    pieces[2 * first + side : 2 * (first + count) : 2],
                    tok_rows,
                    range(cut // 128),
                ),
                (((1,), (1,)), ((), ())),
                preferred_element_type=jnp.float32,
            )
            scores = part if scores is None else scores + part
        for i in range(first, first + count):
            here = scores[:, (i - first) * tok_rows : (i - first + 1) * tok_rows]
            picks.append(jnp.concatenate(pick(here, facts[i]) * 2, axis=0))
    return picks


def gradient_blocks(facts, pieces, width):
    tok_rows = facts[0].shape[1]
    cut = width // 2
    dense = jnp.concatenate([coefficients(here) for here in facts], axis=1)
    for side in range(2):
        for j in range(0, cut // 128, 2):
            rows = columns_of(pieces[side::2], tok_rows, (j, j + 1))
            part = jnp.dot(dense, rows, preferred_element_type=jnp.float32)
            yield slice(side * cut + j * 128, side * cut + (j + 2) * 128), part


def last_facts_in(piece):
    return piece[piece.shape[0] - LAST_FACTS :, :].astype(jnp.float32)[: 2 * KPB]


def facts_of(distances, own_facts, pieces):
    facts = []
    for i, d in enumerate(distances):
        if d == 0:
            facts.append(own_facts[...])
        elif d == 4:
            facts.append(last_facts_in(pieces[2 * i]))
        else:
            facts.append(facts_in(pieces[2 * i + (d < 0)], d, own_facts.shape[1]))
    return facts


def scores_kernel(distances, split, decoder, own_facts, *refs):
    pieces, picked = refs[: 2 * len(distances)], refs[2 * len(distances) :]
    picks = picks_of(facts_of(distances, own_facts, pieces), decoder, pieces)
    if split:
        first = lax.axis_index("width") == 0
        picks = [jnp.where(first, *picks), jnp.where(first, *picks[::-1])]
    for target, values in zip(picked, picks):
        target[...] = values


def scores_of(distances, pairs, decoder, own_facts, split=False):
    pieces = [kept(piece) for pair in pairs for piece in pair]
    shape = pltpu.VMEM(own_facts.shape, jnp.float32)
    return pl.pallas_call(
        functools.partial(scores_kernel, distances, split),
        out_shape=(shape,) * len(distances),
        in_specs=[VMEM] * (2 + len(pieces)),
        out_specs=(VMEM,) * len(distances),
        compiler_params=limit(12),
        name="scores",
    )(kept(decoder), kept(own_facts), *pieces)


def half_kernel(decoder, piece, partial):
    cut = decoder.shape[1] // 2
    rows = columns_of([piece], partial.shape[1], range(cut // 128))
    partial[...] = lax.dot_general(
        decoder[:, :cut], rows, (((1,), (1,)), ((), ())), preferred_element_type=jnp.float32
    )


def half_scores(decoder, piece, tok_rows):
    return pl.pallas_call(
        half_kernel,
        out_shape=pltpu.VMEM((decoder.shape[0], tok_rows), jnp.float32),
        in_specs=[VMEM] * 2,
        out_specs=VMEM,
        compiler_params=limit(8),
        name="half_scores",
    )(kept(decoder), kept(piece))


def rest_kernel(decoder, partial, left, right, picked):
    cut = decoder.shape[1] // 2
    rows = columns_of([right], partial.shape[1], range(cut // 128))
    scores = partial[...] + lax.dot_general(
        decoder[:, cut:], rows, (((1,), (1,)), ((), ())), preferred_element_type=jnp.float32
    )
    picked[...] = jnp.concatenate(pick(scores, last_facts_in(left)) * 2, axis=0)


def rest_scores(decoder, partial, left, right):
    return pl.pallas_call(
        rest_kernel,
        out_shape=pltpu.VMEM((2 * KPB, partial.shape[1]), jnp.float32),
        in_specs=[VMEM] * 4,
        out_specs=VMEM,
        compiler_params=limit(8),
        name="rest_scores",
    )(kept(decoder), kept(partial), kept(left), kept(right))


def gradients_kernel(distances, own_facts, *refs):
    pieces, refs = refs[: 2 * len(distances)], refs[2 * len(distances) :]
    total = refs[-1]
    facts = facts_of(distances, own_facts, pieces)
    for columns, part in gradient_blocks(facts, pieces, total.shape[1]):
        total[:, columns] = part if len(refs) == 1 else refs[0][:, columns] + part


def gradients_of(distances, pairs, own_facts, shape, total=None):
    operands = [kept(own_facts)] + [kept(piece) for pair in pairs for piece in pair]
    operands += [] if total is None else [kept(total)]
    return pl.pallas_call(
        functools.partial(gradients_kernel, distances),
        out_shape=pltpu.VMEM(shape, jnp.float32),
        in_specs=[VMEM] * len(operands),
        out_specs=VMEM,
        input_output_aliases={} if total is None else {len(operands) - 1: 0},
        compiler_params=limit(16),
        name="gradients",
    )(*operands)


def last_gradients_kernel(left, right, total, out, rounded, sems):
    copies = []
    facts = [last_facts_in(left)]
    for columns, part in gradient_blocks(facts, (left, right), out.shape[1]):
        rounded[:, columns] = (total[:, columns] + part).astype(out.dtype)
        copies.append(
            pltpu.make_async_copy(
                rounded.at[:, columns], out.at[:, columns], sems.at[len(copies)]
            )
        )
        copies[-1].start()
    for copy in copies:
        copy.wait()


def last_gradients(pair, total):
    return pl.pallas_call(
        last_gradients_kernel,
        out_shape=jax.ShapeDtypeStruct(total.shape, jnp.bfloat16),
        in_specs=[VMEM] * 3,
        out_specs=ANY,
        scratch_shapes=[
            pltpu.VMEM(total.shape, jnp.bfloat16),
            pltpu.SemaphoreType.DMA((total.shape[1] // 256,)),
        ],
        compiler_params=limit(16),
        name="last_gradients",
    )(kept(pair[0]), kept(pair[1]), kept(total))


def stamp_kernel(onward, back, for_onward, for_back, onward_out, back_out, rows, sems):
    start = onward.shape[0] - FACTS
    targets = (onward_out, back_out)
    for i, piece in enumerate((onward, back)):
        pltpu.make_async_copy(
            piece.at[start : start + 16, :], rows.at[i], sems.at[i]
        ).start()
    for i, values in enumerate((for_onward, for_back)):
        pltpu.make_async_copy(
            onward.at[start : start + 16, :], rows.at[i], sems.at[i]
        ).wait()
        value = values[:KPB]
        high = value.astype(jnp.bfloat16).astype(jnp.float32)
        low = value - high
        facts = rows[i].astype(jnp.float32)[2 * KPB :]
        rows[i] = jnp.concatenate([high, low, facts], axis=0).astype(jnp.bfloat16)
        pltpu.make_async_copy(
            rows.at[i], targets[i].at[start : start + 16, :], sems.at[2 + i]
        ).start()
    for i in range(2):
        pltpu.make_async_copy(
            rows.at[i], targets[i].at[start : start + 16, :], sems.at[2 + i]
        ).wait()


def stamp(pieces, values):
    return pl.pallas_call(
        stamp_kernel,
        out_shape=tuple(pltpu.VMEM(piece.shape, piece.dtype) for piece in pieces),
        in_specs=[ANY, ANY, VMEM, VMEM],
        out_specs=(ANY, ANY),
        scratch_shapes=[
            pltpu.VMEM((2, 16, 128), jnp.bfloat16),
            pltpu.SemaphoreType.DMA((4,)),
        ],
        input_output_aliases={0: 0, 1: 1},
        compiler_params=limit(4),
        name="stamp",
    )(*[kept(piece) for piece in pieces], *[kept(value) for value in values])


def unpack_kernel(owners, slots, own, onward, back, second, third, opposite, out):
    owner = slots[...] // BLK_DEV
    start = onward.shape[0] - FACTS
    way = 1 - 2 * lax.axis_index("width")
    returned = [(0, own[...])]
    for distance, piece in ((-1, onward), (1, back)):
        rows = piece[start : start + 16, :].astype(jnp.float32)
        returned.append((distance, rows[:KPB] + rows[KPB : 2 * KPB]))
    returned += [(2 * way, second[...]), (3 * way, third[...]), (4, opposite[...])]
    mine = [owner == peer_at(distance, owners) for distance, _ in returned]
    for k in range(KPB):
        total = jnp.zeros(owner.shape, jnp.float32)
        for here, (_, values) in zip(mine, returned):
            total = jnp.where(here, values[k : k + 1, :], total)
        out[pl.ds(k, ACT, stride=KPB), :] = total


def unpack(slots, *returned):
    tok_rows = slots.shape[1]
    return pl.pallas_call(
        functools.partial(unpack_kernel, lax.axis_size("dp")),
        out_shape=pltpu.VMEM((ACT * KPB, tok_rows), jnp.float32),
        in_specs=[VMEM] * (1 + len(returned)),
        out_specs=VMEM,
        compiler_params=limit(4),
        name="unpack",
    )(kept(slots), *[kept(x) for x in returned])


def every_owner(decoder, grad_out, active_blocks, feature_idx, acts, block_slot):
    tok_rows = grad_out.shape[0]
    owners = lax.axis_size("dp")
    ring = ring_of(owners)

    def shift(x, by):
        pairs = [(ring[i], ring[(i + by) % owners]) for i in range(owners)]
        return lax.ppermute(x, "dp", pairs)

    def hop(pieces):
        left, right = pieces
        return shift(left, 1), shift(right, -1)

    def crossed(pieces):
        right, left = pieces
        return shift(right, 1), shift(left, -1)

    def other_core(x):
        return lax.ppermute(x, "width", ((0, 1), (1, 0)))

    def return_by(distance, x):
        pairs = []
        for i in range(owners):
            pairs.append((2 * ring[i], 2 * ring[(i - distance) % owners]))
            pairs.append((2 * ring[i] + 1, 2 * ring[(i + distance) % owners] + 1))
        return lax.ppermute(x, ("dp", "width"), pairs)

    first_left, first_right, left, right, own_facts, slots = prepare(
        block_slot, active_blocks, feature_idx, acts, grad_out, owners
    )
    first_1 = hop((first_left, first_right))
    second_1 = crossed((right, left))
    decoder = fetch(decoder)
    first_1, decoder = lax.optimization_barrier((first_1, decoder))
    first_2 = hop(first_1)
    second_2 = crossed(second_1)
    pairs = [(first_left, first_right), (first_1[0], second_1[0]), (second_1[1], first_1[1])]
    distances = (0, -1, 1)
    own, onward, back = scores_of(distances, pairs, decoder, own_facts)
    total = gradients_of(distances, pairs, own_facts, decoder.shape)
    first_3 = hop(first_2)
    second_2 = stamp(second_2, (back, onward))
    second_3 = crossed(second_2)
    pairs = [(first_2[0], second_2[0]), (second_2[1], first_2[1])]
    mine, others = scores_of((-2, 2), pairs, decoder, own_facts, True)
    total = gradients_of((-2, 2), pairs, own_facts, decoder.shape, total)
    second = mine + other_core(others)
    total, first_3, second = lax.optimization_barrier((total, first_3, second))
    second = return_by(2, jnp.concatenate([second, jnp.zeros((24, 128), jnp.float32)]))[:8]
    first_4 = hop(first_3)
    pairs = [(first_3[0], second_3[0]), (second_3[1], first_3[1])]
    mine, others = scores_of((-3, 3), pairs, decoder, own_facts, True)
    total = gradients_of((-3, 3), pairs, own_facts, decoder.shape, total)
    third = mine + other_core(others)
    total, third = lax.optimization_barrier((total, third))
    third = return_by(3, third)
    last_left, last_right = first_4
    total, last_left = lax.optimization_barrier((total, last_left))
    partial = half_scores(decoder, last_left, tok_rows)
    partial, last_right = lax.optimization_barrier((partial, last_right))
    opposite = rest_scores(decoder, partial, last_left, last_right)
    first_4 = last_left, last_right
    opposite = shift(opposite, -owners // 2)
    total, third = lax.optimization_barrier((total, third))
    decoder_grad = last_gradients(first_4, total)
    decoder_grad, opposite = lax.optimization_barrier((decoder_grad, opposite))
    act_grad = unpack(slots, own, *second_3, second, third, opposite)
    act_grad = act_grad + other_core(act_grad)
    return (decoder_grad, act_grad.T)


def send_back(picked):
    return lax.all_to_all(picked, "dp", split_axis=1, concat_axis=1, tiled=True)


def pack_slots(grad_out, target, slots_all, pair_coeffs, pair_columns, source_row):
    slot_row = jnp.zeros((slots_all,), jnp.int32).at[target].set(source_row)
    used = jnp.zeros((slots_all,), jnp.bool_).at[target].set(True)
    send_rows = jnp.where(used[:, None], grad_out[slot_row], jnp.zeros((), grad_out.dtype))
    send_acts = jnp.zeros((slots_all, KPB), pair_coeffs.dtype).at[target].set(pair_coeffs)
    send_cols = jnp.zeros((slots_all, KPB), jnp.int32).at[target].set(pair_columns)
    return (send_rows, send_acts, send_cols)


def some_owners(decoder, grad_out, active_blocks, feature_idx, acts, block_slot):
    tok_rows, half_width = grad_out.shape
    owners = lax.axis_size("dp")
    mean_load = tok_rows * ACT // owners
    owner_cap = mean_load + min(mean_load // 2, tok_rows - mean_load)
    block_cap = (owner_cap + 2) // 3
    block_ids = active_blocks.reshape(-1)
    pair_count = block_ids.shape[0]
    table_pos = jnp.arange(block_slot.shape[0], dtype=jnp.int32)
    slot_of = jnp.sum(
        jnp.where(block_ids[:, None] == table_pos[None, :], block_slot[None, :], 0), axis=1
    )
    pair_pos = jnp.arange(pair_count, dtype=jnp.int32)
    source_row = pair_pos // ACT
    pair_coeffs = acts.reshape(pair_count, KPB)
    pair_feats = feature_idx.reshape(pair_count, KPB)
    earlier = (block_ids[:, None] == block_ids[None, :]) & (pair_pos[None, :] < pair_pos[:, None])
    position = jnp.sum(earlier.astype(jnp.int32), axis=1)
    slot_cols = owners * block_cap
    target = slot_of % BLK_DEV * slot_cols + slot_of // BLK_DEV * block_cap + position
    slots_all = BLK_DEV * slot_cols
    send_rows, send_acts, send_cols = pack_slots(
        grad_out, target, slots_all, pair_coeffs, pair_feats, source_row
    )
    rows, coeffs, feature_pos = (
        lax.all_to_all(
            send_rows.reshape(BLK_DEV, slot_cols, half_width),
            "dp",
            split_axis=1,
            concat_axis=1,
            tiled=True,
        ),
        lax.all_to_all(
            send_acts.reshape(BLK_DEV, slot_cols, KPB),
            "dp",
            split_axis=1,
            concat_axis=1,
            tiled=True,
        ),
        lax.all_to_all(
            send_cols.reshape(BLK_DEV, slot_cols, KPB),
            "dp",
            split_axis=1,
            concat_axis=1,
            tiled=True,
        ),
    )
    weights = decoder.reshape(BLK_DEV, BW, half_width)
    scores = jnp.einsum("bnd,bfd->bnf", rows, weights, preferred_element_type=jnp.float32)
    picked = jnp.take_along_axis(scores, feature_pos, axis=2)
    returned = send_back(picked)
    feature_axis = jnp.arange(BW, dtype=jnp.int32)
    matches = feature_pos[..., None] == feature_axis
    dense = jnp.sum(jnp.where(matches, coeffs[..., None].astype(jnp.float32), 0.0), axis=2).astype(
        jnp.bfloat16
    )
    grads = jnp.einsum("bnf,bnd->bfd", dense, rows, preferred_element_type=jnp.float32)
    decoder_grad = grads.astype(jnp.bfloat16).reshape(BLK_DEV * BW, half_width)
    pair_vals = returned.reshape(slots_all, KPB)[target]
    act_grad = pair_vals.reshape(tok_rows, ACT * KPB)
    act_grad = lax.psum(act_grad, "width")
    return (decoder_grad, act_grad)


def per_device(*args):
    if lax.axis_size("dp") == ACT:
        return every_owner(*args)
    return some_owners(*args)


def solution(mesh):
    in_specs = (
        P(("groups", "dp"), "width"),
        P(("groups", "dp"), "width"),
        P(("groups", "dp"), None),
        P(("groups", "dp"), None),
        P(("groups", "dp"), None),
        P("groups"),
    )
    out_specs = (P(("groups", "dp"), "width"), P(("groups", "dp"), None))
    return jax.shard_map(
        per_device, mesh=mesh, in_specs=in_specs, out_specs=out_specs, check_vma=False
    )
```

```python
import functools

import jax
import jax.numpy as jnp
from jax import lax
from jax.experimental import pallas as pl
from jax.experimental.pallas import tpu as pltpu
from jax.sharding import PartitionSpec as P

BW = 128
BLK_DEV = 4
ACT = 8
KPB = 4
SMEM = pl.BlockSpec(memory_space=pltpu.SMEM)
VMEM = pl.BlockSpec(memory_space=pltpu.VMEM)
ANY = pl.BlockSpec(memory_space=pl.ANY)
HBM = pl.BlockSpec(memory_space=pltpu.HBM)


def limit(mebibytes):
    return pltpu.CompilerParams(vmem_limit_bytes=mebibytes * 2**20)


def kept(x):
    return pltpu.with_memory_space_constraint(x, pltpu.VMEM)


def far(x):
    return pltpu.with_memory_space_constraint(x, pltpu.HBM)


def ring_of(owners):
    return list(range(0, owners, 2)) + list(range(owners - 1, 0, -2))


def peer_at(distance, owners):
    me = lax.axis_index("dp")
    half_ring = owners // 2
    place = jnp.where(lax.rem(me, 2) == 0, lax.div(me, 2), owners - 1 - lax.div(me, 2))
    at = lax.rem(place + owners + distance, owners)
    return jnp.where(at < half_ring, 2 * at, 2 * (owners - 1 - at) + 1)


ROW_SHIFT = BLK_DEV * BW // 2
FACTS = ACT // 2 * 2 * KPB
LAST_FACTS = 16


def facts_for(owner_id, owner, first_row, feats, acts):
    mine = owner == owner_id
    rows = [
        jnp.sum(jnp.where(mine, first_row + feats[k], 0.0), axis=0, keepdims=True) - ROW_SHIFT
        for k in range(KPB)
    ]
    values = [
        jnp.sum(jnp.where(mine, acts[k], 0.0), axis=0, keepdims=True) for k in range(KPB)
    ]
    return jnp.concatenate(rows + values, axis=0)


def prepare_kernel(owners, *refs):
    sources, refs = refs[:5], refs[5:]
    outs, refs = refs[:6], refs[6:]
    first_left, first_right, left, right, own_facts, slots = outs
    block_slot, active, feats, acts, halves, wide_feats, wide_acts, sems = refs
    cut = halves.shape[2]
    copies = []
    for source, target in zip(sources[:4], (block_slot, active, feats, acts)):
        copies.append(pltpu.make_async_copy(source, target, sems.at[len(copies)]))
    for side in range(2):
        copies.append(
            pltpu.make_async_copy(
                sources[4].at[:, side * cut : (side + 1) * cut],
                halves.at[side],
                sems.at[len(copies)],
            )
        )
    for copy in copies:
        copy.start()
    for copy in copies[:4]:
        copy.wait()
    named = active[...]
    slot = jnp.zeros_like(named)
    for block in range(block_slot.shape[0]):
        slot = jnp.where(named == block, block_slot[block], slot)
    slots[...] = slot
    wide_feats[...] = feats[...].astype(jnp.float32)
    wide_acts[...] = acts[...].astype(jnp.float32)
    features = [wide_feats[pl.ds(k, ACT, stride=KPB), :] for k in range(KPB)]
    values = [wide_acts[pl.ds(k, ACT, stride=KPB), :] for k in range(KPB)]
    first_row = (slot % BLK_DEV * BW).astype(jnp.float32)

    def facts(distance):
        return facts_for(
            peer_at(distance, owners), slot // BLK_DEV, first_row, features, values
        )

    def store_facts(target, blocks):
        rows = jnp.concatenate(blocks, axis=0)
        target[target.shape[0] - rows.shape[0] :, :] = rows.astype(jnp.bfloat16)

    own_facts[...] = facts(0)
    opposite = facts(owners // 2)
    none = jnp.zeros_like(opposite)
    store_facts(first_left, [opposite, none])
    for target, sign in ((left, -1), (right, 1)):
        store_facts(target, [facts(sign * d) for d in range(1, owners // 2)] + [none])
    tok_rows = halves.shape[1]
    for side, targets in ((0, (first_left, left)), (1, (first_right, right))):
        copies[4 + side].wait()
        for j in range(cut // 128):
            part = halves[side, :, j * 128 : (j + 1) * 128]
            for target in targets:
                target[j * tok_rows : (j + 1) * tok_rows, :] = part


def prepare(block_slot, active_blocks, feature_idx, acts, grad_out, owners):
    tok_rows, width = grad_out.shape
    plain = width // 256 * tok_rows

    def piece(extra):
        return pltpu.VMEM((plain + extra, 128), grad_out.dtype)

    return pl.pallas_call(
        functools.partial(prepare_kernel, owners),
        out_shape=(
            piece(LAST_FACTS),
            piece(0),
            piece(FACTS),
            piece(FACTS),
            pltpu.VMEM((2 * KPB, tok_rows), jnp.float32),
            pltpu.VMEM((ACT, tok_rows), jnp.int32),
        ),
        in_specs=[HBM] * 5,
        out_specs=(VMEM,) * 6,
        scratch_shapes=[
            pltpu.SMEM(block_slot.shape, jnp.int32),
            pltpu.VMEM((ACT, tok_rows), jnp.int32),
            pltpu.VMEM((ACT * KPB, tok_rows), jnp.int32),
            pltpu.VMEM((ACT * KPB, tok_rows), acts.dtype),
            pltpu.VMEM((2, tok_rows, width // 2), grad_out.dtype),
            pltpu.VMEM((ACT * KPB, tok_rows), jnp.float32),
            pltpu.VMEM((ACT * KPB, tok_rows), jnp.float32),
            pltpu.SemaphoreType.DMA((6,)),
        ],
        compiler_params=limit(8),
        name="prepare",
    )(far(block_slot), far(active_blocks.T), far(feature_idx.T), far(acts.T), far(grad_out))


def fetch_kernel(source, target, sem):
    copy = pltpu.make_async_copy(source, target, sem)
    copy.start()
    copy.wait()


def fetch(x):
    return pl.pallas_call(
        fetch_kernel,
        out_shape=pltpu.VMEM(x.shape, x.dtype),
        in_specs=[HBM],
        out_specs=VMEM,
        scratch_shapes=[pltpu.SemaphoreType.DMA],
        compiler_params=limit(8),
        name="fetch",
    )(far(x))


def block_and_rows(here):
    at_row = here[:KPB].astype(jnp.int32) + ROW_SHIFT
    return at_row[:1] // BW, at_row % BW


def row_axis_of(tok_rows):
    return lax.broadcasted_iota(jnp.int32, (BW, tok_rows), 0)


def coefficients(here):
    block, feats = block_and_rows(here)
    row_axis = row_axis_of(here.shape[1])
    dense = jnp.zeros(row_axis.shape, jnp.float32)
    for k in range(KPB):
        dense = jnp.where(row_axis == feats[k : k + 1], here[KPB + k : KPB + k + 1], dense)
    parts = [jnp.where(block == b, dense, 0.0) for b in range(BLK_DEV)]
    return jnp.concatenate(parts, axis=0).astype(jnp.bfloat16)


def pick(scores, here):
    block, feats = block_and_rows(here)
    row_axis = row_axis_of(here.shape[1])
    mine = scores[:BW]
    for b in range(1, BLK_DEV):
        mine = jnp.where(block == b, scores[b * BW : (b + 1) * BW], mine)
    return [
        jnp.sum(jnp.where(row_axis == feats[k : k + 1], mine, 0.0), axis=0, keepdims=True)
        for k in range(KPB)
    ]


def facts_in(piece, distance, tok_rows):
    facts = piece[piece.shape[0] - FACTS :, :].astype(jnp.float32)
    return facts[(abs(distance) - 1) * 2 * KPB : abs(distance) * 2 * KPB]


def columns_of(pieces, tok_rows, parts):
    rows = [
        jnp.concatenate([piece[j * tok_rows : (j + 1) * tok_rows, :] for j in parts], axis=1)
        for piece in pieces
    ]
    return jnp.concatenate(rows, axis=0) if len(rows) > 1 else rows[0]


def picks_of(facts, decoder, pieces):
    picks = []
    tok_rows = facts[0].shape[1]
    cut = decoder.shape[1] // 2
    for first in range(0, len(facts), 2):
        count = min(2, len(facts) - first)
        scores = None
        for side in range(2):
            part = lax.dot_general(
                decoder[:, side * cut : (side + 1) * cut],
                columns_of(
                    pieces[2 * first + side : 2 * (first + count) : 2],
                    tok_rows,
                    range(cut // 128),
                ),
                (((1,), (1,)), ((), ())),
                preferred_element_type=jnp.float32,
            )
            scores = part if scores is None else scores + part
        for i in range(first, first + count):
            here = scores[:, (i - first) * tok_rows : (i - first + 1) * tok_rows]
            picks.append(jnp.concatenate(pick(here, facts[i]) * 2, axis=0))
    return picks


def gradient_blocks(facts, pieces, width):
    tok_rows = facts[0].shape[1]
    cut = width // 2
    dense = jnp.concatenate([coefficients(here) for here in facts], axis=1)
    for side in range(2):
        for j in range(0, cut // 128, 2):
            rows = columns_of(pieces[side::2], tok_rows, (j, j + 1))
            part = jnp.dot(dense, rows, preferred_element_type=jnp.float32)
            yield slice(side * cut + j * 128, side * cut + (j + 2) * 128), part


def last_facts_in(piece):
    return piece[piece.shape[0] - LAST_FACTS :, :].astype(jnp.float32)[: 2 * KPB]


def facts_of(distances, own_facts, pieces):
    facts = []
    for i, d in enumerate(distances):
        if d == 0:
            facts.append(own_facts[...])
        elif d == 4:
            facts.append(last_facts_in(pieces[2 * i]))
        else:
            facts.append(facts_in(pieces[2 * i + (d < 0)], d, own_facts.shape[1]))
    return facts


def scores_kernel(distances, split, decoder, own_facts, *refs):
    pieces, picked = refs[: 2 * len(distances)], refs[2 * len(distances) :]
    picks = picks_of(facts_of(distances, own_facts, pieces), decoder, pieces)
    if split:
        first = lax.axis_index("width") == 0
        picks = [jnp.where(first, *picks), jnp.where(first, *picks[::-1])]
    for target, values in zip(picked, picks):
        target[...] = values


def scores_of(distances, pairs, decoder, own_facts, split=False):
    pieces = [kept(piece) for pair in pairs for piece in pair]
    shape = pltpu.VMEM(own_facts.shape, jnp.float32)
    return pl.pallas_call(
        functools.partial(scores_kernel, distances, split),
        out_shape=(shape,) * len(distances),
        in_specs=[VMEM] * (2 + len(pieces)),
        out_specs=(VMEM,) * len(distances),
        compiler_params=limit(12),
        name="scores",
    )(kept(decoder), kept(own_facts), *pieces)


def gradients_kernel(distances, own_facts, *refs):
    pieces, refs = refs[: 2 * len(distances)], refs[2 * len(distances) :]
    total = refs[-1]
    facts = facts_of(distances, own_facts, pieces)
    for columns, part in gradient_blocks(facts, pieces, total.shape[1]):
        total[:, columns] = part if len(refs) == 1 else refs[0][:, columns] + part


def gradients_of(distances, pairs, own_facts, shape, total=None):
    operands = [kept(own_facts)] + [kept(piece) for pair in pairs for piece in pair]
    operands += [] if total is None else [kept(total)]
    return pl.pallas_call(
        functools.partial(gradients_kernel, distances),
        out_shape=pltpu.VMEM(shape, jnp.float32),
        in_specs=[VMEM] * len(operands),
        out_specs=VMEM,
        input_output_aliases={} if total is None else {len(operands) - 1: 0},
        compiler_params=limit(16),
        name="gradients",
    )(*operands)


def last_gradients_kernel(distances, own_facts, *refs):
    pieces, (total, out, rounded, sems) = refs[:-4], refs[-4:]
    copies = []
    facts = facts_of(distances, own_facts, pieces)
    for columns, part in gradient_blocks(facts, pieces, out.shape[1]):
        rounded[:, columns] = (total[:, columns] + part).astype(out.dtype)
        copies.append(
            pltpu.make_async_copy(
                rounded.at[:, columns], out.at[:, columns], sems.at[len(copies)]
            )
        )
        copies[-1].start()
    for copy in copies:
        copy.wait()


def last_gradients(distances, pairs, own_facts, total):
    operands = [kept(own_facts)] + [kept(piece) for pair in pairs for piece in pair]
    operands.append(kept(total))
    return pl.pallas_call(
        functools.partial(last_gradients_kernel, distances),
        out_shape=jax.ShapeDtypeStruct(total.shape, jnp.bfloat16),
        in_specs=[VMEM] * len(operands),
        out_specs=ANY,
        scratch_shapes=[
            pltpu.VMEM(total.shape, jnp.bfloat16),
            pltpu.SemaphoreType.DMA((total.shape[1] // 256,)),
        ],
        compiler_params=limit(16),
        name="last_gradients",
    )(*operands)


def stamp_kernel(onward, back, for_onward, for_back, onward_out, back_out, rows, sems):
    start = onward.shape[0] - FACTS
    targets = (onward_out, back_out)
    for i, piece in enumerate((onward, back)):
        pltpu.make_async_copy(
            piece.at[start : start + 16, :], rows.at[i], sems.at[i]
        ).start()
    for i, values in enumerate((for_onward, for_back)):
        pltpu.make_async_copy(
            onward.at[start : start + 16, :], rows.at[i], sems.at[i]
        ).wait()
        value = values[:KPB]
        high = value.astype(jnp.bfloat16).astype(jnp.float32)
        low = value - high
        facts = rows[i].astype(jnp.float32)[2 * KPB :]
        rows[i] = jnp.concatenate([high, low, facts], axis=0).astype(jnp.bfloat16)
        pltpu.make_async_copy(
            rows.at[i], targets[i].at[start : start + 16, :], sems.at[2 + i]
        ).start()
    for i in range(2):
        pltpu.make_async_copy(
            rows.at[i], targets[i].at[start : start + 16, :], sems.at[2 + i]
        ).wait()


def stamp(pieces, values):
    return pl.pallas_call(
        stamp_kernel,
        out_shape=tuple(pltpu.VMEM(piece.shape, piece.dtype) for piece in pieces),
        in_specs=[ANY, ANY, VMEM, VMEM],
        out_specs=(ANY, ANY),
        scratch_shapes=[
            pltpu.VMEM((2, 16, 128), jnp.bfloat16),
            pltpu.SemaphoreType.DMA((4,)),
        ],
        input_output_aliases={0: 0, 1: 1},
        compiler_params=limit(4),
        name="stamp",
    )(*[kept(piece) for piece in pieces], *[kept(value) for value in values])


def unpack_kernel(owners, slots, own, onward, back, second, ahead, behind, opposite, out):
    owner = slots[...] // BLK_DEV
    start = onward.shape[0] - FACTS
    way = 1 - 2 * lax.axis_index("width")
    returned = [(0, own[...])]
    for distance, piece in ((-1, onward), (1, back)):
        rows = piece[start : start + 16, :].astype(jnp.float32)
        returned.append((distance, rows[:KPB] + rows[KPB : 2 * KPB]))
    returned += [(2 * way, second[...]), (3, ahead[...]), (-3, behind[...])]
    returned.append((4, opposite[...]))
    mine = [owner == peer_at(distance, owners) for distance, _ in returned]
    for k in range(KPB):
        total = jnp.zeros(owner.shape, jnp.float32)
        for here, (_, values) in zip(mine, returned):
            total = jnp.where(here, values[k : k + 1, :], total)
        out[pl.ds(k, ACT, stride=KPB), :] = total


def unpack(slots, *returned):
    tok_rows = slots.shape[1]
    return pl.pallas_call(
        functools.partial(unpack_kernel, lax.axis_size("dp")),
        out_shape=pltpu.VMEM((ACT * KPB, tok_rows), jnp.float32),
        in_specs=[VMEM] * (1 + len(returned)),
        out_specs=VMEM,
        compiler_params=limit(4),
        name="unpack",
    )(kept(slots), *[kept(x) for x in returned])


def every_owner(decoder, grad_out, active_blocks, feature_idx, acts, block_slot):
    tok_rows = grad_out.shape[0]
    owners = lax.axis_size("dp")
    ring = ring_of(owners)

    def shift(x, by):
        pairs = [(ring[i], ring[(i + by) % owners]) for i in range(owners)]
        return lax.ppermute(x, "dp", pairs)

    def hop(pieces):
        left, right = pieces
        return shift(left, 1), shift(right, -1)

    def crossed(pieces):
        right, left = pieces
        return shift(right, 1), shift(left, -1)

    def other_core(x):
        return lax.ppermute(x, "width", ((0, 1), (1, 0)))

    def return_by(distance, x):
        pairs = []
        for i in range(owners):
            pairs.append((2 * ring[i], 2 * ring[(i - distance) % owners]))
            pairs.append((2 * ring[i] + 1, 2 * ring[(i + distance) % owners] + 1))
        return lax.ppermute(x, ("dp", "width"), pairs)

    first_left, first_right, left, right, own_facts, slots = prepare(
        block_slot, active_blocks, feature_idx, acts, grad_out, owners
    )
    first_1 = hop((first_left, first_right))
    second_1 = crossed((right, left))
    decoder = fetch(decoder)
    first_1, decoder = lax.optimization_barrier((first_1, decoder))
    first_2 = hop(first_1)
    second_2 = crossed(second_1)
    pairs = [(first_left, first_right), (first_1[0], second_1[0]), (second_1[1], first_1[1])]
    distances = (0, -1, 1)
    own, onward, back = scores_of(distances, pairs, decoder, own_facts)
    total = gradients_of(distances, pairs, own_facts, decoder.shape)
    first_3 = hop(first_2)
    second_2 = stamp(second_2, (back, onward))
    second_3 = crossed(second_2)
    pairs = [(first_2[0], second_2[0]), (second_2[1], first_2[1])]
    mine, others = scores_of((-2, 2), pairs, decoder, own_facts, True)
    total = gradients_of((-2, 2), pairs, own_facts, decoder.shape, total)
    second = mine + other_core(others)
    total, first_3, second = lax.optimization_barrier((total, first_3, second))
    second = return_by(2, jnp.concatenate([second, jnp.zeros((24, 128), jnp.float32)]))[:8]
    first_4 = hop(first_3)
    pairs = [(first_3[0], second_3[0]), (second_3[1], first_3[1])]
    onward, back = scores_of((-3, 3), pairs, decoder, own_facts)
    ahead, behind = shift(onward, -3), shift(back, 3)
    (opposite,) = scores_of((4,), [first_4], decoder, own_facts)
    opposite = shift(opposite, -owners // 2)
    total, ahead, behind = lax.optimization_barrier((total, ahead, behind))
    decoder_grad = last_gradients((-3, 3, 4), pairs + [first_4], own_facts, total)
    decoder_grad, opposite = lax.optimization_barrier((decoder_grad, opposite))
    act_grad = unpack(slots, own, *second_3, second, ahead, behind, opposite)
    act_grad = act_grad + other_core(act_grad)
    return (decoder_grad, act_grad.T)


def send_back(picked):
    return lax.all_to_all(picked, "dp", split_axis=1, concat_axis=1, tiled=True)


def pack_slots(grad_out, target, slots_all, pair_coeffs, pair_columns, source_row):
    slot_row = jnp.zeros((slots_all,), jnp.int32).at[target].set(source_row)
    used = jnp.zeros((slots_all,), jnp.bool_).at[target].set(True)
    send_rows = jnp.where(used[:, None], grad_out[slot_row], jnp.zeros((), grad_out.dtype))
    send_acts = jnp.zeros((slots_all, KPB), pair_coeffs.dtype).at[target].set(pair_coeffs)
    send_cols = jnp.zeros((slots_all, KPB), jnp.int32).at[target].set(pair_columns)
    return (send_rows, send_acts, send_cols)


def some_owners(decoder, grad_out, active_blocks, feature_idx, acts, block_slot):
    tok_rows, half_width = grad_out.shape
    owners = lax.axis_size("dp")
    mean_load = tok_rows * ACT // owners
    owner_cap = mean_load + min(mean_load // 2, tok_rows - mean_load)
    block_cap = (owner_cap + 2) // 3
    block_ids = active_blocks.reshape(-1)
    pair_count = block_ids.shape[0]
    table_pos = jnp.arange(block_slot.shape[0], dtype=jnp.int32)
    slot_of = jnp.sum(
        jnp.where(block_ids[:, None] == table_pos[None, :], block_slot[None, :], 0), axis=1
    )
    pair_pos = jnp.arange(pair_count, dtype=jnp.int32)
    source_row = pair_pos // ACT
    pair_coeffs = acts.reshape(pair_count, KPB)
    pair_feats = feature_idx.reshape(pair_count, KPB)
    earlier = (block_ids[:, None] == block_ids[None, :]) & (pair_pos[None, :] < pair_pos[:, None])
    position = jnp.sum(earlier.astype(jnp.int32), axis=1)
    slot_cols = owners * block_cap
    target = slot_of % BLK_DEV * slot_cols + slot_of // BLK_DEV * block_cap + position
    slots_all = BLK_DEV * slot_cols
    send_rows, send_acts, send_cols = pack_slots(
        grad_out, target, slots_all, pair_coeffs, pair_feats, source_row
    )
    rows, coeffs, feature_pos = (
        lax.all_to_all(
            send_rows.reshape(BLK_DEV, slot_cols, half_width),
            "dp",
            split_axis=1,
            concat_axis=1,
            tiled=True,
        ),
        lax.all_to_all(
            send_acts.reshape(BLK_DEV, slot_cols, KPB),
            "dp",
            split_axis=1,
            concat_axis=1,
            tiled=True,
        ),
        lax.all_to_all(
            send_cols.reshape(BLK_DEV, slot_cols, KPB),
            "dp",
            split_axis=1,
            concat_axis=1,
            tiled=True,
        ),
    )
    weights = decoder.reshape(BLK_DEV, BW, half_width)
    scores = jnp.einsum("bnd,bfd->bnf", rows, weights, preferred_element_type=jnp.float32)
    picked = jnp.take_along_axis(scores, feature_pos, axis=2)
    returned = send_back(picked)
    feature_axis = jnp.arange(BW, dtype=jnp.int32)
    matches = feature_pos[..., None] == feature_axis
    dense = jnp.sum(jnp.where(matches, coeffs[..., None].astype(jnp.float32), 0.0), axis=2).astype(
        jnp.bfloat16
    )
    grads = jnp.einsum("bnf,bnd->bfd", dense, rows, preferred_element_type=jnp.float32)
    decoder_grad = grads.astype(jnp.bfloat16).reshape(BLK_DEV * BW, half_width)
    pair_vals = returned.reshape(slots_all, KPB)[target]
    act_grad = pair_vals.reshape(tok_rows, ACT * KPB)
    act_grad = lax.psum(act_grad, "width")
    return (decoder_grad, act_grad)


def per_device(*args):
    if lax.axis_size("dp") == ACT:
        return every_owner(*args)
    return some_owners(*args)


def solution(mesh):
    in_specs = (
        P(("groups", "dp"), "width"),
        P(("groups", "dp"), "width"),
        P(("groups", "dp"), None),
        P(("groups", "dp"), None),
        P(("groups", "dp"), None),
        P("groups"),
    )
    out_specs = (P(("groups", "dp"), "width"), P(("groups", "dp"), None))
    return jax.shard_map(
        per_device, mesh=mesh, in_specs=in_specs, out_specs=out_specs, check_vma=False
    )
```

```python
import functools

import jax
import jax.numpy as jnp
from jax import lax
from jax.experimental import pallas as pl
from jax.experimental.pallas import tpu as pltpu
from jax.sharding import PartitionSpec as P

BW = 128
BLK_DEV = 4
ACT = 8
KPB = 4
SMEM = pl.BlockSpec(memory_space=pltpu.SMEM)
VMEM = pl.BlockSpec(memory_space=pltpu.VMEM)
ANY = pl.BlockSpec(memory_space=pl.ANY)
HBM = pl.BlockSpec(memory_space=pltpu.HBM)


def limit(mebibytes):
    return pltpu.CompilerParams(vmem_limit_bytes=mebibytes * 2**20)


def kept(x):
    return pltpu.with_memory_space_constraint(x, pltpu.VMEM)


def far(x):
    return pltpu.with_memory_space_constraint(x, pltpu.HBM)


def ring_of(owners):
    return list(range(0, owners, 2)) + list(range(owners - 1, 0, -2))


def peer_at(distance, owners):
    me = lax.axis_index("dp")
    half_ring = owners // 2
    place = jnp.where(lax.rem(me, 2) == 0, lax.div(me, 2), owners - 1 - lax.div(me, 2))
    at = lax.rem(place + owners + distance, owners)
    return jnp.where(at < half_ring, 2 * at, 2 * (owners - 1 - at) + 1)


ROW_SHIFT = BLK_DEV * BW // 2
FACTS = ACT // 2 * 2 * KPB
LAST_FACTS = 16


def facts_for(owner_id, owner, first_row, feats, acts):
    mine = owner == owner_id
    rows = [
        jnp.sum(jnp.where(mine, first_row + feats[k], 0.0), axis=0, keepdims=True) - ROW_SHIFT
        for k in range(KPB)
    ]
    values = [
        jnp.sum(jnp.where(mine, acts[k], 0.0), axis=0, keepdims=True) for k in range(KPB)
    ]
    return jnp.concatenate(rows + values, axis=0)


def prepare_kernel(owners, *refs):
    sources, refs = refs[:5], refs[5:]
    outs, refs = refs[:6], refs[6:]
    first_left, first_right, left, right, own_facts, slots = outs
    block_slot, active, feats, acts, halves, wide_feats, wide_acts, sems = refs
    cut = halves.shape[2]
    copies = []
    for source, target in zip(sources[:4], (block_slot, active, feats, acts)):
        copies.append(pltpu.make_async_copy(source, target, sems.at[len(copies)]))
    for side in range(2):
        copies.append(
            pltpu.make_async_copy(
                sources[4].at[:, side * cut : (side + 1) * cut],
                halves.at[side],
                sems.at[len(copies)],
            )
        )
    for copy in copies:
        copy.start()
    for copy in copies[:4]:
        copy.wait()
    named = active[...]
    slot = jnp.zeros_like(named)
    for block in range(block_slot.shape[0]):
        slot = jnp.where(named == block, block_slot[block], slot)
    slots[...] = slot
    wide_feats[...] = feats[...].astype(jnp.float32)
    wide_acts[...] = acts[...].astype(jnp.float32)
    features = [wide_feats[pl.ds(k, ACT, stride=KPB), :] for k in range(KPB)]
    values = [wide_acts[pl.ds(k, ACT, stride=KPB), :] for k in range(KPB)]
    first_row = (slot % BLK_DEV * BW).astype(jnp.float32)

    def facts(distance):
        return facts_for(
            peer_at(distance, owners), slot // BLK_DEV, first_row, features, values
        )

    def store_facts(target, blocks):
        rows = jnp.concatenate(blocks, axis=0)
        target[target.shape[0] - rows.shape[0] :, :] = rows.astype(jnp.bfloat16)

    own_facts[...] = facts(0)
    opposite = facts(owners // 2)
    none = jnp.zeros_like(opposite)
    store_facts(first_left, [opposite, none])
    for target, sign in ((left, -1), (right, 1)):
        store_facts(target, [facts(sign * d) for d in range(1, owners // 2)] + [none])
    tok_rows = halves.shape[1]
    for side, targets in ((0, (first_left, left)), (1, (first_right, right))):
        copies[4 + side].wait()
        for j in range(cut // 128):
            part = halves[side, :, j * 128 : (j + 1) * 128]
            for target in targets:
                target[j * tok_rows : (j + 1) * tok_rows, :] = part


def prepare(block_slot, active_blocks, feature_idx, acts, grad_out, owners):
    tok_rows, width = grad_out.shape
    plain = width // 256 * tok_rows

    def piece(extra):
        return pltpu.VMEM((plain + extra, 128), grad_out.dtype)

    return pl.pallas_call(
        functools.partial(prepare_kernel, owners),
        out_shape=(
            piece(LAST_FACTS),
            piece(0),
            piece(FACTS),
            piece(FACTS),
            pltpu.VMEM((2 * KPB, tok_rows), jnp.float32),
            pltpu.VMEM((ACT, tok_rows), jnp.int32),
        ),
        in_specs=[HBM] * 5,
        out_specs=(VMEM,) * 6,
        scratch_shapes=[
            pltpu.SMEM(block_slot.shape, jnp.int32),
            pltpu.VMEM((ACT, tok_rows), jnp.int32),
            pltpu.VMEM((ACT * KPB, tok_rows), jnp.int32),
            pltpu.VMEM((ACT * KPB, tok_rows), acts.dtype),
            pltpu.VMEM((2, tok_rows, width // 2), grad_out.dtype),
            pltpu.VMEM((ACT * KPB, tok_rows), jnp.float32),
            pltpu.VMEM((ACT * KPB, tok_rows), jnp.float32),
            pltpu.SemaphoreType.DMA((6,)),
        ],
        compiler_params=limit(8),
        name="prepare",
    )(far(block_slot), far(active_blocks.T), far(feature_idx.T), far(acts.T), far(grad_out))


def fetch_kernel(source, target, sem):
    copy = pltpu.make_async_copy(source, target, sem)
    copy.start()
    copy.wait()


def fetch(x):
    return pl.pallas_call(
        fetch_kernel,
        out_shape=pltpu.VMEM(x.shape, x.dtype),
        in_specs=[HBM],
        out_specs=VMEM,
        scratch_shapes=[pltpu.SemaphoreType.DMA],
        compiler_params=limit(8),
        name="fetch",
    )(far(x))


def block_and_rows(here):
    at_row = here[:KPB].astype(jnp.int32) + ROW_SHIFT
    return at_row[:1] // BW, at_row % BW


def row_axis_of(tok_rows):
    return lax.broadcasted_iota(jnp.int32, (BW, tok_rows), 0)


def coefficients(here):
    block, feats = block_and_rows(here)
    row_axis = row_axis_of(here.shape[1])
    dense = jnp.zeros(row_axis.shape, jnp.float32)
    for k in range(KPB):
        dense = jnp.where(row_axis == feats[k : k + 1], here[KPB + k : KPB + k + 1], dense)
    parts = [jnp.where(block == b, dense, 0.0) for b in range(BLK_DEV)]
    return jnp.concatenate(parts, axis=0).astype(jnp.bfloat16)


def pick(scores, here):
    block, feats = block_and_rows(here)
    row_axis = row_axis_of(here.shape[1])
    mine = scores[:BW]
    for b in range(1, BLK_DEV):
        mine = jnp.where(block == b, scores[b * BW : (b + 1) * BW], mine)
    return [
        jnp.sum(jnp.where(row_axis == feats[k : k + 1], mine, 0.0), axis=0, keepdims=True)
        for k in range(KPB)
    ]


def facts_in(piece, distance, tok_rows):
    facts = piece[piece.shape[0] - FACTS :, :].astype(jnp.float32)
    return facts[(abs(distance) - 1) * 2 * KPB : abs(distance) * 2 * KPB]


def columns_of(pieces, tok_rows, parts):
    rows = [
        jnp.concatenate([piece[j * tok_rows : (j + 1) * tok_rows, :] for j in parts], axis=1)
        for piece in pieces
    ]
    return jnp.concatenate(rows, axis=0) if len(rows) > 1 else rows[0]


def picks_of(facts, decoder, pieces):
    picks = []
    tok_rows = facts[0].shape[1]
    cut = decoder.shape[1] // 2
    for first in range(0, len(facts), 2):
        count = min(2, len(facts) - first)
        scores = None
        for side in range(2):
            part = lax.dot_general(
                decoder[:, side * cut : (side + 1) * cut],
                columns_of(
                    pieces[2 * first + side : 2 * (first + count) : 2],
                    tok_rows,
                    range(cut // 128),
                ),
                (((1,), (1,)), ((), ())),
                preferred_element_type=jnp.float32,
            )
            scores = part if scores is None else scores + part
        for i in range(first, first + count):
            here = scores[:, (i - first) * tok_rows : (i - first + 1) * tok_rows]
            picks.append(jnp.concatenate(pick(here, facts[i]) * 2, axis=0))
    return picks


def gradient_blocks(facts, pieces, width):
    tok_rows = facts[0].shape[1]
    cut = width // 2
    dense = jnp.concatenate([coefficients(here) for here in facts], axis=1)
    for side in range(2):
        for j in range(0, cut // 128, 2):
            rows = columns_of(pieces[side::2], tok_rows, (j, j + 1))
            part = jnp.dot(dense, rows, preferred_element_type=jnp.float32)
            yield slice(side * cut + j * 128, side * cut + (j + 2) * 128), part


def last_facts_in(piece):
    return piece[piece.shape[0] - LAST_FACTS :, :].astype(jnp.float32)[: 2 * KPB]


def facts_of(distances, own_facts, pieces):
    facts = []
    for i, d in enumerate(distances):
        if d == 0:
            facts.append(own_facts[...])
        elif d == 4:
            facts.append(last_facts_in(pieces[2 * i]))
        else:
            facts.append(facts_in(pieces[2 * i + (d < 0)], d, own_facts.shape[1]))
    return facts


def scores_kernel(distances, split, decoder, own_facts, *refs):
    pieces, picked = refs[: 2 * len(distances)], refs[2 * len(distances) :]
    picks = picks_of(facts_of(distances, own_facts, pieces), decoder, pieces)
    if split:
        first = lax.axis_index("width") == 0
        picks = [jnp.where(first, *picks), jnp.where(first, *picks[::-1])]
    for target, values in zip(picked, picks):
        target[...] = values


def scores_of(distances, pairs, decoder, own_facts, split=False):
    pieces = [kept(piece) for pair in pairs for piece in pair]
    shape = pltpu.VMEM(own_facts.shape, jnp.float32)
    return pl.pallas_call(
        functools.partial(scores_kernel, distances, split),
        out_shape=(shape,) * len(distances),
        in_specs=[VMEM] * (2 + len(pieces)),
        out_specs=(VMEM,) * len(distances),
        compiler_params=limit(12),
        name="scores",
    )(kept(decoder), kept(own_facts), *pieces)


def gradients_kernel(distances, own_facts, *refs):
    pieces, refs = refs[: 2 * len(distances)], refs[2 * len(distances) :]
    total = refs[-1]
    facts = facts_of(distances, own_facts, pieces)
    for columns, part in gradient_blocks(facts, pieces, total.shape[1]):
        total[:, columns] = part if len(refs) == 1 else refs[0][:, columns] + part


def gradients_of(distances, pairs, own_facts, shape, total=None):
    operands = [kept(own_facts)] + [kept(piece) for pair in pairs for piece in pair]
    operands += [] if total is None else [kept(total)]
    return pl.pallas_call(
        functools.partial(gradients_kernel, distances),
        out_shape=pltpu.VMEM(shape, jnp.float32),
        in_specs=[VMEM] * len(operands),
        out_specs=VMEM,
        input_output_aliases={} if total is None else {len(operands) - 1: 0},
        compiler_params=limit(16),
        name="gradients",
    )(*operands)


def last_gradients_kernel(distances, own_facts, *refs):
    pieces, (total, out, rounded, sems) = refs[:-4], refs[-4:]
    copies = []
    facts = facts_of(distances, own_facts, pieces)
    for columns, part in gradient_blocks(facts, pieces, out.shape[1]):
        rounded[:, columns] = (total[:, columns] + part).astype(out.dtype)
        copies.append(
            pltpu.make_async_copy(
                rounded.at[:, columns], out.at[:, columns], sems.at[len(copies)]
            )
        )
        copies[-1].start()
    for copy in copies:
        copy.wait()


def last_gradients(distances, pairs, own_facts, total):
    operands = [kept(own_facts)] + [kept(piece) for pair in pairs for piece in pair]
    operands.append(kept(total))
    return pl.pallas_call(
        functools.partial(last_gradients_kernel, distances),
        out_shape=jax.ShapeDtypeStruct(total.shape, jnp.bfloat16),
        in_specs=[VMEM] * len(operands),
        out_specs=ANY,
        scratch_shapes=[
            pltpu.VMEM(total.shape, jnp.bfloat16),
            pltpu.SemaphoreType.DMA((total.shape[1] // 256,)),
        ],
        compiler_params=limit(16),
        name="last_gradients",
    )(*operands)


def stamp_kernel(onward, back, for_onward, for_back, onward_out, back_out, rows, sems):
    start = onward.shape[0] - FACTS
    targets = (onward_out, back_out)
    for i, piece in enumerate((onward, back)):
        pltpu.make_async_copy(
            piece.at[start : start + 16, :], rows.at[i], sems.at[i]
        ).start()
    for i, values in enumerate((for_onward, for_back)):
        pltpu.make_async_copy(
            onward.at[start : start + 16, :], rows.at[i], sems.at[i]
        ).wait()
        value = values[:KPB]
        high = value.astype(jnp.bfloat16).astype(jnp.float32)
        low = value - high
        facts = rows[i].astype(jnp.float32)[2 * KPB :]
        rows[i] = jnp.concatenate([high, low, facts], axis=0).astype(jnp.bfloat16)
        pltpu.make_async_copy(
            rows.at[i], targets[i].at[start : start + 16, :], sems.at[2 + i]
        ).start()
    for i in range(2):
        pltpu.make_async_copy(
            rows.at[i], targets[i].at[start : start + 16, :], sems.at[2 + i]
        ).wait()


def stamp(pieces, values):
    return pl.pallas_call(
        stamp_kernel,
        out_shape=tuple(pltpu.VMEM(piece.shape, piece.dtype) for piece in pieces),
        in_specs=[ANY, ANY, VMEM, VMEM],
        out_specs=(ANY, ANY),
        scratch_shapes=[
            pltpu.VMEM((2, 16, 128), jnp.bfloat16),
            pltpu.SemaphoreType.DMA((4,)),
        ],
        input_output_aliases={0: 0, 1: 1},
        compiler_params=limit(4),
        name="stamp",
    )(*[kept(piece) for piece in pieces], *[kept(value) for value in values])


def unpack_kernel(owners, slots, own, onward, back, second, ahead, behind, opposite, out):
    owner = slots[...] // BLK_DEV
    start = onward.shape[0] - FACTS
    way = 1 - 2 * lax.axis_index("width")
    returned = [(0, own[...])]
    for distance, piece in ((-1, onward), (1, back)):
        rows = piece[start : start + 16, :].astype(jnp.float32)
        returned.append((distance, rows[:KPB] + rows[KPB : 2 * KPB]))
    returned += [(2 * way, second[...]), (3, ahead[...]), (-3, behind[...])]
    returned.append((4, opposite[...]))
    mine = [owner == peer_at(distance, owners) for distance, _ in returned]
    for k in range(KPB):
        total = jnp.zeros(owner.shape, jnp.float32)
        for here, (_, values) in zip(mine, returned):
            total = jnp.where(here, values[k : k + 1, :], total)
        out[pl.ds(k, ACT, stride=KPB), :] = total


def unpack(slots, *returned):
    tok_rows = slots.shape[1]
    return pl.pallas_call(
        functools.partial(unpack_kernel, lax.axis_size("dp")),
        out_shape=pltpu.VMEM((ACT * KPB, tok_rows), jnp.float32),
        in_specs=[VMEM] * (1 + len(returned)),
        out_specs=VMEM,
        compiler_params=limit(4),
        name="unpack",
    )(kept(slots), *[kept(x) for x in returned])


def every_owner(decoder, grad_out, active_blocks, feature_idx, acts, block_slot):
    tok_rows = grad_out.shape[0]
    owners = lax.axis_size("dp")
    ring = ring_of(owners)

    def shift(x, by):
        pairs = [(ring[i], ring[(i + by) % owners]) for i in range(owners)]
        return lax.ppermute(x, "dp", pairs)

    def hop(pieces):
        left, right = pieces
        return shift(left, 1), shift(right, -1)

    def crossed(pieces):
        right, left = pieces
        return shift(right, 1), shift(left, -1)

    def other_core(x):
        return lax.ppermute(x, "width", ((0, 1), (1, 0)))

    def return_by(distance, x):
        pairs = []
        for i in range(owners):
            pairs.append((2 * ring[i], 2 * ring[(i - distance) % owners]))
            pairs.append((2 * ring[i] + 1, 2 * ring[(i + distance) % owners] + 1))
        return lax.ppermute(x, ("dp", "width"), pairs)

    first_left, first_right, left, right, own_facts, slots = prepare(
        block_slot, active_blocks, feature_idx, acts, grad_out, owners
    )
    first_1 = hop((first_left, first_right))
    second_1 = crossed((right, left))
    decoder = fetch(decoder)
    first_1, decoder = lax.optimization_barrier((first_1, decoder))
    first_2 = hop(first_1)
    second_2 = crossed(second_1)
    pairs = [(first_left, first_right), (first_1[0], second_1[0]), (second_1[1], first_1[1])]
    distances = (0, -1, 1)
    own, onward, back = scores_of(distances, pairs, decoder, own_facts)
    total = gradients_of(distances, pairs, own_facts, decoder.shape)
    first_3 = hop(first_2)
    second_2 = stamp(second_2, (back, onward))
    second_3 = crossed(second_2)
    pairs = [(first_2[0], second_2[0]), (second_2[1], first_2[1])]
    mine, others = scores_of((-2, 2), pairs, decoder, own_facts, True)
    total = gradients_of((-2, 2), pairs, own_facts, decoder.shape, total)
    second = mine + other_core(others)
    total, first_3, second = lax.optimization_barrier((total, first_3, second))
    second = return_by(2, jnp.concatenate([second, jnp.zeros((8, 128), jnp.float32)]))[:8]
    first_4 = hop(first_3)
    pairs = [(first_3[0], second_3[0]), (second_3[1], first_3[1])]
    (onward,) = scores_of((-3,), pairs[:1], decoder, own_facts)
    ahead = shift(onward, -3)
    (back,) = scores_of((3,), pairs[1:], decoder, own_facts)
    behind = shift(back, 3)
    (opposite,) = scores_of((4,), [first_4], decoder, own_facts)
    opposite = shift(opposite, -owners // 2)
    total, ahead, behind = lax.optimization_barrier((total, ahead, behind))
    decoder_grad = last_gradients((-3, 3, 4), pairs + [first_4], own_facts, total)
    decoder_grad, opposite = lax.optimization_barrier((decoder_grad, opposite))
    act_grad = unpack(slots, own, *second_3, second, ahead, behind, opposite)
    act_grad = act_grad + other_core(act_grad)
    return (decoder_grad, act_grad.T)


def send_back(picked):
    return lax.all_to_all(picked, "dp", split_axis=1, concat_axis=1, tiled=True)


def pack_slots(grad_out, target, slots_all, pair_coeffs, pair_columns, source_row):
    slot_row = jnp.zeros((slots_all,), jnp.int32).at[target].set(source_row)
    used = jnp.zeros((slots_all,), jnp.bool_).at[target].set(True)
    send_rows = jnp.where(used[:, None], grad_out[slot_row], jnp.zeros((), grad_out.dtype))
    send_acts = jnp.zeros((slots_all, KPB), pair_coeffs.dtype).at[target].set(pair_coeffs)
    send_cols = jnp.zeros((slots_all, KPB), jnp.int32).at[target].set(pair_columns)
    return (send_rows, send_acts, send_cols)


def some_owners(decoder, grad_out, active_blocks, feature_idx, acts, block_slot):
    tok_rows, half_width = grad_out.shape
    owners = lax.axis_size("dp")
    mean_load = tok_rows * ACT // owners
    owner_cap = mean_load + min(mean_load // 2, tok_rows - mean_load)
    block_cap = (owner_cap + 2) // 3
    block_ids = active_blocks.reshape(-1)
    pair_count = block_ids.shape[0]
    table_pos = jnp.arange(block_slot.shape[0], dtype=jnp.int32)
    slot_of = jnp.sum(
        jnp.where(block_ids[:, None] == table_pos[None, :], block_slot[None, :], 0), axis=1
    )
    pair_pos = jnp.arange(pair_count, dtype=jnp.int32)
    source_row = pair_pos // ACT
    pair_coeffs = acts.reshape(pair_count, KPB)
    pair_feats = feature_idx.reshape(pair_count, KPB)
    earlier = (block_ids[:, None] == block_ids[None, :]) & (pair_pos[None, :] < pair_pos[:, None])
    position = jnp.sum(earlier.astype(jnp.int32), axis=1)
    slot_cols = owners * block_cap
    target = slot_of % BLK_DEV * slot_cols + slot_of // BLK_DEV * block_cap + position
    slots_all = BLK_DEV * slot_cols
    send_rows, send_acts, send_cols = pack_slots(
        grad_out, target, slots_all, pair_coeffs, pair_feats, source_row
    )
    rows, coeffs, feature_pos = (
        lax.all_to_all(
            send_rows.reshape(BLK_DEV, slot_cols, half_width),
            "dp",
            split_axis=1,
            concat_axis=1,
            tiled=True,
        ),
        lax.all_to_all(
            send_acts.reshape(BLK_DEV, slot_cols, KPB),
            "dp",
            split_axis=1,
            concat_axis=1,
            tiled=True,
        ),
        lax.all_to_all(
            send_cols.reshape(BLK_DEV, slot_cols, KPB),
            "dp",
            split_axis=1,
            concat_axis=1,
            tiled=True,
        ),
    )
    weights = decoder.reshape(BLK_DEV, BW, half_width)
    scores = jnp.einsum("bnd,bfd->bnf", rows, weights, preferred_element_type=jnp.float32)
    picked = jnp.take_along_axis(scores, feature_pos, axis=2)
    returned = send_back(picked)
    feature_axis = jnp.arange(BW, dtype=jnp.int32)
    matches = feature_pos[..., None] == feature_axis
    dense = jnp.sum(jnp.where(matches, coeffs[..., None].astype(jnp.float32), 0.0), axis=2).astype(
        jnp.bfloat16
    )
    grads = jnp.einsum("bnf,bnd->bfd", dense, rows, preferred_element_type=jnp.float32)
    decoder_grad = grads.astype(jnp.bfloat16).reshape(BLK_DEV * BW, half_width)
    pair_vals = returned.reshape(slots_all, KPB)[target]
    act_grad = pair_vals.reshape(tok_rows, ACT * KPB)
    act_grad = lax.psum(act_grad, "width")
    return (decoder_grad, act_grad)


def per_device(*args):
    if lax.axis_size("dp") == ACT:
        return every_owner(*args)
    return some_owners(*args)


def solution(mesh):
    in_specs = (
        P(("groups", "dp"), "width"),
        P(("groups", "dp"), "width"),
        P(("groups", "dp"), None),
        P(("groups", "dp"), None),
        P(("groups", "dp"), None),
        P("groups"),
    )
    out_specs = (P(("groups", "dp"), "width"), P(("groups", "dp"), None))
    return jax.shard_map(
        per_device, mesh=mesh, in_specs=in_specs, out_specs=out_specs, check_vma=False
    )
```

```python
import functools

import jax
import jax.numpy as jnp
from jax import lax
from jax.experimental import pallas as pl
from jax.experimental.pallas import tpu as pltpu
from jax.sharding import PartitionSpec as P

BW = 128
BLK_DEV = 4
ACT = 8
KPB = 4
SMEM = pl.BlockSpec(memory_space=pltpu.SMEM)
VMEM = pl.BlockSpec(memory_space=pltpu.VMEM)
ANY = pl.BlockSpec(memory_space=pl.ANY)
HBM = pl.BlockSpec(memory_space=pltpu.HBM)


def limit(mebibytes):
    return pltpu.CompilerParams(vmem_limit_bytes=mebibytes * 2**20)


def kept(x):
    return pltpu.with_memory_space_constraint(x, pltpu.VMEM)


def far(x):
    return pltpu.with_memory_space_constraint(x, pltpu.HBM)


def ring_of(owners):
    return list(range(0, owners, 2)) + list(range(owners - 1, 0, -2))


def peer_at(distance, owners):
    me = lax.axis_index("dp")
    half_ring = owners // 2
    place = jnp.where(lax.rem(me, 2) == 0, lax.div(me, 2), owners - 1 - lax.div(me, 2))
    at = lax.rem(place + owners + distance, owners)
    return jnp.where(at < half_ring, 2 * at, 2 * (owners - 1 - at) + 1)


ROW_SHIFT = BLK_DEV * BW // 2
FACTS = ACT // 2 * 2 * KPB
LAST_FACTS = 16


def facts_for(owner_id, owner, first_row, feats, acts):
    mine = owner == owner_id
    rows = [
        jnp.sum(jnp.where(mine, first_row + feats[k], 0.0), axis=0, keepdims=True) - ROW_SHIFT
        for k in range(KPB)
    ]
    values = [
        jnp.sum(jnp.where(mine, acts[k], 0.0), axis=0, keepdims=True) for k in range(KPB)
    ]
    return jnp.concatenate(rows + values, axis=0)


def prepare_kernel(owners, *refs):
    sources, refs = refs[:5], refs[5:]
    outs, refs = refs[:6], refs[6:]
    first_left, first_right, left, right, own_facts, slots = outs
    block_slot, active, feats, acts, halves, wide_feats, wide_acts, sems = refs
    cut = halves.shape[2]
    copies = []
    for source, target in zip(sources[:4], (block_slot, active, feats, acts)):
        copies.append(pltpu.make_async_copy(source, target, sems.at[len(copies)]))
    for side in range(2):
        copies.append(
            pltpu.make_async_copy(
                sources[4].at[:, side * cut : (side + 1) * cut],
                halves.at[side],
                sems.at[len(copies)],
            )
        )
    for copy in copies:
        copy.start()
    for copy in copies[:4]:
        copy.wait()
    named = active[...]
    slot = jnp.zeros_like(named)
    for block in range(block_slot.shape[0]):
        slot = jnp.where(named == block, block_slot[block], slot)
    slots[...] = slot
    wide_feats[...] = feats[...].astype(jnp.float32)
    wide_acts[...] = acts[...].astype(jnp.float32)
    features = [wide_feats[pl.ds(k, ACT, stride=KPB), :] for k in range(KPB)]
    values = [wide_acts[pl.ds(k, ACT, stride=KPB), :] for k in range(KPB)]
    first_row = (slot % BLK_DEV * BW).astype(jnp.float32)

    def facts(distance):
        return facts_for(
            peer_at(distance, owners), slot // BLK_DEV, first_row, features, values
        )

    def store_facts(target, blocks):
        rows = jnp.concatenate(blocks, axis=0)
        target[target.shape[0] - rows.shape[0] :, :] = rows.astype(jnp.bfloat16)

    own_facts[...] = facts(0)
    opposite = facts(owners // 2)
    none = jnp.zeros_like(opposite)
    store_facts(first_left, [opposite, none])
    for target, sign in ((left, -1), (right, 1)):
        store_facts(target, [facts(sign * d) for d in range(1, owners // 2)] + [none])
    tok_rows = halves.shape[1]
    for side, targets in ((0, (first_left, left)), (1, (first_right, right))):
        copies[4 + side].wait()
        for j in range(cut // 128):
            part = halves[side, :, j * 128 : (j + 1) * 128]
            for target in targets:
                target[j * tok_rows : (j + 1) * tok_rows, :] = part


def prepare(block_slot, active_blocks, feature_idx, acts, grad_out, owners):
    tok_rows, width = grad_out.shape
    plain = width // 256 * tok_rows

    def piece(extra):
        return pltpu.VMEM((plain + extra, 128), grad_out.dtype)

    return pl.pallas_call(
        functools.partial(prepare_kernel, owners),
        out_shape=(
            piece(LAST_FACTS),
            piece(0),
            piece(FACTS),
            piece(FACTS),
            pltpu.VMEM((2 * KPB, tok_rows), jnp.float32),
            pltpu.VMEM((ACT, tok_rows), jnp.int32),
        ),
        in_specs=[HBM] * 5,
        out_specs=(VMEM,) * 6,
        scratch_shapes=[
            pltpu.SMEM(block_slot.shape, jnp.int32),
            pltpu.VMEM((ACT, tok_rows), jnp.int32),
            pltpu.VMEM((ACT * KPB, tok_rows), jnp.int32),
            pltpu.VMEM((ACT * KPB, tok_rows), acts.dtype),
            pltpu.VMEM((2, tok_rows, width // 2), grad_out.dtype),
            pltpu.VMEM((ACT * KPB, tok_rows), jnp.float32),
            pltpu.VMEM((ACT * KPB, tok_rows), jnp.float32),
            pltpu.SemaphoreType.DMA((6,)),
        ],
        compiler_params=limit(8),
        name="prepare",
    )(far(block_slot), far(active_blocks.T), far(feature_idx.T), far(acts.T), far(grad_out))


def fetch_kernel(source, target, sem):
    copy = pltpu.make_async_copy(source, target, sem)
    copy.start()
    copy.wait()


def fetch(x):
    return pl.pallas_call(
        fetch_kernel,
        out_shape=pltpu.VMEM(x.shape, x.dtype),
        in_specs=[HBM],
        out_specs=VMEM,
        scratch_shapes=[pltpu.SemaphoreType.DMA],
        compiler_params=limit(8),
        name="fetch",
    )(far(x))


def block_and_rows(here):
    at_row = here[:KPB].astype(jnp.int32) + ROW_SHIFT
    return at_row[:1] // BW, at_row % BW


def row_axis_of(tok_rows):
    return lax.broadcasted_iota(jnp.int32, (BW, tok_rows), 0)


def coefficients(here):
    block, feats = block_and_rows(here)
    row_axis = row_axis_of(here.shape[1])
    dense = jnp.zeros(row_axis.shape, jnp.float32)
    for k in range(KPB):
        dense = jnp.where(row_axis == feats[k : k + 1], here[KPB + k : KPB + k + 1], dense)
    parts = [jnp.where(block == b, dense, 0.0) for b in range(BLK_DEV)]
    return jnp.concatenate(parts, axis=0).astype(jnp.bfloat16)


def pick(scores, here):
    block, feats = block_and_rows(here)
    row_axis = row_axis_of(here.shape[1])
    mine = scores[:BW]
    for b in range(1, BLK_DEV):
        mine = jnp.where(block == b, scores[b * BW : (b + 1) * BW], mine)
    return [
        jnp.sum(jnp.where(row_axis == feats[k : k + 1], mine, 0.0), axis=0, keepdims=True)
        for k in range(KPB)
    ]


def facts_in(piece, distance, tok_rows):
    facts = piece[piece.shape[0] - FACTS :, :].astype(jnp.float32)
    return facts[(abs(distance) - 1) * 2 * KPB : abs(distance) * 2 * KPB]


def columns_of(pieces, tok_rows, parts):
    rows = [
        jnp.concatenate([piece[j * tok_rows : (j + 1) * tok_rows, :] for j in parts], axis=1)
        for piece in pieces
    ]
    return jnp.concatenate(rows, axis=0) if len(rows) > 1 else rows[0]


def picks_of(facts, decoder, pieces):
    picks = []
    tok_rows = facts[0].shape[1]
    cut = decoder.shape[1] // 2
    for first in range(0, len(facts), 2):
        count = min(2, len(facts) - first)
        scores = None
        for side in range(2):
            part = lax.dot_general(
                decoder[:, side * cut : (side + 1) * cut],
                columns_of(
                    pieces[2 * first + side : 2 * (first + count) : 2],
                    tok_rows,
                    range(cut // 128),
                ),
                (((1,), (1,)), ((), ())),
                preferred_element_type=jnp.float32,
            )
            scores = part if scores is None else scores + part
        for i in range(first, first + count):
            here = scores[:, (i - first) * tok_rows : (i - first + 1) * tok_rows]
            picks.append(jnp.concatenate(pick(here, facts[i]) * 2, axis=0))
    return picks


def gradient_blocks(facts, pieces, width):
    tok_rows = facts[0].shape[1]
    cut = width // 2
    dense = jnp.concatenate([coefficients(here) for here in facts], axis=1)
    for side in range(2):
        for j in range(0, cut // 128, 2):
            rows = columns_of(pieces[side::2], tok_rows, (j, j + 1))
            part = jnp.dot(dense, rows, preferred_element_type=jnp.float32)
            yield slice(side * cut + j * 128, side * cut + (j + 2) * 128), part


def last_facts_in(piece):
    return piece[piece.shape[0] - LAST_FACTS :, :].astype(jnp.float32)[: 2 * KPB]


def facts_of(distances, own_facts, pieces):
    facts = []
    for i, d in enumerate(distances):
        if d == 0:
            facts.append(own_facts[...])
        elif d == 4:
            facts.append(last_facts_in(pieces[2 * i]))
        else:
            facts.append(facts_in(pieces[2 * i + (d < 0)], d, own_facts.shape[1]))
    return facts


def scores_kernel(distances, split, decoder, own_facts, *refs):
    pieces, picked = refs[: 2 * len(distances)], refs[2 * len(distances) :]
    picks = picks_of(facts_of(distances, own_facts, pieces), decoder, pieces)
    if split:
        first = lax.axis_index("width") == 0
        picks = [jnp.where(first, *picks), jnp.where(first, *picks[::-1])]
    for target, values in zip(picked, picks):
        target[...] = values


def scores_of(distances, pairs, decoder, own_facts, split=False):
    pieces = [kept(piece) for pair in pairs for piece in pair]
    shape = pltpu.VMEM(own_facts.shape, jnp.float32)
    return pl.pallas_call(
        functools.partial(scores_kernel, distances, split),
        out_shape=(shape,) * len(distances),
        in_specs=[VMEM] * (2 + len(pieces)),
        out_specs=(VMEM,) * len(distances),
        compiler_params=limit(12),
        name="scores",
    )(kept(decoder), kept(own_facts), *pieces)


def gradients_kernel(distances, own_facts, *refs):
    pieces, refs = refs[: 2 * len(distances)], refs[2 * len(distances) :]
    total = refs[-1]
    facts = facts_of(distances, own_facts, pieces)
    for columns, part in gradient_blocks(facts, pieces, total.shape[1]):
        total[:, columns] = part if len(refs) == 1 else refs[0][:, columns] + part


def gradients_of(distances, pairs, own_facts, shape, total=None):
    operands = [kept(own_facts)] + [kept(piece) for pair in pairs for piece in pair]
    operands += [] if total is None else [kept(total)]
    return pl.pallas_call(
        functools.partial(gradients_kernel, distances),
        out_shape=pltpu.VMEM(shape, jnp.float32),
        in_specs=[VMEM] * len(operands),
        out_specs=VMEM,
        input_output_aliases={} if total is None else {len(operands) - 1: 0},
        compiler_params=limit(16),
        name="gradients",
    )(*operands)


def last_gradients_kernel(distances, own_facts, *refs):
    pieces, (total, out, rounded, sems) = refs[:-4], refs[-4:]
    copies = []
    facts = facts_of(distances, own_facts, pieces)
    for columns, part in gradient_blocks(facts, pieces, out.shape[1]):
        rounded[:, columns] = (total[:, columns] + part).astype(out.dtype)
        copies.append(
            pltpu.make_async_copy(
                rounded.at[:, columns], out.at[:, columns], sems.at[len(copies)]
            )
        )
        copies[-1].start()
    for copy in copies:
        copy.wait()


def last_gradients(distances, pairs, own_facts, total):
    operands = [kept(own_facts)] + [kept(piece) for pair in pairs for piece in pair]
    operands.append(kept(total))
    return pl.pallas_call(
        functools.partial(last_gradients_kernel, distances),
        out_shape=jax.ShapeDtypeStruct(total.shape, jnp.bfloat16),
        in_specs=[VMEM] * len(operands),
        out_specs=ANY,
        scratch_shapes=[
            pltpu.VMEM(total.shape, jnp.bfloat16),
            pltpu.SemaphoreType.DMA((total.shape[1] // 256,)),
        ],
        compiler_params=limit(16),
        name="last_gradients",
    )(*operands)


def stamp_kernel(piece, values, out, rows, sems):
    place = pl.ds(piece.shape[0] - FACTS, 16)
    load = pltpu.make_async_copy(piece.at[place, :], rows, sems.at[0])
    load.start()
    load.wait()
    value = values[:KPB]
    high = value.astype(jnp.bfloat16).astype(jnp.float32)
    facts = rows[...].astype(jnp.float32)[2 * KPB :]
    rows[...] = jnp.concatenate([high, value - high, facts], axis=0).astype(jnp.bfloat16)
    store = pltpu.make_async_copy(rows, out.at[place, :], sems.at[1])
    store.start()
    store.wait()


def stamp(piece, values):
    return pl.pallas_call(
        stamp_kernel,
        out_shape=pltpu.VMEM(piece.shape, piece.dtype),
        in_specs=[ANY, VMEM],
        out_specs=ANY,
        scratch_shapes=[
            pltpu.VMEM((16, 128), jnp.bfloat16),
            pltpu.SemaphoreType.DMA((2,)),
        ],
        input_output_aliases={0: 0},
        compiler_params=limit(4),
        name="stamp",
    )(kept(piece), kept(values))


def unpack_kernel(owners, slots, own, onward, back, second, ahead, behind, opposite, out):
    owner = slots[...] // BLK_DEV
    start = onward.shape[0] - FACTS
    way = 1 - 2 * lax.axis_index("width")
    returned = [(0, own[...])]
    for distance, piece in ((-1, onward), (1, back)):
        rows = piece[start : start + 16, :].astype(jnp.float32)
        returned.append((distance, rows[:KPB] + rows[KPB : 2 * KPB]))
    returned += [(2 * way, second[...]), (3, ahead[...]), (-3, behind[...])]
    returned.append((4, opposite[...]))
    mine = [owner == peer_at(distance, owners) for distance, _ in returned]
    for k in range(KPB):
        total = jnp.zeros(owner.shape, jnp.float32)
        for here, (_, values) in zip(mine, returned):
            total = jnp.where(here, values[k : k + 1, :], total)
        out[pl.ds(k, ACT, stride=KPB), :] = total


def unpack(slots, *returned):
    tok_rows = slots.shape[1]
    return pl.pallas_call(
        functools.partial(unpack_kernel, lax.axis_size("dp")),
        out_shape=pltpu.VMEM((ACT * KPB, tok_rows), jnp.float32),
        in_specs=[VMEM] * (1 + len(returned)),
        out_specs=VMEM,
        compiler_params=limit(4),
        name="unpack",
    )(kept(slots), *[kept(x) for x in returned])


def every_owner(decoder, grad_out, active_blocks, feature_idx, acts, block_slot):
    tok_rows = grad_out.shape[0]
    owners = lax.axis_size("dp")
    ring = ring_of(owners)

    def shift(x, by):
        pairs = [(ring[i], ring[(i + by) % owners]) for i in range(owners)]
        return lax.ppermute(x, "dp", pairs)

    def hop(pieces):
        left, right = pieces
        return shift(left, 1), shift(right, -1)

    def crossed(pieces):
        right, left = pieces
        return shift(right, 1), shift(left, -1)

    def other_core(x):
        return lax.ppermute(x, "width", ((0, 1), (1, 0)))

    def return_by(distance, x):
        pairs = []
        for i in range(owners):
            pairs.append((2 * ring[i], 2 * ring[(i - distance) % owners]))
            pairs.append((2 * ring[i] + 1, 2 * ring[(i + distance) % owners] + 1))
        return lax.ppermute(x, ("dp", "width"), pairs)

    first_left, first_right, left, right, own_facts, slots = prepare(
        block_slot, active_blocks, feature_idx, acts, grad_out, owners
    )
    first_1 = hop((first_left, first_right))
    second_1 = crossed((right, left))
    decoder = fetch(decoder)
    first_1, decoder = lax.optimization_barrier((first_1, decoder))
    first_2 = hop(first_1)
    second_2 = crossed(second_1)
    pairs = [(first_left, first_right), (first_1[0], second_1[0]), (second_1[1], first_1[1])]
    distances = (0, -1, 1)
    own, onward, back = scores_of(distances, pairs, decoder, own_facts)
    total = gradients_of(distances, pairs, own_facts, decoder.shape)
    first_3 = hop(first_2)
    right_2, left_2 = second_2
    total, right_2 = lax.optimization_barrier((total, right_2))
    second_2 = stamp(right_2, back), stamp(left_2, onward)
    second_3 = crossed(second_2)
    pairs = [(first_2[0], second_2[0]), (second_2[1], first_2[1])]
    mine, others = scores_of((-2, 2), pairs, decoder, own_facts, True)
    total = gradients_of((-2, 2), pairs, own_facts, decoder.shape, total)
    second = mine + other_core(others)
    total, first_3, second = lax.optimization_barrier((total, first_3, second))
    second = return_by(2, jnp.concatenate([second, jnp.zeros((24, 128), jnp.float32)]))[:8]
    first_4 = hop(first_3)
    pairs = [(first_3[0], second_3[0]), (second_3[1], first_3[1])]
    onward, back = scores_of((-3, 3), pairs, decoder, own_facts)
    ahead, behind = shift(onward, -3), shift(back, 3)
    (opposite,) = scores_of((4,), [first_4], decoder, own_facts)
    opposite = shift(opposite, -owners // 2)
    total, ahead, behind = lax.optimization_barrier((total, ahead, behind))
    decoder_grad = last_gradients((-3, 3, 4), pairs + [first_4], own_facts, total)
    decoder_grad, opposite = lax.optimization_barrier((decoder_grad, opposite))
    act_grad = unpack(slots, own, *second_3, second, ahead, behind, opposite)
    act_grad = act_grad + other_core(act_grad)
    return (decoder_grad, act_grad.T)


def send_back(picked):
    return lax.all_to_all(picked, "dp", split_axis=1, concat_axis=1, tiled=True)


def pack_slots(grad_out, target, slots_all, pair_coeffs, pair_columns, source_row):
    slot_row = jnp.zeros((slots_all,), jnp.int32).at[target].set(source_row)
    used = jnp.zeros((slots_all,), jnp.bool_).at[target].set(True)
    send_rows = jnp.where(used[:, None], grad_out[slot_row], jnp.zeros((), grad_out.dtype))
    send_acts = jnp.zeros((slots_all, KPB), pair_coeffs.dtype).at[target].set(pair_coeffs)
    send_cols = jnp.zeros((slots_all, KPB), jnp.int32).at[target].set(pair_columns)
    return (send_rows, send_acts, send_cols)


def some_owners(decoder, grad_out, active_blocks, feature_idx, acts, block_slot):
    tok_rows, half_width = grad_out.shape
    owners = lax.axis_size("dp")
    mean_load = tok_rows * ACT // owners
    owner_cap = mean_load + min(mean_load // 2, tok_rows - mean_load)
    block_cap = (owner_cap + 2) // 3
    block_ids = active_blocks.reshape(-1)
    pair_count = block_ids.shape[0]
    table_pos = jnp.arange(block_slot.shape[0], dtype=jnp.int32)
    slot_of = jnp.sum(
        jnp.where(block_ids[:, None] == table_pos[None, :], block_slot[None, :], 0), axis=1
    )
    pair_pos = jnp.arange(pair_count, dtype=jnp.int32)
    source_row = pair_pos // ACT
    pair_coeffs = acts.reshape(pair_count, KPB)
    pair_feats = feature_idx.reshape(pair_count, KPB)
    earlier = (block_ids[:, None] == block_ids[None, :]) & (pair_pos[None, :] < pair_pos[:, None])
    position = jnp.sum(earlier.astype(jnp.int32), axis=1)
    slot_cols = owners * block_cap
    target = slot_of % BLK_DEV * slot_cols + slot_of // BLK_DEV * block_cap + position
    slots_all = BLK_DEV * slot_cols
    send_rows, send_acts, send_cols = pack_slots(
        grad_out, target, slots_all, pair_coeffs, pair_feats, source_row
    )
    rows, coeffs, feature_pos = (
        lax.all_to_all(
            send_rows.reshape(BLK_DEV, slot_cols, half_width),
            "dp",
            split_axis=1,
            concat_axis=1,
            tiled=True,
        ),
        lax.all_to_all(
            send_acts.reshape(BLK_DEV, slot_cols, KPB),
            "dp",
            split_axis=1,
            concat_axis=1,
            tiled=True,
        ),
        lax.all_to_all(
            send_cols.reshape(BLK_DEV, slot_cols, KPB),
            "dp",
            split_axis=1,
            concat_axis=1,
            tiled=True,
        ),
    )
    weights = decoder.reshape(BLK_DEV, BW, half_width)
    scores = jnp.einsum("bnd,bfd->bnf", rows, weights, preferred_element_type=jnp.float32)
    picked = jnp.take_along_axis(scores, feature_pos, axis=2)
    returned = send_back(picked)
    feature_axis = jnp.arange(BW, dtype=jnp.int32)
    matches = feature_pos[..., None] == feature_axis
    dense = jnp.sum(jnp.where(matches, coeffs[..., None].astype(jnp.float32), 0.0), axis=2).astype(
        jnp.bfloat16
    )
    grads = jnp.einsum("bnf,bnd->bfd", dense, rows, preferred_element_type=jnp.float32)
    decoder_grad = grads.astype(jnp.bfloat16).reshape(BLK_DEV * BW, half_width)
    pair_vals = returned.reshape(slots_all, KPB)[target]
    act_grad = pair_vals.reshape(tok_rows, ACT * KPB)
    act_grad = lax.psum(act_grad, "width")
    return (decoder_grad, act_grad)


def per_device(*args):
    if lax.axis_size("dp") == ACT:
        return every_owner(*args)
    return some_owners(*args)


def solution(mesh):
    in_specs = (
        P(("groups", "dp"), "width"),
        P(("groups", "dp"), "width"),
        P(("groups", "dp"), None),
        P(("groups", "dp"), None),
        P(("groups", "dp"), None),
        P("groups"),
    )
    out_specs = (P(("groups", "dp"), "width"), P(("groups", "dp"), None))
    return jax.shard_map(
        per_device, mesh=mesh, in_specs=in_specs, out_specs=out_specs, check_vma=False
    )
```

```python
import functools

import jax
import jax.numpy as jnp
from jax import lax
from jax.experimental import pallas as pl
from jax.experimental.pallas import tpu as pltpu
from jax.sharding import PartitionSpec as P

BW = 128
BLK_DEV = 4
ACT = 8
KPB = 4
SMEM = pl.BlockSpec(memory_space=pltpu.SMEM)
VMEM = pl.BlockSpec(memory_space=pltpu.VMEM)
ANY = pl.BlockSpec(memory_space=pl.ANY)
HBM = pl.BlockSpec(memory_space=pltpu.HBM)


def limit(mebibytes):
    return pltpu.CompilerParams(vmem_limit_bytes=mebibytes * 2**20)


def kept(x):
    return pltpu.with_memory_space_constraint(x, pltpu.VMEM)


def far(x):
    return pltpu.with_memory_space_constraint(x, pltpu.HBM)


def ring_of(owners):
    return list(range(0, owners, 2)) + list(range(owners - 1, 0, -2))


def peer_at(distance, owners):
    me = lax.axis_index("dp")
    half_ring = owners // 2
    place = jnp.where(lax.rem(me, 2) == 0, lax.div(me, 2), owners - 1 - lax.div(me, 2))
    at = lax.rem(place + owners + distance, owners)
    return jnp.where(at < half_ring, 2 * at, 2 * (owners - 1 - at) + 1)


ROW_SHIFT = BLK_DEV * BW // 2
FACTS = ACT // 2 * 2 * KPB
LAST_FACTS = 16


def facts_for(owner_id, owner, first_row, feats, acts):
    mine = owner == owner_id
    rows = [
        jnp.sum(jnp.where(mine, first_row + feats[k], 0.0), axis=0, keepdims=True) - ROW_SHIFT
        for k in range(KPB)
    ]
    values = [
        jnp.sum(jnp.where(mine, acts[k], 0.0), axis=0, keepdims=True) for k in range(KPB)
    ]
    return jnp.concatenate(rows + values, axis=0)


def prepare_kernel(owners, *refs):
    sources, refs = refs[:5], refs[5:]
    outs, refs = refs[:6], refs[6:]
    first_left, first_right, left, right, own_facts, slots = outs
    block_slot, active, feats, acts, halves, wide_feats, wide_acts, sems = refs
    cut = halves.shape[2]
    copies = []
    for source, target in zip(sources[:4], (block_slot, active, feats, acts)):
        copies.append(pltpu.make_async_copy(source, target, sems.at[len(copies)]))
    for side in range(2):
        copies.append(
            pltpu.make_async_copy(
                sources[4].at[:, side * cut : (side + 1) * cut],
                halves.at[side],
                sems.at[len(copies)],
            )
        )
    for copy in copies:
        copy.start()
    for copy in copies[:4]:
        copy.wait()
    named = active[...]
    slot = jnp.zeros_like(named)
    for block in range(block_slot.shape[0]):
        slot = jnp.where(named == block, block_slot[block], slot)
    slots[...] = slot
    wide_feats[...] = feats[...].astype(jnp.float32)
    wide_acts[...] = acts[...].astype(jnp.float32)
    features = [wide_feats[pl.ds(k, ACT, stride=KPB), :] for k in range(KPB)]
    values = [wide_acts[pl.ds(k, ACT, stride=KPB), :] for k in range(KPB)]
    first_row = (slot % BLK_DEV * BW).astype(jnp.float32)

    def facts(distance):
        return facts_for(
            peer_at(distance, owners), slot // BLK_DEV, first_row, features, values
        )

    def store_facts(target, blocks):
        rows = jnp.concatenate(blocks, axis=0)
        target[target.shape[0] - rows.shape[0] :, :] = rows.astype(jnp.bfloat16)

    own_facts[...] = facts(0)
    opposite = facts(owners // 2)
    none = jnp.zeros_like(opposite)
    store_facts(first_left, [opposite, none])
    for target, sign in ((left, -1), (right, 1)):
        store_facts(target, [facts(sign * d) for d in range(1, owners // 2)] + [none])
    tok_rows = halves.shape[1]
    for side, targets in ((0, (first_left, left)), (1, (first_right, right))):
        copies[4 + side].wait()
        for j in range(cut // 128):
            part = halves[side, :, j * 128 : (j + 1) * 128]
            for target in targets:
                target[j * tok_rows : (j + 1) * tok_rows, :] = part


def prepare(block_slot, active_blocks, feature_idx, acts, grad_out, owners):
    tok_rows, width = grad_out.shape
    plain = width // 256 * tok_rows

    def piece(extra):
        return pltpu.VMEM((plain + extra, 128), grad_out.dtype)

    return pl.pallas_call(
        functools.partial(prepare_kernel, owners),
        out_shape=(
            piece(LAST_FACTS),
            piece(0),
            piece(FACTS),
            piece(FACTS),
            pltpu.VMEM((2 * KPB, tok_rows), jnp.float32),
            pltpu.VMEM((ACT, tok_rows), jnp.int32),
        ),
        in_specs=[HBM] * 5,
        out_specs=(VMEM,) * 6,
        scratch_shapes=[
            pltpu.SMEM(block_slot.shape, jnp.int32),
            pltpu.VMEM((ACT, tok_rows), jnp.int32),
            pltpu.VMEM((ACT * KPB, tok_rows), jnp.int32),
            pltpu.VMEM((ACT * KPB, tok_rows), acts.dtype),
            pltpu.VMEM((2, tok_rows, width // 2), grad_out.dtype),
            pltpu.VMEM((ACT * KPB, tok_rows), jnp.float32),
            pltpu.VMEM((ACT * KPB, tok_rows), jnp.float32),
            pltpu.SemaphoreType.DMA((6,)),
        ],
        compiler_params=limit(8),
        name="prepare",
    )(far(block_slot), far(active_blocks.T), far(feature_idx.T), far(acts.T), far(grad_out))


def fetch_kernel(source, target, sem):
    copy = pltpu.make_async_copy(source, target, sem)
    copy.start()
    copy.wait()


def fetch(x):
    return pl.pallas_call(
        fetch_kernel,
        out_shape=pltpu.VMEM(x.shape, x.dtype),
        in_specs=[HBM],
        out_specs=VMEM,
        scratch_shapes=[pltpu.SemaphoreType.DMA],
        compiler_params=limit(8),
        name="fetch",
    )(far(x))


def block_and_rows(here):
    at_row = here[:KPB].astype(jnp.int32) + ROW_SHIFT
    return at_row[:1] // BW, at_row % BW


def row_axis_of(tok_rows):
    return lax.broadcasted_iota(jnp.int32, (BW, tok_rows), 0)


def coefficients(here):
    block, feats = block_and_rows(here)
    row_axis = row_axis_of(here.shape[1])
    dense = jnp.zeros(row_axis.shape, jnp.float32)
    for k in range(KPB):
        dense = jnp.where(row_axis == feats[k : k + 1], here[KPB + k : KPB + k + 1], dense)
    parts = [jnp.where(block == b, dense, 0.0) for b in range(BLK_DEV)]
    return jnp.concatenate(parts, axis=0).astype(jnp.bfloat16)


def pick(scores, here):
    block, feats = block_and_rows(here)
    row_axis = row_axis_of(here.shape[1])
    mine = scores[:BW]
    for b in range(1, BLK_DEV):
        mine = jnp.where(block == b, scores[b * BW : (b + 1) * BW], mine)
    return [
        jnp.sum(jnp.where(row_axis == feats[k : k + 1], mine, 0.0), axis=0, keepdims=True)
        for k in range(KPB)
    ]


def facts_in(piece, distance, tok_rows):
    facts = piece[piece.shape[0] - FACTS :, :].astype(jnp.float32)
    return facts[(abs(distance) - 1) * 2 * KPB : abs(distance) * 2 * KPB]


def columns_of(pieces, tok_rows, parts):
    rows = [
        jnp.concatenate([piece[j * tok_rows : (j + 1) * tok_rows, :] for j in parts], axis=1)
        for piece in pieces
    ]
    return jnp.concatenate(rows, axis=0) if len(rows) > 1 else rows[0]


def picks_of(facts, decoder, pieces):
    picks = []
    tok_rows = facts[0].shape[1]
    cut = decoder.shape[1] // 2
    for first in range(0, len(facts), 2):
        count = min(2, len(facts) - first)
        scores = None
        for side in range(2):
            part = lax.dot_general(
                decoder[:, side * cut : (side + 1) * cut],
                columns_of(
                    pieces[2 * first + side : 2 * (first + count) : 2],
                    tok_rows,
                    range(cut // 128),
                ),
                (((1,), (1,)), ((), ())),
                preferred_element_type=jnp.float32,
            )
            scores = part if scores is None else scores + part
        for i in range(first, first + count):
            here = scores[:, (i - first) * tok_rows : (i - first + 1) * tok_rows]
            picks.append(jnp.concatenate(pick(here, facts[i]) * 2, axis=0))
    return picks


def gradient_blocks(facts, pieces, width):
    tok_rows = facts[0].shape[1]
    cut = width // 2
    dense = jnp.concatenate([coefficients(here) for here in facts], axis=1)
    for side in range(2):
        for j in range(0, cut // 128, 2):
            rows = columns_of(pieces[side::2], tok_rows, (j, j + 1))
            part = jnp.dot(dense, rows, preferred_element_type=jnp.float32)
            yield slice(side * cut + j * 128, side * cut + (j + 2) * 128), part


def last_facts_in(piece):
    return piece[piece.shape[0] - LAST_FACTS :, :].astype(jnp.float32)[: 2 * KPB]


def facts_of(distances, own_facts, pieces):
    facts = []
    for i, d in enumerate(distances):
        if d == 0:
            facts.append(own_facts[...])
        elif d == 4:
            facts.append(last_facts_in(pieces[2 * i]))
        else:
            facts.append(facts_in(pieces[2 * i + (d < 0)], d, own_facts.shape[1]))
    return facts


def scores_kernel(distances, split, decoder, own_facts, *refs):
    pieces, picked = refs[: 2 * len(distances)], refs[2 * len(distances) :]
    picks = picks_of(facts_of(distances, own_facts, pieces), decoder, pieces)
    if split:
        first = lax.axis_index("width") == 0
        picks = [jnp.where(first, *picks), jnp.where(first, *picks[::-1])]
    for target, values in zip(picked, picks):
        target[...] = values


def scores_of(distances, pairs, decoder, own_facts, split=False):
    pieces = [kept(piece) for pair in pairs for piece in pair]
    shape = pltpu.VMEM(own_facts.shape, jnp.float32)
    return pl.pallas_call(
        functools.partial(scores_kernel, distances, split),
        out_shape=(shape,) * len(distances),
        in_specs=[VMEM] * (2 + len(pieces)),
        out_specs=(VMEM,) * len(distances),
        compiler_params=limit(12),
        name="scores",
    )(kept(decoder), kept(own_facts), *pieces)


def gradients_kernel(distances, own_facts, *refs):
    pieces, refs = refs[: 2 * len(distances)], refs[2 * len(distances) :]
    total = refs[-1]
    facts = facts_of(distances, own_facts, pieces)
    for columns, part in gradient_blocks(facts, pieces, total.shape[1]):
        total[:, columns] = part if len(refs) == 1 else refs[0][:, columns] + part


def gradients_of(distances, pairs, own_facts, shape, total=None):
    operands = [kept(own_facts)] + [kept(piece) for pair in pairs for piece in pair]
    operands += [] if total is None else [kept(total)]
    return pl.pallas_call(
        functools.partial(gradients_kernel, distances),
        out_shape=pltpu.VMEM(shape, jnp.float32),
        in_specs=[VMEM] * len(operands),
        out_specs=VMEM,
        input_output_aliases={} if total is None else {len(operands) - 1: 0},
        compiler_params=limit(16),
        name="gradients",
    )(*operands)


def last_gradients_kernel(distances, own_facts, *refs):
    pieces, (total, out, rounded, sems) = refs[:-4], refs[-4:]
    copies = []
    facts = facts_of(distances, own_facts, pieces)
    for columns, part in gradient_blocks(facts, pieces, out.shape[1]):
        rounded[:, columns] = (total[:, columns] + part).astype(out.dtype)
        copies.append(
            pltpu.make_async_copy(
                rounded.at[:, columns], out.at[:, columns], sems.at[len(copies)]
            )
        )
        copies[-1].start()
    for copy in copies:
        copy.wait()


def last_gradients(distances, pairs, own_facts, total):
    operands = [kept(own_facts)] + [kept(piece) for pair in pairs for piece in pair]
    operands.append(kept(total))
    return pl.pallas_call(
        functools.partial(last_gradients_kernel, distances),
        out_shape=jax.ShapeDtypeStruct(total.shape, jnp.bfloat16),
        in_specs=[VMEM] * len(operands),
        out_specs=ANY,
        scratch_shapes=[
            pltpu.VMEM(total.shape, jnp.bfloat16),
            pltpu.SemaphoreType.DMA((total.shape[1] // 256,)),
        ],
        compiler_params=limit(16),
        name="last_gradients",
    )(*operands)


def stamp_kernel(onward, back, for_onward, for_back, onward_out, back_out, rows, sems):
    start = onward.shape[0] - FACTS
    targets = (onward_out, back_out)
    for i, piece in enumerate((onward, back)):
        pltpu.make_async_copy(
            piece.at[start : start + 16, :], rows.at[i], sems.at[i]
        ).start()
    for i, values in enumerate((for_onward, for_back)):
        pltpu.make_async_copy(
            onward.at[start : start + 16, :], rows.at[i], sems.at[i]
        ).wait()
        value = values[:KPB]
        high = value.astype(jnp.bfloat16).astype(jnp.float32)
        low = value - high
        facts = rows[i].astype(jnp.float32)[2 * KPB :]
        rows[i] = jnp.concatenate([high, low, facts], axis=0).astype(jnp.bfloat16)
        pltpu.make_async_copy(
            rows.at[i], targets[i].at[start : start + 16, :], sems.at[2 + i]
        ).start()
    for i in range(2):
        pltpu.make_async_copy(
            rows.at[i], targets[i].at[start : start + 16, :], sems.at[2 + i]
        ).wait()


def stamp(pieces, values):
    return pl.pallas_call(
        stamp_kernel,
        out_shape=tuple(pltpu.VMEM(piece.shape, piece.dtype) for piece in pieces),
        in_specs=[ANY, ANY, VMEM, VMEM],
        out_specs=(ANY, ANY),
        scratch_shapes=[
            pltpu.VMEM((2, 16, 128), jnp.bfloat16),
            pltpu.SemaphoreType.DMA((4,)),
        ],
        input_output_aliases={0: 0, 1: 1},
        compiler_params=limit(4),
        name="stamp",
    )(*[kept(piece) for piece in pieces], *[kept(value) for value in values])


def unpack_kernel(owners, slots, own, onward, back, second, ahead, behind, opposite, out):
    owner = slots[...] // BLK_DEV
    start = onward.shape[0] - FACTS
    way = 1 - 2 * lax.axis_index("width")
    returned = [(0, own[...])]
    for distance, piece in ((-1, onward), (1, back)):
        rows = piece[start : start + 16, :].astype(jnp.float32)
        returned.append((distance, rows[:KPB] + rows[KPB : 2 * KPB]))
    returned += [(2 * way, second[...]), (3, ahead[...]), (-3, behind[...])]
    returned.append((4, opposite[...]))
    mine = [owner == peer_at(distance, owners) for distance, _ in returned]
    for k in range(KPB):
        total = jnp.zeros(owner.shape, jnp.float32)
        for here, (_, values) in zip(mine, returned):
            total = jnp.where(here, values[k : k + 1, :], total)
        out[pl.ds(k, ACT, stride=KPB), :] = total


def unpack(slots, *returned):
    tok_rows = slots.shape[1]
    return pl.pallas_call(
        functools.partial(unpack_kernel, lax.axis_size("dp")),
        out_shape=pltpu.VMEM((ACT * KPB, tok_rows), jnp.float32),
        in_specs=[VMEM] * (1 + len(returned)),
        out_specs=VMEM,
        compiler_params=limit(4),
        name="unpack",
    )(kept(slots), *[kept(x) for x in returned])


def every_owner(decoder, grad_out, active_blocks, feature_idx, acts, block_slot):
    tok_rows = grad_out.shape[0]
    owners = lax.axis_size("dp")
    ring = ring_of(owners)

    def shift(x, by):
        pairs = [(ring[i], ring[(i + by) % owners]) for i in range(owners)]
        return lax.ppermute(x, "dp", pairs)

    def hop(pieces):
        left, right = pieces
        return shift(left, 1), shift(right, -1)

    def crossed(pieces):
        right, left = pieces
        return shift(right, 1), shift(left, -1)

    def other_core(x):
        return lax.ppermute(x, "width", ((0, 1), (1, 0)))

    def return_by(distance, x):
        pairs = []
        for i in range(owners):
            pairs.append((2 * ring[i], 2 * ring[(i - distance) % owners]))
            pairs.append((2 * ring[i] + 1, 2 * ring[(i + distance) % owners] + 1))
        return lax.ppermute(x, ("dp", "width"), pairs)

    first_left, first_right, left, right, own_facts, slots = prepare(
        block_slot, active_blocks, feature_idx, acts, grad_out, owners
    )
    first_1 = hop((first_left, first_right))
    second_1 = crossed((right, left))
    decoder = fetch(decoder)
    first_1, decoder = lax.optimization_barrier((first_1, decoder))
    first_2 = hop(first_1)
    second_2 = crossed(second_1)
    pairs = [(first_left, first_right), (first_1[0], second_1[0]), (second_1[1], first_1[1])]
    distances = (0, -1, 1)
    own, onward, back = scores_of(distances, pairs, decoder, own_facts)
    total = gradients_of(distances, pairs, own_facts, decoder.shape)
    first_3 = hop(first_2)
    second_2 = stamp(second_2, (back, onward))
    second_3 = crossed(second_2)
    pairs = [(first_2[0], second_2[0]), (second_2[1], first_2[1])]
    mine, others = scores_of((-2, 2), pairs, decoder, own_facts, True)
    total = gradients_of((-2, 2), pairs, own_facts, decoder.shape, total)
    second = mine + other_core(others)
    total, first_3, second = lax.optimization_barrier((total, first_3, second))
    second = return_by(2, jnp.concatenate([second, jnp.zeros((8, 128), jnp.float32)]))[:8]
    first_4 = hop(first_3)
    pairs = [(first_3[0], second_3[0]), (second_3[1], first_3[1])]
    onward, back = scores_of((-3, 3), pairs, decoder, own_facts)
    ahead, behind = shift(onward, -3), shift(back, 3)
    (opposite,) = scores_of((4,), [first_4], decoder, own_facts)
    opposite = shift(opposite, -owners // 2)
    total, ahead, behind = lax.optimization_barrier((total, ahead, behind))
    decoder_grad = last_gradients((-3, 3, 4), pairs + [first_4], own_facts, total)
    decoder_grad, opposite = lax.optimization_barrier((decoder_grad, opposite))
    act_grad = unpack(slots, own, *second_3, second, ahead, behind, opposite)
    act_grad = act_grad + other_core(act_grad)
    return (decoder_grad, act_grad.T)


def send_back(picked):
    return lax.all_to_all(picked, "dp", split_axis=1, concat_axis=1, tiled=True)


def pack_slots(grad_out, target, slots_all, pair_coeffs, pair_columns, source_row):
    slot_row = jnp.zeros((slots_all,), jnp.int32).at[target].set(source_row)
    used = jnp.zeros((slots_all,), jnp.bool_).at[target].set(True)
    send_rows = jnp.where(used[:, None], grad_out[slot_row], jnp.zeros((), grad_out.dtype))
    send_acts = jnp.zeros((slots_all, KPB), pair_coeffs.dtype).at[target].set(pair_coeffs)
    send_cols = jnp.zeros((slots_all, KPB), jnp.int32).at[target].set(pair_columns)
    return (send_rows, send_acts, send_cols)


def some_owners(decoder, grad_out, active_blocks, feature_idx, acts, block_slot):
    tok_rows, half_width = grad_out.shape
    owners = lax.axis_size("dp")
    mean_load = tok_rows * ACT // owners
    owner_cap = mean_load + min(mean_load // 2, tok_rows - mean_load)
    block_cap = (owner_cap + 2) // 3
    block_ids = active_blocks.reshape(-1)
    pair_count = block_ids.shape[0]
    table_pos = jnp.arange(block_slot.shape[0], dtype=jnp.int32)
    slot_of = jnp.sum(
        jnp.where(block_ids[:, None] == table_pos[None, :], block_slot[None, :], 0), axis=1
    )
    pair_pos = jnp.arange(pair_count, dtype=jnp.int32)
    source_row = pair_pos // ACT
    pair_coeffs = acts.reshape(pair_count, KPB)
    pair_feats = feature_idx.reshape(pair_count, KPB)
    earlier = (block_ids[:, None] == block_ids[None, :]) & (pair_pos[None, :] < pair_pos[:, None])
    position = jnp.sum(earlier.astype(jnp.int32), axis=1)
    slot_cols = owners * block_cap
    target = slot_of % BLK_DEV * slot_cols + slot_of // BLK_DEV * block_cap + position
    slots_all = BLK_DEV * slot_cols
    send_rows, send_acts, send_cols = pack_slots(
        grad_out, target, slots_all, pair_coeffs, pair_feats, source_row
    )
    rows, coeffs, feature_pos = (
        lax.all_to_all(
            send_rows.reshape(BLK_DEV, slot_cols, half_width),
            "dp",
            split_axis=1,
            concat_axis=1,
            tiled=True,
        ),
        lax.all_to_all(
            send_acts.reshape(BLK_DEV, slot_cols, KPB),
            "dp",
            split_axis=1,
            concat_axis=1,
            tiled=True,
        ),
        lax.all_to_all(
            send_cols.reshape(BLK_DEV, slot_cols, KPB),
            "dp",
            split_axis=1,
            concat_axis=1,
            tiled=True,
        ),
    )
    weights = decoder.reshape(BLK_DEV, BW, half_width)
    scores = jnp.einsum("bnd,bfd->bnf", rows, weights, preferred_element_type=jnp.float32)
    picked = jnp.take_along_axis(scores, feature_pos, axis=2)
    returned = send_back(picked)
    feature_axis = jnp.arange(BW, dtype=jnp.int32)
    matches = feature_pos[..., None] == feature_axis
    dense = jnp.sum(jnp.where(matches, coeffs[..., None].astype(jnp.float32), 0.0), axis=2).astype(
        jnp.bfloat16
    )
    grads = jnp.einsum("bnf,bnd->bfd", dense, rows, preferred_element_type=jnp.float32)
    decoder_grad = grads.astype(jnp.bfloat16).reshape(BLK_DEV * BW, half_width)
    pair_vals = returned.reshape(slots_all, KPB)[target]
    act_grad = pair_vals.reshape(tok_rows, ACT * KPB)
    act_grad = lax.psum(act_grad, "width")
    return (decoder_grad, act_grad)


def per_device(*args):
    if lax.axis_size("dp") == ACT:
        return every_owner(*args)
    return some_owners(*args)


def solution(mesh):
    in_specs = (
        P(("groups", "dp"), "width"),
        P(("groups", "dp"), "width"),
        P(("groups", "dp"), None),
        P(("groups", "dp"), None),
        P(("groups", "dp"), None),
        P("groups"),
    )
    out_specs = (P(("groups", "dp"), "width"), P(("groups", "dp"), None))
    return jax.shard_map(
        per_device, mesh=mesh, in_specs=in_specs, out_specs=out_specs, check_vma=False
    )
```

```python
import functools

import jax
import jax.numpy as jnp
from jax import lax
from jax.experimental import pallas as pl
from jax.experimental.pallas import tpu as pltpu
from jax.sharding import PartitionSpec as P

BW = 128
BLK_DEV = 4
ACT = 8
KPB = 4
SMEM = pl.BlockSpec(memory_space=pltpu.SMEM)
VMEM = pl.BlockSpec(memory_space=pltpu.VMEM)
ANY = pl.BlockSpec(memory_space=pl.ANY)
HBM = pl.BlockSpec(memory_space=pltpu.HBM)


def limit(mebibytes):
    return pltpu.CompilerParams(vmem_limit_bytes=mebibytes * 2**20)


def kept(x):
    return pltpu.with_memory_space_constraint(x, pltpu.VMEM)


def far(x):
    return pltpu.with_memory_space_constraint(x, pltpu.HBM)


def ring_of(owners):
    return [0] + list(range(1, owners, 2)) + list(range(owners - 2, 0, -2))


def peer_at(distance, owners):
    me = lax.axis_index("dp")
    half_ring = owners // 2
    up = lax.rem(me, 2) == 1
    place = jnp.where(up, lax.div(me, 2) + 1, lax.rem(owners - lax.div(me, 2), owners))
    at = lax.rem(place + owners + distance, owners)
    other = lax.rem(2 * (owners - at), 2 * owners)
    return jnp.where((at > 0) & (at <= half_ring), 2 * at - 1, other)


ROW_SHIFT = BLK_DEV * BW // 2
FACTS = ACT // 2 * 2 * KPB
LAST_FACTS = 16


def facts_for(owner_id, owner, first_row, feats, acts):
    mine = owner == owner_id
    rows = [
        jnp.sum(jnp.where(mine, first_row + feats[k], 0.0), axis=0, keepdims=True) - ROW_SHIFT
        for k in range(KPB)
    ]
    values = [
        jnp.sum(jnp.where(mine, acts[k], 0.0), axis=0, keepdims=True) for k in range(KPB)
    ]
    return jnp.concatenate(rows + values, axis=0)


def prepare_kernel(owners, *refs):
    sources, refs = refs[:5], refs[5:]
    outs, refs = refs[:6], refs[6:]
    first_left, first_right, left, right, own_facts, slots = outs
    block_slot, active, feats, acts, halves, wide_feats, wide_acts, sems = refs
    cut = halves.shape[2]
    copies = []
    for source, target in zip(sources[:4], (block_slot, active, feats, acts)):
        copies.append(pltpu.make_async_copy(source, target, sems.at[len(copies)]))
    for side in range(2):
        copies.append(
            pltpu.make_async_copy(
                sources[4].at[:, side * cut : (side + 1) * cut],
                halves.at[side],
                sems.at[len(copies)],
            )
        )
    for copy in copies:
        copy.start()
    for copy in copies[:4]:
        copy.wait()
    named = active[...]
    slot = jnp.zeros_like(named)
    for block in range(block_slot.shape[0]):
        slot = jnp.where(named == block, block_slot[block], slot)
    slots[...] = slot
    wide_feats[...] = feats[...].astype(jnp.float32)
    wide_acts[...] = acts[...].astype(jnp.float32)
    features = [wide_feats[pl.ds(k, ACT, stride=KPB), :] for k in range(KPB)]
    values = [wide_acts[pl.ds(k, ACT, stride=KPB), :] for k in range(KPB)]
    first_row = (slot % BLK_DEV * BW).astype(jnp.float32)

    def facts(distance):
        return facts_for(
            peer_at(distance, owners), slot // BLK_DEV, first_row, features, values
        )

    def store_facts(target, blocks):
        rows = jnp.concatenate(blocks, axis=0)
        target[target.shape[0] - rows.shape[0] :, :] = rows.astype(jnp.bfloat16)

    own_facts[...] = facts(0)
    opposite = facts(owners // 2)
    none = jnp.zeros_like(opposite)
    store_facts(first_left, [opposite, none])
    for target, sign in ((left, -1), (right, 1)):
        store_facts(target, [facts(sign * d) for d in range(1, owners // 2)] + [none])
    tok_rows = halves.shape[1]
    for side, targets in ((0, (first_left, left)), (1, (first_right, right))):
        copies[4 + side].wait()
        for j in range(cut // 128):
            part = halves[side, :, j * 128 : (j + 1) * 128]
            for target in targets:
                target[j * tok_rows : (j + 1) * tok_rows, :] = part


def prepare(block_slot, active_blocks, feature_idx, acts, grad_out, owners):
    tok_rows, width = grad_out.shape
    plain = width // 256 * tok_rows

    def piece(extra):
        return pltpu.VMEM((plain + extra, 128), grad_out.dtype)

    return pl.pallas_call(
        functools.partial(prepare_kernel, owners),
        out_shape=(
            piece(LAST_FACTS),
            piece(0),
            piece(FACTS),
            piece(FACTS),
            pltpu.VMEM((2 * KPB, tok_rows), jnp.float32),
            pltpu.VMEM((ACT, tok_rows), jnp.int32),
        ),
        in_specs=[HBM] * 5,
        out_specs=(VMEM,) * 6,
        scratch_shapes=[
            pltpu.SMEM(block_slot.shape, jnp.int32),
            pltpu.VMEM((ACT, tok_rows), jnp.int32),
            pltpu.VMEM((ACT * KPB, tok_rows), jnp.int32),
            pltpu.VMEM((ACT * KPB, tok_rows), acts.dtype),
            pltpu.VMEM((2, tok_rows, width // 2), grad_out.dtype),
            pltpu.VMEM((ACT * KPB, tok_rows), jnp.float32),
            pltpu.VMEM((ACT * KPB, tok_rows), jnp.float32),
            pltpu.SemaphoreType.DMA((6,)),
        ],
        compiler_params=limit(8),
        name="prepare",
    )(far(block_slot), far(active_blocks.T), far(feature_idx.T), far(acts.T), far(grad_out))


def fetch_kernel(source, target, sem):
    copy = pltpu.make_async_copy(source, target, sem)
    copy.start()
    copy.wait()


def fetch(x):
    return pl.pallas_call(
        fetch_kernel,
        out_shape=pltpu.VMEM(x.shape, x.dtype),
        in_specs=[HBM],
        out_specs=VMEM,
        scratch_shapes=[pltpu.SemaphoreType.DMA],
        compiler_params=limit(8),
        name="fetch",
    )(far(x))


def block_and_rows(here):
    at_row = here[:KPB].astype(jnp.int32) + ROW_SHIFT
    return at_row[:1] // BW, at_row % BW


def row_axis_of(tok_rows):
    return lax.broadcasted_iota(jnp.int32, (BW, tok_rows), 0)


def coefficients(here):
    block, feats = block_and_rows(here)
    row_axis = row_axis_of(here.shape[1])
    dense = jnp.zeros(row_axis.shape, jnp.float32)
    for k in range(KPB):
        dense = jnp.where(row_axis == feats[k : k + 1], here[KPB + k : KPB + k + 1], dense)
    parts = [jnp.where(block == b, dense, 0.0) for b in range(BLK_DEV)]
    return jnp.concatenate(parts, axis=0).astype(jnp.bfloat16)


def pick(scores, here):
    block, feats = block_and_rows(here)
    row_axis = row_axis_of(here.shape[1])
    mine = scores[:BW]
    for b in range(1, BLK_DEV):
        mine = jnp.where(block == b, scores[b * BW : (b + 1) * BW], mine)
    return [
        jnp.sum(jnp.where(row_axis == feats[k : k + 1], mine, 0.0), axis=0, keepdims=True)
        for k in range(KPB)
    ]


def facts_in(piece, distance, tok_rows):
    facts = piece[piece.shape[0] - FACTS :, :].astype(jnp.float32)
    return facts[(abs(distance) - 1) * 2 * KPB : abs(distance) * 2 * KPB]


def columns_of(pieces, tok_rows, parts):
    rows = [
        jnp.concatenate([piece[j * tok_rows : (j + 1) * tok_rows, :] for j in parts], axis=1)
        for piece in pieces
    ]
    return jnp.concatenate(rows, axis=0) if len(rows) > 1 else rows[0]


def picks_of(facts, decoder, pieces):
    picks = []
    tok_rows = facts[0].shape[1]
    cut = decoder.shape[1] // 2
    for first in range(0, len(facts), 2):
        count = min(2, len(facts) - first)
        scores = None
        for side in range(2):
            part = lax.dot_general(
                decoder[:, side * cut : (side + 1) * cut],
                columns_of(
                    pieces[2 * first + side : 2 * (first + count) : 2],
                    tok_rows,
                    range(cut // 128),
                ),
                (((1,), (1,)), ((), ())),
                preferred_element_type=jnp.float32,
            )
            scores = part if scores is None else scores + part
        for i in range(first, first + count):
            here = scores[:, (i - first) * tok_rows : (i - first + 1) * tok_rows]
            picks.append(jnp.concatenate(pick(here, facts[i]) * 2, axis=0))
    return picks


def gradient_blocks(facts, pieces, width):
    tok_rows = facts[0].shape[1]
    cut = width // 2
    dense = jnp.concatenate([coefficients(here) for here in facts], axis=1)
    for side in range(2):
        for j in range(0, cut // 128, 2):
            rows = columns_of(pieces[side::2], tok_rows, (j, j + 1))
            part = jnp.dot(dense, rows, preferred_element_type=jnp.float32)
            yield slice(side * cut + j * 128, side * cut + (j + 2) * 128), part


def last_facts_in(piece):
    return piece[piece.shape[0] - LAST_FACTS :, :].astype(jnp.float32)[: 2 * KPB]


def facts_of(distances, own_facts, pieces):
    facts = []
    for i, d in enumerate(distances):
        if d == 0:
            facts.append(own_facts[...])
        elif d == 4:
            facts.append(last_facts_in(pieces[2 * i]))
        else:
            facts.append(facts_in(pieces[2 * i + (d < 0)], d, own_facts.shape[1]))
    return facts


def scores_kernel(distances, split, decoder, own_facts, *refs):
    pieces, picked = refs[: 2 * len(distances)], refs[2 * len(distances) :]
    picks = picks_of(facts_of(distances, own_facts, pieces), decoder, pieces)
    if split:
        first = lax.axis_index("width") == 0
        picks = [jnp.where(first, *picks), jnp.where(first, *picks[::-1])]
    for target, values in zip(picked, picks):
        target[...] = values


def scores_of(distances, pairs, decoder, own_facts, split=False):
    pieces = [kept(piece) for pair in pairs for piece in pair]
    shape = pltpu.VMEM(own_facts.shape, jnp.float32)
    return pl.pallas_call(
        functools.partial(scores_kernel, distances, split),
        out_shape=(shape,) * len(distances),
        in_specs=[VMEM] * (2 + len(pieces)),
        out_specs=(VMEM,) * len(distances),
        compiler_params=limit(12),
        name="scores",
    )(kept(decoder), kept(own_facts), *pieces)


def gradients_kernel(distances, own_facts, *refs):
    pieces, refs = refs[: 2 * len(distances)], refs[2 * len(distances) :]
    total = refs[-1]
    facts = facts_of(distances, own_facts, pieces)
    for columns, part in gradient_blocks(facts, pieces, total.shape[1]):
        total[:, columns] = part if len(refs) == 1 else refs[0][:, columns] + part


def gradients_of(distances, pairs, own_facts, shape, total=None):
    operands = [kept(own_facts)] + [kept(piece) for pair in pairs for piece in pair]
    operands += [] if total is None else [kept(total)]
    return pl.pallas_call(
        functools.partial(gradients_kernel, distances),
        out_shape=pltpu.VMEM(shape, jnp.float32),
        in_specs=[VMEM] * len(operands),
        out_specs=VMEM,
        input_output_aliases={} if total is None else {len(operands) - 1: 0},
        compiler_params=limit(16),
        name="gradients",
    )(*operands)


def last_gradients_kernel(left, right, total, out, rounded, sems):
    copies = []
    facts = [last_facts_in(left)]
    for columns, part in gradient_blocks(facts, (left, right), out.shape[1]):
        rounded[:, columns] = (total[:, columns] + part).astype(out.dtype)
        copies.append(
            pltpu.make_async_copy(
                rounded.at[:, columns], out.at[:, columns], sems.at[len(copies)]
            )
        )
        copies[-1].start()
    for copy in copies:
        copy.wait()


def last_gradients(pair, total):
    return pl.pallas_call(
        last_gradients_kernel,
        out_shape=jax.ShapeDtypeStruct(total.shape, jnp.bfloat16),
        in_specs=[VMEM] * 3,
        out_specs=ANY,
        scratch_shapes=[
            pltpu.VMEM(total.shape, jnp.bfloat16),
            pltpu.SemaphoreType.DMA((total.shape[1] // 256,)),
        ],
        compiler_params=limit(16),
        name="last_gradients",
    )(kept(pair[0]), kept(pair[1]), kept(total))


def stamp_kernel(onward, back, for_onward, for_back, onward_out, back_out, rows, sems):
    start = onward.shape[0] - FACTS
    targets = (onward_out, back_out)
    for i, piece in enumerate((onward, back)):
        pltpu.make_async_copy(
            piece.at[start : start + 16, :], rows.at[i], sems.at[i]
        ).start()
    for i, values in enumerate((for_onward, for_back)):
        pltpu.make_async_copy(
            onward.at[start : start + 16, :], rows.at[i], sems.at[i]
        ).wait()
        value = values[:KPB]
        high = value.astype(jnp.bfloat16).astype(jnp.float32)
        low = value - high
        facts = rows[i].astype(jnp.float32)[2 * KPB :]
        rows[i] = jnp.concatenate([high, low, facts], axis=0).astype(jnp.bfloat16)
        pltpu.make_async_copy(
            rows.at[i], targets[i].at[start : start + 16, :], sems.at[2 + i]
        ).start()
    for i in range(2):
        pltpu.make_async_copy(
            rows.at[i], targets[i].at[start : start + 16, :], sems.at[2 + i]
        ).wait()


def stamp(pieces, values):
    return pl.pallas_call(
        stamp_kernel,
        out_shape=tuple(pltpu.VMEM(piece.shape, piece.dtype) for piece in pieces),
        in_specs=[ANY, ANY, VMEM, VMEM],
        out_specs=(ANY, ANY),
        scratch_shapes=[
            pltpu.VMEM((2, 16, 128), jnp.bfloat16),
            pltpu.SemaphoreType.DMA((4,)),
        ],
        input_output_aliases={0: 0, 1: 1},
        compiler_params=limit(4),
        name="stamp",
    )(*[kept(piece) for piece in pieces], *[kept(value) for value in values])


def unpack_kernel(owners, slots, own, onward, back, second, third, opposite, out):
    owner = slots[...] // BLK_DEV
    start = onward.shape[0] - FACTS
    way = 1 - 2 * lax.axis_index("width")
    returned = [(0, own[...])]
    for distance, piece in ((-1, onward), (1, back)):
        rows = piece[start : start + 16, :].astype(jnp.float32)
        returned.append((distance, rows[:KPB] + rows[KPB : 2 * KPB]))
    returned += [(2 * way, second[...]), (3 * way, third[...]), (4, opposite[...])]
    mine = [owner == peer_at(distance, owners) for distance, _ in returned]
    for k in range(KPB):
        total = jnp.zeros(owner.shape, jnp.float32)
        for here, (_, values) in zip(mine, returned):
            total = jnp.where(here, values[k : k + 1, :], total)
        out[pl.ds(k, ACT, stride=KPB), :] = total


def unpack(slots, *returned):
    tok_rows = slots.shape[1]
    return pl.pallas_call(
        functools.partial(unpack_kernel, lax.axis_size("dp")),
        out_shape=pltpu.VMEM((ACT * KPB, tok_rows), jnp.float32),
        in_specs=[VMEM] * (1 + len(returned)),
        out_specs=VMEM,
        compiler_params=limit(4),
        name="unpack",
    )(kept(slots), *[kept(x) for x in returned])


def every_owner(decoder, grad_out, active_blocks, feature_idx, acts, block_slot):
    tok_rows = grad_out.shape[0]
    owners = lax.axis_size("dp")
    ring = ring_of(owners)

    def shift(x, by):
        pairs = [(ring[i], ring[(i + by) % owners]) for i in range(owners)]
        return lax.ppermute(x, "dp", pairs)

    def hop(pieces):
        left, right = pieces
        return shift(left, 1), shift(right, -1)

    def crossed(pieces):
        right, left = pieces
        return shift(right, 1), shift(left, -1)

    def other_core(x):
        return lax.ppermute(x, "width", ((0, 1), (1, 0)))

    def return_by(distance, x):
        pairs = []
        for i in range(owners):
            pairs.append((2 * ring[i], 2 * ring[(i - distance) % owners]))
            pairs.append((2 * ring[i] + 1, 2 * ring[(i + distance) % owners] + 1))
        return lax.ppermute(x, ("dp", "width"), pairs)

    first_left, first_right, left, right, own_facts, slots = prepare(
        block_slot, active_blocks, feature_idx, acts, grad_out, owners
    )
    first_1 = hop((first_left, first_right))
    second_1 = crossed((right, left))
    decoder = fetch(decoder)
    first_1, decoder = lax.optimization_barrier((first_1, decoder))
    first_2 = hop(first_1)
    second_2 = crossed(second_1)
    pairs = [(first_left, first_right), (first_1[0], second_1[0]), (second_1[1], first_1[1])]
    distances = (0, -1, 1)
    own, onward, back = scores_of(distances, pairs, decoder, own_facts)
    total = gradients_of(distances, pairs, own_facts, decoder.shape)
    first_3 = hop(first_2)
    second_2 = stamp(second_2, (back, onward))
    second_3 = crossed(second_2)
    pairs = [(first_2[0], second_2[0]), (second_2[1], first_2[1])]
    mine, others = scores_of((-2, 2), pairs, decoder, own_facts, True)
    total = gradients_of((-2, 2), pairs, own_facts, decoder.shape, total)
    second = mine + other_core(others)
    total, first_3, second = lax.optimization_barrier((total, first_3, second))
    second = return_by(2, jnp.concatenate([second, jnp.zeros((24, 128), jnp.float32)]))[:8]
    first_4 = hop(first_3)
    pairs = [(first_3[0], second_3[0]), (second_3[1], first_3[1])]
    mine, others = scores_of((-3, 3), pairs, decoder, own_facts, True)
    total = gradients_of((-3, 3), pairs, own_facts, decoder.shape, total)
    third = mine + other_core(others)
    total, third = lax.optimization_barrier((total, third))
    third = return_by(3, third)
    total, first_4 = lax.optimization_barrier((total, first_4))
    (opposite,) = scores_of((4,), [first_4], decoder, own_facts)
    opposite = shift(opposite, -owners // 2)
    total, third = lax.optimization_barrier((total, third))
    decoder_grad = last_gradients(first_4, total)
    decoder_grad, opposite = lax.optimization_barrier((decoder_grad, opposite))
    act_grad = unpack(slots, own, *second_3, second, third, opposite)
    act_grad = act_grad + other_core(act_grad)
    return (decoder_grad, act_grad.T)


def send_back(picked):
    return lax.all_to_all(picked, "dp", split_axis=1, concat_axis=1, tiled=True)


def pack_slots(grad_out, target, slots_all, pair_coeffs, pair_columns, source_row):
    slot_row = jnp.zeros((slots_all,), jnp.int32).at[target].set(source_row)
    used = jnp.zeros((slots_all,), jnp.bool_).at[target].set(True)
    send_rows = jnp.where(used[:, None], grad_out[slot_row], jnp.zeros((), grad_out.dtype))
    send_acts = jnp.zeros((slots_all, KPB), pair_coeffs.dtype).at[target].set(pair_coeffs)
    send_cols = jnp.zeros((slots_all, KPB), jnp.int32).at[target].set(pair_columns)
    return (send_rows, send_acts, send_cols)


def some_owners(decoder, grad_out, active_blocks, feature_idx, acts, block_slot):
    tok_rows, half_width = grad_out.shape
    owners = lax.axis_size("dp")
    mean_load = tok_rows * ACT // owners
    owner_cap = mean_load + min(mean_load // 2, tok_rows - mean_load)
    block_cap = (owner_cap + 2) // 3
    block_ids = active_blocks.reshape(-1)
    pair_count = block_ids.shape[0]
    table_pos = jnp.arange(block_slot.shape[0], dtype=jnp.int32)
    slot_of = jnp.sum(
        jnp.where(block_ids[:, None] == table_pos[None, :], block_slot[None, :], 0), axis=1
    )
    pair_pos = jnp.arange(pair_count, dtype=jnp.int32)
    source_row = pair_pos // ACT
    pair_coeffs = acts.reshape(pair_count, KPB)
    pair_feats = feature_idx.reshape(pair_count, KPB)
    earlier = (block_ids[:, None] == block_ids[None, :]) & (pair_pos[None, :] < pair_pos[:, None])
    position = jnp.sum(earlier.astype(jnp.int32), axis=1)
    slot_cols = owners * block_cap
    target = slot_of % BLK_DEV * slot_cols + slot_of // BLK_DEV * block_cap + position
    slots_all = BLK_DEV * slot_cols
    send_rows, send_acts, send_cols = pack_slots(
        grad_out, target, slots_all, pair_coeffs, pair_feats, source_row
    )
    rows, coeffs, feature_pos = (
        lax.all_to_all(
            send_rows.reshape(BLK_DEV, slot_cols, half_width),
            "dp",
            split_axis=1,
            concat_axis=1,
            tiled=True,
        ),
        lax.all_to_all(
            send_acts.reshape(BLK_DEV, slot_cols, KPB),
            "dp",
            split_axis=1,
            concat_axis=1,
            tiled=True,
        ),
        lax.all_to_all(
            send_cols.reshape(BLK_DEV, slot_cols, KPB),
            "dp",
            split_axis=1,
            concat_axis=1,
            tiled=True,
        ),
    )
    weights = decoder.reshape(BLK_DEV, BW, half_width)
    scores = jnp.einsum("bnd,bfd->bnf", rows, weights, preferred_element_type=jnp.float32)
    picked = jnp.take_along_axis(scores, feature_pos, axis=2)
    returned = send_back(picked)
    feature_axis = jnp.arange(BW, dtype=jnp.int32)
    matches = feature_pos[..., None] == feature_axis
    dense = jnp.sum(jnp.where(matches, coeffs[..., None].astype(jnp.float32), 0.0), axis=2).astype(
        jnp.bfloat16
    )
    grads = jnp.einsum("bnf,bnd->bfd", dense, rows, preferred_element_type=jnp.float32)
    decoder_grad = grads.astype(jnp.bfloat16).reshape(BLK_DEV * BW, half_width)
    pair_vals = returned.reshape(slots_all, KPB)[target]
    act_grad = pair_vals.reshape(tok_rows, ACT * KPB)
    act_grad = lax.psum(act_grad, "width")
    return (decoder_grad, act_grad)


def per_device(*args):
    if lax.axis_size("dp") == ACT:
        return every_owner(*args)
    return some_owners(*args)


def solution(mesh):
    in_specs = (
        P(("groups", "dp"), "width"),
        P(("groups", "dp"), "width"),
        P(("groups", "dp"), None),
        P(("groups", "dp"), None),
        P(("groups", "dp"), None),
        P("groups"),
    )
    out_specs = (P(("groups", "dp"), "width"), P(("groups", "dp"), None))
    return jax.shard_map(
        per_device, mesh=mesh, in_specs=in_specs, out_specs=out_specs, check_vma=False
    )
```

```python
import functools

import jax
import jax.numpy as jnp
from jax import lax
from jax.experimental import pallas as pl
from jax.experimental.pallas import tpu as pltpu
from jax.sharding import PartitionSpec as P

BW = 128
BLK_DEV = 4
ACT = 8
KPB = 4
SMEM = pl.BlockSpec(memory_space=pltpu.SMEM)
VMEM = pl.BlockSpec(memory_space=pltpu.VMEM)
ANY = pl.BlockSpec(memory_space=pl.ANY)
HBM = pl.BlockSpec(memory_space=pltpu.HBM)


def limit(mebibytes):
    return pltpu.CompilerParams(vmem_limit_bytes=mebibytes * 2**20)


def kept(x):
    return pltpu.with_memory_space_constraint(x, pltpu.VMEM)


def far(x):
    return pltpu.with_memory_space_constraint(x, pltpu.HBM)


def ring_of(owners):
    return [0] + list(range(1, owners, 2)) + list(range(owners - 2, 0, -2))


def peer_at(distance, owners):
    me = lax.axis_index("dp")
    half_ring = owners // 2
    up = lax.rem(me, 2) == 1
    place = jnp.where(up, lax.div(me, 2) + 1, lax.rem(owners - lax.div(me, 2), owners))
    at = lax.rem(place + owners + distance, owners)
    other = lax.rem(2 * (owners - at), 2 * owners)
    return jnp.where((at > 0) & (at <= half_ring), 2 * at - 1, other)


ROW_SHIFT = BLK_DEV * BW // 2
FACTS = ACT // 2 * 2 * KPB
LAST_FACTS = 16


def facts_for(owner_id, owner, first_row, feats, acts):
    mine = owner == owner_id
    rows = [
        jnp.sum(jnp.where(mine, first_row + feats[k], 0.0), axis=0, keepdims=True) - ROW_SHIFT
        for k in range(KPB)
    ]
    values = [
        jnp.sum(jnp.where(mine, acts[k], 0.0), axis=0, keepdims=True) for k in range(KPB)
    ]
    return jnp.concatenate(rows + values, axis=0)


def prepare_kernel(owners, *refs):
    sources, refs = refs[:5], refs[5:]
    outs, refs = refs[:6], refs[6:]
    first_left, first_right, left, right, own_facts, slots = outs
    block_slot, active, feats, acts, halves, wide_feats, wide_acts, sems = refs
    cut = halves.shape[2]
    copies = []
    for source, target in zip(sources[:4], (block_slot, active, feats, acts)):
        copies.append(pltpu.make_async_copy(source, target, sems.at[len(copies)]))
    for side in range(2):
        copies.append(
            pltpu.make_async_copy(
                sources[4].at[:, side * cut : (side + 1) * cut],
                halves.at[side],
                sems.at[len(copies)],
            )
        )
    for copy in copies:
        copy.start()
    for copy in copies[:4]:
        copy.wait()
    named = active[...]
    slot = jnp.zeros_like(named)
    for block in range(block_slot.shape[0]):
        slot = jnp.where(named == block, block_slot[block], slot)
    slots[...] = slot
    wide_feats[...] = feats[...].astype(jnp.float32)
    wide_acts[...] = acts[...].astype(jnp.float32)
    features = [wide_feats[pl.ds(k, ACT, stride=KPB), :] for k in range(KPB)]
    values = [wide_acts[pl.ds(k, ACT, stride=KPB), :] for k in range(KPB)]
    first_row = (slot % BLK_DEV * BW).astype(jnp.float32)

    def facts(distance):
        return facts_for(
            peer_at(distance, owners), slot // BLK_DEV, first_row, features, values
        )

    def store_facts(target, blocks):
        rows = jnp.concatenate(blocks, axis=0)
        target[target.shape[0] - rows.shape[0] :, :] = rows.astype(jnp.bfloat16)

    own_facts[...] = facts(0)
    opposite = facts(owners // 2)
    none = jnp.zeros_like(opposite)
    store_facts(first_left, [opposite, none])
    for target, sign in ((left, -1), (right, 1)):
        store_facts(target, [facts(sign * d) for d in range(1, owners // 2)] + [none])
    tok_rows = halves.shape[1]
    for side, targets in ((0, (first_left, left)), (1, (first_right, right))):
        copies[4 + side].wait()
        for j in range(cut // 128):
            part = halves[side, :, j * 128 : (j + 1) * 128]
            for target in targets:
                target[j * tok_rows : (j + 1) * tok_rows, :] = part


def prepare(block_slot, active_blocks, feature_idx, acts, grad_out, owners):
    tok_rows, width = grad_out.shape
    plain = width // 256 * tok_rows

    def piece(extra):
        return pltpu.VMEM((plain + extra, 128), grad_out.dtype)

    return pl.pallas_call(
        functools.partial(prepare_kernel, owners),
        out_shape=(
            piece(LAST_FACTS),
            piece(0),
            piece(FACTS),
            piece(FACTS),
            pltpu.VMEM((2 * KPB, tok_rows), jnp.float32),
            pltpu.VMEM((ACT, tok_rows), jnp.int32),
        ),
        in_specs=[HBM] * 5,
        out_specs=(VMEM,) * 6,
        scratch_shapes=[
            pltpu.SMEM(block_slot.shape, jnp.int32),
            pltpu.VMEM((ACT, tok_rows), jnp.int32),
            pltpu.VMEM((ACT * KPB, tok_rows), jnp.int32),
            pltpu.VMEM((ACT * KPB, tok_rows), acts.dtype),
            pltpu.VMEM((2, tok_rows, width // 2), grad_out.dtype),
            pltpu.VMEM((ACT * KPB, tok_rows), jnp.float32),
            pltpu.VMEM((ACT * KPB, tok_rows), jnp.float32),
            pltpu.SemaphoreType.DMA((6,)),
        ],
        compiler_params=limit(8),
        name="prepare",
    )(far(block_slot), far(active_blocks.T), far(feature_idx.T), far(acts.T), far(grad_out))


def fetch_kernel(source, target, sem):
    copy = pltpu.make_async_copy(source, target, sem)
    copy.start()
    copy.wait()


def fetch(x):
    return pl.pallas_call(
        fetch_kernel,
        out_shape=pltpu.VMEM(x.shape, x.dtype),
        in_specs=[HBM],
        out_specs=VMEM,
        scratch_shapes=[pltpu.SemaphoreType.DMA],
        compiler_params=limit(8),
        name="fetch",
    )(far(x))


def block_and_rows(here):
    at_row = here[:KPB].astype(jnp.int32) + ROW_SHIFT
    return at_row[:1] // BW, at_row % BW


def row_axis_of(tok_rows):
    return lax.broadcasted_iota(jnp.int32, (BW, tok_rows), 0)


def coefficients(here):
    block, feats = block_and_rows(here)
    row_axis = row_axis_of(here.shape[1])
    dense = jnp.zeros(row_axis.shape, jnp.float32)
    for k in range(KPB):
        dense = jnp.where(row_axis == feats[k : k + 1], here[KPB + k : KPB + k + 1], dense)
    parts = [jnp.where(block == b, dense, 0.0) for b in range(BLK_DEV)]
    return jnp.concatenate(parts, axis=0).astype(jnp.bfloat16)


def pick(scores, here):
    block, feats = block_and_rows(here)
    row_axis = row_axis_of(here.shape[1])
    mine = scores[:BW]
    for b in range(1, BLK_DEV):
        mine = jnp.where(block == b, scores[b * BW : (b + 1) * BW], mine)
    return [
        jnp.sum(jnp.where(row_axis == feats[k : k + 1], mine, 0.0), axis=0, keepdims=True)
        for k in range(KPB)
    ]


def facts_in(piece, distance, tok_rows):
    facts = piece[piece.shape[0] - FACTS :, :].astype(jnp.float32)
    return facts[(abs(distance) - 1) * 2 * KPB : abs(distance) * 2 * KPB]


def columns_of(pieces, tok_rows, parts):
    rows = [
        jnp.concatenate([piece[j * tok_rows : (j + 1) * tok_rows, :] for j in parts], axis=1)
        for piece in pieces
    ]
    return jnp.concatenate(rows, axis=0) if len(rows) > 1 else rows[0]


def picks_of(facts, decoder, pieces):
    picks = []
    tok_rows = facts[0].shape[1]
    cut = decoder.shape[1] // 2
    for first in range(0, len(facts), 2):
        count = min(2, len(facts) - first)
        scores = None
        for side in range(2):
            part = lax.dot_general(
                decoder[:, side * cut : (side + 1) * cut],
                columns_of(
                    pieces[2 * first + side : 2 * (first + count) : 2],
                    tok_rows,
                    range(cut // 128),
                ),
                (((1,), (1,)), ((), ())),
                preferred_element_type=jnp.float32,
            )
            scores = part if scores is None else scores + part
        for i in range(first, first + count):
            here = scores[:, (i - first) * tok_rows : (i - first + 1) * tok_rows]
            picks.append(jnp.concatenate(pick(here, facts[i]) * 2, axis=0))
    return picks


def gradient_blocks(facts, pieces, width):
    tok_rows = facts[0].shape[1]
    cut = width // 2
    dense = jnp.concatenate([coefficients(here) for here in facts], axis=1)
    for side in range(2):
        for j in range(0, cut // 128, 2):
            rows = columns_of(pieces[side::2], tok_rows, (j, j + 1))
            part = jnp.dot(dense, rows, preferred_element_type=jnp.float32)
            yield slice(side * cut + j * 128, side * cut + (j + 2) * 128), part


def last_facts_in(piece):
    return piece[piece.shape[0] - LAST_FACTS :, :].astype(jnp.float32)[: 2 * KPB]


def facts_of(distances, own_facts, pieces):
    facts = []
    for i, d in enumerate(distances):
        if d == 0:
            facts.append(own_facts[...])
        elif d == 4:
            facts.append(last_facts_in(pieces[2 * i]))
        else:
            facts.append(facts_in(pieces[2 * i + (d < 0)], d, own_facts.shape[1]))
    return facts


def scores_kernel(distances, split, decoder, own_facts, *refs):
    pieces, picked = refs[: 2 * len(distances)], refs[2 * len(distances) :]
    picks = picks_of(facts_of(distances, own_facts, pieces), decoder, pieces)
    if split:
        first = lax.axis_index("width") == 0
        picks = [jnp.where(first, *picks), jnp.where(first, *picks[::-1])]
    for target, values in zip(picked, picks):
        target[...] = values


def scores_of(distances, pairs, decoder, own_facts, split=False):
    pieces = [kept(piece) for pair in pairs for piece in pair]
    shape = pltpu.VMEM(own_facts.shape, jnp.float32)
    return pl.pallas_call(
        functools.partial(scores_kernel, distances, split),
        out_shape=(shape,) * len(distances),
        in_specs=[VMEM] * (2 + len(pieces)),
        out_specs=(VMEM,) * len(distances),
        compiler_params=limit(12),
        name="scores",
    )(kept(decoder), kept(own_facts), *pieces)


def gradients_kernel(distances, own_facts, *refs):
    pieces, refs = refs[: 2 * len(distances)], refs[2 * len(distances) :]
    total = refs[-1]
    facts = facts_of(distances, own_facts, pieces)
    for columns, part in gradient_blocks(facts, pieces, total.shape[1]):
        total[:, columns] = part if len(refs) == 1 else refs[0][:, columns] + part


def gradients_of(distances, pairs, own_facts, shape, total=None):
    operands = [kept(own_facts)] + [kept(piece) for pair in pairs for piece in pair]
    operands += [] if total is None else [kept(total)]
    return pl.pallas_call(
        functools.partial(gradients_kernel, distances),
        out_shape=pltpu.VMEM(shape, jnp.float32),
        in_specs=[VMEM] * len(operands),
        out_specs=VMEM,
        input_output_aliases={} if total is None else {len(operands) - 1: 0},
        compiler_params=limit(16),
        name="gradients",
    )(*operands)


def last_gradients_kernel(distances, own_facts, *refs):
    pieces, (total, out, rounded, sems) = refs[:-4], refs[-4:]
    copies = []
    facts = facts_of(distances, own_facts, pieces)
    for columns, part in gradient_blocks(facts, pieces, out.shape[1]):
        rounded[:, columns] = (total[:, columns] + part).astype(out.dtype)
        copies.append(
            pltpu.make_async_copy(
                rounded.at[:, columns], out.at[:, columns], sems.at[len(copies)]
            )
        )
        copies[-1].start()
    for copy in copies:
        copy.wait()


def last_gradients(distances, pairs, own_facts, total):
    operands = [kept(own_facts)] + [kept(piece) for pair in pairs for piece in pair]
    operands.append(kept(total))
    return pl.pallas_call(
        functools.partial(last_gradients_kernel, distances),
        out_shape=jax.ShapeDtypeStruct(total.shape, jnp.bfloat16),
        in_specs=[VMEM] * len(operands),
        out_specs=ANY,
        scratch_shapes=[
            pltpu.VMEM(total.shape, jnp.bfloat16),
            pltpu.SemaphoreType.DMA((total.shape[1] // 256,)),
        ],
        compiler_params=limit(16),
        name="last_gradients",
    )(*operands)


def stamp_kernel(onward, back, for_onward, for_back, onward_out, back_out, rows, sems):
    start = onward.shape[0] - FACTS
    targets = (onward_out, back_out)
    for i, piece in enumerate((onward, back)):
        pltpu.make_async_copy(
            piece.at[start : start + 16, :], rows.at[i], sems.at[i]
        ).start()
    for i, values in enumerate((for_onward, for_back)):
        pltpu.make_async_copy(
            onward.at[start : start + 16, :], rows.at[i], sems.at[i]
        ).wait()
        value = values[:KPB]
        high = value.astype(jnp.bfloat16).astype(jnp.float32)
        low = value - high
        facts = rows[i].astype(jnp.float32)[2 * KPB :]
        rows[i] = jnp.concatenate([high, low, facts], axis=0).astype(jnp.bfloat16)
        pltpu.make_async_copy(
            rows.at[i], targets[i].at[start : start + 16, :], sems.at[2 + i]
        ).start()
    for i in range(2):
        pltpu.make_async_copy(
            rows.at[i], targets[i].at[start : start + 16, :], sems.at[2 + i]
        ).wait()


def stamp(pieces, values):
    return pl.pallas_call(
        stamp_kernel,
        out_shape=tuple(pltpu.VMEM(piece.shape, piece.dtype) for piece in pieces),
        in_specs=[ANY, ANY, VMEM, VMEM],
        out_specs=(ANY, ANY),
        scratch_shapes=[
            pltpu.VMEM((2, 16, 128), jnp.bfloat16),
            pltpu.SemaphoreType.DMA((4,)),
        ],
        input_output_aliases={0: 0, 1: 1},
        compiler_params=limit(4),
        name="stamp",
    )(*[kept(piece) for piece in pieces], *[kept(value) for value in values])


def unpack_kernel(owners, slots, own, onward, back, second, ahead, behind, opposite, out):
    owner = slots[...] // BLK_DEV
    start = onward.shape[0] - FACTS
    way = 1 - 2 * lax.axis_index("width")
    returned = [(0, own[...])]
    for distance, piece in ((-1, onward), (1, back)):
        rows = piece[start : start + 16, :].astype(jnp.float32)
        returned.append((distance, rows[:KPB] + rows[KPB : 2 * KPB]))
    returned += [(2 * way, second[...]), (3, ahead[...]), (-3, behind[...])]
    returned.append((4, opposite[...]))
    mine = [owner == peer_at(distance, owners) for distance, _ in returned]
    for k in range(KPB):
        total = jnp.zeros(owner.shape, jnp.float32)
        for here, (_, values) in zip(mine, returned):
            total = jnp.where(here, values[k : k + 1, :], total)
        out[pl.ds(k, ACT, stride=KPB), :] = total


def unpack(slots, *returned):
    tok_rows = slots.shape[1]
    return pl.pallas_call(
        functools.partial(unpack_kernel, lax.axis_size("dp")),
        out_shape=pltpu.VMEM((ACT * KPB, tok_rows), jnp.float32),
        in_specs=[VMEM] * (1 + len(returned)),
        out_specs=VMEM,
        compiler_params=limit(4),
        name="unpack",
    )(kept(slots), *[kept(x) for x in returned])


def every_owner(decoder, grad_out, active_blocks, feature_idx, acts, block_slot):
    tok_rows = grad_out.shape[0]
    owners = lax.axis_size("dp")
    ring = ring_of(owners)

    def shift(x, by):
        pairs = [(ring[i], ring[(i + by) % owners]) for i in range(owners)]
        return lax.ppermute(x, "dp", pairs)

    def hop(pieces):
        left, right = pieces
        return shift(left, 1), shift(right, -1)

    def crossed(pieces):
        right, left = pieces
        return shift(right, 1), shift(left, -1)

    def other_core(x):
        return lax.ppermute(x, "width", ((0, 1), (1, 0)))

    def return_by(distance, x):
        pairs = []
        for i in range(owners):
            pairs.append((2 * ring[i], 2 * ring[(i - distance) % owners]))
            pairs.append((2 * ring[i] + 1, 2 * ring[(i + distance) % owners] + 1))
        return lax.ppermute(x, ("dp", "width"), pairs)

    first_left, first_right, left, right, own_facts, slots = prepare(
        block_slot, active_blocks, feature_idx, acts, grad_out, owners
    )
    first_1 = hop((first_left, first_right))
    second_1 = crossed((right, left))
    decoder = fetch(decoder)
    first_1, decoder = lax.optimization_barrier((first_1, decoder))
    first_2 = hop(first_1)
    second_2 = crossed(second_1)
    pairs = [(first_left, first_right), (first_1[0], second_1[0]), (second_1[1], first_1[1])]
    distances = (0, -1, 1)
    own, onward, back = scores_of(distances, pairs, decoder, own_facts)
    total = gradients_of(distances, pairs, own_facts, decoder.shape)
    first_3 = hop(first_2)
    second_2 = stamp(second_2, (back, onward))
    second_3 = crossed(second_2)
    pairs = [(first_2[0], second_2[0]), (second_2[1], first_2[1])]
    mine, others = scores_of((-2, 2), pairs, decoder, own_facts, True)
    total = gradients_of((-2, 2), pairs, own_facts, decoder.shape, total)
    second = mine + other_core(others)
    total, first_3, second = lax.optimization_barrier((total, first_3, second))
    second = return_by(2, jnp.concatenate([second, jnp.zeros((24, 128), jnp.float32)]))[:8]
    first_4 = hop(first_3)
    pairs = [(first_3[0], second_3[0]), (second_3[1], first_3[1])]
    onward, back = scores_of((-3, 3), pairs, decoder, own_facts)
    ahead, behind = shift(onward, -3), shift(back, 3)
    (opposite,) = scores_of((4,), [first_4], decoder, own_facts)
    opposite = shift(opposite, -owners // 2)
    total, ahead, behind = lax.optimization_barrier((total, ahead, behind))
    decoder_grad = last_gradients((-3, 3, 4), pairs + [first_4], own_facts, total)
    decoder_grad, opposite = lax.optimization_barrier((decoder_grad, opposite))
    act_grad = unpack(slots, own, *second_3, second, ahead, behind, opposite)
    act_grad = act_grad + other_core(act_grad)
    return (decoder_grad, act_grad.T)


def send_back(picked):
    return lax.all_to_all(picked, "dp", split_axis=1, concat_axis=1, tiled=True)


def pack_slots(grad_out, target, slots_all, pair_coeffs, pair_columns, source_row):
    slot_row = jnp.zeros((slots_all,), jnp.int32).at[target].set(source_row)
    used = jnp.zeros((slots_all,), jnp.bool_).at[target].set(True)
    send_rows = jnp.where(used[:, None], grad_out[slot_row], jnp.zeros((), grad_out.dtype))
    send_acts = jnp.zeros((slots_all, KPB), pair_coeffs.dtype).at[target].set(pair_coeffs)
    send_cols = jnp.zeros((slots_all, KPB), jnp.int32).at[target].set(pair_columns)
    return (send_rows, send_acts, send_cols)


def some_owners(decoder, grad_out, active_blocks, feature_idx, acts, block_slot):
    tok_rows, half_width = grad_out.shape
    owners = lax.axis_size("dp")
    mean_load = tok_rows * ACT // owners
    owner_cap = mean_load + min(mean_load // 2, tok_rows - mean_load)
    block_cap = (owner_cap + 2) // 3
    block_ids = active_blocks.reshape(-1)
    pair_count = block_ids.shape[0]
    table_pos = jnp.arange(block_slot.shape[0], dtype=jnp.int32)
    slot_of = jnp.sum(
        jnp.where(block_ids[:, None] == table_pos[None, :], block_slot[None, :], 0), axis=1
    )
    pair_pos = jnp.arange(pair_count, dtype=jnp.int32)
    source_row = pair_pos // ACT
    pair_coeffs = acts.reshape(pair_count, KPB)
    pair_feats = feature_idx.reshape(pair_count, KPB)
    earlier = (block_ids[:, None] == block_ids[None, :]) & (pair_pos[None, :] < pair_pos[:, None])
    position = jnp.sum(earlier.astype(jnp.int32), axis=1)
    slot_cols = owners * block_cap
    target = slot_of % BLK_DEV * slot_cols + slot_of // BLK_DEV * block_cap + position
    slots_all = BLK_DEV * slot_cols
    send_rows, send_acts, send_cols = pack_slots(
        grad_out, target, slots_all, pair_coeffs, pair_feats, source_row
    )
    rows, coeffs, feature_pos = (
        lax.all_to_all(
            send_rows.reshape(BLK_DEV, slot_cols, half_width),
            "dp",
            split_axis=1,
            concat_axis=1,
            tiled=True,
        ),
        lax.all_to_all(
            send_acts.reshape(BLK_DEV, slot_cols, KPB),
            "dp",
            split_axis=1,
            concat_axis=1,
            tiled=True,
        ),
        lax.all_to_all(
            send_cols.reshape(BLK_DEV, slot_cols, KPB),
            "dp",
            split_axis=1,
            concat_axis=1,
            tiled=True,
        ),
    )
    weights = decoder.reshape(BLK_DEV, BW, half_width)
    scores = jnp.einsum("bnd,bfd->bnf", rows, weights, preferred_element_type=jnp.float32)
    picked = jnp.take_along_axis(scores, feature_pos, axis=2)
    returned = send_back(picked)
    feature_axis = jnp.arange(BW, dtype=jnp.int32)
    matches = feature_pos[..., None] == feature_axis
    dense = jnp.sum(jnp.where(matches, coeffs[..., None].astype(jnp.float32), 0.0), axis=2).astype(
        jnp.bfloat16
    )
    grads = jnp.einsum("bnf,bnd->bfd", dense, rows, preferred_element_type=jnp.float32)
    decoder_grad = grads.astype(jnp.bfloat16).reshape(BLK_DEV * BW, half_width)
    pair_vals = returned.reshape(slots_all, KPB)[target]
    act_grad = pair_vals.reshape(tok_rows, ACT * KPB)
    act_grad = lax.psum(act_grad, "width")
    return (decoder_grad, act_grad)


def per_device(*args):
    if lax.axis_size("dp") == ACT:
        return every_owner(*args)
    return some_owners(*args)


def solution(mesh):
    in_specs = (
        P(("groups", "dp"), "width"),
        P(("groups", "dp"), "width"),
        P(("groups", "dp"), None),
        P(("groups", "dp"), None),
        P(("groups", "dp"), None),
        P("groups"),
    )
    out_specs = (P(("groups", "dp"), "width"), P(("groups", "dp"), None))
    return jax.shard_map(
        per_device, mesh=mesh, in_specs=in_specs, out_specs=out_specs, check_vma=False
    )
```

```python
import functools

import jax
import jax.numpy as jnp
from jax import lax
from jax.experimental import pallas as pl
from jax.experimental.pallas import tpu as pltpu
from jax.sharding import PartitionSpec as P

BW = 128
BLK_DEV = 4
ACT = 8
KPB = 4
SMEM = pl.BlockSpec(memory_space=pltpu.SMEM)
VMEM = pl.BlockSpec(memory_space=pltpu.VMEM)
ANY = pl.BlockSpec(memory_space=pl.ANY)
HBM = pl.BlockSpec(memory_space=pltpu.HBM)


def limit(mebibytes):
    return pltpu.CompilerParams(vmem_limit_bytes=mebibytes * 2**20)


def kept(x):
    return pltpu.with_memory_space_constraint(x, pltpu.VMEM)


def far(x):
    return pltpu.with_memory_space_constraint(x, pltpu.HBM)


def ring_of(owners):
    return list(range(0, owners, 2)) + list(range(owners - 1, 0, -2))


def peer_at(distance, owners):
    me = lax.axis_index("dp")
    half_ring = owners // 2
    place = jnp.where(lax.rem(me, 2) == 0, lax.div(me, 2), owners - 1 - lax.div(me, 2))
    at = lax.rem(place + owners + distance, owners)
    return jnp.where(at < half_ring, 2 * at, 2 * (owners - 1 - at) + 1)


ROW_SHIFT = BLK_DEV * BW // 2
FACTS = 2 * 2 * KPB


def facts_for(owner_id, owner, first_row, feats, acts):
    mine = owner == owner_id
    rows = [
        jnp.sum(jnp.where(mine, first_row + feats[k], 0.0), axis=0, keepdims=True) - ROW_SHIFT
        for k in range(KPB)
    ]
    values = [
        jnp.sum(jnp.where(mine, acts[k], 0.0), axis=0, keepdims=True) for k in range(KPB)
    ]
    return jnp.concatenate(rows + values, axis=0)


def prepare_kernel(owners, *refs):
    sources, refs = refs[:5], refs[5:]
    outs, refs = refs[:6], refs[6:]
    block_slot, active, feats, acts, halves, wide_feats, wide_acts, sems = refs
    cut = halves.shape[2]
    copies = []
    for source, target in zip(sources[:4], (block_slot, active, feats, acts)):
        copies.append(pltpu.make_async_copy(source, target, sems.at[len(copies)]))
    for side in range(2):
        copies.append(
            pltpu.make_async_copy(
                sources[4].at[:, side * cut : (side + 1) * cut],
                halves.at[side],
                sems.at[len(copies)],
            )
        )
    for copy in copies:
        copy.start()
    for copy in copies[:4]:
        copy.wait()
    named = active[...]
    slot = jnp.zeros_like(named)
    for block in range(block_slot.shape[0]):
        slot = jnp.where(named == block, block_slot[block], slot)
    wide_feats[...] = feats[...].astype(jnp.float32)
    wide_acts[...] = acts[...].astype(jnp.float32)
    features = [wide_feats[pl.ds(k, ACT, stride=KPB), :] for k in range(KPB)]
    values = [wide_acts[pl.ds(k, ACT, stride=KPB), :] for k in range(KPB)]
    first_row = (slot % BLK_DEV * BW).astype(jnp.float32)

    def facts(distance):
        return facts_for(
            peer_at(distance, owners), slot // BLK_DEV, first_row, features, values
        )

    outs[4][...] = facts(0)
    outs[5][...] = slot
    for piece, sign, distances in (
        (outs[0], 1, (3, 4)), (outs[1], -1, (3, 4)), (outs[2], -1, (1, 2)), (outs[3], 1, (1, 2))
    ):
        rows = jnp.concatenate([facts(sign * d) for d in distances], axis=0)
        piece[piece.shape[0] - FACTS :, :] = rows.astype(jnp.bfloat16)
    tok_rows = halves.shape[1]
    for side in range(2):
        copies[4 + side].wait()
        for j in range(cut // 128):
            part = halves[side, :, j * 128 : (j + 1) * 128]
            for piece in (outs[side], outs[2 + side]):
                piece[j * tok_rows : (j + 1) * tok_rows, :] = part


def prepare(block_slot, active_blocks, feature_idx, acts, grad_out, owners):
    tok_rows, width = grad_out.shape
    piece = pltpu.VMEM((width // 256 * tok_rows + FACTS, 128), grad_out.dtype)
    facts = pltpu.VMEM((2 * KPB, tok_rows), jnp.float32)
    slots = pltpu.VMEM((ACT, tok_rows), jnp.int32)
    out_shape = (piece,) * 4 + (facts, slots)
    return pl.pallas_call(
        functools.partial(prepare_kernel, owners),
        out_shape=out_shape,
        in_specs=[HBM] * 5,
        out_specs=(VMEM,) * len(out_shape),
        scratch_shapes=[
            pltpu.SMEM(block_slot.shape, jnp.int32),
            pltpu.VMEM((ACT, tok_rows), jnp.int32),
            pltpu.VMEM((ACT * KPB, tok_rows), jnp.int32),
            pltpu.VMEM((ACT * KPB, tok_rows), acts.dtype),
            pltpu.VMEM((2, tok_rows, width // 2), grad_out.dtype),
            pltpu.VMEM((ACT * KPB, tok_rows), jnp.float32),
            pltpu.VMEM((ACT * KPB, tok_rows), jnp.float32),
            pltpu.SemaphoreType.DMA((6,)),
        ],
        compiler_params=limit(8),
        name="prepare",
    )(far(block_slot), far(active_blocks.T), far(feature_idx.T), far(acts.T), far(grad_out))


def fetch_kernel(source, target, sem):
    copy = pltpu.make_async_copy(source, target, sem)
    copy.start()
    copy.wait()


def fetch(x):
    return pl.pallas_call(
        fetch_kernel,
        out_shape=pltpu.VMEM(x.shape, x.dtype),
        in_specs=[HBM],
        out_specs=VMEM,
        scratch_shapes=[pltpu.SemaphoreType.DMA],
        compiler_params=limit(8),
        name="fetch",
    )(far(x))


def block_and_rows(here):
    at_row = here[:KPB].astype(jnp.int32) + ROW_SHIFT
    return at_row[:1] // BW, at_row % BW


def row_axis_of(tok_rows):
    return lax.broadcasted_iota(jnp.int32, (BW, tok_rows), 0)


def coefficients(here):
    block, feats = block_and_rows(here)
    row_axis = row_axis_of(here.shape[1])
    dense = jnp.zeros(row_axis.shape, jnp.float32)
    for k in range(KPB):
        dense = jnp.where(row_axis == feats[k : k + 1], here[KPB + k : KPB + k + 1], dense)
    parts = [jnp.where(block == b, dense, 0.0) for b in range(BLK_DEV)]
    return jnp.concatenate(parts, axis=0).astype(jnp.bfloat16)


def pick(scores, here):
    block, feats = block_and_rows(here)
    row_axis = row_axis_of(here.shape[1])
    mine = scores[:BW]
    for b in range(1, BLK_DEV):
        mine = jnp.where(block == b, scores[b * BW : (b + 1) * BW], mine)
    return [
        jnp.sum(jnp.where(row_axis == feats[k : k + 1], mine, 0.0), axis=0, keepdims=True)
        for k in range(KPB)
    ]


def facts_in(left, right, distance):
    near = abs(distance) <= 2
    piece = (right if near else left) if distance in (-1, -2, -3, 4) else (left if near else right)
    facts = piece[piece.shape[0] - FACTS :, :].astype(jnp.float32)
    slot = (abs(distance) - 1) % 2
    return facts[slot * 2 * KPB : (slot + 1) * 2 * KPB]


def columns_of(pieces, tok_rows, parts):
    rows = [
        jnp.concatenate([piece[j * tok_rows : (j + 1) * tok_rows, :] for j in parts], axis=1)
        for piece in pieces
    ]
    return jnp.concatenate(rows, axis=0) if len(rows) > 1 else rows[0]


def picks_of(facts, decoder, pieces):
    picks = []
    tok_rows = facts[0].shape[1]
    cut = decoder.shape[1] // 2
    for first in range(0, len(facts), 2):
        count = min(2, len(facts) - first)
        scores = None
        for side in range(2):
            part = lax.dot_general(
                decoder[:, side * cut : (side + 1) * cut],
                columns_of(
                    pieces[2 * first + side : 2 * (first + count) : 2],
                    tok_rows,
                    range(cut // 128),
                ),
                (((1,), (1,)), ((), ())),
                preferred_element_type=jnp.float32,
            )
            scores = part if scores is None else scores + part
        for i in range(first, first + count):
            here = scores[:, (i - first) * tok_rows : (i - first + 1) * tok_rows]
            picks.append(jnp.concatenate(pick(here, facts[i]) * 2, axis=0))
    return picks


def gradient_blocks(facts, pieces, width):
    tok_rows = facts[0].shape[1]
    cut = width // 2
    dense = jnp.concatenate([coefficients(here) for here in facts], axis=1)
    for side in range(2):
        for j in range(0, cut // 128, 2):
            rows = columns_of(pieces[side::2], tok_rows, (j, j + 1))
            part = jnp.dot(dense, rows, preferred_element_type=jnp.float32)
            yield slice(side * cut + j * 128, side * cut + (j + 2) * 128), part


def facts_of(distances, own_facts, pieces):
    return [
        own_facts[...] if d == 0 else facts_in(pieces[2 * i], pieces[2 * i + 1], d)
        for i, d in enumerate(distances)
    ]


def scores_kernel(distances, split, decoder, own_facts, *refs):
    pieces, picked = refs[: 2 * len(distances)], refs[2 * len(distances) :]
    picks = picks_of(facts_of(distances, own_facts, pieces), decoder, pieces)
    if split:
        first = lax.axis_index("width") == 0
        picks = [jnp.where(first, *picks), jnp.where(first, *picks[::-1])]
    for target, values in zip(picked, picks):
        target[...] = values


def scores_of(distances, pairs, decoder, own_facts, split=False):
    pieces = [kept(piece) for pair in pairs for piece in pair]
    shape = pltpu.VMEM(own_facts.shape, jnp.float32)
    return pl.pallas_call(
        functools.partial(scores_kernel, distances, split),
        out_shape=(shape,) * len(distances),
        in_specs=[VMEM] * (2 + len(pieces)),
        out_specs=(VMEM,) * len(distances),
        compiler_params=limit(12),
        name="scores",
    )(kept(decoder), kept(own_facts), *pieces)


def gradients_kernel(distances, own_facts, *refs):
    pieces, refs = refs[: 2 * len(distances)], refs[2 * len(distances) :]
    total = refs[-1]
    facts = facts_of(distances, own_facts, pieces)
    for columns, part in gradient_blocks(facts, pieces, total.shape[1]):
        total[:, columns] = part if len(refs) == 1 else refs[0][:, columns] + part


def gradients_of(distances, pairs, own_facts, shape, total=None):
    operands = [kept(own_facts)] + [kept(piece) for pair in pairs for piece in pair]
    operands += [] if total is None else [kept(total)]
    return pl.pallas_call(
        functools.partial(gradients_kernel, distances),
        out_shape=pltpu.VMEM(shape, jnp.float32),
        in_specs=[VMEM] * len(operands),
        out_specs=VMEM,
        input_output_aliases={} if total is None else {len(operands) - 1: 0},
        compiler_params=limit(16),
        name="gradients",
    )(*operands)


def last_gradients_kernel(distances, own_facts, *refs):
    pieces, (total, out, rounded, sems) = refs[:-4], refs[-4:]
    copies = []
    facts = facts_of(distances, own_facts, pieces)
    for columns, part in gradient_blocks(facts, pieces, out.shape[1]):
        rounded[:, columns] = (total[:, columns] + part).astype(out.dtype)
        copies.append(
            pltpu.make_async_copy(
                rounded.at[:, columns], out.at[:, columns], sems.at[len(copies)]
            )
        )
        copies[-1].start()
    for copy in copies:
        copy.wait()


def last_gradients(distances, pairs, own_facts, total):
    operands = [kept(own_facts)] + [kept(piece) for pair in pairs for piece in pair]
    operands.append(kept(total))
    return pl.pallas_call(
        functools.partial(last_gradients_kernel, distances),
        out_shape=jax.ShapeDtypeStruct(total.shape, jnp.bfloat16),
        in_specs=[VMEM] * len(operands),
        out_specs=ANY,
        scratch_shapes=[
            pltpu.VMEM(total.shape, jnp.bfloat16),
            pltpu.SemaphoreType.DMA((total.shape[1] // 256,)),
        ],
        compiler_params=limit(16),
        name="last_gradients",
    )(*operands)


def stamp_kernel(onward, back, for_onward, for_back, onward_out, back_out, rows, sems):
    start = onward.shape[0] - FACTS
    targets = (onward_out, back_out)
    for i, piece in enumerate((onward, back)):
        pltpu.make_async_copy(
            piece.at[start : start + 16, :], rows.at[i], sems.at[i]
        ).start()
    for i, values in enumerate((for_onward, for_back)):
        pltpu.make_async_copy(
            onward.at[start : start + 16, :], rows.at[i], sems.at[i]
        ).wait()
        value = values[:KPB]
        high = value.astype(jnp.bfloat16).astype(jnp.float32)
        low = value - high
        facts = rows[i].astype(jnp.float32)[2 * KPB :]
        rows[i] = jnp.concatenate([high, low, facts], axis=0).astype(jnp.bfloat16)
        pltpu.make_async_copy(
            rows.at[i], targets[i].at[start : start + 16, :], sems.at[2 + i]
        ).start()
    for i in range(2):
        pltpu.make_async_copy(
            rows.at[i], targets[i].at[start : start + 16, :], sems.at[2 + i]
        ).wait()


def stamp(pieces, values):
    return pl.pallas_call(
        stamp_kernel,
        out_shape=tuple(pltpu.VMEM(piece.shape, piece.dtype) for piece in pieces),
        in_specs=[ANY, ANY, VMEM, VMEM],
        out_specs=(ANY, ANY),
        scratch_shapes=[
            pltpu.VMEM((2, 16, 128), jnp.bfloat16),
            pltpu.SemaphoreType.DMA((4,)),
        ],
        input_output_aliases={0: 0, 1: 1},
        compiler_params=limit(4),
        name="stamp",
    )(*[kept(piece) for piece in pieces], *[kept(value) for value in values])


def unpack_kernel(owners, slots, own, onward, back, second, ahead, behind, opposite, out):
    owner = slots[...] // BLK_DEV
    start = onward.shape[0] - FACTS
    way = 1 - 2 * lax.axis_index("width")
    returned = [(0, own[...])]
    for distance, piece in ((-1, onward), (1, back)):
        rows = piece[start : start + 16, :].astype(jnp.float32)
        returned.append((distance, rows[:KPB] + rows[KPB : 2 * KPB]))
    returned += [(2 * way, second[...]), (3, ahead[...]), (-3, behind[...])]
    returned.append((4, opposite[...]))
    mine = [owner == peer_at(distance, owners) for distance, _ in returned]
    for k in range(KPB):
        total = jnp.zeros(owner.shape, jnp.float32)
        for here, (_, values) in zip(mine, returned):
            total = jnp.where(here, values[k : k + 1, :], total)
        out[pl.ds(k, ACT, stride=KPB), :] = total


def unpack(slots, *returned):
    tok_rows = slots.shape[1]
    return pl.pallas_call(
        functools.partial(unpack_kernel, lax.axis_size("dp")),
        out_shape=pltpu.VMEM((ACT * KPB, tok_rows), jnp.float32),
        in_specs=[VMEM] * (1 + len(returned)),
        out_specs=VMEM,
        compiler_params=limit(4),
        name="unpack",
    )(kept(slots), *[kept(x) for x in returned])


def every_owner(decoder, grad_out, active_blocks, feature_idx, acts, block_slot):
    tok_rows = grad_out.shape[0]
    owners = lax.axis_size("dp")
    ring = ring_of(owners)

    def shift(x, by):
        pairs = [(ring[i], ring[(i + by) % owners]) for i in range(owners)]
        return lax.ppermute(x, "dp", pairs)

    def hop(pieces):
        left, right = pieces
        return shift(left, 1), shift(right, -1)

    def crossed(pieces):
        right, left = pieces
        return shift(right, 1), shift(left, -1)

    def other_core(x):
        return lax.ppermute(x, "width", ((0, 1), (1, 0)))

    def return_by(distance, x):
        pairs = []
        for i in range(owners):
            pairs.append((2 * ring[i], 2 * ring[(i - distance) % owners]))
            pairs.append((2 * ring[i] + 1, 2 * ring[(i + distance) % owners] + 1))
        return lax.ppermute(x, ("dp", "width"), pairs)

    first_left, first_right, left, right, own_facts, slots = prepare(
        block_slot, active_blocks, feature_idx, acts, grad_out, owners
    )
    first_1 = hop((first_left, first_right))
    second_1 = crossed((right, left))
    decoder = fetch(decoder)
    first_1, decoder = lax.optimization_barrier((first_1, decoder))
    first_2 = hop(first_1)
    second_2 = crossed(second_1)
    pairs = [(first_left, first_right), (first_1[0], second_1[0]), (second_1[1], first_1[1])]
    distances = (0, -1, 1)
    own, onward, back = scores_of(distances, pairs, decoder, own_facts)
    total = gradients_of(distances, pairs, own_facts, decoder.shape)
    first_3 = hop(first_2)
    second_2 = stamp(second_2, (back, onward))
    second_3 = crossed(second_2)
    pairs = [(first_2[0], second_2[0]), (second_2[1], first_2[1])]
    mine, others = scores_of((-2, 2), pairs, decoder, own_facts, True)
    total = gradients_of((-2, 2), pairs, own_facts, decoder.shape, total)
    second = mine + other_core(others)
    total, first_3, second = lax.optimization_barrier((total, first_3, second))
    second = return_by(2, jnp.concatenate([second, jnp.zeros((16, 128), jnp.float32)]))[:8]
    first_4 = hop(first_3)
    pairs = [(first_3[0], second_3[0]), (second_3[1], first_3[1])]
    onward, back = scores_of((-3, 3), pairs, decoder, own_facts)
    ahead, behind = shift(onward, -3), shift(back, 3)
    (opposite,) = scores_of((4,), [first_4], decoder, own_facts)
    opposite = shift(opposite, -owners // 2)
    total, ahead, behind = lax.optimization_barrier((total, ahead, behind))
    decoder_grad = last_gradients((-3, 3, 4), pairs + [first_4], own_facts, total)
    decoder_grad, opposite = lax.optimization_barrier((decoder_grad, opposite))
    act_grad = unpack(slots, own, *second_3, second, ahead, behind, opposite)
    act_grad = act_grad + other_core(act_grad)
    return (decoder_grad, act_grad.T)


def send_back(picked):
    return lax.all_to_all(picked, "dp", split_axis=1, concat_axis=1, tiled=True)


def pack_slots(grad_out, target, slots_all, pair_coeffs, pair_columns, source_row):
    slot_row = jnp.zeros((slots_all,), jnp.int32).at[target].set(source_row)
    used = jnp.zeros((slots_all,), jnp.bool_).at[target].set(True)
    send_rows = jnp.where(used[:, None], grad_out[slot_row], jnp.zeros((), grad_out.dtype))
    send_acts = jnp.zeros((slots_all, KPB), pair_coeffs.dtype).at[target].set(pair_coeffs)
    send_cols = jnp.zeros((slots_all, KPB), jnp.int32).at[target].set(pair_columns)
    return (send_rows, send_acts, send_cols)


def some_owners(decoder, grad_out, active_blocks, feature_idx, acts, block_slot):
    tok_rows, half_width = grad_out.shape
    owners = lax.axis_size("dp")
    mean_load = tok_rows * ACT // owners
    owner_cap = mean_load + min(mean_load // 2, tok_rows - mean_load)
    block_cap = (owner_cap + 2) // 3
    block_ids = active_blocks.reshape(-1)
    pair_count = block_ids.shape[0]
    table_pos = jnp.arange(block_slot.shape[0], dtype=jnp.int32)
    slot_of = jnp.sum(
        jnp.where(block_ids[:, None] == table_pos[None, :], block_slot[None, :], 0), axis=1
    )
    pair_pos = jnp.arange(pair_count, dtype=jnp.int32)
    source_row = pair_pos // ACT
    pair_coeffs = acts.reshape(pair_count, KPB)
    pair_feats = feature_idx.reshape(pair_count, KPB)
    earlier = (block_ids[:, None] == block_ids[None, :]) & (pair_pos[None, :] < pair_pos[:, None])
    position = jnp.sum(earlier.astype(jnp.int32), axis=1)
    slot_cols = owners * block_cap
    target = slot_of % BLK_DEV * slot_cols + slot_of // BLK_DEV * block_cap + position
    slots_all = BLK_DEV * slot_cols
    send_rows, send_acts, send_cols = pack_slots(
        grad_out, target, slots_all, pair_coeffs, pair_feats, source_row
    )
    rows, coeffs, feature_pos = (
        lax.all_to_all(
            send_rows.reshape(BLK_DEV, slot_cols, half_width),
            "dp",
            split_axis=1,
            concat_axis=1,
            tiled=True,
        ),
        lax.all_to_all(
            send_acts.reshape(BLK_DEV, slot_cols, KPB),
            "dp",
            split_axis=1,
            concat_axis=1,
            tiled=True,
        ),
        lax.all_to_all(
            send_cols.reshape(BLK_DEV, slot_cols, KPB),
            "dp",
            split_axis=1,
            concat_axis=1,
            tiled=True,
        ),
    )
    weights = decoder.reshape(BLK_DEV, BW, half_width)
    scores = jnp.einsum("bnd,bfd->bnf", rows, weights, preferred_element_type=jnp.float32)
    picked = jnp.take_along_axis(scores, feature_pos, axis=2)
    returned = send_back(picked)
    feature_axis = jnp.arange(BW, dtype=jnp.int32)
    matches = feature_pos[..., None] == feature_axis
    dense = jnp.sum(jnp.where(matches, coeffs[..., None].astype(jnp.float32), 0.0), axis=2).astype(
        jnp.bfloat16
    )
    grads = jnp.einsum("bnf,bnd->bfd", dense, rows, preferred_element_type=jnp.float32)
    decoder_grad = grads.astype(jnp.bfloat16).reshape(BLK_DEV * BW, half_width)
    pair_vals = returned.reshape(slots_all, KPB)[target]
    act_grad = pair_vals.reshape(tok_rows, ACT * KPB)
    act_grad = lax.psum(act_grad, "width")
    return (decoder_grad, act_grad)


def per_device(*args):
    if lax.axis_size("dp") == ACT:
        return every_owner(*args)
    return some_owners(*args)


def solution(mesh):
    in_specs = (
        P(("groups", "dp"), "width"),
        P(("groups", "dp"), "width"),
        P(("groups", "dp"), None),
        P(("groups", "dp"), None),
        P(("groups", "dp"), None),
        P("groups"),
    )
    out_specs = (P(("groups", "dp"), "width"), P(("groups", "dp"), None))
    return jax.shard_map(
        per_device, mesh=mesh, in_specs=in_specs, out_specs=out_specs, check_vma=False
    )
```

```python
import functools

import jax
import jax.numpy as jnp
from jax import lax
from jax.experimental import pallas as pl
from jax.experimental.pallas import tpu as pltpu
from jax.sharding import PartitionSpec as P

BW = 128
BLK_DEV = 4
ACT = 8
KPB = 4
SMEM = pl.BlockSpec(memory_space=pltpu.SMEM)
VMEM = pl.BlockSpec(memory_space=pltpu.VMEM)
ANY = pl.BlockSpec(memory_space=pl.ANY)
HBM = pl.BlockSpec(memory_space=pltpu.HBM)


def limit(mebibytes):
    return pltpu.CompilerParams(vmem_limit_bytes=mebibytes * 2**20)


def kept(x):
    return pltpu.with_memory_space_constraint(x, pltpu.VMEM)


def far(x):
    return pltpu.with_memory_space_constraint(x, pltpu.HBM)


def ring_of(owners):
    return list(range(0, owners, 2)) + list(range(owners - 1, 0, -2))


def peer_at(distance, owners):
    me = lax.axis_index("dp")
    half_ring = owners // 2
    place = jnp.where(lax.rem(me, 2) == 0, lax.div(me, 2), owners - 1 - lax.div(me, 2))
    at = lax.rem(place + owners + distance, owners)
    return jnp.where(at < half_ring, 2 * at, 2 * (owners - 1 - at) + 1)


ROW_SHIFT = BLK_DEV * BW // 2
FACTS = ACT // 2 * 2 * KPB
LAST_FACTS = 16


def facts_for(owner_id, owner, first_row, feats, acts):
    mine = owner == owner_id
    rows = [
        jnp.sum(jnp.where(mine, first_row + feats[k], 0.0), axis=0, keepdims=True) - ROW_SHIFT
        for k in range(KPB)
    ]
    values = [
        jnp.sum(jnp.where(mine, acts[k], 0.0), axis=0, keepdims=True) for k in range(KPB)
    ]
    return jnp.concatenate(rows + values, axis=0)


def prepare_kernel(owners, *refs):
    sources, refs = refs[:5], refs[5:]
    outs, refs = refs[:6], refs[6:]
    first_left, first_right, left, right, own_facts, slots = outs
    block_slot, active, feats, acts, halves, wide_feats, wide_acts, sems = refs
    cut = halves.shape[2]
    copies = []
    for source, target in zip(sources[:4], (block_slot, active, feats, acts)):
        copies.append(pltpu.make_async_copy(source, target, sems.at[len(copies)]))
    for side in range(2):
        copies.append(
            pltpu.make_async_copy(
                sources[4].at[:, side * cut : (side + 1) * cut],
                halves.at[side],
                sems.at[len(copies)],
            )
        )
    for copy in copies:
        copy.start()
    for copy in copies[:4]:
        copy.wait()
    named = active[...]
    slot = jnp.zeros_like(named)
    for block in range(block_slot.shape[0]):
        slot = jnp.where(named == block, block_slot[block], slot)
    slots[...] = slot
    wide_feats[...] = feats[...].astype(jnp.float32)
    wide_acts[...] = acts[...].astype(jnp.float32)
    features = [wide_feats[pl.ds(k, ACT, stride=KPB), :] for k in range(KPB)]
    values = [wide_acts[pl.ds(k, ACT, stride=KPB), :] for k in range(KPB)]
    first_row = (slot % BLK_DEV * BW).astype(jnp.float32)

    def facts(distance):
        return facts_for(
            peer_at(distance, owners), slot // BLK_DEV, first_row, features, values
        )

    def store_facts(target, blocks):
        rows = jnp.concatenate(blocks, axis=0)
        target[target.shape[0] - rows.shape[0] :, :] = rows.astype(jnp.bfloat16)

    own_facts[...] = facts(0)
    opposite = facts(owners // 2)
    none = jnp.zeros_like(opposite)
    store_facts(first_left, [opposite, none])
    for target, sign in ((left, -1), (right, 1)):
        store_facts(target, [facts(sign * d) for d in range(1, owners // 2)] + [none])
    tok_rows = halves.shape[1]
    for side, targets in ((0, (first_left, left)), (1, (first_right, right))):
        copies[4 + side].wait()
        for j in range(cut // 128):
            part = halves[side, :, j * 128 : (j + 1) * 128]
            for target in targets:
                target[j * tok_rows : (j + 1) * tok_rows, :] = part


def prepare(block_slot, active_blocks, feature_idx, acts, grad_out, owners):
    tok_rows, width = grad_out.shape
    plain = width // 256 * tok_rows

    def piece(extra):
        return pltpu.VMEM((plain + extra, 128), grad_out.dtype)

    return pl.pallas_call(
        functools.partial(prepare_kernel, owners),
        out_shape=(
            piece(LAST_FACTS),
            piece(0),
            piece(FACTS),
            piece(FACTS),
            pltpu.VMEM((2 * KPB, tok_rows), jnp.float32),
            pltpu.VMEM((ACT, tok_rows), jnp.int32),
        ),
        in_specs=[HBM] * 5,
        out_specs=(VMEM,) * 6,
        scratch_shapes=[
            pltpu.SMEM(block_slot.shape, jnp.int32),
            pltpu.VMEM((ACT, tok_rows), jnp.int32),
            pltpu.VMEM((ACT * KPB, tok_rows), jnp.int32),
            pltpu.VMEM((ACT * KPB, tok_rows), acts.dtype),
            pltpu.VMEM((2, tok_rows, width // 2), grad_out.dtype),
            pltpu.VMEM((ACT * KPB, tok_rows), jnp.float32),
            pltpu.VMEM((ACT * KPB, tok_rows), jnp.float32),
            pltpu.SemaphoreType.DMA((6,)),
        ],
        compiler_params=limit(8),
        name="prepare",
    )(far(block_slot), far(active_blocks.T), far(feature_idx.T), far(acts.T), far(grad_out))


def fetch_kernel(source, target, sem):
    copy = pltpu.make_async_copy(source, target, sem)
    copy.start()
    copy.wait()


def fetch(x):
    return pl.pallas_call(
        fetch_kernel,
        out_shape=pltpu.VMEM(x.shape, x.dtype),
        in_specs=[HBM],
        out_specs=VMEM,
        scratch_shapes=[pltpu.SemaphoreType.DMA],
        compiler_params=limit(8),
        name="fetch",
    )(far(x))


def block_and_rows(here):
    at_row = here[:KPB].astype(jnp.int32) + ROW_SHIFT
    return at_row[:1] // BW, at_row % BW


def row_axis_of(tok_rows):
    return lax.broadcasted_iota(jnp.int32, (BW, tok_rows), 0)


def coefficients(here):
    block, feats = block_and_rows(here)
    row_axis = row_axis_of(here.shape[1])
    dense = jnp.zeros(row_axis.shape, jnp.float32)
    for k in range(KPB):
        dense = jnp.where(row_axis == feats[k : k + 1], here[KPB + k : KPB + k + 1], dense)
    parts = [jnp.where(block == b, dense, 0.0) for b in range(BLK_DEV)]
    return jnp.concatenate(parts, axis=0).astype(jnp.bfloat16)


def pick(scores, here):
    block, feats = block_and_rows(here)
    row_axis = row_axis_of(here.shape[1])
    mine = scores[:BW]
    for b in range(1, BLK_DEV):
        mine = jnp.where(block == b, scores[b * BW : (b + 1) * BW], mine)
    return [
        jnp.sum(jnp.where(row_axis == feats[k : k + 1], mine, 0.0), axis=0, keepdims=True)
        for k in range(KPB)
    ]


def facts_in(piece, distance, tok_rows):
    facts = piece[piece.shape[0] - FACTS :, :].astype(jnp.float32)
    return facts[(abs(distance) - 1) * 2 * KPB : abs(distance) * 2 * KPB]


def columns_of(pieces, tok_rows, parts):
    rows = [
        jnp.concatenate([piece[j * tok_rows : (j + 1) * tok_rows, :] for j in parts], axis=1)
        for piece in pieces
    ]
    return jnp.concatenate(rows, axis=0) if len(rows) > 1 else rows[0]


def picks_of(facts, decoder, pieces):
    picks = []
    tok_rows = facts[0].shape[1]
    cut = decoder.shape[1] // 2
    for first in range(0, len(facts), 2):
        count = min(2, len(facts) - first)
        scores = None
        for side in range(2):
            part = lax.dot_general(
                decoder[:, side * cut : (side + 1) * cut],
                columns_of(
                    pieces[2 * first + side : 2 * (first + count) : 2],
                    tok_rows,
                    range(cut // 128),
                ),
                (((1,), (1,)), ((), ())),
                preferred_element_type=jnp.float32,
            )
            scores = part if scores is None else scores + part
        for i in range(first, first + count):
            here = scores[:, (i - first) * tok_rows : (i - first + 1) * tok_rows]
            picks.append(jnp.concatenate(pick(here, facts[i]) * 2, axis=0))
    return picks


def gradient_blocks(facts, pieces, width):
    tok_rows = facts[0].shape[1]
    cut = width // 2
    dense = jnp.concatenate([coefficients(here) for here in facts], axis=1)
    for side in range(2):
        for j in range(0, cut // 128, 2):
            rows = columns_of(pieces[side::2], tok_rows, (j, j + 1))
            part = jnp.dot(dense, rows, preferred_element_type=jnp.float32)
            yield slice(side * cut + j * 128, side * cut + (j + 2) * 128), part


def last_facts_in(piece):
    return piece[piece.shape[0] - LAST_FACTS :, :].astype(jnp.float32)[: 2 * KPB]


def facts_of(distances, own_facts, pieces):
    facts = []
    for i, d in enumerate(distances):
        if d == 0:
            facts.append(own_facts[...])
        elif d == 4:
            facts.append(last_facts_in(pieces[2 * i]))
        else:
            facts.append(facts_in(pieces[2 * i + (d < 0)], d, own_facts.shape[1]))
    return facts


def scores_kernel(distances, split, decoder, own_facts, *refs):
    pieces, picked = refs[: 2 * len(distances)], refs[2 * len(distances) :]
    picks = picks_of(facts_of(distances, own_facts, pieces), decoder, pieces)
    if split:
        first = lax.axis_index("width") == 0
        picks = [jnp.where(first, *picks), jnp.where(first, *picks[::-1])]
    for target, values in zip(picked, picks):
        target[...] = values


def scores_of(distances, pairs, decoder, own_facts, split=False):
    pieces = [kept(piece) for pair in pairs for piece in pair]
    shape = pltpu.VMEM(own_facts.shape, jnp.float32)
    return pl.pallas_call(
        functools.partial(scores_kernel, distances, split),
        out_shape=(shape,) * len(distances),
        in_specs=[VMEM] * (2 + len(pieces)),
        out_specs=(VMEM,) * len(distances),
        compiler_params=limit(12),
        name="scores",
    )(kept(decoder), kept(own_facts), *pieces)


def gradients_kernel(distances, own_facts, *refs):
    pieces, refs = refs[: 2 * len(distances)], refs[2 * len(distances) :]
    total = refs[-1]
    facts = facts_of(distances, own_facts, pieces)
    for columns, part in gradient_blocks(facts, pieces, total.shape[1]):
        total[:, columns] = part if len(refs) == 1 else refs[0][:, columns] + part


def gradients_of(distances, pairs, own_facts, shape, total=None):
    operands = [kept(own_facts)] + [kept(piece) for pair in pairs for piece in pair]
    operands += [] if total is None else [kept(total)]
    return pl.pallas_call(
        functools.partial(gradients_kernel, distances),
        out_shape=pltpu.VMEM(shape, jnp.float32),
        in_specs=[VMEM] * len(operands),
        out_specs=VMEM,
        input_output_aliases={} if total is None else {len(operands) - 1: 0},
        compiler_params=limit(16),
        name="gradients",
    )(*operands)


def last_gradients_kernel(distances, own_facts, *refs):
    pieces, (total, out, rounded, sems) = refs[:-4], refs[-4:]
    copies = []
    facts = facts_of(distances, own_facts, pieces)
    for columns, part in gradient_blocks(facts, pieces, out.shape[1]):
        rounded[:, columns] = (total[:, columns] + part).astype(out.dtype)
        copies.append(
            pltpu.make_async_copy(
                rounded.at[:, columns], out.at[:, columns], sems.at[len(copies)]
            )
        )
        copies[-1].start()
    for copy in copies:
        copy.wait()


def last_gradients(distances, pairs, own_facts, total):
    operands = [kept(own_facts)] + [kept(piece) for pair in pairs for piece in pair]
    operands.append(kept(total))
    return pl.pallas_call(
        functools.partial(last_gradients_kernel, distances),
        out_shape=jax.ShapeDtypeStruct(total.shape, jnp.bfloat16),
        in_specs=[VMEM] * len(operands),
        out_specs=ANY,
        scratch_shapes=[
            pltpu.VMEM(total.shape, jnp.bfloat16),
            pltpu.SemaphoreType.DMA((total.shape[1] // 256,)),
        ],
        compiler_params=limit(16),
        name="last_gradients",
    )(*operands)


def stamp_kernel(onward, back, for_onward, for_back, onward_out, back_out, rows, sems):
    start = onward.shape[0] - FACTS
    targets = (onward_out, back_out)
    for i, piece in enumerate((onward, back)):
        pltpu.make_async_copy(
            piece.at[start : start + 16, :], rows.at[i], sems.at[i]
        ).start()
    for i, values in enumerate((for_onward, for_back)):
        pltpu.make_async_copy(
            onward.at[start : start + 16, :], rows.at[i], sems.at[i]
        ).wait()
        value = values[:KPB]
        high = value.astype(jnp.bfloat16).astype(jnp.float32)
        low = value - high
        facts = rows[i].astype(jnp.float32)[2 * KPB :]
        rows[i] = jnp.concatenate([high, low, facts], axis=0).astype(jnp.bfloat16)
        pltpu.make_async_copy(
            rows.at[i], targets[i].at[start : start + 16, :], sems.at[2 + i]
        ).start()
    for i in range(2):
        pltpu.make_async_copy(
            rows.at[i], targets[i].at[start : start + 16, :], sems.at[2 + i]
        ).wait()


def stamp(pieces, values):
    return pl.pallas_call(
        stamp_kernel,
        out_shape=tuple(pltpu.VMEM(piece.shape, piece.dtype) for piece in pieces),
        in_specs=[ANY, ANY, VMEM, VMEM],
        out_specs=(ANY, ANY),
        scratch_shapes=[
            pltpu.VMEM((2, 16, 128), jnp.bfloat16),
            pltpu.SemaphoreType.DMA((4,)),
        ],
        input_output_aliases={0: 0, 1: 1},
        compiler_params=limit(4),
        name="stamp",
    )(*[kept(piece) for piece in pieces], *[kept(value) for value in values])


def unpack_kernel(owners, slots, own, onward, back, second, ahead, behind, opposite, out):
    owner = slots[...] // BLK_DEV
    start = onward.shape[0] - FACTS
    way = 1 - 2 * lax.axis_index("width")
    returned = [(0, own[...])]
    for distance, piece in ((-1, onward), (1, back)):
        rows = piece[start : start + 16, :].astype(jnp.float32)
        returned.append((distance, rows[:KPB] + rows[KPB : 2 * KPB]))
    returned += [(2 * way, second[...]), (3, ahead[...]), (-3, behind[...])]
    returned.append((4, opposite[...]))
    mine = [owner == peer_at(distance, owners) for distance, _ in returned]
    for k in range(KPB):
        total = jnp.zeros(owner.shape, jnp.float32)
        for here, (_, values) in zip(mine, returned):
            total = jnp.where(here, values[k : k + 1, :], total)
        out[pl.ds(k, ACT, stride=KPB), :] = total


def unpack(slots, *returned):
    tok_rows = slots.shape[1]
    return pl.pallas_call(
        functools.partial(unpack_kernel, lax.axis_size("dp")),
        out_shape=pltpu.VMEM((ACT * KPB, tok_rows), jnp.float32),
        in_specs=[VMEM] * (1 + len(returned)),
        out_specs=VMEM,
        compiler_params=limit(4),
        name="unpack",
    )(kept(slots), *[kept(x) for x in returned])


def every_owner(decoder, grad_out, active_blocks, feature_idx, acts, block_slot):
    tok_rows = grad_out.shape[0]
    owners = lax.axis_size("dp")
    ring = ring_of(owners)

    def shift(x, by):
        pairs = [(ring[i], ring[(i + by) % owners]) for i in range(owners)]
        return lax.ppermute(x, "dp", pairs)

    def hop(pieces):
        left, right = pieces
        return shift(left, 1), shift(right, -1)

    def crossed(pieces):
        right, left = pieces
        return shift(right, 1), shift(left, -1)

    def other_core(x):
        return lax.ppermute(x, "width", ((0, 1), (1, 0)))

    def return_by(distance, x):
        pairs = []
        for i in range(owners):
            pairs.append((2 * ring[i], 2 * ring[(i - distance) % owners]))
            pairs.append((2 * ring[i] + 1, 2 * ring[(i + distance) % owners] + 1))
        return lax.ppermute(x, ("dp", "width"), pairs)

    first_left, first_right, left, right, own_facts, slots = prepare(
        block_slot, active_blocks, feature_idx, acts, grad_out, owners
    )
    first_1 = hop((first_left, first_right))
    second_1 = crossed((right, left))
    decoder = fetch(decoder)
    first_1, decoder = lax.optimization_barrier((first_1, decoder))
    first_2 = hop(first_1)
    second_2 = crossed(second_1)
    pairs = [(first_left, first_right), (first_1[0], second_1[0]), (second_1[1], first_1[1])]
    distances = (0, -1, 1)
    own, onward, back = scores_of(distances, pairs, decoder, own_facts)
    total = gradients_of(distances, pairs, own_facts, decoder.shape)
    first_3 = hop(first_2)
    total, second_2 = lax.optimization_barrier((total, second_2))
    second_2 = stamp(second_2, (back, onward))
    second_3 = crossed(second_2)
    pairs = [(first_2[0], second_2[0]), (second_2[1], first_2[1])]
    mine, others = scores_of((-2, 2), pairs, decoder, own_facts, True)
    total = gradients_of((-2, 2), pairs, own_facts, decoder.shape, total)
    second = mine + other_core(others)
    total, first_3, second = lax.optimization_barrier((total, first_3, second))
    second = return_by(2, jnp.concatenate([second, jnp.zeros((24, 128), jnp.float32)]))[:8]
    first_4 = hop(first_3)
    pairs = [(first_3[0], second_3[0]), (second_3[1], first_3[1])]
    onward, back = scores_of((-3, 3), pairs, decoder, own_facts)
    ahead, behind = shift(onward, -3), shift(back, 3)
    (opposite,) = scores_of((4,), [first_4], decoder, own_facts)
    opposite = shift(opposite, -owners // 2)
    total, ahead, behind = lax.optimization_barrier((total, ahead, behind))
    decoder_grad = last_gradients((-3, 3, 4), pairs + [first_4], own_facts, total)
    decoder_grad, opposite = lax.optimization_barrier((decoder_grad, opposite))
    act_grad = unpack(slots, own, *second_3, second, ahead, behind, opposite)
    act_grad = act_grad + other_core(act_grad)
    return (decoder_grad, act_grad.T)


def send_back(picked):
    return lax.all_to_all(picked, "dp", split_axis=1, concat_axis=1, tiled=True)


def pack_slots(grad_out, target, slots_all, pair_coeffs, pair_columns, source_row):
    slot_row = jnp.zeros((slots_all,), jnp.int32).at[target].set(source_row)
    used = jnp.zeros((slots_all,), jnp.bool_).at[target].set(True)
    send_rows = jnp.where(used[:, None], grad_out[slot_row], jnp.zeros((), grad_out.dtype))
    send_acts = jnp.zeros((slots_all, KPB), pair_coeffs.dtype).at[target].set(pair_coeffs)
    send_cols = jnp.zeros((slots_all, KPB), jnp.int32).at[target].set(pair_columns)
    return (send_rows, send_acts, send_cols)


def some_owners(decoder, grad_out, active_blocks, feature_idx, acts, block_slot):
    tok_rows, half_width = grad_out.shape
    owners = lax.axis_size("dp")
    mean_load = tok_rows * ACT // owners
    owner_cap = mean_load + min(mean_load // 2, tok_rows - mean_load)
    block_cap = (owner_cap + 2) // 3
    block_ids = active_blocks.reshape(-1)
    pair_count = block_ids.shape[0]
    table_pos = jnp.arange(block_slot.shape[0], dtype=jnp.int32)
    slot_of = jnp.sum(
        jnp.where(block_ids[:, None] == table_pos[None, :], block_slot[None, :], 0), axis=1
    )
    pair_pos = jnp.arange(pair_count, dtype=jnp.int32)
    source_row = pair_pos // ACT
    pair_coeffs = acts.reshape(pair_count, KPB)
    pair_feats = feature_idx.reshape(pair_count, KPB)
    earlier = (block_ids[:, None] == block_ids[None, :]) & (pair_pos[None, :] < pair_pos[:, None])
    position = jnp.sum(earlier.astype(jnp.int32), axis=1)
    slot_cols = owners * block_cap
    target = slot_of % BLK_DEV * slot_cols + slot_of // BLK_DEV * block_cap + position
    slots_all = BLK_DEV * slot_cols
    send_rows, send_acts, send_cols = pack_slots(
        grad_out, target, slots_all, pair_coeffs, pair_feats, source_row
    )
    rows, coeffs, feature_pos = (
        lax.all_to_all(
            send_rows.reshape(BLK_DEV, slot_cols, half_width),
            "dp",
            split_axis=1,
            concat_axis=1,
            tiled=True,
        ),
        lax.all_to_all(
            send_acts.reshape(BLK_DEV, slot_cols, KPB),
            "dp",
            split_axis=1,
            concat_axis=1,
            tiled=True,
        ),
        lax.all_to_all(
            send_cols.reshape(BLK_DEV, slot_cols, KPB),
            "dp",
            split_axis=1,
            concat_axis=1,
            tiled=True,
        ),
    )
    weights = decoder.reshape(BLK_DEV, BW, half_width)
    scores = jnp.einsum("bnd,bfd->bnf", rows, weights, preferred_element_type=jnp.float32)
    picked = jnp.take_along_axis(scores, feature_pos, axis=2)
    returned = send_back(picked)
    feature_axis = jnp.arange(BW, dtype=jnp.int32)
    matches = feature_pos[..., None] == feature_axis
    dense = jnp.sum(jnp.where(matches, coeffs[..., None].astype(jnp.float32), 0.0), axis=2).astype(
        jnp.bfloat16
    )
    grads = jnp.einsum("bnf,bnd->bfd", dense, rows, preferred_element_type=jnp.float32)
    decoder_grad = grads.astype(jnp.bfloat16).reshape(BLK_DEV * BW, half_width)
    pair_vals = returned.reshape(slots_all, KPB)[target]
    act_grad = pair_vals.reshape(tok_rows, ACT * KPB)
    act_grad = lax.psum(act_grad, "width")
    return (decoder_grad, act_grad)


def per_device(*args):
    if lax.axis_size("dp") == ACT:
        return every_owner(*args)
    return some_owners(*args)


def solution(mesh):
    in_specs = (
        P(("groups", "dp"), "width"),
        P(("groups", "dp"), "width"),
        P(("groups", "dp"), None),
        P(("groups", "dp"), None),
        P(("groups", "dp"), None),
        P("groups"),
    )
    out_specs = (P(("groups", "dp"), "width"), P(("groups", "dp"), None))
    return jax.shard_map(
        per_device, mesh=mesh, in_specs=in_specs, out_specs=out_specs, check_vma=False
    )
```

```python
import functools

import jax
import jax.numpy as jnp
from jax import lax
from jax.experimental import pallas as pl
from jax.experimental.pallas import tpu as pltpu
from jax.sharding import PartitionSpec as P

BW = 128
BLK_DEV = 4
ACT = 8
KPB = 4
SMEM = pl.BlockSpec(memory_space=pltpu.SMEM)
VMEM = pl.BlockSpec(memory_space=pltpu.VMEM)
ANY = pl.BlockSpec(memory_space=pl.ANY)
HBM = pl.BlockSpec(memory_space=pltpu.HBM)


def limit(mebibytes):
    return pltpu.CompilerParams(vmem_limit_bytes=mebibytes * 2**20)


def kept(x):
    return pltpu.with_memory_space_constraint(x, pltpu.VMEM)


def far(x):
    return pltpu.with_memory_space_constraint(x, pltpu.HBM)


def ring_of(owners):
    return list(range(0, owners, 2)) + list(range(owners - 1, 0, -2))


def peer_at(distance, owners):
    me = lax.axis_index("dp")
    half_ring = owners // 2
    place = jnp.where(lax.rem(me, 2) == 0, lax.div(me, 2), owners - 1 - lax.div(me, 2))
    at = lax.rem(place + owners + distance, owners)
    return jnp.where(at < half_ring, 2 * at, 2 * (owners - 1 - at) + 1)


ROW_SHIFT = BLK_DEV * BW // 2
FACTS = ACT // 2 * 2 * KPB
LAST_FACTS = 16


def facts_for(owner_id, owner, first_row, feats, acts):
    mine = owner == owner_id
    rows = [
        jnp.sum(jnp.where(mine, first_row + feats[k], 0.0), axis=0, keepdims=True) - ROW_SHIFT
        for k in range(KPB)
    ]
    values = [
        jnp.sum(jnp.where(mine, acts[k], 0.0), axis=0, keepdims=True) for k in range(KPB)
    ]
    return jnp.concatenate(rows + values, axis=0)


def prepare_kernel(owners, *refs):
    sources, refs = refs[:5], refs[5:]
    outs, refs = refs[:6], refs[6:]
    first_left, first_right, left, right, own_facts, slots = outs
    block_slot, active, feats, acts, halves, wide_feats, wide_acts, sems = refs
    cut = halves.shape[2]
    copies = []
    for source, target in zip(sources[:4], (block_slot, active, feats, acts)):
        copies.append(pltpu.make_async_copy(source, target, sems.at[len(copies)]))
    for side in range(2):
        copies.append(
            pltpu.make_async_copy(
                sources[4].at[:, side * cut : (side + 1) * cut],
                halves.at[side],
                sems.at[len(copies)],
            )
        )
    for copy in copies:
        copy.start()
    for copy in copies[:4]:
        copy.wait()
    named = active[...]
    slot = jnp.zeros_like(named)
    for block in range(block_slot.shape[0]):
        slot = jnp.where(named == block, block_slot[block], slot)
    slots[...] = slot
    wide_feats[...] = feats[...].astype(jnp.float32)
    wide_acts[...] = acts[...].astype(jnp.float32)
    features = [wide_feats[pl.ds(k, ACT, stride=KPB), :] for k in range(KPB)]
    values = [wide_acts[pl.ds(k, ACT, stride=KPB), :] for k in range(KPB)]
    first_row = (slot % BLK_DEV * BW).astype(jnp.float32)

    def facts(distance):
        return facts_for(
            peer_at(distance, owners), slot // BLK_DEV, first_row, features, values
        )

    def store_facts(target, blocks):
        rows = jnp.concatenate(blocks, axis=0)
        target[target.shape[0] - rows.shape[0] :, :] = rows.astype(jnp.bfloat16)

    own_facts[...] = facts(0)
    opposite = facts(owners // 2)
    none = jnp.zeros_like(opposite)
    store_facts(first_left, [opposite, none])
    for target, sign in ((left, -1), (right, 1)):
        store_facts(target, [facts(sign * d) for d in range(1, owners // 2)] + [none])
    tok_rows = halves.shape[1]
    for side, targets in ((0, (first_left, left)), (1, (first_right, right))):
        copies[4 + side].wait()
        for j in range(cut // 128):
            part = halves[side, :, j * 128 : (j + 1) * 128]
            for target in targets:
                target[j * tok_rows : (j + 1) * tok_rows, :] = part


def prepare(block_slot, active_blocks, feature_idx, acts, grad_out, owners):
    tok_rows, width = grad_out.shape
    plain = width // 256 * tok_rows

    def piece(extra):
        return pltpu.VMEM((plain + extra, 128), grad_out.dtype)

    return pl.pallas_call(
        functools.partial(prepare_kernel, owners),
        out_shape=(
            piece(LAST_FACTS),
            piece(0),
            piece(FACTS),
            piece(FACTS),
            pltpu.VMEM((2 * KPB, tok_rows), jnp.float32),
            pltpu.VMEM((ACT, tok_rows), jnp.int32),
        ),
        in_specs=[HBM] * 5,
        out_specs=(VMEM,) * 6,
        scratch_shapes=[
            pltpu.SMEM(block_slot.shape, jnp.int32),
            pltpu.VMEM((ACT, tok_rows), jnp.int32),
            pltpu.VMEM((ACT * KPB, tok_rows), jnp.int32),
            pltpu.VMEM((ACT * KPB, tok_rows), acts.dtype),
            pltpu.VMEM((2, tok_rows, width // 2), grad_out.dtype),
            pltpu.VMEM((ACT * KPB, tok_rows), jnp.float32),
            pltpu.VMEM((ACT * KPB, tok_rows), jnp.float32),
            pltpu.SemaphoreType.DMA((6,)),
        ],
        compiler_params=limit(8),
        name="prepare",
    )(far(block_slot), far(active_blocks.T), far(feature_idx.T), far(acts.T), far(grad_out))


def fetch_kernel(source, target, sem):
    copy = pltpu.make_async_copy(source, target, sem)
    copy.start()
    copy.wait()


def fetch(x):
    return pl.pallas_call(
        fetch_kernel,
        out_shape=pltpu.VMEM(x.shape, x.dtype),
        in_specs=[HBM],
        out_specs=VMEM,
        scratch_shapes=[pltpu.SemaphoreType.DMA],
        compiler_params=limit(8),
        name="fetch",
    )(far(x))


def block_and_rows(here):
    at_row = here[:KPB].astype(jnp.int32) + ROW_SHIFT
    return at_row[:1] // BW, at_row % BW


def row_axis_of(tok_rows):
    return lax.broadcasted_iota(jnp.int32, (BW, tok_rows), 0)


def coefficients(here):
    block, feats = block_and_rows(here)
    row_axis = row_axis_of(here.shape[1])
    dense = jnp.zeros(row_axis.shape, jnp.float32)
    for k in range(KPB):
        dense = jnp.where(row_axis == feats[k : k + 1], here[KPB + k : KPB + k + 1], dense)
    parts = [jnp.where(block == b, dense, 0.0) for b in range(BLK_DEV)]
    return jnp.concatenate(parts, axis=0).astype(jnp.bfloat16)


def pick(scores, here):
    block, feats = block_and_rows(here)
    row_axis = row_axis_of(here.shape[1])
    mine = scores[:BW]
    for b in range(1, BLK_DEV):
        mine = jnp.where(block == b, scores[b * BW : (b + 1) * BW], mine)
    return [
        jnp.sum(jnp.where(row_axis == feats[k : k + 1], mine, 0.0), axis=0, keepdims=True)
        for k in range(KPB)
    ]


def facts_in(piece, distance, tok_rows):
    facts = piece[piece.shape[0] - FACTS :, :].astype(jnp.float32)
    return facts[(abs(distance) - 1) * 2 * KPB : abs(distance) * 2 * KPB]


def columns_of(pieces, tok_rows, parts):
    rows = [
        jnp.concatenate([piece[j * tok_rows : (j + 1) * tok_rows, :] for j in parts], axis=1)
        for piece in pieces
    ]
    return jnp.concatenate(rows, axis=0) if len(rows) > 1 else rows[0]


def picks_of(facts, decoder, pieces):
    picks = []
    tok_rows = facts[0].shape[1]
    cut = decoder.shape[1] // 2
    for first in range(0, len(facts), 2):
        count = min(2, len(facts) - first)
        scores = None
        for side in range(2):
            part = lax.dot_general(
                decoder[:, side * cut : (side + 1) * cut],
                columns_of(
                    pieces[2 * first + side : 2 * (first + count) : 2],
                    tok_rows,
                    range(cut // 128),
                ),
                (((1,), (1,)), ((), ())),
                preferred_element_type=jnp.float32,
            )
            scores = part if scores is None else scores + part
        for i in range(first, first + count):
            here = scores[:, (i - first) * tok_rows : (i - first + 1) * tok_rows]
            picks.append(jnp.concatenate(pick(here, facts[i]) * 2, axis=0))
    return picks


def gradient_blocks(facts, pieces, width):
    tok_rows = facts[0].shape[1]
    cut = width // 2
    dense = jnp.concatenate([coefficients(here) for here in facts], axis=1)
    for side in range(2):
        for j in range(0, cut // 128, 2):
            rows = columns_of(pieces[side::2], tok_rows, (j, j + 1))
            part = jnp.dot(dense, rows, preferred_element_type=jnp.float32)
            yield slice(side * cut + j * 128, side * cut + (j + 2) * 128), part


def last_facts_in(piece):
    return piece[piece.shape[0] - LAST_FACTS :, :].astype(jnp.float32)[: 2 * KPB]


def facts_of(distances, own_facts, pieces):
    facts = []
    for i, d in enumerate(distances):
        if d == 0:
            facts.append(own_facts[...])
        elif d == 4:
            facts.append(last_facts_in(pieces[2 * i]))
        else:
            facts.append(facts_in(pieces[2 * i + (d < 0)], d, own_facts.shape[1]))
    return facts


def scores_kernel(distances, split, decoder, own_facts, *refs):
    pieces, picked = refs[: 2 * len(distances)], refs[2 * len(distances) :]
    picks = picks_of(facts_of(distances, own_facts, pieces), decoder, pieces)
    if split:
        first = lax.axis_index("width") == 0
        picks = [jnp.where(first, *picks), jnp.where(first, *picks[::-1])]
    for target, values in zip(picked, picks):
        target[...] = values


def scores_of(distances, pairs, decoder, own_facts, split=False):
    pieces = [kept(piece) for pair in pairs for piece in pair]
    shape = pltpu.VMEM(own_facts.shape, jnp.float32)
    return pl.pallas_call(
        functools.partial(scores_kernel, distances, split),
        out_shape=(shape,) * len(distances),
        in_specs=[VMEM] * (2 + len(pieces)),
        out_specs=(VMEM,) * len(distances),
        compiler_params=limit(12),
        name="scores",
    )(kept(decoder), kept(own_facts), *pieces)


def gradients_kernel(distances, own_facts, *refs):
    pieces, refs = refs[: 2 * len(distances)], refs[2 * len(distances) :]
    total = refs[-1]
    facts = facts_of(distances, own_facts, pieces)
    for columns, part in gradient_blocks(facts, pieces, total.shape[1]):
        total[:, columns] = part if len(refs) == 1 else refs[0][:, columns] + part


def gradients_of(distances, pairs, own_facts, shape, total=None):
    operands = [kept(own_facts)] + [kept(piece) for pair in pairs for piece in pair]
    operands += [] if total is None else [kept(total)]
    return pl.pallas_call(
        functools.partial(gradients_kernel, distances),
        out_shape=pltpu.VMEM(shape, jnp.float32),
        in_specs=[VMEM] * len(operands),
        out_specs=VMEM,
        input_output_aliases={} if total is None else {len(operands) - 1: 0},
        compiler_params=limit(16),
        name="gradients",
    )(*operands)


def last_gradients_kernel(distances, own_facts, *refs):
    pieces, (total, out, rounded, sems) = refs[:-4], refs[-4:]
    copies = []
    facts = facts_of(distances, own_facts, pieces)
    for columns, part in gradient_blocks(facts, pieces, out.shape[1]):
        rounded[:, columns] = (total[:, columns] + part).astype(out.dtype)
        copies.append(
            pltpu.make_async_copy(
                rounded.at[:, columns], out.at[:, columns], sems.at[len(copies)]
            )
        )
        copies[-1].start()
    for copy in copies:
        copy.wait()


def last_gradients(distances, pairs, own_facts, total):
    operands = [kept(own_facts)] + [kept(piece) for pair in pairs for piece in pair]
    operands.append(kept(total))
    return pl.pallas_call(
        functools.partial(last_gradients_kernel, distances),
        out_shape=jax.ShapeDtypeStruct(total.shape, jnp.bfloat16),
        in_specs=[VMEM] * len(operands),
        out_specs=ANY,
        scratch_shapes=[
            pltpu.VMEM(total.shape, jnp.bfloat16),
            pltpu.SemaphoreType.DMA((total.shape[1] // 256,)),
        ],
        compiler_params=limit(16),
        name="last_gradients",
    )(*operands)


def stamp_kernel(onward, back, for_onward, for_back, onward_out, back_out, rows, sems):
    start = onward.shape[0] - FACTS
    targets = (onward_out, back_out)
    for i, piece in enumerate((onward, back)):
        pltpu.make_async_copy(
            piece.at[start : start + 16, :], rows.at[i], sems.at[i]
        ).start()
    for i, values in enumerate((for_onward, for_back)):
        pltpu.make_async_copy(
            onward.at[start : start + 16, :], rows.at[i], sems.at[i]
        ).wait()
        value = values[:KPB]
        high = value.astype(jnp.bfloat16).astype(jnp.float32)
        low = value - high
        facts = rows[i].astype(jnp.float32)[2 * KPB :]
        rows[i] = jnp.concatenate([high, low, facts], axis=0).astype(jnp.bfloat16)
        pltpu.make_async_copy(
            rows.at[i], targets[i].at[start : start + 16, :], sems.at[2 + i]
        ).start()
    for i in range(2):
        pltpu.make_async_copy(
            rows.at[i], targets[i].at[start : start + 16, :], sems.at[2 + i]
        ).wait()


def stamp(pieces, values):
    return pl.pallas_call(
        stamp_kernel,
        out_shape=tuple(pltpu.VMEM(piece.shape, piece.dtype) for piece in pieces),
        in_specs=[ANY, ANY, VMEM, VMEM],
        out_specs=(ANY, ANY),
        scratch_shapes=[
            pltpu.VMEM((2, 16, 128), jnp.bfloat16),
            pltpu.SemaphoreType.DMA((4,)),
        ],
        input_output_aliases={0: 0, 1: 1},
        compiler_params=limit(4),
        name="stamp",
    )(*[kept(piece) for piece in pieces], *[kept(value) for value in values])


def unpack_kernel(owners, slots, own, onward, back, second, third, opposite, out):
    owner = slots[...] // BLK_DEV
    start = onward.shape[0] - FACTS
    way = 1 - 2 * lax.axis_index("width")
    returned = [(0, own[...])]
    for distance, piece in ((-1, onward), (1, back)):
        rows = piece[start : start + 16, :].astype(jnp.float32)
        returned.append((distance, rows[:KPB] + rows[KPB : 2 * KPB]))
    returned += [(2 * way, second[...]), (3 * way, third[...]), (4, opposite[...])]
    mine = [owner == peer_at(distance, owners) for distance, _ in returned]
    for k in range(KPB):
        total = jnp.zeros(owner.shape, jnp.float32)
        for here, (_, values) in zip(mine, returned):
            total = jnp.where(here, values[k : k + 1, :], total)
        out[pl.ds(k, ACT, stride=KPB), :] = total


def unpack(slots, *returned):
    tok_rows = slots.shape[1]
    return pl.pallas_call(
        functools.partial(unpack_kernel, lax.axis_size("dp")),
        out_shape=pltpu.VMEM((ACT * KPB, tok_rows), jnp.float32),
        in_specs=[VMEM] * (1 + len(returned)),
        out_specs=VMEM,
        compiler_params=limit(4),
        name="unpack",
    )(kept(slots), *[kept(x) for x in returned])


def every_owner(decoder, grad_out, active_blocks, feature_idx, acts, block_slot):
    tok_rows = grad_out.shape[0]
    owners = lax.axis_size("dp")
    ring = ring_of(owners)

    def shift(x, by):
        pairs = [(ring[i], ring[(i + by) % owners]) for i in range(owners)]
        return lax.ppermute(x, "dp", pairs)

    def hop(pieces):
        left, right = pieces
        return shift(left, 1), shift(right, -1)

    def crossed(pieces):
        right, left = pieces
        return shift(right, 1), shift(left, -1)

    def other_core(x):
        return lax.ppermute(x, "width", ((0, 1), (1, 0)))

    def return_by(distance, x):
        pairs = []
        for i in range(owners):
            pairs.append((2 * ring[i], 2 * ring[(i - distance) % owners]))
            pairs.append((2 * ring[i] + 1, 2 * ring[(i + distance) % owners] + 1))
        return lax.ppermute(x, ("dp", "width"), pairs)

    first_left, first_right, left, right, own_facts, slots = prepare(
        block_slot, active_blocks, feature_idx, acts, grad_out, owners
    )
    first_1 = hop((first_left, first_right))
    second_1 = crossed((right, left))
    decoder = fetch(decoder)
    first_1, decoder = lax.optimization_barrier((first_1, decoder))
    first_2 = hop(first_1)
    second_2 = crossed(second_1)
    pairs = [(first_left, first_right), (first_1[0], second_1[0]), (second_1[1], first_1[1])]
    distances = (0, -1, 1)
    own, onward, back = scores_of(distances, pairs, decoder, own_facts)
    total = gradients_of(distances, pairs, own_facts, decoder.shape)
    first_3 = hop(first_2)
    second_2 = stamp(second_2, (back, onward))
    second_3 = crossed(second_2)
    pairs = [(first_2[0], second_2[0]), (second_2[1], first_2[1])]
    mine, others = scores_of((-2, 2), pairs, decoder, own_facts, True)
    total = gradients_of((-2, 2), pairs, own_facts, decoder.shape, total)
    second = mine + other_core(others)
    total, first_3, second = lax.optimization_barrier((total, first_3, second))
    second = return_by(2, jnp.concatenate([second, jnp.zeros((24, 128), jnp.float32)]))[:8]
    first_4 = hop(first_3)
    pairs = [(first_3[0], second_3[0]), (second_3[1], first_3[1])]
    mine, others = scores_of((-3, 3), pairs, decoder, own_facts, True)
    third = mine + other_core(others)
    third = return_by(3, third)
    total, first_4 = lax.optimization_barrier((total, first_4))
    (opposite,) = scores_of((4,), [first_4], decoder, own_facts)
    opposite = shift(opposite, -owners // 2)
    total, third = lax.optimization_barrier((total, third))
    decoder_grad = last_gradients((-3, 3, 4), pairs + [first_4], own_facts, total)
    decoder_grad, opposite = lax.optimization_barrier((decoder_grad, opposite))
    act_grad = unpack(slots, own, *second_3, second, third, opposite)
    act_grad = act_grad + other_core(act_grad)
    return (decoder_grad, act_grad.T)


def send_back(picked):
    return lax.all_to_all(picked, "dp", split_axis=1, concat_axis=1, tiled=True)


def pack_slots(grad_out, target, slots_all, pair_coeffs, pair_columns, source_row):
    slot_row = jnp.zeros((slots_all,), jnp.int32).at[target].set(source_row)
    used = jnp.zeros((slots_all,), jnp.bool_).at[target].set(True)
    send_rows = jnp.where(used[:, None], grad_out[slot_row], jnp.zeros((), grad_out.dtype))
    send_acts = jnp.zeros((slots_all, KPB), pair_coeffs.dtype).at[target].set(pair_coeffs)
    send_cols = jnp.zeros((slots_all, KPB), jnp.int32).at[target].set(pair_columns)
    return (send_rows, send_acts, send_cols)


def some_owners(decoder, grad_out, active_blocks, feature_idx, acts, block_slot):
    tok_rows, half_width = grad_out.shape
    owners = lax.axis_size("dp")
    mean_load = tok_rows * ACT // owners
    owner_cap = mean_load + min(mean_load // 2, tok_rows - mean_load)
    block_cap = (owner_cap + 2) // 3
    block_ids = active_blocks.reshape(-1)
    pair_count = block_ids.shape[0]
    table_pos = jnp.arange(block_slot.shape[0], dtype=jnp.int32)
    slot_of = jnp.sum(
        jnp.where(block_ids[:, None] == table_pos[None, :], block_slot[None, :], 0), axis=1
    )
    pair_pos = jnp.arange(pair_count, dtype=jnp.int32)
    source_row = pair_pos // ACT
    pair_coeffs = acts.reshape(pair_count, KPB)
    pair_feats = feature_idx.reshape(pair_count, KPB)
    earlier = (block_ids[:, None] == block_ids[None, :]) & (pair_pos[None, :] < pair_pos[:, None])
    position = jnp.sum(earlier.astype(jnp.int32), axis=1)
    slot_cols = owners * block_cap
    target = slot_of % BLK_DEV * slot_cols + slot_of // BLK_DEV * block_cap + position
    slots_all = BLK_DEV * slot_cols
    send_rows, send_acts, send_cols = pack_slots(
        grad_out, target, slots_all, pair_coeffs, pair_feats, source_row
    )
    rows, coeffs, feature_pos = (
        lax.all_to_all(
            send_rows.reshape(BLK_DEV, slot_cols, half_width),
            "dp",
            split_axis=1,
            concat_axis=1,
            tiled=True,
        ),
        lax.all_to_all(
            send_acts.reshape(BLK_DEV, slot_cols, KPB),
            "dp",
            split_axis=1,
            concat_axis=1,
            tiled=True,
        ),
        lax.all_to_all(
            send_cols.reshape(BLK_DEV, slot_cols, KPB),
            "dp",
            split_axis=1,
            concat_axis=1,
            tiled=True,
        ),
    )
    weights = decoder.reshape(BLK_DEV, BW, half_width)
    scores = jnp.einsum("bnd,bfd->bnf", rows, weights, preferred_element_type=jnp.float32)
    picked = jnp.take_along_axis(scores, feature_pos, axis=2)
    returned = send_back(picked)
    feature_axis = jnp.arange(BW, dtype=jnp.int32)
    matches = feature_pos[..., None] == feature_axis
    dense = jnp.sum(jnp.where(matches, coeffs[..., None].astype(jnp.float32), 0.0), axis=2).astype(
        jnp.bfloat16
    )
    grads = jnp.einsum("bnf,bnd->bfd", dense, rows, preferred_element_type=jnp.float32)
    decoder_grad = grads.astype(jnp.bfloat16).reshape(BLK_DEV * BW, half_width)
    pair_vals = returned.reshape(slots_all, KPB)[target]
    act_grad = pair_vals.reshape(tok_rows, ACT * KPB)
    act_grad = lax.psum(act_grad, "width")
    return (decoder_grad, act_grad)


def per_device(*args):
    if lax.axis_size("dp") == ACT:
        return every_owner(*args)
    return some_owners(*args)


def solution(mesh):
    in_specs = (
        P(("groups", "dp"), "width"),
        P(("groups", "dp"), "width"),
        P(("groups", "dp"), None),
        P(("groups", "dp"), None),
        P(("groups", "dp"), None),
        P("groups"),
    )
    out_specs = (P(("groups", "dp"), "width"), P(("groups", "dp"), None))
    return jax.shard_map(
        per_device, mesh=mesh, in_specs=in_specs, out_specs=out_specs, check_vma=False
    )
```

```python
import functools

import jax
import jax.numpy as jnp
from jax import lax
from jax.experimental import pallas as pl
from jax.experimental.pallas import tpu as pltpu
from jax.sharding import PartitionSpec as P

BW = 128
BLK_DEV = 4
ACT = 8
KPB = 4
SMEM = pl.BlockSpec(memory_space=pltpu.SMEM)
VMEM = pl.BlockSpec(memory_space=pltpu.VMEM)
ANY = pl.BlockSpec(memory_space=pl.ANY)
HBM = pl.BlockSpec(memory_space=pltpu.HBM)


def limit(mebibytes):
    return pltpu.CompilerParams(vmem_limit_bytes=mebibytes * 2**20)


def kept(x):
    return pltpu.with_memory_space_constraint(x, pltpu.VMEM)


def far(x):
    return pltpu.with_memory_space_constraint(x, pltpu.HBM)


def ring_of(owners):
    return list(range(0, owners, 2)) + list(range(owners - 1, 0, -2))


def peer_at(distance, owners):
    me = lax.axis_index("dp")
    half_ring = owners // 2
    place = jnp.where(lax.rem(me, 2) == 0, lax.div(me, 2), owners - 1 - lax.div(me, 2))
    at = lax.rem(place + owners + distance, owners)
    return jnp.where(at < half_ring, 2 * at, 2 * (owners - 1 - at) + 1)


ROW_SHIFT = BLK_DEV * BW // 2
FACTS = ACT // 2 * 2 * KPB
LAST_FACTS = 16


def facts_for(owner_id, owner, first_row, feats, acts):
    mine = owner == owner_id
    rows = [
        jnp.sum(jnp.where(mine, first_row + feats[k], 0.0), axis=0, keepdims=True) - ROW_SHIFT
        for k in range(KPB)
    ]
    values = [
        jnp.sum(jnp.where(mine, acts[k], 0.0), axis=0, keepdims=True) for k in range(KPB)
    ]
    return jnp.concatenate(rows + values, axis=0)


def prepare_kernel(owners, *refs):
    sources, refs = refs[:5], refs[5:]
    outs, refs = refs[:6], refs[6:]
    first_left, first_right, left, right, own_facts, slots = outs
    block_slot, active, feats, acts, halves, wide_feats, wide_acts, sems = refs
    cut = halves.shape[2]
    copies = []
    for source, target in zip(sources[:4], (block_slot, active, feats, acts)):
        copies.append(pltpu.make_async_copy(source, target, sems.at[len(copies)]))
    for side in range(2):
        copies.append(
            pltpu.make_async_copy(
                sources[4].at[:, side * cut : (side + 1) * cut],
                halves.at[side],
                sems.at[len(copies)],
            )
        )
    for copy in copies:
        copy.start()
    for copy in copies[:4]:
        copy.wait()
    named = active[...]
    slot = jnp.zeros_like(named)
    for block in range(block_slot.shape[0]):
        slot = jnp.where(named == block, block_slot[block], slot)
    slots[...] = slot
    wide_feats[...] = feats[...].astype(jnp.float32)
    wide_acts[...] = acts[...].astype(jnp.float32)
    features = [wide_feats[pl.ds(k, ACT, stride=KPB), :] for k in range(KPB)]
    values = [wide_acts[pl.ds(k, ACT, stride=KPB), :] for k in range(KPB)]
    first_row = (slot % BLK_DEV * BW).astype(jnp.float32)

    def facts(distance):
        return facts_for(
            peer_at(distance, owners), slot // BLK_DEV, first_row, features, values
        )

    def store_facts(target, blocks):
        rows = jnp.concatenate(blocks, axis=0)
        target[target.shape[0] - rows.shape[0] :, :] = rows.astype(jnp.bfloat16)

    own_facts[...] = facts(0)
    opposite = facts(owners // 2)
    none = jnp.zeros_like(opposite)
    store_facts(first_left, [opposite, none])
    for target, sign in ((left, -1), (right, 1)):
        store_facts(target, [facts(sign * d) for d in range(1, owners // 2)] + [none])
    tok_rows = halves.shape[1]
    for side, targets in ((0, (first_left, left)), (1, (first_right, right))):
        copies[4 + side].wait()
        for j in range(cut // 128):
            part = halves[side, :, j * 128 : (j + 1) * 128]
            for target in targets:
                target[j * tok_rows : (j + 1) * tok_rows, :] = part


def prepare(block_slot, active_blocks, feature_idx, acts, grad_out, owners):
    tok_rows, width = grad_out.shape
    plain = width // 256 * tok_rows

    def piece(extra):
        return pltpu.VMEM((plain + extra, 128), grad_out.dtype)

    return pl.pallas_call(
        functools.partial(prepare_kernel, owners),
        out_shape=(
            piece(LAST_FACTS),
            piece(0),
            piece(FACTS),
            piece(FACTS),
            pltpu.VMEM((2 * KPB, tok_rows), jnp.float32),
            pltpu.VMEM((ACT, tok_rows), jnp.int32),
        ),
        in_specs=[HBM] * 5,
        out_specs=(VMEM,) * 6,
        scratch_shapes=[
            pltpu.SMEM(block_slot.shape, jnp.int32),
            pltpu.VMEM((ACT, tok_rows), jnp.int32),
            pltpu.VMEM((ACT * KPB, tok_rows), jnp.int32),
            pltpu.VMEM((ACT * KPB, tok_rows), acts.dtype),
            pltpu.VMEM((2, tok_rows, width // 2), grad_out.dtype),
            pltpu.VMEM((ACT * KPB, tok_rows), jnp.float32),
            pltpu.VMEM((ACT * KPB, tok_rows), jnp.float32),
            pltpu.SemaphoreType.DMA((6,)),
        ],
        compiler_params=limit(8),
        name="prepare",
    )(far(block_slot), far(active_blocks.T), far(feature_idx.T), far(acts.T), far(grad_out))


def fetch_kernel(source, target, sem):
    copy = pltpu.make_async_copy(source, target, sem)
    copy.start()
    copy.wait()


def fetch(x):
    return pl.pallas_call(
        fetch_kernel,
        out_shape=pltpu.VMEM(x.shape, x.dtype),
        in_specs=[HBM],
        out_specs=VMEM,
        scratch_shapes=[pltpu.SemaphoreType.DMA],
        compiler_params=limit(8),
        name="fetch",
    )(far(x))


def block_and_rows(here):
    at_row = here[:KPB].astype(jnp.int32) + ROW_SHIFT
    return at_row[:1] // BW, at_row % BW


def row_axis_of(tok_rows):
    return lax.broadcasted_iota(jnp.int32, (BW, tok_rows), 0)


def coefficients(here):
    block, feats = block_and_rows(here)
    row_axis = row_axis_of(here.shape[1])
    dense = jnp.zeros(row_axis.shape, jnp.float32)
    for k in range(KPB):
        dense = jnp.where(row_axis == feats[k : k + 1], here[KPB + k : KPB + k + 1], dense)
    parts = [jnp.where(block == b, dense, 0.0) for b in range(BLK_DEV)]
    return jnp.concatenate(parts, axis=0).astype(jnp.bfloat16)


def pick(scores, here):
    block, feats = block_and_rows(here)
    row_axis = row_axis_of(here.shape[1])
    mine = scores[:BW]
    for b in range(1, BLK_DEV):
        mine = jnp.where(block == b, scores[b * BW : (b + 1) * BW], mine)
    return [
        jnp.sum(jnp.where(row_axis == feats[k : k + 1], mine, 0.0), axis=0, keepdims=True)
        for k in range(KPB)
    ]


def facts_in(piece, distance, tok_rows):
    facts = piece[piece.shape[0] - FACTS :, :].astype(jnp.float32)
    return facts[(abs(distance) - 1) * 2 * KPB : abs(distance) * 2 * KPB]


def columns_of(pieces, tok_rows, parts):
    rows = [
        jnp.concatenate([piece[j * tok_rows : (j + 1) * tok_rows, :] for j in parts], axis=1)
        for piece in pieces
    ]
    return jnp.concatenate(rows, axis=0) if len(rows) > 1 else rows[0]


def picks_of(facts, decoder, pieces):
    picks = []
    tok_rows = facts[0].shape[1]
    cut = decoder.shape[1] // 2
    for first in range(0, len(facts), 2):
        count = min(2, len(facts) - first)
        scores = None
        for side in range(2):
            part = lax.dot_general(
                decoder[:, side * cut : (side + 1) * cut],
                columns_of(
                    pieces[2 * first + side : 2 * (first + count) : 2],
                    tok_rows,
                    range(cut // 128),
                ),
                (((1,), (1,)), ((), ())),
                preferred_element_type=jnp.float32,
            )
            scores = part if scores is None else scores + part
        for i in range(first, first + count):
            here = scores[:, (i - first) * tok_rows : (i - first + 1) * tok_rows]
            picks.append(jnp.concatenate(pick(here, facts[i]) * 2, axis=0))
    return picks


def gradient_blocks(facts, pieces, width):
    tok_rows = facts[0].shape[1]
    cut = width // 2
    dense = jnp.concatenate([coefficients(here) for here in facts], axis=1)
    for side in range(2):
        for j in range(0, cut // 128, 2):
            rows = columns_of(pieces[side::2], tok_rows, (j, j + 1))
            part = jnp.dot(dense, rows, preferred_element_type=jnp.float32)
            yield slice(side * cut + j * 128, side * cut + (j + 2) * 128), part


def last_facts_in(piece):
    return piece[piece.shape[0] - LAST_FACTS :, :].astype(jnp.float32)[: 2 * KPB]


def facts_of(distances, own_facts, pieces):
    facts = []
    for i, d in enumerate(distances):
        if d == 0:
            facts.append(own_facts[...])
        elif d == 4:
            facts.append(last_facts_in(pieces[2 * i]))
        else:
            facts.append(facts_in(pieces[2 * i + (d < 0)], d, own_facts.shape[1]))
    return facts


def scores_kernel(distances, split, decoder, own_facts, *refs):
    pieces, picked = refs[: 2 * len(distances)], refs[2 * len(distances) :]
    picks = picks_of(facts_of(distances, own_facts, pieces), decoder, pieces)
    if split:
        first = lax.axis_index("width") == 0
        picks = [jnp.where(first, *picks), jnp.where(first, *picks[::-1])]
    for target, values in zip(picked, picks):
        target[...] = values


def scores_of(distances, pairs, decoder, own_facts, split=False):
    pieces = [kept(piece) for pair in pairs for piece in pair]
    shape = pltpu.VMEM(own_facts.shape, jnp.float32)
    return pl.pallas_call(
        functools.partial(scores_kernel, distances, split),
        out_shape=(shape,) * len(distances),
        in_specs=[VMEM] * (2 + len(pieces)),
        out_specs=(VMEM,) * len(distances),
        compiler_params=limit(12),
        name="scores",
    )(kept(decoder), kept(own_facts), *pieces)


def gradients_kernel(distances, own_facts, *refs):
    pieces, refs = refs[: 2 * len(distances)], refs[2 * len(distances) :]
    total = refs[-1]
    facts = facts_of(distances, own_facts, pieces)
    for columns, part in gradient_blocks(facts, pieces, total.shape[1]):
        total[:, columns] = part if len(refs) == 1 else refs[0][:, columns] + part


def gradients_of(distances, pairs, own_facts, shape, total=None):
    operands = [kept(own_facts)] + [kept(piece) for pair in pairs for piece in pair]
    operands += [] if total is None else [kept(total)]
    return pl.pallas_call(
        functools.partial(gradients_kernel, distances),
        out_shape=pltpu.VMEM(shape, jnp.float32),
        in_specs=[VMEM] * len(operands),
        out_specs=VMEM,
        input_output_aliases={} if total is None else {len(operands) - 1: 0},
        compiler_params=limit(16),
        name="gradients",
    )(*operands)


def last_gradients_kernel(left, right, total, out, rounded, sems):
    copies = []
    facts = [last_facts_in(left)]
    for columns, part in gradient_blocks(facts, (left, right), out.shape[1]):
        rounded[:, columns] = (total[:, columns] + part).astype(out.dtype)
        copies.append(
            pltpu.make_async_copy(
                rounded.at[:, columns], out.at[:, columns], sems.at[len(copies)]
            )
        )
        copies[-1].start()
    for copy in copies:
        copy.wait()


def last_gradients(pair, total):
    return pl.pallas_call(
        last_gradients_kernel,
        out_shape=jax.ShapeDtypeStruct(total.shape, jnp.bfloat16),
        in_specs=[VMEM] * 3,
        out_specs=ANY,
        scratch_shapes=[
            pltpu.VMEM(total.shape, jnp.bfloat16),
            pltpu.SemaphoreType.DMA((total.shape[1] // 256,)),
        ],
        compiler_params=limit(16),
        name="last_gradients",
    )(kept(pair[0]), kept(pair[1]), kept(total))


def stamp_kernel(onward, back, for_onward, for_back, onward_out, back_out, rows, sems):
    start = onward.shape[0] - FACTS
    targets = (onward_out, back_out)
    for i, piece in enumerate((onward, back)):
        pltpu.make_async_copy(
            piece.at[start : start + 16, :], rows.at[i], sems.at[i]
        ).start()
    for i, values in enumerate((for_onward, for_back)):
        pltpu.make_async_copy(
            onward.at[start : start + 16, :], rows.at[i], sems.at[i]
        ).wait()
        value = values[:KPB]
        high = value.astype(jnp.bfloat16).astype(jnp.float32)
        low = value - high
        facts = rows[i].astype(jnp.float32)[2 * KPB :]
        rows[i] = jnp.concatenate([high, low, facts], axis=0).astype(jnp.bfloat16)
        pltpu.make_async_copy(
            rows.at[i], targets[i].at[start : start + 16, :], sems.at[2 + i]
        ).start()
    for i in range(2):
        pltpu.make_async_copy(
            rows.at[i], targets[i].at[start : start + 16, :], sems.at[2 + i]
        ).wait()


def stamp(pieces, values):
    return pl.pallas_call(
        stamp_kernel,
        out_shape=tuple(pltpu.VMEM(piece.shape, piece.dtype) for piece in pieces),
        in_specs=[ANY, ANY, VMEM, VMEM],
        out_specs=(ANY, ANY),
        scratch_shapes=[
            pltpu.VMEM((2, 16, 128), jnp.bfloat16),
            pltpu.SemaphoreType.DMA((4,)),
        ],
        input_output_aliases={0: 0, 1: 1},
        compiler_params=limit(4),
        name="stamp",
    )(*[kept(piece) for piece in pieces], *[kept(value) for value in values])


def unpack_kernel(owners, slots, own, onward, back, second, third, opposite, out):
    owner = slots[...] // BLK_DEV
    start = onward.shape[0] - FACTS
    way = 1 - 2 * lax.axis_index("width")
    returned = [(0, own[...])]
    for distance, piece in ((-1, onward), (1, back)):
        rows = piece[start : start + 16, :].astype(jnp.float32)
        returned.append((distance, rows[:KPB] + rows[KPB : 2 * KPB]))
    returned += [(2 * way, second[...]), (3 * way, third[...]), (4, opposite[...])]
    mine = [owner == peer_at(distance, owners) for distance, _ in returned]
    for k in range(KPB):
        total = jnp.zeros(owner.shape, jnp.float32)
        for here, (_, values) in zip(mine, returned):
            total = jnp.where(here, values[k : k + 1, :], total)
        out[pl.ds(k, ACT, stride=KPB), :] = total


def unpack(slots, *returned):
    tok_rows = slots.shape[1]
    return pl.pallas_call(
        functools.partial(unpack_kernel, lax.axis_size("dp")),
        out_shape=pltpu.VMEM((ACT * KPB, tok_rows), jnp.float32),
        in_specs=[VMEM] * (1 + len(returned)),
        out_specs=VMEM,
        compiler_params=limit(4),
        name="unpack",
    )(kept(slots), *[kept(x) for x in returned])


def every_owner(decoder, grad_out, active_blocks, feature_idx, acts, block_slot):
    tok_rows = grad_out.shape[0]
    owners = lax.axis_size("dp")
    ring = ring_of(owners)

    def shift(x, by):
        pairs = [(ring[i], ring[(i + by) % owners]) for i in range(owners)]
        return lax.ppermute(x, "dp", pairs)

    def hop(pieces):
        left, right = pieces
        return shift(left, 1), shift(right, -1)

    def crossed(pieces):
        right, left = pieces
        return shift(right, 1), shift(left, -1)

    def other_core(x):
        return lax.ppermute(x, "width", ((0, 1), (1, 0)))

    def return_by(distance, x):
        pairs = []
        for i in range(owners):
            pairs.append((2 * ring[i], 2 * ring[(i - distance) % owners]))
            pairs.append((2 * ring[i] + 1, 2 * ring[(i + distance) % owners] + 1))
        return lax.ppermute(x, ("dp", "width"), pairs)

    first_left, first_right, left, right, own_facts, slots = prepare(
        block_slot, active_blocks, feature_idx, acts, grad_out, owners
    )
    first_1 = hop((first_left, first_right))
    second_1 = crossed((right, left))
    decoder = fetch(decoder)
    first_1, decoder = lax.optimization_barrier((first_1, decoder))
    first_2 = hop(first_1)
    second_2 = crossed(second_1)
    pairs = [(first_left, first_right), (first_1[0], second_1[0]), (second_1[1], first_1[1])]
    distances = (0, -1, 1)
    own, onward, back = scores_of(distances, pairs, decoder, own_facts)
    total = gradients_of(distances, pairs, own_facts, decoder.shape)
    first_3 = hop(first_2)
    second_2 = stamp(second_2, (back, onward))
    second_3 = crossed(second_2)
    pairs = [(first_2[0], second_2[0]), (second_2[1], first_2[1])]
    mine, others = scores_of((-2, 2), pairs, decoder, own_facts, True)
    total = gradients_of((-2, 2), pairs, own_facts, decoder.shape, total)
    second = mine + other_core(others)
    total, first_3, second = lax.optimization_barrier((total, first_3, second))
    second = return_by(2, jnp.concatenate([second, jnp.zeros((16, 128), jnp.float32)]))[:8]
    first_4 = hop(first_3)
    pairs = [(first_3[0], second_3[0]), (second_3[1], first_3[1])]
    mine, others = scores_of((-3, 3), pairs, decoder, own_facts, True)
    total = gradients_of((-3, 3), pairs, own_facts, decoder.shape, total)
    third = mine + other_core(others)
    total, third = lax.optimization_barrier((total, third))
    third = return_by(3, third)
    total, first_4 = lax.optimization_barrier((total, first_4))
    (opposite,) = scores_of((4,), [first_4], decoder, own_facts)
    opposite = shift(opposite, -owners // 2)
    total, third = lax.optimization_barrier((total, third))
    decoder_grad = last_gradients(first_4, total)
    decoder_grad, opposite = lax.optimization_barrier((decoder_grad, opposite))
    act_grad = unpack(slots, own, *second_3, second, third, opposite)
    act_grad = act_grad + other_core(act_grad)
    return (decoder_grad, act_grad.T)


def send_back(picked):
    return lax.all_to_all(picked, "dp", split_axis=1, concat_axis=1, tiled=True)


def pack_slots(grad_out, target, slots_all, pair_coeffs, pair_columns, source_row):
    slot_row = jnp.zeros((slots_all,), jnp.int32).at[target].set(source_row)
    used = jnp.zeros((slots_all,), jnp.bool_).at[target].set(True)
    send_rows = jnp.where(used[:, None], grad_out[slot_row], jnp.zeros((), grad_out.dtype))
    send_acts = jnp.zeros((slots_all, KPB), pair_coeffs.dtype).at[target].set(pair_coeffs)
    send_cols = jnp.zeros((slots_all, KPB), jnp.int32).at[target].set(pair_columns)
    return (send_rows, send_acts, send_cols)


def some_owners(decoder, grad_out, active_blocks, feature_idx, acts, block_slot):
    tok_rows, half_width = grad_out.shape
    owners = lax.axis_size("dp")
    mean_load = tok_rows * ACT // owners
    owner_cap = mean_load + min(mean_load // 2, tok_rows - mean_load)
    block_cap = (owner_cap + 2) // 3
    block_ids = active_blocks.reshape(-1)
    pair_count = block_ids.shape[0]
    table_pos = jnp.arange(block_slot.shape[0], dtype=jnp.int32)
    slot_of = jnp.sum(
        jnp.where(block_ids[:, None] == table_pos[None, :], block_slot[None, :], 0), axis=1
    )
    pair_pos = jnp.arange(pair_count, dtype=jnp.int32)
    source_row = pair_pos // ACT
    pair_coeffs = acts.reshape(pair_count, KPB)
    pair_feats = feature_idx.reshape(pair_count, KPB)
    earlier = (block_ids[:, None] == block_ids[None, :]) & (pair_pos[None, :] < pair_pos[:, None])
    position = jnp.sum(earlier.astype(jnp.int32), axis=1)
    slot_cols = owners * block_cap
    target = slot_of % BLK_DEV * slot_cols + slot_of // BLK_DEV * block_cap + position
    slots_all = BLK_DEV * slot_cols
    send_rows, send_acts, send_cols = pack_slots(
        grad_out, target, slots_all, pair_coeffs, pair_feats, source_row
    )
    rows, coeffs, feature_pos = (
        lax.all_to_all(
            send_rows.reshape(BLK_DEV, slot_cols, half_width),
            "dp",
            split_axis=1,
            concat_axis=1,
            tiled=True,
        ),
        lax.all_to_all(
            send_acts.reshape(BLK_DEV, slot_cols, KPB),
            "dp",
            split_axis=1,
            concat_axis=1,
            tiled=True,
        ),
        lax.all_to_all(
            send_cols.reshape(BLK_DEV, slot_cols, KPB),
            "dp",
            split_axis=1,
            concat_axis=1,
            tiled=True,
        ),
    )
    weights = decoder.reshape(BLK_DEV, BW, half_width)
    scores = jnp.einsum("bnd,bfd->bnf", rows, weights, preferred_element_type=jnp.float32)
    picked = jnp.take_along_axis(scores, feature_pos, axis=2)
    returned = send_back(picked)
    feature_axis = jnp.arange(BW, dtype=jnp.int32)
    matches = feature_pos[..., None] == feature_axis
    dense = jnp.sum(jnp.where(matches, coeffs[..., None].astype(jnp.float32), 0.0), axis=2).astype(
        jnp.bfloat16
    )
    grads = jnp.einsum("bnf,bnd->bfd", dense, rows, preferred_element_type=jnp.float32)
    decoder_grad = grads.astype(jnp.bfloat16).reshape(BLK_DEV * BW, half_width)
    pair_vals = returned.reshape(slots_all, KPB)[target]
    act_grad = pair_vals.reshape(tok_rows, ACT * KPB)
    act_grad = lax.psum(act_grad, "width")
    return (decoder_grad, act_grad)


def per_device(*args):
    if lax.axis_size("dp") == ACT:
        return every_owner(*args)
    return some_owners(*args)


def solution(mesh):
    in_specs = (
        P(("groups", "dp"), "width"),
        P(("groups", "dp"), "width"),
        P(("groups", "dp"), None),
        P(("groups", "dp"), None),
        P(("groups", "dp"), None),
        P("groups"),
    )
    out_specs = (P(("groups", "dp"), "width"), P(("groups", "dp"), None))
    return jax.shard_map(
        per_device, mesh=mesh, in_specs=in_specs, out_specs=out_specs, check_vma=False
    )
```

```python
import functools

import jax
import jax.numpy as jnp
from jax import lax
from jax.experimental import pallas as pl
from jax.experimental.pallas import tpu as pltpu
from jax.sharding import PartitionSpec as P

BW = 128
BLK_DEV = 4
ACT = 8
KPB = 4
SMEM = pl.BlockSpec(memory_space=pltpu.SMEM)
VMEM = pl.BlockSpec(memory_space=pltpu.VMEM)
ANY = pl.BlockSpec(memory_space=pl.ANY)
HBM = pl.BlockSpec(memory_space=pltpu.HBM)


def limit(mebibytes):
    return pltpu.CompilerParams(vmem_limit_bytes=mebibytes * 2**20)


def kept(x):
    return pltpu.with_memory_space_constraint(x, pltpu.VMEM)


def far(x):
    return pltpu.with_memory_space_constraint(x, pltpu.HBM)


def ring_of(owners):
    return [0] + list(range(1, owners, 2)) + list(range(owners - 2, 0, -2))


def peer_at(distance, owners):
    me = lax.axis_index("dp")
    half_ring = owners // 2
    up = lax.rem(me, 2) == 1
    place = jnp.where(up, lax.div(me, 2) + 1, lax.rem(owners - lax.div(me, 2), owners))
    at = lax.rem(place + owners + distance, owners)
    other = lax.rem(2 * (owners - at), 2 * owners)
    return jnp.where((at > 0) & (at <= half_ring), 2 * at - 1, other)


ROW_SHIFT = BLK_DEV * BW // 2
FACTS = ACT // 2 * 2 * KPB
LAST_FACTS = 16


def facts_for(owner_id, owner, first_row, feats, acts):
    mine = owner == owner_id
    rows = [
        jnp.sum(jnp.where(mine, first_row + feats[k], 0.0), axis=0, keepdims=True) - ROW_SHIFT
        for k in range(KPB)
    ]
    values = [
        jnp.sum(jnp.where(mine, acts[k], 0.0), axis=0, keepdims=True) for k in range(KPB)
    ]
    return jnp.concatenate(rows + values, axis=0)


def prepare_kernel(owners, *refs):
    sources, refs = refs[:5], refs[5:]
    outs, refs = refs[:6], refs[6:]
    first_left, first_right, left, right, own_facts, slots = outs
    block_slot, active, feats, acts, halves, wide_feats, wide_acts, sems = refs
    cut = halves.shape[2]
    copies = []
    for source, target in zip(sources[:4], (block_slot, active, feats, acts)):
        copies.append(pltpu.make_async_copy(source, target, sems.at[len(copies)]))
    for side in range(2):
        copies.append(
            pltpu.make_async_copy(
                sources[4].at[:, side * cut : (side + 1) * cut],
                halves.at[side],
                sems.at[len(copies)],
            )
        )
    for copy in copies:
        copy.start()
    for copy in copies[:4]:
        copy.wait()
    named = active[...]
    slot = jnp.zeros_like(named)
    for block in range(block_slot.shape[0]):
        slot = jnp.where(named == block, block_slot[block], slot)
    slots[...] = slot
    wide_feats[...] = feats[...].astype(jnp.float32)
    wide_acts[...] = acts[...].astype(jnp.float32)
    features = [wide_feats[pl.ds(k, ACT, stride=KPB), :] for k in range(KPB)]
    values = [wide_acts[pl.ds(k, ACT, stride=KPB), :] for k in range(KPB)]
    first_row = (slot % BLK_DEV * BW).astype(jnp.float32)

    def facts(distance):
        return facts_for(
            peer_at(distance, owners), slot // BLK_DEV, first_row, features, values
        )

    def store_facts(target, blocks):
        rows = jnp.concatenate(blocks, axis=0)
        target[target.shape[0] - rows.shape[0] :, :] = rows.astype(jnp.bfloat16)

    own_facts[...] = facts(0)
    opposite = facts(owners // 2)
    none = jnp.zeros_like(opposite)
    store_facts(first_left, [opposite, none])
    for target, sign in ((left, -1), (right, 1)):
        store_facts(target, [facts(sign * d) for d in range(1, owners // 2)] + [none])
    tok_rows = halves.shape[1]
    for side, targets in ((0, (first_left, left)), (1, (first_right, right))):
        copies[4 + side].wait()
        for j in range(cut // 128):
            part = halves[side, :, j * 128 : (j + 1) * 128]
            for target in targets:
                target[j * tok_rows : (j + 1) * tok_rows, :] = part


def prepare(block_slot, active_blocks, feature_idx, acts, grad_out, owners):
    tok_rows, width = grad_out.shape
    plain = width // 256 * tok_rows

    def piece(extra):
        return pltpu.VMEM((plain + extra, 128), grad_out.dtype)

    return pl.pallas_call(
        functools.partial(prepare_kernel, owners),
        out_shape=(
            piece(LAST_FACTS),
            piece(0),
            piece(FACTS),
            piece(FACTS),
            pltpu.VMEM((2 * KPB, tok_rows), jnp.float32),
            pltpu.VMEM((ACT, tok_rows), jnp.int32),
        ),
        in_specs=[HBM] * 5,
        out_specs=(VMEM,) * 6,
        scratch_shapes=[
            pltpu.SMEM(block_slot.shape, jnp.int32),
            pltpu.VMEM((ACT, tok_rows), jnp.int32),
            pltpu.VMEM((ACT * KPB, tok_rows), jnp.int32),
            pltpu.VMEM((ACT * KPB, tok_rows), acts.dtype),
            pltpu.VMEM((2, tok_rows, width // 2), grad_out.dtype),
            pltpu.VMEM((ACT * KPB, tok_rows), jnp.float32),
            pltpu.VMEM((ACT * KPB, tok_rows), jnp.float32),
            pltpu.SemaphoreType.DMA((6,)),
        ],
        compiler_params=limit(8),
        name="prepare",
    )(far(block_slot), far(active_blocks.T), far(feature_idx.T), far(acts.T), far(grad_out))


def fetch_kernel(source, target, sem):
    copy = pltpu.make_async_copy(source, target, sem)
    copy.start()
    copy.wait()


def fetch(x):
    return pl.pallas_call(
        fetch_kernel,
        out_shape=pltpu.VMEM(x.shape, x.dtype),
        in_specs=[HBM],
        out_specs=VMEM,
        scratch_shapes=[pltpu.SemaphoreType.DMA],
        compiler_params=limit(8),
        name="fetch",
    )(far(x))


def block_and_rows(here):
    at_row = here[:KPB].astype(jnp.int32) + ROW_SHIFT
    return at_row[:1] // BW, at_row % BW


def row_axis_of(tok_rows):
    return lax.broadcasted_iota(jnp.int32, (BW, tok_rows), 0)


def coefficients(here):
    block, feats = block_and_rows(here)
    row_axis = row_axis_of(here.shape[1])
    dense = jnp.zeros(row_axis.shape, jnp.float32)
    for k in range(KPB):
        dense = jnp.where(row_axis == feats[k : k + 1], here[KPB + k : KPB + k + 1], dense)
    parts = [jnp.where(block == b, dense, 0.0) for b in range(BLK_DEV)]
    return jnp.concatenate(parts, axis=0).astype(jnp.bfloat16)


def pick(scores, here):
    block, feats = block_and_rows(here)
    row_axis = row_axis_of(here.shape[1])
    mine = scores[:BW]
    for b in range(1, BLK_DEV):
        mine = jnp.where(block == b, scores[b * BW : (b + 1) * BW], mine)
    return [
        jnp.sum(jnp.where(row_axis == feats[k : k + 1], mine, 0.0), axis=0, keepdims=True)
        for k in range(KPB)
    ]


def facts_in(piece, distance, tok_rows):
    facts = piece[piece.shape[0] - FACTS :, :].astype(jnp.float32)
    return facts[(abs(distance) - 1) * 2 * KPB : abs(distance) * 2 * KPB]


def columns_of(pieces, tok_rows, parts):
    rows = [
        jnp.concatenate([piece[j * tok_rows : (j + 1) * tok_rows, :] for j in parts], axis=1)
        for piece in pieces
    ]
    return jnp.concatenate(rows, axis=0) if len(rows) > 1 else rows[0]


def picks_of(facts, decoder, pieces):
    picks = []
    tok_rows = facts[0].shape[1]
    cut = decoder.shape[1] // 2
    for first in range(0, len(facts), 2):
        count = min(2, len(facts) - first)
        scores = None
        for side in range(2):
            part = lax.dot_general(
                decoder[:, side * cut : (side + 1) * cut],
                columns_of(
                    pieces[2 * first + side : 2 * (first + count) : 2],
                    tok_rows,
                    range(cut // 128),
                ),
                (((1,), (1,)), ((), ())),
                preferred_element_type=jnp.float32,
            )
            scores = part if scores is None else scores + part
        for i in range(first, first + count):
            here = scores[:, (i - first) * tok_rows : (i - first + 1) * tok_rows]
            picks.append(jnp.concatenate(pick(here, facts[i]) * 2, axis=0))
    return picks


def gradient_blocks(facts, pieces, width):
    tok_rows = facts[0].shape[1]
    cut = width // 2
    dense = jnp.concatenate([coefficients(here) for here in facts], axis=1)
    for side in range(2):
        for j in range(0, cut // 128, 2):
            rows = columns_of(pieces[side::2], tok_rows, (j, j + 1))
            part = jnp.dot(dense, rows, preferred_element_type=jnp.float32)
            yield slice(side * cut + j * 128, side * cut + (j + 2) * 128), part


def last_facts_in(piece):
    return piece[piece.shape[0] - LAST_FACTS :, :].astype(jnp.float32)[: 2 * KPB]


def facts_of(distances, own_facts, pieces):
    facts = []
    for i, d in enumerate(distances):
        if d == 0:
            facts.append(own_facts[...])
        elif d == 4:
            facts.append(last_facts_in(pieces[2 * i]))
        else:
            facts.append(facts_in(pieces[2 * i + (d < 0)], d, own_facts.shape[1]))
    return facts


def scores_kernel(distances, split, decoder, own_facts, *refs):
    pieces, picked = refs[: 2 * len(distances)], refs[2 * len(distances) :]
    picks = picks_of(facts_of(distances, own_facts, pieces), decoder, pieces)
    if split:
        first = lax.axis_index("width") == 0
        picks = [jnp.where(first, *picks), jnp.where(first, *picks[::-1])]
    for target, values in zip(picked, picks):
        target[...] = values


def scores_of(distances, pairs, decoder, own_facts, split=False):
    pieces = [kept(piece) for pair in pairs for piece in pair]
    shape = pltpu.VMEM(own_facts.shape, jnp.float32)
    return pl.pallas_call(
        functools.partial(scores_kernel, distances, split),
        out_shape=(shape,) * len(distances),
        in_specs=[VMEM] * (2 + len(pieces)),
        out_specs=(VMEM,) * len(distances),
        compiler_params=limit(12),
        name="scores",
    )(kept(decoder), kept(own_facts), *pieces)


def gradients_kernel(distances, own_facts, *refs):
    pieces, refs = refs[: 2 * len(distances)], refs[2 * len(distances) :]
    total = refs[-1]
    facts = facts_of(distances, own_facts, pieces)
    for columns, part in gradient_blocks(facts, pieces, total.shape[1]):
        total[:, columns] = part if len(refs) == 1 else refs[0][:, columns] + part


def gradients_of(distances, pairs, own_facts, shape, total=None):
    operands = [kept(own_facts)] + [kept(piece) for pair in pairs for piece in pair]
    operands += [] if total is None else [kept(total)]
    return pl.pallas_call(
        functools.partial(gradients_kernel, distances),
        out_shape=pltpu.VMEM(shape, jnp.float32),
        in_specs=[VMEM] * len(operands),
        out_specs=VMEM,
        input_output_aliases={} if total is None else {len(operands) - 1: 0},
        compiler_params=limit(16),
        name="gradients",
    )(*operands)


def last_gradients_kernel(left, right, total, out, rounded, sems):
    copies = []
    facts = [last_facts_in(left)]
    for columns, part in gradient_blocks(facts, (left, right), out.shape[1]):
        rounded[:, columns] = (total[:, columns] + part).astype(out.dtype)
        copies.append(
            pltpu.make_async_copy(
                rounded.at[:, columns], out.at[:, columns], sems.at[len(copies)]
            )
        )
        copies[-1].start()
    for copy in copies:
        copy.wait()


def last_gradients(pair, total):
    return pl.pallas_call(
        last_gradients_kernel,
        out_shape=jax.ShapeDtypeStruct(total.shape, jnp.bfloat16),
        in_specs=[VMEM] * 3,
        out_specs=ANY,
        scratch_shapes=[
            pltpu.VMEM(total.shape, jnp.bfloat16),
            pltpu.SemaphoreType.DMA((total.shape[1] // 256,)),
        ],
        compiler_params=limit(16),
        name="last_gradients",
    )(kept(pair[0]), kept(pair[1]), kept(total))


def stamp_kernel(onward, back, for_onward, for_back, onward_out, back_out, rows, sems):
    start = onward.shape[0] - FACTS
    targets = (onward_out, back_out)
    for i, piece in enumerate((onward, back)):
        pltpu.make_async_copy(
            piece.at[start : start + 16, :], rows.at[i], sems.at[i]
        ).start()
    for i, values in enumerate((for_onward, for_back)):
        pltpu.make_async_copy(
            onward.at[start : start + 16, :], rows.at[i], sems.at[i]
        ).wait()
        value = values[:KPB]
        high = value.astype(jnp.bfloat16).astype(jnp.float32)
        low = value - high
        facts = rows[i].astype(jnp.float32)[2 * KPB :]
        rows[i] = jnp.concatenate([high, low, facts], axis=0).astype(jnp.bfloat16)
        pltpu.make_async_copy(
            rows.at[i], targets[i].at[start : start + 16, :], sems.at[2 + i]
        ).start()
    for i in range(2):
        pltpu.make_async_copy(
            rows.at[i], targets[i].at[start : start + 16, :], sems.at[2 + i]
        ).wait()


def stamp(pieces, values):
    return pl.pallas_call(
        stamp_kernel,
        out_shape=tuple(pltpu.VMEM(piece.shape, piece.dtype) for piece in pieces),
        in_specs=[ANY, ANY, VMEM, VMEM],
        out_specs=(ANY, ANY),
        scratch_shapes=[
            pltpu.VMEM((2, 16, 128), jnp.bfloat16),
            pltpu.SemaphoreType.DMA((4,)),
        ],
        input_output_aliases={0: 0, 1: 1},
        compiler_params=limit(4),
        name="stamp",
    )(*[kept(piece) for piece in pieces], *[kept(value) for value in values])


def unpack_kernel(owners, slots, own, onward, back, second, third, opposite, out):
    owner = slots[...] // BLK_DEV
    start = onward.shape[0] - FACTS
    way = 1 - 2 * lax.axis_index("width")
    returned = [(0, own[...])]
    for distance, piece in ((-1, onward), (1, back)):
        rows = piece[start : start + 16, :].astype(jnp.float32)
        returned.append((distance, rows[:KPB] + rows[KPB : 2 * KPB]))
    returned += [(2 * way, second[...]), (3 * way, third[...]), (4, opposite[...])]
    mine = [owner == peer_at(distance, owners) for distance, _ in returned]
    for k in range(KPB):
        total = jnp.zeros(owner.shape, jnp.float32)
        for here, (_, values) in zip(mine, returned):
            total = jnp.where(here, values[k : k + 1, :], total)
        out[pl.ds(k, ACT, stride=KPB), :] = total


def unpack(slots, *returned):
    tok_rows = slots.shape[1]
    return pl.pallas_call(
        functools.partial(unpack_kernel, lax.axis_size("dp")),
        out_shape=pltpu.VMEM((ACT * KPB, tok_rows), jnp.float32),
        in_specs=[VMEM] * (1 + len(returned)),
        out_specs=VMEM,
        compiler_params=limit(4),
        name="unpack",
    )(kept(slots), *[kept(x) for x in returned])


def every_owner(decoder, grad_out, active_blocks, feature_idx, acts, block_slot):
    tok_rows = grad_out.shape[0]
    owners = lax.axis_size("dp")
    ring = ring_of(owners)

    def shift(x, by):
        pairs = [(ring[i], ring[(i + by) % owners]) for i in range(owners)]
        return lax.ppermute(x, "dp", pairs)

    def hop(pieces):
        left, right = pieces
        return shift(left, 1), shift(right, -1)

    def crossed(pieces):
        right, left = pieces
        return shift(right, 1), shift(left, -1)

    def other_core(x):
        return lax.ppermute(x, "width", ((0, 1), (1, 0)))

    def return_by(distance, x):
        pairs = []
        for i in range(owners):
            pairs.append((2 * ring[i], 2 * ring[(i - distance) % owners]))
            pairs.append((2 * ring[i] + 1, 2 * ring[(i + distance) % owners] + 1))
        return lax.ppermute(x, ("dp", "width"), pairs)

    first_left, first_right, left, right, own_facts, slots = prepare(
        block_slot, active_blocks, feature_idx, acts, grad_out, owners
    )
    first_1 = hop((first_left, first_right))
    second_1 = crossed((right, left))
    decoder = fetch(decoder)
    first_1, decoder = lax.optimization_barrier((first_1, decoder))
    first_2 = hop(first_1)
    second_2 = crossed(second_1)
    pairs = [(first_left, first_right), (first_1[0], second_1[0]), (second_1[1], first_1[1])]
    distances = (0, -1, 1)
    own, onward, back = scores_of(distances, pairs, decoder, own_facts)
    total = gradients_of(distances, pairs, own_facts, decoder.shape)
    first_3 = hop(first_2)
    second_2 = stamp(second_2, (back, onward))
    second_3 = crossed(second_2)
    pairs = [(first_2[0], second_2[0]), (second_2[1], first_2[1])]
    mine, others = scores_of((-2, 2), pairs, decoder, own_facts, True)
    total = gradients_of((-2, 2), pairs, own_facts, decoder.shape, total)
    second = mine + other_core(others)
    total, first_3, second = lax.optimization_barrier((total, first_3, second))
    second = return_by(2, jnp.concatenate([second, jnp.zeros((16, 128), jnp.float32)]))[:8]
    first_4 = hop(first_3)
    pairs = [(first_3[0], second_3[0]), (second_3[1], first_3[1])]
    mine, others = scores_of((-3, 3), pairs, decoder, own_facts, True)
    total = gradients_of((-3, 3), pairs, own_facts, decoder.shape, total)
    third = mine + other_core(others)
    total, third = lax.optimization_barrier((total, third))
    third = return_by(3, third)
    total, first_4 = lax.optimization_barrier((total, first_4))
    (opposite,) = scores_of((4,), [first_4], decoder, own_facts)
    opposite = shift(opposite, -owners // 2)
    total, third = lax.optimization_barrier((total, third))
    decoder_grad = last_gradients(first_4, total)
    decoder_grad, opposite = lax.optimization_barrier((decoder_grad, opposite))
    act_grad = unpack(slots, own, *second_3, second, third, opposite)
    act_grad = act_grad + other_core(act_grad)
    return (decoder_grad, act_grad.T)


def send_back(picked):
    return lax.all_to_all(picked, "dp", split_axis=1, concat_axis=1, tiled=True)


def pack_slots(grad_out, target, slots_all, pair_coeffs, pair_columns, source_row):
    slot_row = jnp.zeros((slots_all,), jnp.int32).at[target].set(source_row)
    used = jnp.zeros((slots_all,), jnp.bool_).at[target].set(True)
    send_rows = jnp.where(used[:, None], grad_out[slot_row], jnp.zeros((), grad_out.dtype))
    send_acts = jnp.zeros((slots_all, KPB), pair_coeffs.dtype).at[target].set(pair_coeffs)
    send_cols = jnp.zeros((slots_all, KPB), jnp.int32).at[target].set(pair_columns)
    return (send_rows, send_acts, send_cols)


def some_owners(decoder, grad_out, active_blocks, feature_idx, acts, block_slot):
    tok_rows, half_width = grad_out.shape
    owners = lax.axis_size("dp")
    mean_load = tok_rows * ACT // owners
    owner_cap = mean_load + min(mean_load // 2, tok_rows - mean_load)
    block_cap = (owner_cap + 2) // 3
    block_ids = active_blocks.reshape(-1)
    pair_count = block_ids.shape[0]
    table_pos = jnp.arange(block_slot.shape[0], dtype=jnp.int32)
    slot_of = jnp.sum(
        jnp.where(block_ids[:, None] == table_pos[None, :], block_slot[None, :], 0), axis=1
    )
    pair_pos = jnp.arange(pair_count, dtype=jnp.int32)
    source_row = pair_pos // ACT
    pair_coeffs = acts.reshape(pair_count, KPB)
    pair_feats = feature_idx.reshape(pair_count, KPB)
    earlier = (block_ids[:, None] == block_ids[None, :]) & (pair_pos[None, :] < pair_pos[:, None])
    position = jnp.sum(earlier.astype(jnp.int32), axis=1)
    slot_cols = owners * block_cap
    target = slot_of % BLK_DEV * slot_cols + slot_of // BLK_DEV * block_cap + position
    slots_all = BLK_DEV * slot_cols
    send_rows, send_acts, send_cols = pack_slots(
        grad_out, target, slots_all, pair_coeffs, pair_feats, source_row
    )
    rows, coeffs, feature_pos = (
        lax.all_to_all(
            send_rows.reshape(BLK_DEV, slot_cols, half_width),
            "dp",
            split_axis=1,
            concat_axis=1,
            tiled=True,
        ),
        lax.all_to_all(
            send_acts.reshape(BLK_DEV, slot_cols, KPB),
            "dp",
            split_axis=1,
            concat_axis=1,
            tiled=True,
        ),
        lax.all_to_all(
            send_cols.reshape(BLK_DEV, slot_cols, KPB),
            "dp",
            split_axis=1,
            concat_axis=1,
            tiled=True,
        ),
    )
    weights = decoder.reshape(BLK_DEV, BW, half_width)
    scores = jnp.einsum("bnd,bfd->bnf", rows, weights, preferred_element_type=jnp.float32)
    picked = jnp.take_along_axis(scores, feature_pos, axis=2)
    returned = send_back(picked)
    feature_axis = jnp.arange(BW, dtype=jnp.int32)
    matches = feature_pos[..., None] == feature_axis
    dense = jnp.sum(jnp.where(matches, coeffs[..., None].astype(jnp.float32), 0.0), axis=2).astype(
        jnp.bfloat16
    )
    grads = jnp.einsum("bnf,bnd->bfd", dense, rows, preferred_element_type=jnp.float32)
    decoder_grad = grads.astype(jnp.bfloat16).reshape(BLK_DEV * BW, half_width)
    pair_vals = returned.reshape(slots_all, KPB)[target]
    act_grad = pair_vals.reshape(tok_rows, ACT * KPB)
    act_grad = lax.psum(act_grad, "width")
    return (decoder_grad, act_grad)


def per_device(*args):
    if lax.axis_size("dp") == ACT:
        return every_owner(*args)
    return some_owners(*args)


def solution(mesh):
    in_specs = (
        P(("groups", "dp"), "width"),
        P(("groups", "dp"), "width"),
        P(("groups", "dp"), None),
        P(("groups", "dp"), None),
        P(("groups", "dp"), None),
        P("groups"),
    )
    out_specs = (P(("groups", "dp"), "width"), P(("groups", "dp"), None))
    return jax.shard_map(
        per_device, mesh=mesh, in_specs=in_specs, out_specs=out_specs, check_vma=False
    )
```
